32 devices in a mesh: grp: 2 (over y), seq: 16 (over z, x, core).
Axes of the slice: x: 2, y: 2, z: 4, core: 2. Of those that a mesh axis runs over, the one named last changes fastest.
Arguments:
- hidden_in: bfloat16 [2, 2048, 1536], P('grp', 'seq'), may hold values from -6 to 6
- lengths: int32 [2], P('grp'), may hold values from 1921 to 2048, as said below
- attn_gain: bfloat16 [1536], P(('grp', 'seq')), may hold values from 0.5 to 1.5
- w_query: bfloat16 [1536, 1536], P(('grp', 'seq')), may hold values from -0.3125 to 0.3125
- w_key: bfloat16 [1536, 768], P(('grp', 'seq')), may hold values from -0.15625 to 0.15625
- w_value: bfloat16 [1536, 768], P(('grp', 'seq')), may hold values from -0.15625 to 0.15625
- w_out: bfloat16 [1536, 1536], P(('grp', 'seq')), may hold values from -0.625 to 0.625
- mlp_gain: bfloat16 [1536], P(('grp', 'seq')), may hold values from 0.5 to 1.5
- w_gate: bfloat16 [1536, 4096], P(('grp', 'seq')), may hold values from -0.15625 to 0.15625
- w_up: bfloat16 [1536, 4096], P(('grp', 'seq')), may hold values from -0.15625 to 0.15625
- w_down: bfloat16 [4096, 1536], P(('grp', 'seq')), may hold values from -0.09375 to 0.09375
- out_grad: bfloat16 [2, 2048, 1536], P('grp', 'seq'), may hold values from -6 to 6
Outputs:
- block_out: bfloat16 [2, 2048, 1536], P('grp', 'seq')
- input_grad: bfloat16 [2, 2048, 1536], P('grp', 'seq')
- attn_gain_grad: float32 [1536], P(('grp', 'seq'))
- w_query_grad: float32 [1536, 1536], P(('grp', 'seq'))
- w_key_grad: float32 [1536, 768], P(('grp', 'seq'))
- w_value_grad: float32 [1536, 768], P(('grp', 'seq'))
- w_out_grad: float32 [1536, 1536], P(('grp', 'seq'))
- mlp_gain_grad: float32 [1536], P(('grp', 'seq'))
- w_gate_grad: float32 [1536, 4096], P(('grp', 'seq'))
- w_up_grad: float32 [1536, 4096], P(('grp', 'seq'))
- w_down_grad: float32 [4096, 1536], P(('grp', 'seq'))
The draws below stay inside these ranges and needn't reach their ends.
Inputs may be any that keep to these rules, and one draw needn't show every extreme that they name: `lengths`: one sequence has all 2048 slots valid.
All inputs are finite; a program needn't handle non-finite values.
Results may differ from the reference program's by a relative error of at most 0.024.
Values may be sent and summed in bfloat16 or wider, within the bound.
A program may use at most 320 MiB of HBM per device.

```python
import math
import jax
import jax.numpy as jnp
from jax import lax

D = 1536
H = 16
KVH = 8
HD = 96
FF = 4096
TOK_DEV = 128
SEQLEN = 2048
GROUPS = 2


def draw_lengths(key, part):
    first_key, second_key = jax.random.split(jax.random.fold_in(key, 11))
    lowest = SEQLEN - TOK_DEV + 1
    drawn = jax.random.randint(first_key, (GROUPS,), lowest, SEQLEN + 1)
    order = jax.random.permutation(second_key, GROUPS)
    drawn = drawn.at[order[0]].set(SEQLEN)
    if GROUPS > 2:
        drawn = drawn.at[order[1]].set(lowest)
    return drawn.astype(jnp.int32)


def steps_of(own_key, shape, cuts, low, high):
    factor_of = 1.0
    for position, shards_of in cuts:
        heights = jax.random.uniform(jax.random.fold_in(jax.random.fold_in(own_key, 6), position), (shards_of,), jnp.float32, low / len(cuts), high / len(cuts))
        factor_of = factor_of * jnp.repeat(jnp.exp(heights), shape[position] // shards_of).reshape((-1,) + (1,) * (len(shape) - 1 - position))
    return factor_of


def gaussian(own_key, shape, deviation, bound, cuts=(), held_as=jnp.bfloat16):
    values = jax.random.normal(own_key, shape, jnp.float32) * deviation
    if len(cuts) > 0:
        values = steps_of(own_key, shape, cuts, -0.22, 0.18) * values
    return jnp.clip(values, min=-bound, max=bound).astype(held_as)


def setup_inputs(seed: int = 0) -> dict:
    arg_keys = jax.random.split(jax.random.key(seed), 13)
    hidden_in = gaussian(arg_keys[0], (GROUPS, SEQLEN, D), 1.0, 6.0, ((0, 2), (1, 16)))
    lengths = draw_lengths(jax.random.fold_in(arg_keys[12], 71), 0)
    attn_gain = jnp.clip(1.0 + 0.1 * jax.random.normal(arg_keys[2], (D,), jnp.float32), 0.5, 1.5).astype(jnp.bfloat16)
    w_query = gaussian(arg_keys[3], (D, D), (D // 4) ** -0.5, 0.3125, ((0, 32),))
    w_key = gaussian(arg_keys[4], (D, KVH * HD), D ** -0.5, 0.15625, ((0, 32),))
    w_value = gaussian(arg_keys[5], (D, KVH * HD), D ** -0.5, 0.15625, ((0, 32),))
    w_out = gaussian(arg_keys[6], (D, D), (D // 16) ** -0.5, 0.625, ((0, 32),))
    mlp_gain = jnp.clip(1.0 + 0.1 * jax.random.normal(arg_keys[7], (D,), jnp.float32), 0.5, 1.5).astype(jnp.bfloat16)
    w_gate = gaussian(arg_keys[8], (D, FF), D ** -0.5, 0.15625, ((0, 32),))
    w_up = gaussian(arg_keys[9], (D, FF), D ** -0.5, 0.15625, ((0, 32),))
    w_down = gaussian(arg_keys[10], (FF, D), FF ** -0.5, 0.09375, ((0, 32),))
    out_grad = gaussian(arg_keys[11], (GROUPS, SEQLEN, D), 1.0, 6.0, ((0, 2), (1, 16)))
    return dict(hidden_in=hidden_in, lengths=lengths, attn_gain=attn_gain, w_query=w_query, w_key=w_key, w_value=w_value, w_out=w_out, mlp_gain=mlp_gain, w_gate=w_gate, w_up=w_up, w_down=w_down, out_grad=out_grad)


@jax.custom_vjp
def low(v):
    return lax.optimization_barrier(v.astype(jnp.bfloat16)).astype(jnp.float32)

@jax.custom_vjp
def low_back(v):
    return v

def low_keep(v):
    return (low(v), None)

def low_pass(kept, grad):
    return (grad,)

def back_keep(v):
    return (v, None)

def back_low(kept, grad):
    return (low(grad),)
low.defvjp(low_keep, low_pass)
low_back.defvjp(back_keep, back_low)
epsilon = 1e-05
rope_base = 100000.0
neg_big = -1e+30
highest = lax.Precision.HIGHEST

def rope_tables(positions):
    half_dim = HD // 2
    frequency = jnp.exp(-math.log(rope_base) * (2.0 * jnp.arange(half_dim, dtype=jnp.float32) / HD))
    angles = positions.astype(jnp.float32)[:, None] * frequency[None, :]
    return (jnp.cos(angles), jnp.sin(angles))

def rotate(values, cosine, sine_tab):
    half_dim = values.shape[-1] // 2
    first_half = values[..., :half_dim]
    second_half = values[..., half_dim:]
    cos_wide = cosine[:, None, :]
    sin_wide = sine_tab[:, None, :]
    return jnp.concatenate([first_half * cos_wide - second_half * sin_wide, second_half * cos_wide + first_half * sin_wide], axis=-1)

def norm_scale(values):
    return lax.rsqrt(lax.optimization_barrier(jnp.mean(values * values, axis=-1, keepdims=True)) + epsilon)

def sequence_forward(tokens_in, length, params):
    attn_gain, w_query, w_key, w_value, w_out, mlp_gain, w_gate, w_up, w_down = params
    group_size = H // KVH
    score_scale = 1.0 / math.sqrt(HD)
    positions = jnp.arange(SEQLEN, dtype=jnp.int32)
    valid_rows = (positions < length).astype(jnp.float32)[:, None]
    cosine, sine_tab = rope_tables(positions)
    normed = low(tokens_in * norm_scale(tokens_in) * attn_gain)
    query_lin = low_back(jnp.dot(normed, w_query, precision=highest))
    key_lin = low_back(jnp.dot(normed, w_key, precision=highest))
    value_lin = low_back(jnp.dot(normed, w_value, precision=highest))
    queries = low(rotate(query_lin.reshape(SEQLEN, H, HD), cosine, sine_tab))
    key_rot = low(rotate(key_lin.reshape(SEQLEN, KVH, HD), cosine, sine_tab))
    values = low(value_lin).reshape(SEQLEN, KVH, HD)
    keys_wide = jnp.repeat(key_rot, group_size, axis=1)
    values_wide = jnp.repeat(values, group_size, axis=1)
    query_block = min(512, SEQLEN)
    key_pos = jnp.arange(SEQLEN, dtype=jnp.int32)

    def attend(element):
        query_part, offset = element
        query_pos = offset + jnp.arange(query_block, dtype=jnp.int32)
        scores = low_back(score_scale * jnp.einsum('thd,shd->hts', query_part, keys_wide, precision=highest))
        allowed = (key_pos[None, :] <= query_pos[:, None]) & (key_pos[None, :] < length)
        scores = jnp.where(allowed[None], scores, neg_big)
        log_total = jax.nn.logsumexp(scores, axis=-1, keepdims=True)
        weights = low(jnp.exp(scores - log_total))
        return jnp.einsum('hts,shd->thd', weights, values_wide, precision=highest)
    blocks = queries.reshape(SEQLEN // query_block, query_block, H, HD)
    offsets = jnp.arange(SEQLEN // query_block, dtype=jnp.int32) * query_block
    attended = lax.map(jax.checkpoint(attend), (blocks, offsets))
    attn_mix = low(low_back(attended.reshape(SEQLEN, H * HD)))
    hidden = tokens_in + low_back(jnp.dot(attn_mix, w_out, precision=highest))
    normed_mlp = low(hidden * norm_scale(hidden) * mlp_gain)
    gate_lin = low_back(jnp.dot(normed_mlp, w_gate, precision=highest))
    up_lin = low_back(jnp.dot(normed_mlp, w_up, precision=highest))
    inner_act = low(jax.nn.silu(gate_lin) * up_lin)
    branch = low_back(jnp.dot(inner_act, w_down, precision=highest))
    return valid_rows * (hidden + branch)

def reference(hidden_in, lengths, attn_gain, w_query, w_key, w_value, w_out, mlp_gain, w_gate, w_up, w_down, out_grad):
    params = tuple((weight.astype(jnp.float32) for weight in (attn_gain, w_query, w_key, w_value, w_out, mlp_gain, w_gate, w_up, w_down)))
    tokens_all = hidden_in.astype(jnp.float32)

    def whole_layer(tokens_arg, *param_list):

        def each_sequence(element):
            tokens_one, length_one = element
            return sequence_forward(tokens_one, length_one, param_list)
        return lax.map(each_sequence, (tokens_arg, lengths))
    outputs, pullback = jax.vjp(whole_layer, tokens_all, *params)
    gradients = pullback(out_grad.astype(jnp.float32))
    return (outputs.astype(jnp.bfloat16), gradients[0].astype(jnp.bfloat16), gradients[1], gradients[2], gradients[3], gradients[4], gradients[5], gradients[6], gradients[7], gradients[8], gradients[9])
```

```python
import math

import jax
import jax.numpy as jnp
from jax import lax
from jax.experimental import pallas as pl
from jax.experimental.pallas import tpu as pltpu
from jax.sharding import PartitionSpec as P

H = 16
KVH = 8
HD = 96
KBLK = 256


epsilon = 1e-05
rope_base = 100000.0
neg_big = -1e30


def rope_tables(positions):
    half_dim = HD // 2
    frequency = jnp.exp(-math.log(rope_base) * (2.0 * jnp.arange(half_dim, dtype=jnp.float32) / HD))
    angles = positions.astype(jnp.float32)[:, None] * frequency[None, :]
    return (jnp.cos(angles), jnp.sin(angles))


def rotate(values, cosine, sine_tab):
    half_dim = values.shape[-1] // 2
    first_half = values[..., :half_dim]
    second_half = values[..., half_dim:]
    cos_wide = cosine[:, None, :]
    sin_wide = sine_tab[:, None, :]
    return jnp.concatenate(
        [
            first_half * cos_wide - second_half * sin_wide,
            second_half * cos_wide + first_half * sin_wide,
        ],
        axis=-1,
    )


def unrotate(values, cosine, sine_tab):
    half_dim = values.shape[-1] // 2
    first_half = values[..., :half_dim]
    second_half = values[..., half_dim:]
    cos_wide = cosine[:, None, :]
    sin_wide = sine_tab[:, None, :]
    return jnp.concatenate(
        [
            first_half * cos_wide + second_half * sin_wide,
            second_half * cos_wide - first_half * sin_wide,
        ],
        axis=-1,
    )


def norm_scale(values):
    return lax.rsqrt(jnp.mean(values * values, axis=-1, keepdims=True) + epsilon)


def block_scores(queries, key_block, offset, positions, length):
    score_scale = 1.0 / math.sqrt(HD)
    raw_scores = (
        jnp.einsum("tkgd,skd->kgts", queries, key_block, preferred_element_type=jnp.float32)
        * score_scale
    )
    key_pos = offset + jnp.arange(key_block.shape[0], dtype=jnp.int32)
    allowed = (key_pos[None, :] <= positions[:, None]) & (key_pos[None, :] < length)
    return jnp.where(allowed[None, None], raw_scores, neg_big)


def block_needed(offset, positions, length):
    return (offset <= positions[-1]) & (offset < length)


def attend_forward(queries, key_blocks, value_blocks, positions, length):
    tok_count = queries.shape[0]
    group_size = queries.shape[2]
    offsets = jnp.arange(key_blocks.shape[0], dtype=jnp.int32) * KBLK

    def stat_step(carried, element):
        key_block, offset = element

        def stat_update(state):
            running_max, running_total = state
            scores = block_scores(queries, key_block, offset, positions, length)
            new_max = jnp.maximum(running_max, jnp.max(scores, axis=-1))
            new_total = running_total * jnp.exp(running_max - new_max) + jnp.sum(
                jnp.exp(scores - new_max[..., None]), axis=-1
            )
            return (new_max, new_total)

        return (
            lax.cond(
                block_needed(offset, positions, length), stat_update, lambda state: state, carried
            ),
            None,
        )

    start_max = jnp.full((KVH, group_size, tok_count), neg_big, jnp.float32)
    start_total = jnp.zeros((KVH, group_size, tok_count), jnp.float32)
    (row_max, row_total), unused = lax.scan(
        stat_step, (start_max, start_total), (key_blocks, offsets)
    )
    log_total = row_max + jnp.log(row_total)

    def value_step(carried, element):
        key_block, value_block, offset = element

        def value_update(state):
            accumulated, exact_sum = state
            scores = block_scores(queries, key_block, offset, positions, length)
            probs = jnp.exp(scores - log_total[..., None])
            weights = probs.astype(jnp.bfloat16)
            accumulated = accumulated + jnp.einsum(
                "kgts,skd->tkgd", weights, value_block, preferred_element_type=jnp.float32
            )
            exact_sum = exact_sum + jnp.einsum(
                "kgts,skd->tkgd",
                probs,
                value_block.astype(jnp.float32),
                preferred_element_type=jnp.float32,
            )
            return (accumulated, exact_sum)

        return (
            lax.cond(
                block_needed(offset, positions, length), value_update, lambda state: state, carried
            ),
            None,
        )

    start_acc = jnp.zeros((tok_count, KVH, group_size, HD), jnp.float32)
    (attended, exact_out), unused = lax.scan(
        value_step, (start_acc, start_acc), (key_blocks, value_blocks, offsets)
    )
    return (attended, exact_out, log_total)


def attend_backward(
    queries, key_blocks, value_blocks, attn_back, exact_out, log_total, positions, length
):
    tok_count = queries.shape[0]
    group_size = queries.shape[2]
    block_keys = key_blocks.shape[1]
    score_scale = 1.0 / math.sqrt(HD)
    offsets = jnp.arange(key_blocks.shape[0], dtype=jnp.int32) * KBLK
    delta = jnp.einsum("tkgd,tkgd->kgt", attn_back.astype(jnp.float32), exact_out)

    def grad_step(query_acc, element):
        key_block, value_block, offset = element

        def compute(acc):
            scores = block_scores(queries, key_block, offset, positions, length)
            probs = jnp.exp(scores - log_total[..., None])
            weights = probs.astype(jnp.bfloat16)
            dprobs = jnp.einsum(
                "tkgd,skd->kgts", attn_back, value_block, preferred_element_type=jnp.float32
            )
            score_back = (probs * (dprobs - delta[..., None])).astype(jnp.bfloat16)
            acc = acc + score_scale * jnp.einsum(
                "kgts,skd->tkgd", score_back, key_block, preferred_element_type=jnp.float32
            )
            key_part = score_scale * jnp.einsum(
                "kgts,tkgd->skd", score_back, queries, preferred_element_type=jnp.float32
            )
            value_part = jnp.einsum(
                "kgts,tkgd->skd", weights, attn_back, preferred_element_type=jnp.float32
            )
            return (acc, key_part, value_part)

        def skip(acc):
            empty = jnp.zeros((block_keys, KVH, HD), jnp.float32)
            return (acc, empty, empty)

        acc, key_part, value_part = lax.cond(
            block_needed(offset, positions, length), compute, skip, query_acc
        )
        return (acc, (key_part, value_part))

    start_query = jnp.zeros((tok_count, KVH, group_size, HD), jnp.float32)
    query_grad, (key_parts, value_parts) = lax.scan(
        grad_step, start_query, (key_blocks, value_blocks, offsets)
    )
    return (query_grad, key_parts.reshape(-1, KVH * HD), value_parts.reshape(-1, KVH * HD))


def split_rows(values, groups_count, seq_count):
    return values.reshape(
        (groups_count, seq_count, values.shape[0] // (groups_count * seq_count)) + values.shape[1:]
    )


def per_device(
    hidden_in,
    lengths,
    attn_gain,
    w_query,
    w_key,
    w_value,
    w_out,
    mlp_gain,
    w_gate,
    w_up,
    w_down,
    out_grad,
):
    tok_count = hidden_in.shape[1]
    group_size = H // KVH
    groups_count = lax.axis_size("grp")
    seq_count = lax.axis_size("seq")
    positions = lax.axis_index("seq") * tok_count + jnp.arange(tok_count, dtype=jnp.int32)
    length = lengths[0]
    valid_rows = (positions < length).astype(jnp.float32)[:, None]
    cosine, sine_tab = rope_tables(positions)
    front_weights = (
        lax.all_gather(attn_gain, ("grp", "seq"), axis=0, tiled=True),
        lax.all_gather(w_query, ("grp", "seq"), axis=0, tiled=True),
        lax.all_gather(w_key, ("grp", "seq"), axis=0, tiled=True),
        lax.all_gather(w_value, ("grp", "seq"), axis=0, tiled=True),
        lax.all_gather(w_out, ("grp", "seq"), axis=0, tiled=True),
        lax.all_gather(mlp_gain, ("grp", "seq"), axis=0, tiled=True),
        lax.all_gather(w_gate, ("grp", "seq"), axis=0, tiled=True),
        lax.all_gather(w_up, ("grp", "seq"), axis=0, tiled=True),
        lax.all_gather(w_down, ("grp", "seq"), axis=0, tiled=True),
    )
    gain_one, query_w, key_w, value_w, out_w, gain_two, gate_w, up_w, down_w = front_weights
    tokens_in = hidden_in[0].astype(jnp.float32)
    scale_one = norm_scale(tokens_in)
    normed = (tokens_in * scale_one * gain_one.astype(jnp.float32)).astype(jnp.bfloat16)
    query_lin = jnp.dot(normed, query_w, preferred_element_type=jnp.float32)
    key_lin = jnp.dot(normed, key_w, preferred_element_type=jnp.float32)
    value_lin = jnp.dot(normed, value_w, preferred_element_type=jnp.float32)
    queries = (
        rotate(query_lin.reshape(tok_count, H, HD), cosine, sine_tab)
        .astype(jnp.bfloat16)
        .reshape(tok_count, KVH, group_size, HD)
    )
    key_rot = (
        rotate(key_lin.reshape(tok_count, KVH, HD), cosine, sine_tab)
        .astype(jnp.bfloat16)
        .reshape(tok_count, KVH * HD)
    )
    value_low = value_lin.astype(jnp.bfloat16)
    keys_all, values_all = (
        lax.all_gather(key_rot, "seq", axis=0, tiled=True),
        lax.all_gather(value_low, "seq", axis=0, tiled=True),
    )
    key_blocks = keys_all.reshape(-1, KBLK, KVH, HD)
    value_blocks = values_all.reshape(-1, KBLK, KVH, HD)
    attended, exact_out, log_total = attend_forward(
        queries, key_blocks, value_blocks, positions, length
    )
    attn_mix = attended.reshape(tok_count, H * HD).astype(jnp.bfloat16)
    hidden = tokens_in + jnp.dot(attn_mix, out_w, preferred_element_type=jnp.float32)
    scale_two = norm_scale(hidden)
    normed_mlp = (hidden * scale_two * gain_two.astype(jnp.float32)).astype(jnp.bfloat16)
    gate_lin = jnp.dot(normed_mlp, gate_w, preferred_element_type=jnp.float32)
    up_lin = jnp.dot(normed_mlp, up_w, preferred_element_type=jnp.float32)
    silu_act = jax.nn.silu(gate_lin)
    inner_act = (silu_act * up_lin).astype(jnp.bfloat16)
    branch = jnp.dot(inner_act, down_w, preferred_element_type=jnp.float32)
    result = (valid_rows * (hidden + branch)).astype(jnp.bfloat16)[None]
    gain_one, query_w, key_w, value_w, out_w, gain_two, gate_w, up_w, down_w = front_weights
    cotangent = out_grad[0].astype(jnp.float32)
    branch_grad = valid_rows * cotangent
    branch_low = branch_grad.astype(jnp.bfloat16)
    down_grad = jnp.einsum("tf,td->fd", inner_act, branch_low, preferred_element_type=jnp.float32)
    inner_grad = jnp.einsum("td,fd->tf", branch_low, down_w, preferred_element_type=jnp.float32)
    sigma = jax.nn.sigmoid(gate_lin)
    gate_back = (inner_grad * up_lin * (sigma + gate_lin * sigma * (1.0 - sigma))).astype(
        jnp.bfloat16
    )
    up_back = (inner_grad * silu_act).astype(jnp.bfloat16)
    gate_grad = jnp.einsum("td,tf->df", normed_mlp, gate_back, preferred_element_type=jnp.float32)
    up_grad = jnp.einsum("td,tf->df", normed_mlp, up_back, preferred_element_type=jnp.float32)
    mlp_norm_grad = jnp.einsum(
        "tf,df->td", gate_back, gate_w, preferred_element_type=jnp.float32
    ) + jnp.einsum("tf,df->td", up_back, up_w, preferred_element_type=jnp.float32)
    gain_two_grad = jnp.sum(mlp_norm_grad * hidden * scale_two, axis=0)
    weighted_two = mlp_norm_grad * gain_two.astype(jnp.float32)
    hidden_grad = (
        branch_grad
        + scale_two * weighted_two
        - hidden
        * (scale_two * scale_two * scale_two)
        * jnp.mean(weighted_two * hidden, axis=-1, keepdims=True)
    )
    mlp_seq = (
        lax.psum_scatter(
            split_rows(gain_two_grad, groups_count, seq_count).astype(jnp.bfloat16),
            "seq",
            scatter_dimension=1,
            tiled=True,
        ).astype(jnp.float32),
        lax.psum_scatter(
            split_rows(gate_grad, groups_count, seq_count).astype(jnp.bfloat16),
            "seq",
            scatter_dimension=1,
            tiled=True,
        ).astype(jnp.float32),
        lax.psum_scatter(
            split_rows(up_grad, groups_count, seq_count).astype(jnp.bfloat16),
            "seq",
            scatter_dimension=1,
            tiled=True,
        ).astype(jnp.float32),
        lax.psum_scatter(
            split_rows(down_grad, groups_count, seq_count).astype(jnp.bfloat16),
            "seq",
            scatter_dimension=1,
            tiled=True,
        ).astype(jnp.float32),
    )
    mlp_grp = (
        lax.psum_scatter(
            mlp_seq[0].astype(jnp.bfloat16), "grp", scatter_dimension=0, tiled=True
        ).astype(jnp.float32),
        lax.psum_scatter(
            mlp_seq[1].astype(jnp.bfloat16), "grp", scatter_dimension=0, tiled=True
        ).astype(jnp.float32),
        lax.psum_scatter(
            mlp_seq[2].astype(jnp.bfloat16), "grp", scatter_dimension=0, tiled=True
        ).astype(jnp.float32),
        lax.psum_scatter(
            mlp_seq[3].astype(jnp.bfloat16), "grp", scatter_dimension=0, tiled=True
        ).astype(jnp.float32),
    )
    mlp_grads = tuple((piece.reshape(piece.shape[2:]) for piece in mlp_grp))
    mix_back = hidden_grad.astype(jnp.bfloat16)
    out_w_grad = jnp.einsum("td,te->de", attn_mix, mix_back, preferred_element_type=jnp.float32)
    attn_back = (
        jnp.einsum("te,de->td", mix_back, out_w, preferred_element_type=jnp.float32)
        .astype(jnp.bfloat16)
        .reshape(tok_count, KVH, group_size, HD)
    )
    query_grad, key_grad_all, value_grad_all = attend_backward(
        queries, key_blocks, value_blocks, attn_back, exact_out, log_total, positions, length
    )
    key_grad, value_grad = (
        lax.psum_scatter(
            key_grad_all.astype(jnp.bfloat16), "seq", scatter_dimension=0, tiled=True
        ).astype(jnp.float32),
        lax.psum_scatter(
            value_grad_all.astype(jnp.bfloat16), "seq", scatter_dimension=0, tiled=True
        ).astype(jnp.float32),
    )
    query_back = (
        unrotate(query_grad.reshape(tok_count, H, HD), cosine, sine_tab)
        .astype(jnp.bfloat16)
        .reshape(tok_count, H * HD)
    )
    key_back = (
        unrotate(key_grad.reshape(tok_count, KVH, HD), cosine, sine_tab)
        .astype(jnp.bfloat16)
        .reshape(tok_count, KVH * HD)
    )
    value_back = value_grad.astype(jnp.bfloat16)
    query_w_grad = jnp.einsum("td,te->de", normed, query_back, preferred_element_type=jnp.float32)
    key_w_grad = jnp.einsum("td,te->de", normed, key_back, preferred_element_type=jnp.float32)
    value_w_grad = jnp.einsum("td,te->de", normed, value_back, preferred_element_type=jnp.float32)
    attn_norm_grad = (
        jnp.einsum("te,de->td", query_back, query_w, preferred_element_type=jnp.float32)
        + jnp.einsum("te,de->td", key_back, key_w, preferred_element_type=jnp.float32)
        + jnp.einsum("te,de->td", value_back, value_w, preferred_element_type=jnp.float32)
    )
    gain_one_grad = jnp.sum(attn_norm_grad * tokens_in * scale_one, axis=0)
    weighted_one = attn_norm_grad * gain_one.astype(jnp.float32)
    input_back = (
        hidden_grad
        + scale_one * weighted_one
        - tokens_in
        * (scale_one * scale_one * scale_one)
        * jnp.mean(weighted_one * tokens_in, axis=-1, keepdims=True)
    )
    attn_seq = (
        lax.psum_scatter(
            split_rows(gain_one_grad, groups_count, seq_count).astype(jnp.bfloat16),
            "seq",
            scatter_dimension=1,
            tiled=True,
        ).astype(jnp.float32),
        lax.psum_scatter(
            split_rows(query_w_grad, groups_count, seq_count).astype(jnp.bfloat16),
            "seq",
            scatter_dimension=1,
            tiled=True,
        ).astype(jnp.float32),
        lax.psum_scatter(
            split_rows(key_w_grad, groups_count, seq_count).astype(jnp.bfloat16),
            "seq",
            scatter_dimension=1,
            tiled=True,
        ).astype(jnp.float32),
        lax.psum_scatter(
            split_rows(value_w_grad, groups_count, seq_count).astype(jnp.bfloat16),
            "seq",
            scatter_dimension=1,
            tiled=True,
        ).astype(jnp.float32),
        lax.psum_scatter(
            split_rows(out_w_grad, groups_count, seq_count).astype(jnp.bfloat16),
            "seq",
            scatter_dimension=1,
            tiled=True,
        ).astype(jnp.float32),
    )
    attn_grp = (
        lax.psum_scatter(
            attn_seq[0].astype(jnp.bfloat16), "grp", scatter_dimension=0, tiled=True
        ).astype(jnp.float32),
        lax.psum_scatter(
            attn_seq[1].astype(jnp.bfloat16), "grp", scatter_dimension=0, tiled=True
        ).astype(jnp.float32),
        lax.psum_scatter(
            attn_seq[2].astype(jnp.bfloat16), "grp", scatter_dimension=0, tiled=True
        ).astype(jnp.float32),
        lax.psum_scatter(
            attn_seq[3].astype(jnp.bfloat16), "grp", scatter_dimension=0, tiled=True
        ).astype(jnp.float32),
        lax.psum_scatter(
            attn_seq[4].astype(jnp.bfloat16), "grp", scatter_dimension=0, tiled=True
        ).astype(jnp.float32),
    )
    attn_grads = tuple((piece.reshape(piece.shape[2:]) for piece in attn_grp))
    return (
        result,
        input_back.astype(jnp.bfloat16)[None],
        attn_grads[0],
        attn_grads[1],
        attn_grads[2],
        attn_grads[3],
        attn_grads[4],
        mlp_grads[0],
        mlp_grads[1],
        mlp_grads[2],
        mlp_grads[3],
    )


MESH_ID = pl.DeviceIdType.MESH
VMEM = pltpu.VMEM
LINE = 4
CHIPS = 8
TOK = 128
PAD = 128
CHUNKS = 4
ROWS = TOK // CHUNKS
BF = jnp.bfloat16
F32 = jnp.float32
VSPEC = pl.BlockSpec(memory_space=pltpu.VMEM)


def ring_of(chip):
    z = chip // 2
    x = chip % 2
    return x * LINE + z + x * (LINE - 1 - 2 * z)


def chip_of(ring):
    x = ring // LINE
    q = ring % LINE
    return (q + x * (LINE - 1 - 2 * q)) * 2 + x


class Place:
    def __init__(self):
        self.g = lax.axis_index("grp")
        self.s = lax.axis_index("seq")
        self.core = self.s % 2
        self.chip = self.s // 2
        self.x = self.chip % 2
        self.ring = ring_of(self.chip)
        self.step = 1 - 2 * self.core
        self.next = {"seq": self.at(self.step) * 2 + self.core}
        self.prev = {"seq": self.at(-self.step) * 2 + self.core}
        self.sib = {"seq": self.s + 1 - 2 * self.core}
        self.ynb = {"grp": 1 - self.g}
        self.xnb = {"seq": self.s + 2 - 4 * self.x}

    def at(self, offset):
        return chip_of((self.ring + offset + 8 * CHIPS) % CHIPS)

    def behind(self, t):
        return self.at(-t * self.step)

    def off(self, i):
        return {"seq": ((self.chip + i + CHIPS) % CHIPS) * 2 + self.core}

    def src(self, i):
        return (self.chip - i + CHIPS) % CHIPS


def greet(devices):
    barrier = pltpu.get_barrier_semaphore()
    for device in devices:
        pl.semaphore_signal(barrier, inc=1, device_id=device, device_id_type=MESH_ID)
    pl.semaphore_wait(barrier, len(devices))


def remote(src, dst, send, recv, device):
    return pltpu.make_async_remote_copy(
        src_ref=src, dst_ref=dst, send_sem=send, recv_sem=recv, device_id=device,
        device_id_type=MESH_ID,
    )


class RingGather:
    sems = [pltpu.SemaphoreType.DMA((CHIPS, CHUNKS)), pltpu.SemaphoreType.DMA((CHIPS, CHUNKS))]

    def __init__(self, place, all_ref, send, recv):
        self.place, self.all, self.send, self.recv = place, all_ref, send, recv

    def copy(self, t, k):
        part = self.all.at[self.place.behind(t), pl.ds(k * ROWS, ROWS)]
        return remote(part, part, self.send.at[t, k], self.recv.at[t, k], self.place.next)

    def start(self, k=None):
        for k in range(CHUNKS) if k is None else (k,):
            self.copy(0, k).start()

    def pump(self, t):
        for k in range(CHUNKS):
            self.copy(t - 1, k).wait_recv()
            if t < CHIPS - 1:
                self.copy(t, k).start()

    def finish(self):
        for t in range(CHIPS - 1):
            for k in range(CHUNKS):
                self.copy(t, k).wait_send()


class RingScatter:
    sems = [pltpu.SemaphoreType.DMA((CHIPS, CHUNKS)), pltpu.SemaphoreType.DMA((CHIPS, CHUNKS))]
    bufs = [VMEM((CHIPS - 1, TOK, 1536), BF), VMEM((CHIPS - 1, TOK, 1536), BF)]

    def __init__(self, place, out, held, send, recv):
        self.place, self.out, self.held, self.send, self.recv = place, out, held, send, recv

    def copy(self, t, k):
        rows = pl.ds(k * ROWS, ROWS)
        return remote(self.out.at[t, rows], self.held.at[t, rows], self.send.at[t, k],
                      self.recv.at[t, k], self.place.next)

    def dest(self, t):
        return self.place.behind(t + 1)

    def push(self, t, term):
        for k in range(CHUNKS):
            rows = pl.ds(k * ROWS, ROWS)
            value = term(k)
            if t > 0:
                self.copy(t - 1, k).wait_recv()
                value = value + self.held[t - 1, rows].astype(F32)
            self.out[t, rows] = value.astype(BF)
            self.copy(t, k).start()

    def last(self, k):
        self.copy(CHIPS - 2, k).wait_recv()
        return self.held[CHIPS - 2, pl.ds(k * ROWS, ROWS)].astype(F32)

    def finish(self):
        for t in range(CHIPS - 1):
            for k in range(CHUNKS):
                self.copy(t, k).wait_send()


class Spread:
    sems = [pltpu.SemaphoreType.DMA((CHIPS,)), pltpu.SemaphoreType.DMA((CHIPS,)),
            pltpu.SemaphoreType.DMA((CHIPS,)), pltpu.SemaphoreType.DMA((CHIPS,)),
            pltpu.SemaphoreType.DMA((2 * CHIPS,)), pltpu.SemaphoreType.DMA((2 * CHIPS,))]

    def __init__(self, place, slab, all_ref, local, *sems):
        self.place, self.slab, self.all, self.local = place, slab, all_ref, local
        self.s1, self.r1, self.s2, self.r2, self.s3, self.r3 = sems

    def block(self, g, chip):
        return self.all.at[g * 16 + chip * 2 + self.place.core]

    def across(self, i):
        p = self.place
        return remote(self.slab.at[(p.chip + i) % CHIPS], self.block(p.g, p.chip), self.s1.at[i],
                      self.r1.at[i], p.off(i))

    def arrived(self, i):
        p = self.place
        return remote(self.slab.at[0], self.block(p.g, p.src(i)), self.s1.at[i], self.r1.at[i],
                      p.off(i))

    def to_y(self, i):
        p = self.place
        part = self.block(p.g, p.src(i))
        return remote(part, part, self.s2.at[i], self.r2.at[i], p.ynb)

    def from_y(self, i):
        p = self.place
        part = self.block(1 - p.g, p.src(i))
        return remote(part, part, self.s2.at[i], self.r2.at[i], p.ynb)

    def to_sib(self, i, other):
        p = self.place
        part = self.block((1 - p.g) if other else p.g, p.src(i))
        n = i + CHIPS * other
        return remote(part, part, self.s3.at[n], self.r3.at[n], p.sib)

    def from_sib(self, i, other):
        p = self.place
        g = (1 - p.g) if other else p.g
        part = self.all.at[g * 16 + p.src(i) * 2 + 1 - p.core]
        n = i + CHIPS * other
        return remote(part, part, self.s3.at[n], self.r3.at[n], p.sib)

    def start(self):
        p = self.place
        own = pltpu.make_async_copy(self.slab.at[p.chip], self.block(p.g, p.chip), self.local)
        own.start()
        for i in range(1, CHIPS):
            self.across(i).start()
        own.wait()
        self.to_y(0).start()
        self.to_sib(0, 0).start()

    def pump(self, i):
        self.arrived(i).wait_recv()
        self.to_y(i).start()
        self.to_sib(i, 0).start()
        self.from_y(i - 1).wait_recv()
        self.to_sib(i - 1, 1).start()

    def finish(self):
        self.from_y(CHIPS - 1).wait_recv()
        self.to_sib(CHIPS - 1, 1).start()
        for i in range(CHIPS):
            self.from_sib(i, 0).wait_recv()
            self.from_sib(i, 1).wait_recv()
        for i in range(CHIPS):
            if i > 0:
                self.across(i).wait_send()
            self.to_y(i).wait_send()
            self.to_sib(i, 0).wait_send()
            self.to_sib(i, 1).wait_send()


class Collect:
    sems = [pltpu.SemaphoreType.DMA, pltpu.SemaphoreType.DMA, pltpu.SemaphoreType.DMA,
            pltpu.SemaphoreType.DMA, pltpu.SemaphoreType.DMA((CHIPS,)),
            pltpu.SemaphoreType.DMA((CHIPS,))]

    @staticmethod
    def bufs(rows, columns):
        return [VMEM((16, rows, columns), BF), VMEM((16, rows, columns), BF),
                VMEM((8, rows, columns), BF), VMEM((8, rows, columns), BF)]

    def __init__(self, place, grads, got, bufs, sems):
        self.place, self.grads, self.got = place, grads, got
        self.sib_in, self.pair, self.y_in, self.total = bufs
        self.s1, self.r1, self.s2, self.r2, self.s3, self.r3 = sems

    def sib(self):
        p = self.place
        return remote(self.grads.at[:, 1 - p.core], self.sib_in, self.s1, self.r1, p.sib)

    def y(self):
        p = self.place
        return remote(self.pair.at[pl.ds((1 - p.g) * 8, 8)], self.y_in, self.s2, self.r2, p.ynb)

    def across(self, i):
        p = self.place
        return remote(self.total.at[(p.chip + i) % CHIPS], self.got.at[p.chip], self.s3.at[i],
                      self.r3.at[i], p.off(i))

    def arrived(self, i):
        p = self.place
        return remote(self.total.at[0], self.got.at[p.src(i)], self.s3.at[i], self.r3.at[i],
                      p.off(i))

    def start(self):
        self.sib().start()

    def mid(self):
        p = self.place
        self.sib().wait_recv()

        def add(n, carry):
            self.pair[n] = (self.grads[n, p.core].astype(F32) + self.sib_in[n].astype(F32)).astype(BF)
            return carry

        lax.fori_loop(0, 16, add, 0)
        self.y().start()

    def send(self):
        p = self.place
        self.y().wait_recv()

        def add(n, carry):
            self.total[n] = (self.pair[p.g * 8 + n].astype(F32) + self.y_in[n].astype(F32)).astype(BF)
            return carry

        lax.fori_loop(0, 8, add, 0)
        for i in range(1, CHIPS):
            self.across(i).start()
        self.got[p.chip] = self.total[p.chip]

    def finish(self):
        for i in range(1, CHIPS):
            self.arrived(i).wait_recv()
        self.sib().wait_send()
        self.y().wait_send()
        for i in range(1, CHIPS):
            self.across(i).wait_send()


def dot(a, b):
    return lax.dot_general(a, b, (((1,), (0,)), ((), ())), preferred_element_type=F32)


def dot_nt(a, b):
    return lax.dot_general(a, b, (((1,), (1,)), ((), ())), preferred_element_type=F32)


def all_to_all_devices(place):
    return [place.off(i) for i in range(1, CHIPS)]


def call(body, outs, ins, scratch, collective_id, flops=0, nbytes=0):
    kwargs = {}
    if collective_id is not None:
        kwargs = dict(collective_id=collective_id, has_side_effects=True)
    return pl.pallas_call(
        body,
        out_shape=outs,
        in_specs=[VSPEC] * len(ins),
        out_specs=tuple(VSPEC for _ in outs) if isinstance(outs, (tuple, list)) else VSPEC,
        scratch_shapes=scratch,
        compiler_params=pltpu.CompilerParams(vmem_limit_bytes=60 << 20, **kwargs),
        cost_estimate=pl.CostEstimate(flops=flops, bytes_accessed=nbytes, transcendentals=0),
    )(*ins)


def sds(*shape, dtype=BF):
    return jax.ShapeDtypeStruct(shape, dtype)


def rope(u, cosine, sine):
    return u * cosine + pltpu.roll(u, 64, 1) * sine


def whole(ref):
    value = ref[...]
    return value.reshape(value.shape[0] * value.shape[1], value.shape[2])


def front_kernel(xh, slab, wo, cs, sn, xg, wqkv, wout, q, keys, values, wo2,
                 ag_s, ag_r, s1, r1, s2, r2, s3, r3, ws, wr, ks, kr, vs, vr, local):
    p = Place()
    greet(all_to_all_devices(p) + [p.sib, p.ynb])
    gather = RingGather(p, xg, ag_s, ag_r)
    spread = Spread(p, slab, wqkv, local, s1, r1, s2, r2, s3, r3)
    xg[p.chip] = xh[...]
    gather.start()
    wo2[p.g] = wo[...]
    swap = remote(wo2.at[p.g], wo2.at[p.g], ws.at[0], wr.at[0], p.ynb)
    swap.start()
    spread.start()
    gather.pump(1)
    remote(wo2.at[1 - p.g], wo2.at[1 - p.g], ws.at[0], wr.at[0], p.ynb).wait_recv()
    mine = p.x * 2 + p.core
    theirs = (1 - p.x) * 2 + p.core
    wout[mine] = wo2[p.x]
    to_x = remote(wo2.at[1 - p.x], wout.at[mine], ws.at[1], wr.at[1], p.xnb)
    to_x.start()
    to_s = remote(wout.at[mine], wout.at[mine], ws.at[2], wr.at[2], p.sib)
    to_s.start()
    spread.pump(1)
    gather.pump(2)
    remote(wo2.at[0], wout.at[theirs], ws.at[1], wr.at[1], p.xnb).wait_recv()
    to_s2 = remote(wout.at[theirs], wout.at[theirs], ws.at[3], wr.at[3], p.sib)
    to_s2.start()
    spread.pump(2)
    for t in range(3, CHIPS):
        gather.pump(t)
        spread.pump(t)
    spread.finish()

    def kv_copy(i, n):
        ref, send, recv = ((keys, ks, kr), (values, vs, vr))[n]
        part = ref.at[2 * i + p.core]
        return remote(part, part, send.at[i], recv.at[i], p.sib)

    def kv_in(i, n):
        ref, send, recv = ((keys, ks, kr), (values, vs, vr))[n]
        part = ref.at[2 * i + 1 - p.core]
        return remote(part, part, send.at[i], recv.at[i], p.sib)

    def project(i, carry):
        lin = dot(xg[i], whole(wqkv))
        cosine, sine = cs[i], sn[i]
        q[i, pl.ds(0, TOK)] = rope(lin[:, 0:128], cosine, sine).astype(BF)
        q[i, pl.ds(TOK, TOK)] = rope(lin[:, 128:256], cosine, sine).astype(BF)
        keys[2 * i + p.core] = rope(lin[:, 256:384], cosine, sine).astype(BF)
        values[2 * i + p.core] = lin[:, 384:512].astype(BF)
        kv_copy(i, 0).start()
        kv_copy(i, 1).start()
        return carry

    lax.fori_loop(0, CHIPS, project, 0)
    gather.finish()
    swap.wait_send()
    to_x.wait_send()
    to_s.wait_send()
    to_s2.wait_send()
    rest = p.x * 2 + 1 - p.core
    remote(wout.at[rest], wout.at[rest], ws.at[2], wr.at[2], p.sib).wait_recv()
    rest2 = (1 - p.x) * 2 + 1 - p.core
    remote(wout.at[rest2], wout.at[rest2], ws.at[3], wr.at[3], p.sib).wait_recv()
    for i in range(CHIPS):
        for n in range(2):
            kv_copy(i, n).wait_send()
            kv_in(i, n).wait_recv()


def front(xh, slab, wo, cs, sn):
    dma = pltpu.SemaphoreType.DMA
    return call(
        front_kernel,
        (sds(CHIPS, TOK, 1536), sds(32, 48, 512), sds(4, 48, 1536), sds(CHIPS, 2 * TOK, PAD),
         sds(2 * CHIPS, TOK, PAD), sds(2 * CHIPS, TOK, PAD), sds(2, 48, 1536)),
        (xh, slab, wo, cs, sn),
        RingGather.sems + Spread.sems + [dma((4,)), dma((4,))] + [dma((CHIPS,))] * 4 + [dma],
        1, 2 * 1024 * 1536 * 512, 10 << 20,
    )


LOG2E = 1.4426950408889634
SCALE = 1.0 / math.sqrt(96)
SCALE2 = SCALE * LOG2E


def scores_of(keys, query, limit, j):
    s = dot_nt(keys[j], query) * SCALE2
    pos = lax.broadcasted_iota(jnp.int32, s.shape, 0) + j * 256
    return jnp.where(pos.astype(F32) <= limit, s, neg_big)


def attn_kernel(q, keys, values, limits, bg, slab, wd, mix, mix_t, stat, bgg, wgu, wdown,
                vt, ag_s, ag_r, s1, r1, s2, r2, s3, r3, ws, wr, local):
    p = Place()
    greet(all_to_all_devices(p) + [p.sib, p.ynb])
    gather = RingGather(p, bgg, ag_s, ag_r)
    spread = Spread(p, slab, wgu, local, s1, r1, s2, r2, s3, r3)
    bgg[p.chip] = bg[...]
    gather.start()
    spread.start()
    here = p.g * 2 + p.core
    there = (1 - p.g) * 2 + p.core
    wdown[here] = wd[...]
    swap = remote(wdown.at[here], wdown.at[here], ws.at[0], wr.at[0], p.ynb)
    swap.start()
    to_s = remote(wdown.at[here], wdown.at[here], ws.at[1], wr.at[1], p.sib)
    to_s.start()
    to_s2 = remote(wdown.at[there], wdown.at[there], ws.at[2], wr.at[2], p.sib)

    def turn(n, carry):
        vt[n] = values[n].astype(F32).T.astype(BF)
        return carry

    lax.fori_loop(0, CHIPS, turn, 0)

    def attend(i):
        query = q[i]
        limit = limits[i]

        def chunk(j, state):
            top, total, acc = state
            s = scores_of(keys, query, limit, j)
            new_top = jnp.maximum(top, jnp.max(s, axis=0, keepdims=True))
            fade = jnp.exp2(top - new_top)
            w = jnp.exp2(s - new_top)
            total = total * fade + jnp.sum(w, axis=0, keepdims=True)
            acc = acc * fade + dot(vt[j], w.astype(BF))
            return new_top, total, acc

        start = (jnp.full((1, 256), neg_big, F32), jnp.zeros((1, 256), F32),
                 jnp.zeros((PAD, 256), F32))
        top, total, acc = lax.fori_loop(0, i + 1, chunk, start)
        acc = acc / total
        mix_t[i] = acc
        stat[i] = top + jnp.log2(total)
        out = acc.T.astype(BF)
        mix[i, :, pl.ds(0, PAD)] = out[:TOK]
        mix[i, :, pl.ds(PAD, PAD)] = out[TOK:]

    for i in range(CHIPS):
        attend(i)
        if i > 0:
            gather.pump(i)
            spread.pump(i)
        if i == 3:
            remote(wdown.at[there], wdown.at[there], ws.at[0], wr.at[0], p.ynb).wait_recv()
            to_s2.start()
    spread.finish()
    gather.finish()
    swap.wait_send()
    to_s.wait_send()
    to_s2.wait_send()
    rest = p.g * 2 + 1 - p.core
    remote(wdown.at[rest], wdown.at[rest], ws.at[1], wr.at[1], p.sib).wait_recv()
    rest2 = (1 - p.g) * 2 + 1 - p.core
    remote(wdown.at[rest2], wdown.at[rest2], ws.at[2], wr.at[2], p.sib).wait_recv()


def attend_all(q, keys, values, limits, bg, slab, wd):
    dma = pltpu.SemaphoreType.DMA
    return call(
        attn_kernel,
        (sds(CHIPS, TOK, 2 * PAD), sds(CHIPS, PAD, 256, dtype=F32), sds(CHIPS, 1, 256, dtype=F32),
         sds(CHIPS, TOK, 1536), sds(32, 48, 1024), sds(4, 128, 1536)),
        (q, keys, values, limits, bg, slab, wd),
        [VMEM((CHIPS, PAD, 256), BF)] + RingGather.sems + Spread.sems
        + [dma((3,)), dma((3,)), dma],
        2, 2 * 1024 * 2048 * 256, 10 << 20,
    )


def mid_kernel(mix, wout, tokens, hidden, scale, xg, part, out, held, rs_s, rs_r, ag_s, ag_r):
    p = Place()
    greet([p.next, p.prev])
    scatter = RingScatter(p, out, held, rs_s, rs_r)
    gather = RingGather(p, xg, ag_s, ag_r)
    for t in range(CHIPS):
        part[...] = dot(mix[scatter.dest(t)], wout[...])
        if t < CHIPS - 1:
            scatter.push(t, lambda k: part[pl.ds(k * ROWS, ROWS)])
    for k in range(CHUNKS):
        rows = pl.ds(k * ROWS, ROWS)
        h = tokens[rows] + part[rows] + scatter.last(k)
        r = lax.rsqrt(jnp.mean(h * h, axis=-1, keepdims=True) + epsilon)
        hidden[rows] = h
        scale[rows] = jnp.broadcast_to(r, (ROWS, 128))
        xg[p.chip, rows] = (h * r).astype(BF)
        gather.start(k)
    for t in range(1, CHIPS):
        gather.pump(t)
    scatter.finish()
    gather.finish()


def middle(mix, wout, tokens):
    return call(
        mid_kernel,
        (sds(TOK, 1536, dtype=F32), sds(TOK, 128, dtype=F32), sds(CHIPS, TOK, 1536)),
        (mix, wout, tokens),
        [VMEM((TOK, 1536), F32)] + RingScatter.bufs + RingScatter.sems + RingGather.sems,
        3, 2 * 1024 * 256 * 1536, 10 << 20,
    )


def back_kernel(gub, wgu, hidden, scale, bg, grad, low_all, part, out, held, rs_s, rs_r, ag_s, ag_r):
    p = Place()
    greet([p.next, p.prev])
    scatter = RingScatter(p, out, held, rs_s, rs_r)
    gather = RingGather(p, low_all, ag_s, ag_r)
    for t in range(CHIPS):
        part[...] = dot_nt(gub[scatter.dest(t)], wgu[...])
        if t < CHIPS - 1:
            scatter.push(t, lambda k: part[pl.ds(k * ROWS, ROWS)])
    for k in range(CHUNKS):
        rows = pl.ds(k * ROWS, ROWS)
        a = part[rows] + scatter.last(k)
        h = hidden[rows]
        r = scale[rows, pl.ds(0, 1)]
        value = bg[rows].astype(F32) + r * a - h * (r * r * r) * jnp.mean(a * h, axis=-1, keepdims=True)
        grad[rows] = value
        low_all[p.chip, rows] = value.astype(BF)
        gather.start(k)
    for t in range(1, CHIPS):
        gather.pump(t)
    scatter.finish()
    gather.finish()


def back(gub, wgu, hidden, scale, bg):
    return call(
        back_kernel,
        (sds(TOK, 1536, dtype=F32), sds(CHIPS, TOK, 1536)),
        (gub, wgu, hidden, scale, bg),
        [VMEM((TOK, 1536), F32)] + RingScatter.bufs + RingScatter.sems + RingGather.sems,
        4, 2 * 1024 * 1024 * 1536, 10 << 20,
    )


def attn_back_kernel(q, keys, values, limits, grad_t, grad, mix_t, stat, cs, sn, branch, dgu, dwd,
                     back_out, branch_sum, got, dwd_sum,
                     kt, dk, dv, dkv_low, dkv_in, out, held, sib_in, pair, y_in, total,
                     d_in, d_pair, d_y,
                     rs_s, rs_r, c1, c2, c3, c4, c5, c6, ds, dr, xs, xr):
    p = Place()
    greet(all_to_all_devices(p) + [p.sib, p.ynb])
    scatter = RingScatter(p, out, held, rs_s, rs_r)
    collect = Collect(p, dgu, got, (sib_in, pair, y_in, total), (c1, c2, c3, c4, c5, c6))
    collect.start()
    fold = remote(dwd.at[:, 1 - p.core], d_in, ds.at[0], dr.at[0], p.sib)
    fold.start()
    scatter.push(0, lambda k: branch[scatter.dest(0), pl.ds(k * ROWS, ROWS)].astype(F32))

    def turn(n, carry):
        kt[n] = keys[n].astype(F32).T.astype(BF)
        dk[n] = jnp.zeros((256, PAD), F32)
        dv[n] = jnp.zeros((256, PAD), F32)
        return carry

    lax.fori_loop(0, CHIPS, turn, 0)

    def attend(i):
        query = q[i]
        limit = limits[i]
        do = grad[i]
        lse = stat[i]
        delta = jnp.sum(grad_t[i].astype(F32) * mix_t[i], axis=0, keepdims=True)

        def chunk(j, acc):
            w = jnp.exp2(scores_of(keys, query, limit, j) - lse)
            dp = dot_nt(values[j], do)
            ds_low = (w * (dp - delta)).astype(BF)
            dk[j] += dot(ds_low, query)
            dv[j] += dot(w.astype(BF), do)
            return acc + dot(kt[j], ds_low)

        acc = lax.fori_loop(0, i + 1, chunk, jnp.zeros((PAD, 256), F32))
        dq = acc.T * SCALE
        cosine, sine = cs[i], -sn[i]
        back_out[i, :, pl.ds(0, PAD)] = rope(dq[:TOK], cosine, sine).astype(BF)
        back_out[i, :, pl.ds(PAD, PAD)] = rope(dq[TOK:], cosine, sine).astype(BF)

    y_fold = remote(d_pair.at[1 - p.g], d_y, ds.at[1], dr.at[1], p.ynb)
    for i in range(CHIPS):
        attend(i)
        if 0 < i < CHIPS - 1:
            scatter.push(i, lambda k: branch[scatter.dest(i), pl.ds(k * ROWS, ROWS)].astype(F32))
        if i == 1:
            fold.wait_recv()
            for n in range(2):
                d_pair[n] = (dwd[n, p.core].astype(F32) + d_in[n].astype(F32)).astype(BF)
            y_fold.start()
            collect.mid()
        if i == 3:
            collect.send()
    for n in range(CHIPS):
        for c in range(2):
            rows = pl.ds(c * TOK, TOK)
            dkv_low[0, n, c] = dk[n, rows].astype(BF)
            dkv_low[1, n, c] = dv[n, rows].astype(BF)
    swap = remote(dkv_low.at[:, :, 1 - p.core], dkv_in, xs, xr, p.sib)
    swap.start()
    for k in range(CHUNKS):
        rows = pl.ds(k * ROWS, ROWS)
        branch_sum[rows] = branch[p.chip, rows].astype(F32) + scatter.last(k)
    y_fold.wait_recv()
    dwd_sum[...] = d_pair[p.g].astype(F32) + d_y[...].astype(F32)
    swap.wait_recv()

    def keys_back(n, carry):
        own = pl.ds(pl.multiple_of(p.core * TOK, TOK), TOK)
        back_out[n, :, pl.ds(2 * PAD, PAD)] = rope(
            (dk[n, own] + dkv_in[0, n].astype(F32)) * SCALE, cs[n], -sn[n]).astype(BF)
        back_out[n, :, pl.ds(3 * PAD, PAD)] = (dv[n, own] + dkv_in[1, n].astype(F32)).astype(BF)
        return carry

    lax.fori_loop(0, CHIPS, keys_back, 0)
    collect.finish()
    scatter.finish()
    fold.wait_send()
    y_fold.wait_send()
    swap.wait_send()


def attend_back(q, keys, values, limits, grad_t, grad, mix_t, stat, cs, sn, branch, dgu, dwd):
    dma = pltpu.SemaphoreType.DMA
    return call(
        attn_back_kernel,
        (sds(CHIPS, TOK, 4 * PAD), sds(TOK, 1536, dtype=F32), sds(CHIPS, 48, 1024),
         sds(TOK, 1536, dtype=F32)),
        (q, keys, values, limits, grad_t, grad, mix_t, stat, cs, sn, branch, dgu, dwd),
        [VMEM((CHIPS, PAD, 256), BF), VMEM((CHIPS, 256, PAD), F32), VMEM((CHIPS, 256, PAD), F32),
         VMEM((2, CHIPS, 2, TOK, PAD), BF), VMEM((2, CHIPS, TOK, PAD), BF)]
        + RingScatter.bufs + Collect.bufs(48, 1024)
        + [VMEM((2, TOK, 1536), BF), VMEM((2, TOK, 1536), BF), VMEM((TOK, 1536), BF)]
        + RingScatter.sems + Collect.sems + [dma((2,)), dma((2,)), dma, dma],
        5, 5 * 1024 * 2048 * 256, 20 << 20,
    )


def last_kernel(grads, wqkv, dqkv, dout, csum, got, dout_sum,
                part, out, held, sib_in, pair, y_in, total, o_in, o_pair, o_two, o_y,
                rs_s, rs_r, c1, c2, c3, c4, c5, c6, os, orr):
    p = Place()
    greet(all_to_all_devices(p) + [p.sib, p.ynb])
    scatter = RingScatter(p, out, held, rs_s, rs_r)
    collect = Collect(p, dqkv, got, (sib_in, pair, y_in, total), (c1, c2, c3, c4, c5, c6))
    collect.start()
    fold = remote(dout.at[:, 1 - p.core], o_in, os.at[0], orr.at[0], p.sib)
    fold.start()
    x_fold = remote(o_pair.at[1 - p.x], o_two.at[p.x], os.at[1], orr.at[1], p.xnb)
    x_here = remote(o_pair.at[0], o_two.at[1 - p.x], os.at[1], orr.at[1], p.xnb)
    y_fold = remote(o_two.at[1 - p.g], o_y, os.at[2], orr.at[2], p.ynb)
    for t in range(CHIPS):
        part[...] = dot_nt(grads[scatter.dest(t)], whole(wqkv))
        if t < CHIPS - 1:
            scatter.push(t, lambda k: part[pl.ds(k * ROWS, ROWS)])
        if t == 0:
            fold.wait_recv()
            for n in range(2):
                o_pair[n] = (dout[n, p.core].astype(F32) + o_in[n].astype(F32)).astype(BF)
            x_fold.start()
            collect.mid()
        if t == 1:
            o_two[p.x] = o_pair[p.x]
            x_here.wait_recv()
            y_fold.start()
        if t == 2:
            collect.send()
    for k in range(CHUNKS):
        rows = pl.ds(k * ROWS, ROWS)
        csum[rows] = part[rows] + scatter.last(k)
    y_fold.wait_recv()
    dout_sum[...] = o_two[p.g].astype(F32) + o_y[...].astype(F32)
    collect.finish()
    scatter.finish()
    fold.wait_send()
    x_fold.wait_send()
    y_fold.wait_send()


def last(grads, wqkv, dqkv, dout):
    dma = pltpu.SemaphoreType.DMA
    return call(
        last_kernel,
        (sds(TOK, 1536, dtype=F32), sds(CHIPS, 48, 512), sds(48, 1536, dtype=F32)),
        (grads, wqkv, dqkv, dout),
        [VMEM((TOK, 1536), F32)] + RingScatter.bufs + Collect.bufs(48, 512)
        + [VMEM((2, 48, 1536), BF), VMEM((2, 48, 1536), BF), VMEM((2, 48, 1536), BF), VMEM((48, 1536), BF)]
        + RingScatter.sems + Collect.sems + [dma((3,)), dma((3,))],
        6, 2 * 1024 * 512 * 1536, 10 << 20,
    )


def pad_heads(weight, heads):
    w = weight.reshape(weight.shape[0], heads, 2, 48)
    return jnp.pad(w, ((0, 0), (0, 0), (0, 0), (0, 16))).reshape(weight.shape[0], heads, PAD)


def by_chip(slab):
    return slab.reshape((2, LINE) + slab.shape[1:]).swapaxes(0, 1).reshape(slab.shape)


def by_head(slab):
    return slab.reshape((LINE, 2) + slab.shape[1:]).swapaxes(0, 1).reshape(slab.shape)


def plane_device(hidden_in, lengths, attn_gain, w_query, w_key, w_value, w_out, mlp_gain, w_gate, w_up,
                 w_down, out_grad):
    core = lax.axis_index("seq") % 2
    length = lengths[0]
    gain_one = attn_gain.astype(F32)[:, None]
    gain_two = mlp_gain.astype(F32)[:, None]
    tokens = hidden_in[0].astype(F32)
    r_one = norm_scale(tokens)
    xh = (tokens * r_one).astype(BF)
    own_pos = lax.axis_index("seq") * TOK + jnp.arange(TOK, dtype=jnp.int32)
    valid = (own_pos < length).astype(F32)[:, None]
    bg = (valid * out_grad[0].astype(F32)).astype(BF)

    scaled = lambda w, gain: (w.astype(F32) * gain).astype(BF)
    wq = pad_heads(scaled(w_query, gain_one), 16).reshape(48, 8, 2 * PAD)
    wk = pad_heads(scaled(w_key, gain_one), 8)
    wv = pad_heads(scaled(w_value, gain_one), 8)
    slab_qkv = by_chip(jnp.concatenate([wq, wk, wv], axis=-1).swapaxes(0, 1))
    ff = lambda w: scaled(w, gain_two).reshape(48, 2, 8, 256).transpose(2, 0, 1, 3).reshape(8, 48, 512)
    slab_gu = jnp.concatenate([ff(w_gate), ff(w_up)], axis=-1)

    positions = (2 * jnp.arange(CHIPS, dtype=jnp.int32)[:, None] + core) * TOK + jnp.arange(TOK, dtype=jnp.int32)
    cosine, sine = rope_tables(positions.reshape(-1))
    cosine = jnp.pad(cosine, ((0, 0), (0, 16)))
    sine = jnp.pad(sine, ((0, 0), (0, 16)))
    cs = jnp.concatenate([cosine, cosine], axis=-1).reshape(CHIPS, TOK, PAD)
    sn = jnp.concatenate([-sine, sine], axis=-1).reshape(CHIPS, TOK, PAD)
    limit = jnp.minimum(positions, length - 1).astype(F32)
    limits = jnp.concatenate([limit, limit], axis=-1).reshape(CHIPS, 1, 2 * TOK)

    xg, wqkv, wout4, q, keys, values, unused = front(xh, slab_qkv, w_out, cs, sn)
    keys = keys.reshape(CHIPS, 256, PAD)
    values = values.reshape(CHIPS, 256, PAD)
    mix, mix_t, stat, bgg, wgu, wdown = attend_all(q, keys, values, limits, bg, slab_gu, w_down)
    wout = jnp.pad(wout4, ((0, 0), (0, 16), (0, 0))).reshape(256, 1536)
    wgu = wgu.reshape(1536, 1024)
    wdown = wdown.reshape(512, 1536)
    hidden, scale, x2 = middle(mix, wout, tokens)

    x2f = x2.reshape(1024, 1536)
    bgf = bgg.reshape(1024, 1536)
    lin = jnp.dot(x2f, wgu, preferred_element_type=F32)
    gate_lin, up_lin = lin[:, :512], lin[:, 512:]
    sigma = jax.nn.sigmoid(gate_lin)
    silu_act = gate_lin * sigma
    inner = (silu_act * up_lin).astype(BF)
    inner_grad = jnp.einsum("td,fd->tf", bgf, wdown, preferred_element_type=F32)
    gate_back = (inner_grad * up_lin * (sigma + gate_lin * sigma * (1.0 - sigma))).astype(BF)
    up_back = (inner_grad * silu_act).astype(BF)
    gub = jnp.concatenate([gate_back, up_back], axis=-1)
    grad, mix_back = back(gub.reshape(CHIPS, TOK, 1024), wgu, hidden, scale, bg)
    branch = jnp.dot(inner, wdown, preferred_element_type=F32).astype(BF).reshape(CHIPS, TOK, 1536)
    dgu = jnp.einsum("td,tf->df", x2f, gub, preferred_element_type=F32).astype(BF)
    dwd = jnp.einsum("tf,td->fd", inner, bgf, preferred_element_type=F32).astype(BF)

    mixb = mix_back.reshape(1024, 1536)
    attn_back = jnp.einsum("te,de->td", mixb, wout, preferred_element_type=F32).astype(BF)
    dout = jnp.einsum("td,te->de", mix.reshape(1024, 256), mixb, preferred_element_type=F32).astype(BF)
    dout = dout.reshape(2, 2, 64, 1536)[:, :, :48]
    grad_rows = attn_back.reshape(CHIPS, TOK, 2, PAD).swapaxes(1, 2).reshape(CHIPS, 2 * TOK, PAD)
    grads, branch_sum, got_gu, dwd_sum = attend_back(
        q, keys, values, limits, grad_rows.swapaxes(1, 2), grad_rows, mix_t, stat, cs, sn, branch,
        dgu.reshape(16, 2, 48, 1024), dwd.reshape(2, 2, TOK, 1536))
    result = (valid * (hidden + branch_sum)).astype(BF)[None]
    dqkv = jnp.einsum("td,te->de", xg.reshape(1024, 1536), grads.reshape(1024, 512),
                      preferred_element_type=F32).astype(BF)
    csum, got_qkv, dout_sum = last(grads, wqkv, dqkv.reshape(16, 2, 48, 512), dout)
    input_back = grad + r_one * csum - tokens * (r_one * r_one * r_one) * jnp.mean(
        csum * tokens, axis=-1, keepdims=True)

    got_gu = got_gu.astype(F32)
    unff = lambda v: v.reshape(8, 48, 2, 256).transpose(1, 2, 0, 3).reshape(48, 4096)
    d_gate, d_up = unff(got_gu[:, :, :512]), unff(got_gu[:, :, 512:])
    got_qkv = by_head(got_qkv).swapaxes(0, 1).astype(F32)
    unpad = lambda v: v.reshape(48, -1, 2, 64)[:, :, :, :48].reshape(48, -1)
    d_q, d_k, d_v = unpad(got_qkv[:, :, :256]), unpad(got_qkv[:, :, 256:384]), unpad(got_qkv[:, :, 384:])
    along = lambda w, d: jnp.sum(w.astype(F32) * d, axis=-1)
    return (
        result,
        input_back.astype(BF)[None],
        along(w_query, d_q) + along(w_key, d_k) + along(w_value, d_v),
        d_q * gain_one,
        d_k * gain_one,
        d_v * gain_one,
        dout_sum,
        along(w_gate, d_gate) + along(w_up, d_up),
        d_gate * gain_two,
        d_up * gain_two,
        dwd_sum,
    )


def solution(mesh):
    placed = (
        P("grp", "seq", None),
        P("grp"),
        P(("grp", "seq")),
        P(("grp", "seq"), None),
        P(("grp", "seq"), None),
        P(("grp", "seq"), None),
        P(("grp", "seq"), None),
        P(("grp", "seq")),
        P(("grp", "seq"), None),
        P(("grp", "seq"), None),
        P(("grp", "seq"), None),
        P("grp", "seq", None),
    )
    small = mesh.shape["grp"] == 2 and mesh.shape["seq"] == 2 * CHIPS
    return jax.shard_map(
        plane_device if small else per_device,
        mesh=mesh,
        in_specs=placed,
        out_specs=(
            P("grp", "seq", None),
            P("grp", "seq", None),
            P(("grp", "seq")),
            P(("grp", "seq"), None),
            P(("grp", "seq"), None),
            P(("grp", "seq"), None),
            P(("grp", "seq"), None),
            P(("grp", "seq")),
            P(("grp", "seq"), None),
            P(("grp", "seq"), None),
            P(("grp", "seq"), None),
        ),
        check_vma=False,
    )
```

```python
import math

import jax
import jax.numpy as jnp
from jax import lax
from jax.experimental import pallas as pl
from jax.experimental.pallas import tpu as pltpu
from jax.sharding import PartitionSpec as P

H = 16
KVH = 8
HD = 96
KBLK = 256


epsilon = 1e-05
rope_base = 100000.0
neg_big = -1e30


def rope_tables(positions):
    half_dim = HD // 2
    frequency = jnp.exp(-math.log(rope_base) * (2.0 * jnp.arange(half_dim, dtype=jnp.float32) / HD))
    angles = positions.astype(jnp.float32)[:, None] * frequency[None, :]
    return (jnp.cos(angles), jnp.sin(angles))


def rotate(values, cosine, sine_tab):
    half_dim = values.shape[-1] // 2
    first_half = values[..., :half_dim]
    second_half = values[..., half_dim:]
    cos_wide = cosine[:, None, :]
    sin_wide = sine_tab[:, None, :]
    return jnp.concatenate(
        [
            first_half * cos_wide - second_half * sin_wide,
            second_half * cos_wide + first_half * sin_wide,
        ],
        axis=-1,
    )


def unrotate(values, cosine, sine_tab):
    half_dim = values.shape[-1] // 2
    first_half = values[..., :half_dim]
    second_half = values[..., half_dim:]
    cos_wide = cosine[:, None, :]
    sin_wide = sine_tab[:, None, :]
    return jnp.concatenate(
        [
            first_half * cos_wide + second_half * sin_wide,
            second_half * cos_wide - first_half * sin_wide,
        ],
        axis=-1,
    )


def norm_scale(values):
    return lax.rsqrt(jnp.mean(values * values, axis=-1, keepdims=True) + epsilon)


def block_scores(queries, key_block, offset, positions, length):
    score_scale = 1.0 / math.sqrt(HD)
    raw_scores = (
        jnp.einsum("tkgd,skd->kgts", queries, key_block, preferred_element_type=jnp.float32)
        * score_scale
    )
    key_pos = offset + jnp.arange(key_block.shape[0], dtype=jnp.int32)
    allowed = (key_pos[None, :] <= positions[:, None]) & (key_pos[None, :] < length)
    return jnp.where(allowed[None, None], raw_scores, neg_big)


def block_needed(offset, positions, length):
    return (offset <= positions[-1]) & (offset < length)


def attend_forward(queries, key_blocks, value_blocks, positions, length):
    tok_count = queries.shape[0]
    group_size = queries.shape[2]
    offsets = jnp.arange(key_blocks.shape[0], dtype=jnp.int32) * KBLK

    def stat_step(carried, element):
        key_block, offset = element

        def stat_update(state):
            running_max, running_total = state
            scores = block_scores(queries, key_block, offset, positions, length)
            new_max = jnp.maximum(running_max, jnp.max(scores, axis=-1))
            new_total = running_total * jnp.exp(running_max - new_max) + jnp.sum(
                jnp.exp(scores - new_max[..., None]), axis=-1
            )
            return (new_max, new_total)

        return (
            lax.cond(
                block_needed(offset, positions, length), stat_update, lambda state: state, carried
            ),
            None,
        )

    start_max = jnp.full((KVH, group_size, tok_count), neg_big, jnp.float32)
    start_total = jnp.zeros((KVH, group_size, tok_count), jnp.float32)
    (row_max, row_total), unused = lax.scan(
        stat_step, (start_max, start_total), (key_blocks, offsets)
    )
    log_total = row_max + jnp.log(row_total)

    def value_step(carried, element):
        key_block, value_block, offset = element

        def value_update(state):
            accumulated, exact_sum = state
            scores = block_scores(queries, key_block, offset, positions, length)
            probs = jnp.exp(scores - log_total[..., None])
            weights = probs.astype(jnp.bfloat16)
            accumulated = accumulated + jnp.einsum(
                "kgts,skd->tkgd", weights, value_block, preferred_element_type=jnp.float32
            )
            exact_sum = exact_sum + jnp.einsum(
                "kgts,skd->tkgd",
                probs,
                value_block.astype(jnp.float32),
                preferred_element_type=jnp.float32,
            )
            return (accumulated, exact_sum)

        return (
            lax.cond(
                block_needed(offset, positions, length), value_update, lambda state: state, carried
            ),
            None,
        )

    start_acc = jnp.zeros((tok_count, KVH, group_size, HD), jnp.float32)
    (attended, exact_out), unused = lax.scan(
        value_step, (start_acc, start_acc), (key_blocks, value_blocks, offsets)
    )
    return (attended, exact_out, log_total)


def attend_backward(
    queries, key_blocks, value_blocks, attn_back, exact_out, log_total, positions, length
):
    tok_count = queries.shape[0]
    group_size = queries.shape[2]
    block_keys = key_blocks.shape[1]
    score_scale = 1.0 / math.sqrt(HD)
    offsets = jnp.arange(key_blocks.shape[0], dtype=jnp.int32) * KBLK
    delta = jnp.einsum("tkgd,tkgd->kgt", attn_back.astype(jnp.float32), exact_out)

    def grad_step(query_acc, element):
        key_block, value_block, offset = element

        def compute(acc):
            scores = block_scores(queries, key_block, offset, positions, length)
            probs = jnp.exp(scores - log_total[..., None])
            weights = probs.astype(jnp.bfloat16)
            dprobs = jnp.einsum(
                "tkgd,skd->kgts", attn_back, value_block, preferred_element_type=jnp.float32
            )
            score_back = (probs * (dprobs - delta[..., None])).astype(jnp.bfloat16)
            acc = acc + score_scale * jnp.einsum(
                "kgts,skd->tkgd", score_back, key_block, preferred_element_type=jnp.float32
            )
            key_part = score_scale * jnp.einsum(
                "kgts,tkgd->skd", score_back, queries, preferred_element_type=jnp.float32
            )
            value_part = jnp.einsum(
                "kgts,tkgd->skd", weights, attn_back, preferred_element_type=jnp.float32
            )
            return (acc, key_part, value_part)

        def skip(acc):
            empty = jnp.zeros((block_keys, KVH, HD), jnp.float32)
            return (acc, empty, empty)

        acc, key_part, value_part = lax.cond(
            block_needed(offset, positions, length), compute, skip, query_acc
        )
        return (acc, (key_part, value_part))

    start_query = jnp.zeros((tok_count, KVH, group_size, HD), jnp.float32)
    query_grad, (key_parts, value_parts) = lax.scan(
        grad_step, start_query, (key_blocks, value_blocks, offsets)
    )
    return (query_grad, key_parts.reshape(-1, KVH * HD), value_parts.reshape(-1, KVH * HD))


def split_rows(values, groups_count, seq_count):
    return values.reshape(
        (groups_count, seq_count, values.shape[0] // (groups_count * seq_count)) + values.shape[1:]
    )


def per_device(
    hidden_in,
    lengths,
    attn_gain,
    w_query,
    w_key,
    w_value,
    w_out,
    mlp_gain,
    w_gate,
    w_up,
    w_down,
    out_grad,
):
    tok_count = hidden_in.shape[1]
    group_size = H // KVH
    groups_count = lax.axis_size("grp")
    seq_count = lax.axis_size("seq")
    positions = lax.axis_index("seq") * tok_count + jnp.arange(tok_count, dtype=jnp.int32)
    length = lengths[0]
    valid_rows = (positions < length).astype(jnp.float32)[:, None]
    cosine, sine_tab = rope_tables(positions)
    front_weights = (
        lax.all_gather(attn_gain, ("grp", "seq"), axis=0, tiled=True),
        lax.all_gather(w_query, ("grp", "seq"), axis=0, tiled=True),
        lax.all_gather(w_key, ("grp", "seq"), axis=0, tiled=True),
        lax.all_gather(w_value, ("grp", "seq"), axis=0, tiled=True),
        lax.all_gather(w_out, ("grp", "seq"), axis=0, tiled=True),
        lax.all_gather(mlp_gain, ("grp", "seq"), axis=0, tiled=True),
        lax.all_gather(w_gate, ("grp", "seq"), axis=0, tiled=True),
        lax.all_gather(w_up, ("grp", "seq"), axis=0, tiled=True),
        lax.all_gather(w_down, ("grp", "seq"), axis=0, tiled=True),
    )
    gain_one, query_w, key_w, value_w, out_w, gain_two, gate_w, up_w, down_w = front_weights
    tokens_in = hidden_in[0].astype(jnp.float32)
    scale_one = norm_scale(tokens_in)
    normed = (tokens_in * scale_one * gain_one.astype(jnp.float32)).astype(jnp.bfloat16)
    query_lin = jnp.dot(normed, query_w, preferred_element_type=jnp.float32)
    key_lin = jnp.dot(normed, key_w, preferred_element_type=jnp.float32)
    value_lin = jnp.dot(normed, value_w, preferred_element_type=jnp.float32)
    queries = (
        rotate(query_lin.reshape(tok_count, H, HD), cosine, sine_tab)
        .astype(jnp.bfloat16)
        .reshape(tok_count, KVH, group_size, HD)
    )
    key_rot = (
        rotate(key_lin.reshape(tok_count, KVH, HD), cosine, sine_tab)
        .astype(jnp.bfloat16)
        .reshape(tok_count, KVH * HD)
    )
    value_low = value_lin.astype(jnp.bfloat16)
    keys_all, values_all = (
        lax.all_gather(key_rot, "seq", axis=0, tiled=True),
        lax.all_gather(value_low, "seq", axis=0, tiled=True),
    )
    key_blocks = keys_all.reshape(-1, KBLK, KVH, HD)
    value_blocks = values_all.reshape(-1, KBLK, KVH, HD)
    attended, exact_out, log_total = attend_forward(
        queries, key_blocks, value_blocks, positions, length
    )
    attn_mix = attended.reshape(tok_count, H * HD).astype(jnp.bfloat16)
    hidden = tokens_in + jnp.dot(attn_mix, out_w, preferred_element_type=jnp.float32)
    scale_two = norm_scale(hidden)
    normed_mlp = (hidden * scale_two * gain_two.astype(jnp.float32)).astype(jnp.bfloat16)
    gate_lin = jnp.dot(normed_mlp, gate_w, preferred_element_type=jnp.float32)
    up_lin = jnp.dot(normed_mlp, up_w, preferred_element_type=jnp.float32)
    silu_act = jax.nn.silu(gate_lin)
    inner_act = (silu_act * up_lin).astype(jnp.bfloat16)
    branch = jnp.dot(inner_act, down_w, preferred_element_type=jnp.float32)
    result = (valid_rows * (hidden + branch)).astype(jnp.bfloat16)[None]
    gain_one, query_w, key_w, value_w, out_w, gain_two, gate_w, up_w, down_w = front_weights
    cotangent = out_grad[0].astype(jnp.float32)
    branch_grad = valid_rows * cotangent
    branch_low = branch_grad.astype(jnp.bfloat16)
    down_grad = jnp.einsum("tf,td->fd", inner_act, branch_low, preferred_element_type=jnp.float32)
    inner_grad = jnp.einsum("td,fd->tf", branch_low, down_w, preferred_element_type=jnp.float32)
    sigma = jax.nn.sigmoid(gate_lin)
    gate_back = (inner_grad * up_lin * (sigma + gate_lin * sigma * (1.0 - sigma))).astype(
        jnp.bfloat16
    )
    up_back = (inner_grad * silu_act).astype(jnp.bfloat16)
    gate_grad = jnp.einsum("td,tf->df", normed_mlp, gate_back, preferred_element_type=jnp.float32)
    up_grad = jnp.einsum("td,tf->df", normed_mlp, up_back, preferred_element_type=jnp.float32)
    mlp_norm_grad = jnp.einsum(
        "tf,df->td", gate_back, gate_w, preferred_element_type=jnp.float32
    ) + jnp.einsum("tf,df->td", up_back, up_w, preferred_element_type=jnp.float32)
    gain_two_grad = jnp.sum(mlp_norm_grad * hidden * scale_two, axis=0)
    weighted_two = mlp_norm_grad * gain_two.astype(jnp.float32)
    hidden_grad = (
        branch_grad
        + scale_two * weighted_two
        - hidden
        * (scale_two * scale_two * scale_two)
        * jnp.mean(weighted_two * hidden, axis=-1, keepdims=True)
    )
    mlp_seq = (
        lax.psum_scatter(
            split_rows(gain_two_grad, groups_count, seq_count).astype(jnp.bfloat16),
            "seq",
            scatter_dimension=1,
            tiled=True,
        ).astype(jnp.float32),
        lax.psum_scatter(
            split_rows(gate_grad, groups_count, seq_count).astype(jnp.bfloat16),
            "seq",
            scatter_dimension=1,
            tiled=True,
        ).astype(jnp.float32),
        lax.psum_scatter(
            split_rows(up_grad, groups_count, seq_count).astype(jnp.bfloat16),
            "seq",
            scatter_dimension=1,
            tiled=True,
        ).astype(jnp.float32),
        lax.psum_scatter(
            split_rows(down_grad, groups_count, seq_count).astype(jnp.bfloat16),
            "seq",
            scatter_dimension=1,
            tiled=True,
        ).astype(jnp.float32),
    )
    mlp_grp = (
        lax.psum_scatter(
            mlp_seq[0].astype(jnp.bfloat16), "grp", scatter_dimension=0, tiled=True
        ).astype(jnp.float32),
        lax.psum_scatter(
            mlp_seq[1].astype(jnp.bfloat16), "grp", scatter_dimension=0, tiled=True
        ).astype(jnp.float32),
        lax.psum_scatter(
            mlp_seq[2].astype(jnp.bfloat16), "grp", scatter_dimension=0, tiled=True
        ).astype(jnp.float32),
        lax.psum_scatter(
            mlp_seq[3].astype(jnp.bfloat16), "grp", scatter_dimension=0, tiled=True
        ).astype(jnp.float32),
    )
    mlp_grads = tuple((piece.reshape(piece.shape[2:]) for piece in mlp_grp))
    mix_back = hidden_grad.astype(jnp.bfloat16)
    out_w_grad = jnp.einsum("td,te->de", attn_mix, mix_back, preferred_element_type=jnp.float32)
    attn_back = (
        jnp.einsum("te,de->td", mix_back, out_w, preferred_element_type=jnp.float32)
        .astype(jnp.bfloat16)
        .reshape(tok_count, KVH, group_size, HD)
    )
    query_grad, key_grad_all, value_grad_all = attend_backward(
        queries, key_blocks, value_blocks, attn_back, exact_out, log_total, positions, length
    )
    key_grad, value_grad = (
        lax.psum_scatter(
            key_grad_all.astype(jnp.bfloat16), "seq", scatter_dimension=0, tiled=True
        ).astype(jnp.float32),
        lax.psum_scatter(
            value_grad_all.astype(jnp.bfloat16), "seq", scatter_dimension=0, tiled=True
        ).astype(jnp.float32),
    )
    query_back = (
        unrotate(query_grad.reshape(tok_count, H, HD), cosine, sine_tab)
        .astype(jnp.bfloat16)
        .reshape(tok_count, H * HD)
    )
    key_back = (
        unrotate(key_grad.reshape(tok_count, KVH, HD), cosine, sine_tab)
        .astype(jnp.bfloat16)
        .reshape(tok_count, KVH * HD)
    )
    value_back = value_grad.astype(jnp.bfloat16)
    query_w_grad = jnp.einsum("td,te->de", normed, query_back, preferred_element_type=jnp.float32)
    key_w_grad = jnp.einsum("td,te->de", normed, key_back, preferred_element_type=jnp.float32)
    value_w_grad = jnp.einsum("td,te->de", normed, value_back, preferred_element_type=jnp.float32)
    attn_norm_grad = (
        jnp.einsum("te,de->td", query_back, query_w, preferred_element_type=jnp.float32)
        + jnp.einsum("te,de->td", key_back, key_w, preferred_element_type=jnp.float32)
        + jnp.einsum("te,de->td", value_back, value_w, preferred_element_type=jnp.float32)
    )
    gain_one_grad = jnp.sum(attn_norm_grad * tokens_in * scale_one, axis=0)
    weighted_one = attn_norm_grad * gain_one.astype(jnp.float32)
    input_back = (
        hidden_grad
        + scale_one * weighted_one
        - tokens_in
        * (scale_one * scale_one * scale_one)
        * jnp.mean(weighted_one * tokens_in, axis=-1, keepdims=True)
    )
    attn_seq = (
        lax.psum_scatter(
            split_rows(gain_one_grad, groups_count, seq_count).astype(jnp.bfloat16),
            "seq",
            scatter_dimension=1,
            tiled=True,
        ).astype(jnp.float32),
        lax.psum_scatter(
            split_rows(query_w_grad, groups_count, seq_count).astype(jnp.bfloat16),
            "seq",
            scatter_dimension=1,
            tiled=True,
        ).astype(jnp.float32),
        lax.psum_scatter(
            split_rows(key_w_grad, groups_count, seq_count).astype(jnp.bfloat16),
            "seq",
            scatter_dimension=1,
            tiled=True,
        ).astype(jnp.float32),
        lax.psum_scatter(
            split_rows(value_w_grad, groups_count, seq_count).astype(jnp.bfloat16),
            "seq",
            scatter_dimension=1,
            tiled=True,
        ).astype(jnp.float32),
        lax.psum_scatter(
            split_rows(out_w_grad, groups_count, seq_count).astype(jnp.bfloat16),
            "seq",
            scatter_dimension=1,
            tiled=True,
        ).astype(jnp.float32),
    )
    attn_grp = (
        lax.psum_scatter(
            attn_seq[0].astype(jnp.bfloat16), "grp", scatter_dimension=0, tiled=True
        ).astype(jnp.float32),
        lax.psum_scatter(
            attn_seq[1].astype(jnp.bfloat16), "grp", scatter_dimension=0, tiled=True
        ).astype(jnp.float32),
        lax.psum_scatter(
            attn_seq[2].astype(jnp.bfloat16), "grp", scatter_dimension=0, tiled=True
        ).astype(jnp.float32),
        lax.psum_scatter(
            attn_seq[3].astype(jnp.bfloat16), "grp", scatter_dimension=0, tiled=True
        ).astype(jnp.float32),
        lax.psum_scatter(
            attn_seq[4].astype(jnp.bfloat16), "grp", scatter_dimension=0, tiled=True
        ).astype(jnp.float32),
    )
    attn_grads = tuple((piece.reshape(piece.shape[2:]) for piece in attn_grp))
    return (
        result,
        input_back.astype(jnp.bfloat16)[None],
        attn_grads[0],
        attn_grads[1],
        attn_grads[2],
        attn_grads[3],
        attn_grads[4],
        mlp_grads[0],
        mlp_grads[1],
        mlp_grads[2],
        mlp_grads[3],
    )


MESH_ID = pl.DeviceIdType.MESH
VMEM = pltpu.VMEM
LINE = 4
CHIPS = 8
TOK = 128
PAD = 128
CHUNKS = 4
ROWS = TOK // CHUNKS
BF = jnp.bfloat16
F32 = jnp.float32
VSPEC = pl.BlockSpec(memory_space=pltpu.VMEM)


def ring_of(chip):
    z = chip // 2
    x = chip % 2
    return x * LINE + z + x * (LINE - 1 - 2 * z)


def chip_of(ring):
    x = ring // LINE
    q = ring % LINE
    return (q + x * (LINE - 1 - 2 * q)) * 2 + x


class Place:
    def __init__(self):
        self.g = lax.axis_index("grp")
        self.s = lax.axis_index("seq")
        self.core = self.s % 2
        self.chip = self.s // 2
        self.x = self.chip % 2
        self.ring = ring_of(self.chip)
        self.step = 1 - 2 * self.core
        self.next = {"seq": self.at(self.step) * 2 + self.core}
        self.prev = {"seq": self.at(-self.step) * 2 + self.core}
        self.sib = {"seq": self.s + 1 - 2 * self.core}
        self.ynb = {"grp": 1 - self.g}
        self.xnb = {"seq": self.s + 2 - 4 * self.x}

    def at(self, offset):
        return chip_of((self.ring + offset + 8 * CHIPS) % CHIPS)

    def behind(self, t):
        return self.at(-t * self.step)

    def off(self, i):
        return {"seq": ((self.chip + i + CHIPS) % CHIPS) * 2 + self.core}

    def src(self, i):
        return (self.chip - i + CHIPS) % CHIPS


def greet(devices):
    barrier = pltpu.get_barrier_semaphore()
    for device in devices:
        pl.semaphore_signal(barrier, inc=1, device_id=device, device_id_type=MESH_ID)
    pl.semaphore_wait(barrier, len(devices))


def remote(src, dst, send, recv, device):
    return pltpu.make_async_remote_copy(
        src_ref=src, dst_ref=dst, send_sem=send, recv_sem=recv, device_id=device,
        device_id_type=MESH_ID,
    )


class RingGather:
    sems = [pltpu.SemaphoreType.DMA((CHIPS, CHUNKS)), pltpu.SemaphoreType.DMA((CHIPS, CHUNKS))]

    def __init__(self, place, all_ref, send, recv):
        self.place, self.all, self.send, self.recv = place, all_ref, send, recv

    def copy(self, t, k):
        part = self.all.at[self.place.behind(t), pl.ds(k * ROWS, ROWS)]
        return remote(part, part, self.send.at[t, k], self.recv.at[t, k], self.place.next)

    def start(self, k=None):
        for k in range(CHUNKS) if k is None else (k,):
            self.copy(0, k).start()

    def pump(self, t):
        for k in range(CHUNKS):
            self.pass_on(t, k)

    def pass_on(self, t, k):
        self.copy(t - 1, k).wait_recv()
        if t < CHIPS - 1:
            self.copy(t, k).start()

    def pump_some(self, first, last):
        for n in range(first, last):
            self.pass_on(1 + n // CHUNKS, n % CHUNKS)

    def finish(self):
        for t in range(CHIPS - 1):
            for k in range(CHUNKS):
                self.copy(t, k).wait_send()


class RingScatter:
    sems = [pltpu.SemaphoreType.DMA((CHIPS, CHUNKS)), pltpu.SemaphoreType.DMA((CHIPS, CHUNKS))]
    bufs = [VMEM((CHIPS - 1, TOK, 1536), BF), VMEM((CHIPS - 1, TOK, 1536), BF)]

    def __init__(self, place, out, held, send, recv):
        self.place, self.out, self.held, self.send, self.recv = place, out, held, send, recv

    def copy(self, t, k):
        rows = pl.ds(k * ROWS, ROWS)
        return remote(self.out.at[t, rows], self.held.at[t, rows], self.send.at[t, k],
                      self.recv.at[t, k], self.place.next)

    def dest(self, t):
        return self.place.behind(t + 1)

    def push(self, t, term):
        for k in range(CHUNKS):
            rows = pl.ds(k * ROWS, ROWS)
            value = term(k)
            if t > 0:
                self.copy(t - 1, k).wait_recv()
                value = value + self.held[t - 1, rows].astype(F32)
            self.out[t, rows] = value.astype(BF)
            self.copy(t, k).start()

    def last(self, k):
        self.copy(CHIPS - 2, k).wait_recv()
        return self.held[CHIPS - 2, pl.ds(k * ROWS, ROWS)].astype(F32)

    def finish(self):
        for t in range(CHIPS - 1):
            for k in range(CHUNKS):
                self.copy(t, k).wait_send()


class Spread:
    sems = [pltpu.SemaphoreType.DMA((CHIPS,)), pltpu.SemaphoreType.DMA((CHIPS,)),
            pltpu.SemaphoreType.DMA((CHIPS,)), pltpu.SemaphoreType.DMA((CHIPS,)),
            pltpu.SemaphoreType.DMA((2 * CHIPS,)), pltpu.SemaphoreType.DMA((2 * CHIPS,))]

    def __init__(self, place, slab, all_ref, local, *sems):
        self.place, self.slab, self.all, self.local = place, slab, all_ref, local
        self.s1, self.r1, self.s2, self.r2, self.s3, self.r3 = sems

    def block(self, g, chip):
        return self.all.at[g * 16 + chip * 2 + self.place.core]

    def across(self, i):
        p = self.place
        return remote(self.slab.at[(p.chip + i) % CHIPS], self.block(p.g, p.chip), self.s1.at[i],
                      self.r1.at[i], p.off(i))

    def arrived(self, i):
        p = self.place
        return remote(self.slab.at[0], self.block(p.g, p.src(i)), self.s1.at[i], self.r1.at[i],
                      p.off(i))

    def to_y(self, i):
        p = self.place
        part = self.block(p.g, p.src(i))
        return remote(part, part, self.s2.at[i], self.r2.at[i], p.ynb)

    def from_y(self, i):
        p = self.place
        part = self.block(1 - p.g, p.src(i))
        return remote(part, part, self.s2.at[i], self.r2.at[i], p.ynb)

    def to_sib(self, i, other):
        p = self.place
        part = self.block((1 - p.g) if other else p.g, p.src(i))
        n = i + CHIPS * other
        return remote(part, part, self.s3.at[n], self.r3.at[n], p.sib)

    def from_sib(self, i, other):
        p = self.place
        g = (1 - p.g) if other else p.g
        part = self.all.at[g * 16 + p.src(i) * 2 + 1 - p.core]
        n = i + CHIPS * other
        return remote(part, part, self.s3.at[n], self.r3.at[n], p.sib)

    def start(self):
        p = self.place
        own = pltpu.make_async_copy(self.slab.at[p.chip], self.block(p.g, p.chip), self.local)
        own.start()
        for i in range(1, CHIPS):
            self.across(i).start()
        own.wait()
        self.to_y(0).start()
        self.to_sib(0, 0).start()

    def pump(self, i):
        self.arrived(i).wait_recv()
        self.to_y(i).start()
        self.to_sib(i, 0).start()
        self.from_y(i - 1).wait_recv()
        self.to_sib(i - 1, 1).start()

    def finish(self):
        self.from_y(CHIPS - 1).wait_recv()
        self.to_sib(CHIPS - 1, 1).start()
        for i in range(CHIPS):
            self.from_sib(i, 0).wait_recv()
            self.from_sib(i, 1).wait_recv()
        for i in range(CHIPS):
            if i > 0:
                self.across(i).wait_send()
            self.to_y(i).wait_send()
            self.to_sib(i, 0).wait_send()
            self.to_sib(i, 1).wait_send()


class Collect:
    order = tuple(range(1, CHIPS)) + (0,)
    sems = [pltpu.SemaphoreType.DMA((CHIPS,))] * 6

    @staticmethod
    def bufs(rows, columns):
        return [VMEM((CHIPS, 2, rows, columns), BF), VMEM((CHIPS, 2, rows, columns), BF),
                VMEM((CHIPS, rows, columns), BF), VMEM((CHIPS, rows, columns), BF)]

    def __init__(self, place, grads, got, bufs, sems):
        self.place, self.grads, self.got = place, grads, got
        self.sib_in, self.pair, self.y_in, self.total = bufs
        self.s1, self.r1, self.s2, self.r2, self.s3, self.r3 = sems

    def sib(self, n):
        p = self.place
        return remote(self.grads.at[:, (p.chip + n) % CHIPS, 1 - p.core], self.sib_in.at[n],
                      self.s1.at[n], self.r1.at[n], p.sib)

    def y(self, n):
        p = self.place
        return remote(self.pair.at[n, 1 - p.g], self.y_in.at[n], self.s2.at[n], self.r2.at[n], p.ynb)

    def across(self, n):
        p = self.place
        return remote(self.total.at[n], self.got.at[p.chip], self.s3.at[n], self.r3.at[n], p.off(n))

    def arrived(self, n):
        p = self.place
        return remote(self.total.at[n], self.got.at[p.src(n)], self.s3.at[n], self.r3.at[n], p.off(n))

    def start(self):
        for n in self.order:
            self.sib(n).start()

    def pair_up(self, m):
        p, n = self.place, self.order[m]
        self.sib(n).wait_recv()
        for g in range(2):
            self.pair[n, g] = (self.grads[g, (p.chip + n) % CHIPS, p.core].astype(F32)
                               + self.sib_in[n, g].astype(F32)).astype(BF)
        self.y(n).start()

    def send(self, m):
        p, n = self.place, self.order[m]
        self.y(n).wait_recv()
        value = (self.pair[n, p.g].astype(F32) + self.y_in[n].astype(F32)).astype(BF)
        if n == 0:
            self.got[p.chip] = value
        else:
            self.total[n] = value
            self.across(n).start()

    def receive(self):
        for n in range(1, CHIPS):
            self.arrived(n).wait_recv()

    def finish(self):
        for n in range(CHIPS):
            self.sib(n).wait_send()
            self.y(n).wait_send()
            if n > 0:
                self.across(n).wait_send()


def dot(a, b):
    return lax.dot_general(a, b, (((1,), (0,)), ((), ())), preferred_element_type=F32)


def dot_nt(a, b):
    return lax.dot_general(a, b, (((1,), (1,)), ((), ())), preferred_element_type=F32)


def all_to_all_devices(place):
    return [place.off(i) for i in range(1, CHIPS)]


def call(body, outs, ins, scratch, collective_id, flops=0, nbytes=0):
    kwargs = {}
    if collective_id is not None:
        kwargs = dict(collective_id=collective_id, has_side_effects=True)
    return pl.pallas_call(
        body,
        out_shape=outs,
        in_specs=[VSPEC] * len(ins),
        out_specs=tuple(VSPEC for _ in outs) if isinstance(outs, (tuple, list)) else VSPEC,
        scratch_shapes=scratch,
        compiler_params=pltpu.CompilerParams(vmem_limit_bytes=60 << 20, **kwargs),
        cost_estimate=pl.CostEstimate(flops=flops, bytes_accessed=nbytes, transcendentals=0),
    )(*ins)


def sds(*shape, dtype=BF):
    return jax.ShapeDtypeStruct(shape, dtype)


def rope(u, cosine, sine):
    return u * cosine + pltpu.roll(u, 64, 1) * sine


def whole(ref):
    value = ref[...]
    return value.reshape(value.shape[0] * value.shape[1], value.shape[2])


LOG2E = 1.4426950408889634
SCALE = 1.0 / math.sqrt(96)
SCALE2 = SCALE * LOG2E


def scores_of(keys, query, limit, j):
    s = dot_nt(keys[j], query) * SCALE2
    pos = lax.broadcasted_iota(jnp.int32, s.shape, 0) + j * 256
    return jnp.where(pos.astype(F32) <= limit, s, neg_big)


def front_kernel(xh, slab, wo, cs, sn, limits, bg, slab_gu, wd,
                 xg, wqkv, wout, q, keys, values, mix, mix_t, stat, bgg, wgu, wdown,
                 wo2, vt,
                 ag_s, ag_r, s1, r1, s2, r2, s3, r3, bg_s, bg_r, g1, h1, g2, h2, g3, h3,
                 ws, wr, ks, kr, vs, vr, ds, dr, local):
    p = Place()
    greet(all_to_all_devices(p) + [p.sib, p.ynb])
    gather = RingGather(p, xg, ag_s, ag_r)
    spread = Spread(p, slab, wqkv, local, s1, r1, s2, r2, s3, r3)
    gather_bg = RingGather(p, bgg, bg_s, bg_r)
    spread_gu = Spread(p, slab_gu, wgu, local, g1, h1, g2, h2, g3, h3)
    xg[p.chip] = xh[...]
    gather.start()
    wo2[p.g] = wo[...]
    swap = remote(wo2.at[p.g], wo2.at[p.g], ws.at[0], wr.at[0], p.ynb)
    swap.start()
    spread.start()
    bgg[p.chip] = bg[...]
    here = p.g * 2 + p.core
    there = (1 - p.g) * 2 + p.core
    wdown[here] = wd[...]
    d_swap = remote(wdown.at[here], wdown.at[here], ds.at[0], dr.at[0], p.ynb)
    d_sib = remote(wdown.at[here], wdown.at[here], ds.at[1], dr.at[1], p.sib)
    d_sib2 = remote(wdown.at[there], wdown.at[there], ds.at[2], dr.at[2], p.sib)
    gather.pump(1)
    remote(wo2.at[1 - p.g], wo2.at[1 - p.g], ws.at[0], wr.at[0], p.ynb).wait_recv()
    mine = p.x * 2 + p.core
    theirs = (1 - p.x) * 2 + p.core
    wout[mine] = wo2[p.x]
    to_x = remote(wo2.at[1 - p.x], wout.at[mine], ws.at[1], wr.at[1], p.xnb)
    to_x.start()
    to_s = remote(wout.at[mine], wout.at[mine], ws.at[2], wr.at[2], p.sib)
    to_s.start()
    spread.pump(1)
    gather.pump(2)
    remote(wo2.at[0], wout.at[theirs], ws.at[1], wr.at[1], p.xnb).wait_recv()
    to_s2 = remote(wout.at[theirs], wout.at[theirs], ws.at[3], wr.at[3], p.sib)
    to_s2.start()
    spread.pump(2)
    for t in range(3, CHIPS):
        gather.pump(t)
        spread.pump(t)
    gather_bg.start()
    spread_gu.start()
    d_swap.start()
    d_sib.start()
    spread.finish()

    def kv_copy(i, n):
        ref, send, recv = ((keys, ks, kr), (values, vs, vr))[n]
        part = ref.at[i, pl.ds(pl.multiple_of(p.core * TOK, TOK), TOK)]
        return remote(part, part, send.at[i], recv.at[i], p.sib)

    def kv_in(i, n):
        ref, send, recv = ((keys, ks, kr), (values, vs, vr))[n]
        part = ref.at[i, pl.ds(pl.multiple_of((1 - p.core) * TOK, TOK), TOK)]
        return remote(part, part, send.at[i], recv.at[i], p.sib)

    def project(i):
        lin = dot(xg[i], whole(wqkv))
        cosine, sine = cs[i], sn[i]
        q[i, pl.ds(0, TOK)] = rope(lin[:, 0:128], cosine, sine).astype(BF)
        q[i, pl.ds(TOK, TOK)] = rope(lin[:, 128:256], cosine, sine).astype(BF)
        own = pl.ds(pl.multiple_of(p.core * TOK, TOK), TOK)
        keys[i, own] = rope(lin[:, 256:384], cosine, sine).astype(BF)
        values[i, own] = lin[:, 384:512].astype(BF)
        kv_copy(i, 0).start()
        kv_copy(i, 1).start()

    def attend(i):
        query = q[i]
        limit = limits[i]

        def chunk(j, state):
            top, total, acc = state
            s = scores_of(keys, query, limit, j)
            new_top = jnp.maximum(top, jnp.max(s, axis=0, keepdims=True))
            fade = jnp.exp2(top - new_top)
            w = jnp.exp2(s - new_top)
            total = total * fade + jnp.sum(w, axis=0, keepdims=True)
            acc = acc * fade + dot(vt[j], w.astype(BF))
            return new_top, total, acc

        start = (jnp.full((1, 256), neg_big, F32), jnp.zeros((1, 256), F32),
                 jnp.zeros((PAD, 256), F32))
        top, total, acc = lax.fori_loop(0, i + 1, chunk, start)
        acc = acc / total
        mix_t[i] = acc
        stat[i] = top + jnp.log2(total)
        out = acc.T.astype(BF)
        mix[i, :, pl.ds(0, PAD)] = out[:TOK]
        mix[i, :, pl.ds(PAD, PAD)] = out[TOK:]

    for i in range(CHIPS):
        project(i)
        gather_bg.pump_some(i, i + 1)
    spread_gu.pump(1)
    for i in range(CHIPS):
        for n in range(2):
            kv_in(i, n).wait_recv()
        vt[i] = values[i].astype(F32).T.astype(BF)
    done = CHIPS
    for i in range(CHIPS):
        attend(i)
        gather_bg.pump_some(done, done + (2 if i < 4 else 3))
        done += 2 if i < 4 else 3
        if 1 <= i < CHIPS - 1:
            spread_gu.pump(i + 1)
        if i == 3:
            remote(wdown.at[there], wdown.at[there], ds.at[0], dr.at[0], p.ynb).wait_recv()
            d_sib2.start()
    spread_gu.finish()
    gather.finish()
    gather_bg.finish()
    for copy in (swap, to_x, to_s, to_s2, d_swap, d_sib, d_sib2):
        copy.wait_send()
    for n, slot in ((2, p.x), (3, 1 - p.x)):
        rest = slot * 2 + 1 - p.core
        remote(wout.at[rest], wout.at[rest], ws.at[n], wr.at[n], p.sib).wait_recv()
    for n, slot in ((1, p.g), (2, 1 - p.g)):
        rest = slot * 2 + 1 - p.core
        remote(wdown.at[rest], wdown.at[rest], ds.at[n], dr.at[n], p.sib).wait_recv()
    for i in range(CHIPS):
        for n in range(2):
            kv_copy(i, n).wait_send()


def front(*ins):
    dma = pltpu.SemaphoreType.DMA
    return call(
        front_kernel,
        (sds(CHIPS, TOK, 1536), sds(32, 48, 512), sds(4, 48, 1536), sds(CHIPS, 2 * TOK, PAD),
         sds(CHIPS, 2 * TOK, PAD), sds(CHIPS, 2 * TOK, PAD),
         sds(CHIPS, TOK, 2 * PAD), sds(CHIPS, PAD, 256, dtype=F32), sds(CHIPS, 1, 256, dtype=F32),
         sds(CHIPS, TOK, 1536), sds(32, 48, 1024), sds(4, 128, 1536)),
        ins,
        [VMEM((2, 48, 1536), BF), VMEM((CHIPS, PAD, 256), BF)]
        + RingGather.sems + Spread.sems + RingGather.sems + Spread.sems
        + [dma((4,)), dma((4,))] + [dma((CHIPS,))] * 4 + [dma((3,)), dma((3,)), dma],
        1, 5 * 10**9, 20 << 20,
    )


def dot_tn(a, b):
    return lax.dot_general(a, b, (((0,), (0,)), ((), ())), preferred_element_type=F32)


def rows_of(k):
    return pl.ds(k * ROWS, ROWS)


def mid_kernel(mix, wout, tokens, wgu, wdown, bgg, hidden, grad, inner, dgu, dwd, grad_rows, dout,
               x2, gub, low, part, own, scale, out, held, out2, held2,
               rs_s, rs_r, ag_s, ag_r, rs2_s, rs2_r, ag2_s, ag2_r):
    p = Place()
    greet([p.next, p.prev])
    scatter = RingScatter(p, out, held, rs_s, rs_r)
    gather = RingGather(p, x2, ag_s, ag_r)
    scatter2 = RingScatter(p, out2, held2, rs2_s, rs2_r)
    gather2 = RingGather(p, low, ag2_s, ag2_r)
    for t in range(CHIPS):
        part[...] = dot(mix[scatter.dest(t)], wout[...])
        if t < CHIPS - 1:
            scatter.push(t, lambda k: part[rows_of(k)])
    for k in range(CHUNKS):
        rows = rows_of(k)
        h = tokens[rows].astype(F32) + part[rows] + scatter.last(k)
        r = lax.rsqrt(jnp.mean(h * h, axis=-1, keepdims=True) + epsilon)
        hidden[rows] = h
        scale[rows] = jnp.broadcast_to(r, (ROWS, 128))
        x2[p.chip, rows] = (h * r).astype(BF)
        gather.start(k)

    def feed(b, target):
        lin = dot(x2[b], wgu[...])
        gate, up = lin[:, :512], lin[:, 512:]
        sigma = jax.nn.sigmoid(gate)
        act = gate * sigma
        inner[b] = (act * up).astype(BF)
        back = dot_nt(bgg[b], wdown[...])
        gub[b, :, pl.ds(0, 512)] = (back * up * (sigma + act * (1.0 - sigma))).astype(BF)
        gub[b, :, pl.ds(512, 512)] = (back * act).astype(BF)
        target[...] = dot_nt(gub[b], wgu[...])

    feed(p.chip, own)
    for t in range(1, CHIPS):
        gather.pump(t)
        feed(p.behind(t), part)
        scatter2.push(t - 1, lambda k: part[rows_of(k)])
    for k in range(CHUNKS):
        rows = rows_of(k)
        a = own[rows] + scatter2.last(k)
        h = hidden[rows]
        r = scale[rows, pl.ds(0, 1)]
        value = (bgg[p.chip, rows].astype(F32) + r * a
                 - h * (r * r * r) * jnp.mean(a * h, axis=-1, keepdims=True))
        grad[rows] = value
        low[p.chip, rows] = value.astype(BF)
        gather2.start(k)

    def weight_part(n):
        if n < 12:
            cols = pl.ds(n * 128, 128)
            dgu[cols] = dot_tn(whole(x2.at[:, :, cols]), whole(gub)).astype(BF)
        else:
            cols = pl.ds((n - 12) * 128, 128)
            dwd[cols] = dot_tn(whole(inner.at[:, :, cols]), whole(bgg)).astype(BF)

    def head_part(b):
        rows = dot_nt(low[b], wout[...]).astype(BF)
        grad_rows[b, pl.ds(0, TOK)] = rows[:, :PAD]
        grad_rows[b, pl.ds(TOK, TOK)] = rows[:, PAD:]

    head_part(p.chip)
    for t in range(1, CHIPS):
        for n in range(2 * t - 2, 2 * t):
            weight_part(n)
        gather2.pump(t)
        head_part(p.behind(t))
    weight_part(14)
    weight_part(15)
    for n in range(2):
        cols = pl.ds(n * 128, 128)
        dout[cols] = dot_tn(whole(mix.at[:, :, cols]), whole(low)).astype(BF)
    scatter.finish()
    gather.finish()
    scatter2.finish()
    gather2.finish()


def middle(mix, wout, tokens, wgu, wdown, bgg):
    return call(
        mid_kernel,
        (sds(TOK, 1536, dtype=F32), sds(TOK, 1536, dtype=F32), sds(CHIPS, TOK, 512), sds(1536, 1024),
         sds(512, 1536), sds(CHIPS, 2 * TOK, PAD), sds(256, 1536)),
        (mix, wout, tokens, wgu, wdown, bgg),
        [VMEM((CHIPS, TOK, 1536), BF), VMEM((CHIPS, TOK, 1024), BF), VMEM((CHIPS, TOK, 1536), BF),
         VMEM((TOK, 1536), F32), VMEM((TOK, 1536), F32), VMEM((TOK, 128), F32)]
        + RingScatter.bufs * 2 + RingScatter.sems + RingGather.sems + RingScatter.sems + RingGather.sems,
        3, 15 * 10**9, 20 << 20,
    )


def tail_kernel(q, keys, values, limits, grad_rows, mix_t, stat, cs, sn, inner, wdown, hidden, valid, dgu, dwd,
                xg, wqkv, dout, tokens, grad, w_gate, w_up,
                result, input_back, got_qkv, dout_sum, d_gate, d_up, gain_sum, dwd_sum,
                kt, dk, dv, dkv_low, dkv_in, back_out, dqkv, part, out, held, out2, held2,
                gu1, gu2, gu3, gu4, qk1, qk2, qk3, qk4, got_gu, d_in, d_pair, d_y, o_in, o_pair, o_two, o_y,
                rs_s, rs_r, rs2_s, rs2_r, a1, a2, a3, a4, a5, a6, c1, c2, c3, c4, c5, c6,
                ds, dr, xs, xr, os, orr):
    p = Place()
    greet(all_to_all_devices(p) + [p.sib, p.ynb])
    scatter = RingScatter(p, out, held, rs_s, rs_r)
    scatter2 = RingScatter(p, out2, held2, rs2_s, rs2_r)
    collect = Collect(p, dgu, got_gu, (gu1, gu2, gu3, gu4), (a1, a2, a3, a4, a5, a6))
    collect2 = Collect(p, dqkv, got_qkv, (qk1, qk2, qk3, qk4), (c1, c2, c3, c4, c5, c6))
    collect.start()
    fold = remote(dwd.at[:, 1 - p.core], d_in, ds.at[0], dr.at[0], p.sib)
    fold.start()
    y_fold = remote(d_pair.at[1 - p.g], d_y, ds.at[1], dr.at[1], p.ynb)
    o_fold = remote(dout.at[:, 1 - p.core], o_in, os.at[0], orr.at[0], p.sib)
    o_fold.start()
    x_fold = remote(o_pair.at[1 - p.x], o_two.at[p.x], os.at[1], orr.at[1], p.xnb)
    x_here = remote(o_pair.at[0], o_two.at[1 - p.x], os.at[1], orr.at[1], p.xnb)
    oy_fold = remote(o_two.at[1 - p.g], o_y, os.at[2], orr.at[2], p.ynb)

    def branch(t):
        part[...] = dot(inner[scatter.dest(t)], wdown[...])
        if t < CHIPS - 1:
            scatter.push(t, lambda k: part[rows_of(k)])

    branch(0)

    def turn(n, carry):
        kt[n] = keys[n].astype(F32).T.astype(BF)
        dk[n] = jnp.zeros((256, PAD), F32)
        dv[n] = jnp.zeros((256, PAD), F32)
        return carry

    lax.fori_loop(0, CHIPS, turn, 0)

    def attend(i):
        query = q[i]
        limit = limits[i]
        do = grad_rows[i]
        lse = stat[i]
        delta = jnp.sum(do.astype(F32).T * mix_t[i], axis=0, keepdims=True)

        def chunk(j, acc):
            w = jnp.exp2(scores_of(keys, query, limit, j) - lse)
            dp = dot_nt(values[j], do)
            ds_low = (w * (dp - delta)).astype(BF)
            dk[j] += dot(ds_low, query)
            dv[j] += dot(w.astype(BF), do)
            return acc + dot(kt[j], ds_low)

        acc = lax.fori_loop(0, i + 1, chunk, jnp.zeros((PAD, 256), F32))
        dq = acc.T * SCALE
        cosine, sine = cs[i], -sn[i]
        back_out[i, :, pl.ds(0, PAD)] = rope(dq[:TOK], cosine, sine).astype(BF)
        back_out[i, :, pl.ds(PAD, PAD)] = rope(dq[TOK:], cosine, sine).astype(BF)

    def fold_pairs():
        fold.wait_recv()
        for n in range(2):
            d_pair[n] = (dwd[n, p.core].astype(F32) + d_in[n].astype(F32)).astype(BF)
        y_fold.start()
        o_fold.wait_recv()
        for n in range(2):
            o_pair[n] = (dout[n, p.core].astype(F32) + o_in[n].astype(F32)).astype(BF)
        x_fold.start()

    for m in range(3):
        collect.pair_up(m)
    for i in range(CHIPS):
        attend(i)
        if i < 5:
            collect.pair_up(i + 3)
        if 0 < i < CHIPS - 1:
            branch(i)
            collect.send(i - 1)
        if i == 5:
            fold_pairs()
    collect.send(6)
    collect.send(7)
    for n in range(CHIPS):
        for c in range(2):
            rows = pl.ds(c * TOK, TOK)
            dkv_low[0, n, c] = dk[n, rows].astype(BF)
            dkv_low[1, n, c] = dv[n, rows].astype(BF)
    swap = remote(dkv_low.at[:, :, 1 - p.core], dkv_in, xs, xr, p.sib)
    swap.start()
    branch(CHIPS - 1)
    for k in range(CHUNKS):
        rows = rows_of(k)
        result[rows] = (valid[rows] * (hidden[rows] + part[rows] + scatter.last(k))).astype(BF)
    o_two[p.x] = o_pair[p.x]
    x_here.wait_recv()
    oy_fold.start()
    swap.wait_recv()

    def keys_back(n, carry):
        own = pl.ds(pl.multiple_of(p.core * TOK, TOK), TOK)
        back_out[n, :, pl.ds(2 * PAD, PAD)] = rope(
            (dk[n, own] + dkv_in[0, n].astype(F32)) * SCALE, cs[n], -sn[n]).astype(BF)
        back_out[n, :, pl.ds(3 * PAD, PAD)] = (dv[n, own] + dkv_in[1, n].astype(F32)).astype(BF)
        return carry

    lax.fori_loop(0, CHIPS, keys_back, 0)

    def weight_part(n):
        value = dot_tn(whole(xg.at[:, :, pl.ds(n * 384, 384)]), whole(back_out)).astype(BF)
        dqkv[n // 2, pl.ds((n % 2) * 4, 4)] = value.reshape(4, 2, 48, 512)

    for t in range(CHIPS):
        part[...] = dot_nt(back_out[scatter2.dest(t)], whole(wqkv))
        if t < CHIPS - 1:
            scatter2.push(t, lambda k: part[rows_of(k)])
        if t == 0:
            for n in range(4):
                weight_part(n)
            collect2.start()
        if 1 <= t <= 4:
            collect2.pair_up(2 * t - 2)
            collect2.pair_up(2 * t - 1)
        if 2 <= t <= 5:
            collect2.send(2 * t - 4)
            collect2.send(2 * t - 3)
        if t == 5:
            y_fold.wait_recv()
            dwd_sum[...] = d_pair[p.g].astype(F32) + d_y[...].astype(F32)
            oy_fold.wait_recv()
            dout_sum[...] = o_two[p.g].astype(F32) + o_y[...].astype(F32)
        if t == 6:
            collect.receive()
            total = jnp.zeros((48, 128), F32)
            for chip in range(CHIPS):
                for g in range(2):
                    cols = pl.ds(g * 2048 + chip * 256, 256)
                    for n, (target, weight) in enumerate(((d_gate, w_gate), (d_up, w_up))):
                        piece = got_gu[chip, :, pl.ds(n * 512 + g * 256, 256)]
                        target[:, cols] = piece
                        product = piece.astype(F32) * weight[:, cols].astype(F32)
                        total = total + product[:, :128] + product[:, 128:]
            gain_sum[...] = total
    for k in range(CHUNKS):
        rows = rows_of(k)
        c = part[rows] + scatter2.last(k)
        h = tokens[rows].astype(F32)
        r = lax.rsqrt(jnp.mean(h * h, axis=-1, keepdims=True) + epsilon)
        input_back[rows] = (grad[rows] + r * c
                            - h * (r * r * r) * jnp.mean(c * h, axis=-1, keepdims=True)).astype(BF)
    collect2.receive()
    collect.finish()
    collect2.finish()
    scatter.finish()
    scatter2.finish()
    for copy in (fold, y_fold, swap, o_fold, x_fold, oy_fold):
        copy.wait_send()


def tail(*ins):
    dma = pltpu.SemaphoreType.DMA
    return call(
        tail_kernel,
        (sds(TOK, 1536), sds(TOK, 1536), sds(CHIPS, 48, 512), sds(48, 1536, dtype=F32), sds(48, 4096),
         sds(48, 4096), sds(48, 128, dtype=F32), sds(TOK, 1536, dtype=F32)),
        ins,
        [VMEM((CHIPS, PAD, 256), BF), VMEM((CHIPS, 256, PAD), F32), VMEM((CHIPS, 256, PAD), F32),
         VMEM((2, CHIPS, 2, TOK, PAD), BF), VMEM((2, CHIPS, TOK, PAD), BF), VMEM((CHIPS, TOK, 4 * PAD), BF),
         VMEM((2, CHIPS, 2, 48, 512), BF), VMEM((TOK, 1536), F32)]
        + RingScatter.bufs * 2 + Collect.bufs(48, 1024) + Collect.bufs(48, 512)
        + [VMEM((CHIPS, 48, 1024), BF), VMEM((2, TOK, 1536), BF), VMEM((2, TOK, 1536), BF), VMEM((TOK, 1536), BF),
           VMEM((2, 48, 1536), BF), VMEM((2, 48, 1536), BF), VMEM((2, 48, 1536), BF), VMEM((48, 1536), BF)]
        + RingScatter.sems * 2 + Collect.sems * 2 + [dma((2,)), dma((2,)), dma, dma, dma((3,)), dma((3,))],
        5, 10 * 10**9, 20 << 20,
    )


def pad_heads(weight, heads):
    w = weight.reshape(weight.shape[0], heads, 2, 48)
    return jnp.pad(w, ((0, 0), (0, 0), (0, 0), (0, 16))).reshape(weight.shape[0], heads, PAD)


def by_chip(slab):
    return slab.reshape((2, LINE) + slab.shape[1:]).swapaxes(0, 1).reshape(slab.shape)


def by_head(slab):
    return slab.reshape((LINE, 2) + slab.shape[1:]).swapaxes(0, 1).reshape(slab.shape)


def plane_device(hidden_in, lengths, attn_gain, w_query, w_key, w_value, w_out, mlp_gain, w_gate, w_up,
                 w_down, out_grad):
    core = lax.axis_index("seq") % 2
    length = lengths[0]
    gain_one = attn_gain.astype(F32)[:, None]
    gain_two = mlp_gain.astype(F32)[:, None]
    tokens = hidden_in[0].astype(F32)
    r_one = norm_scale(tokens)
    xh = (tokens * r_one).astype(BF)
    own_pos = lax.axis_index("seq") * TOK + jnp.arange(TOK, dtype=jnp.int32)
    valid = (own_pos < length).astype(F32)[:, None]
    bg = (valid * out_grad[0].astype(F32)).astype(BF)

    scaled = lambda w, gain: (w.astype(F32) * gain).astype(BF)
    wq = pad_heads(scaled(w_query, gain_one), 16).reshape(48, 8, 2 * PAD)
    wk = pad_heads(scaled(w_key, gain_one), 8)
    wv = pad_heads(scaled(w_value, gain_one), 8)
    slab_qkv = by_chip(jnp.concatenate([wq, wk, wv], axis=-1).swapaxes(0, 1))
    ff = lambda w: scaled(w, gain_two).reshape(48, 2, 8, 256).transpose(2, 0, 1, 3).reshape(8, 48, 512)
    slab_gu = jnp.concatenate([ff(w_gate), ff(w_up)], axis=-1)

    positions = (2 * jnp.arange(CHIPS, dtype=jnp.int32)[:, None] + core) * TOK + jnp.arange(TOK, dtype=jnp.int32)
    cosine, sine = rope_tables(positions.reshape(-1))
    cosine = jnp.pad(cosine, ((0, 0), (0, 16)))
    sine = jnp.pad(sine, ((0, 0), (0, 16)))
    cs = jnp.concatenate([cosine, cosine], axis=-1).reshape(CHIPS, TOK, PAD)
    sn = jnp.concatenate([-sine, sine], axis=-1).reshape(CHIPS, TOK, PAD)
    limit = jnp.minimum(positions, length - 1).astype(F32)
    limits = jnp.concatenate([limit, limit], axis=-1).reshape(CHIPS, 1, 2 * TOK)

    xg, wqkv, wout4, q, keys, values, mix, mix_t, stat, bgg, wgu, wdown = front(
        xh, slab_qkv, w_out, cs, sn, limits, bg, slab_gu, w_down)
    wout = jnp.pad(wout4, ((0, 0), (0, 16), (0, 0))).reshape(256, 1536)
    wgu = wgu.reshape(1536, 1024)
    wdown = wdown.reshape(512, 1536)
    hidden, grad, inner, dgu, dwd, grad_rows, dout = middle(mix, wout, hidden_in[0], wgu, wdown, bgg)
    dout = dout.reshape(2, 2, 64, 1536)[:, :, :48]
    result, input_back, got_qkv, dout_sum, d_gate, d_up, gain_sum, dwd_sum = tail(
        q, keys, values, limits, grad_rows, mix_t, stat, cs, sn, inner, wdown, hidden, valid,
        dgu.reshape(2, CHIPS, 2, 48, 1024), dwd.reshape(2, 2, TOK, 1536), xg, wqkv, dout, hidden_in[0], grad,
        w_gate, w_up)

    got_qkv = by_head(got_qkv).swapaxes(0, 1).astype(F32)
    unpad = lambda v: v.reshape(48, -1, 2, 64)[:, :, :, :48].reshape(48, -1)
    d_q, d_k, d_v = unpad(got_qkv[:, :, :256]), unpad(got_qkv[:, :, 256:384]), unpad(got_qkv[:, :, 384:])
    along = lambda w, d: jnp.sum(w.astype(F32) * d, axis=-1)
    return (
        result[None],
        input_back[None],
        along(w_query, d_q) + along(w_key, d_k) + along(w_value, d_v),
        d_q * gain_one,
        d_k * gain_one,
        d_v * gain_one,
        dout_sum,
        jnp.sum(gain_sum, axis=-1),
        d_gate.astype(F32) * gain_two,
        d_up.astype(F32) * gain_two,
        dwd_sum,
    )


def solution(mesh):
    placed = (
        P("grp", "seq", None),
        P("grp"),
        P(("grp", "seq")),
        P(("grp", "seq"), None),
        P(("grp", "seq"), None),
        P(("grp", "seq"), None),
        P(("grp", "seq"), None),
        P(("grp", "seq")),
        P(("grp", "seq"), None),
        P(("grp", "seq"), None),
        P(("grp", "seq"), None),
        P("grp", "seq", None),
    )
    small = mesh.shape["grp"] == 2 and mesh.shape["seq"] == 2 * CHIPS
    return jax.shard_map(
        plane_device if small else per_device,
        mesh=mesh,
        in_specs=placed,
        out_specs=(
            P("grp", "seq", None),
            P("grp", "seq", None),
            P(("grp", "seq")),
            P(("grp", "seq"), None),
            P(("grp", "seq"), None),
            P(("grp", "seq"), None),
            P(("grp", "seq"), None),
            P(("grp", "seq")),
            P(("grp", "seq"), None),
            P(("grp", "seq"), None),
            P(("grp", "seq"), None),
        ),
        check_vma=False,
    )
```

```python
import math

import jax
import jax.numpy as jnp
from jax import lax
from jax.experimental import pallas as pl
from jax.experimental.pallas import tpu as pltpu
from jax.sharding import PartitionSpec as P

H = 16
KVH = 8
HD = 96
KBLK = 256


epsilon = 1e-05
rope_base = 100000.0
neg_big = -1e30


def rope_tables(positions):
    half_dim = HD // 2
    frequency = jnp.exp(-math.log(rope_base) * (2.0 * jnp.arange(half_dim, dtype=jnp.float32) / HD))
    angles = positions.astype(jnp.float32)[:, None] * frequency[None, :]
    return (jnp.cos(angles), jnp.sin(angles))


def rotate(values, cosine, sine_tab):
    half_dim = values.shape[-1] // 2
    first_half = values[..., :half_dim]
    second_half = values[..., half_dim:]
    cos_wide = cosine[:, None, :]
    sin_wide = sine_tab[:, None, :]
    return jnp.concatenate(
        [
            first_half * cos_wide - second_half * sin_wide,
            second_half * cos_wide + first_half * sin_wide,
        ],
        axis=-1,
    )


def unrotate(values, cosine, sine_tab):
    half_dim = values.shape[-1] // 2
    first_half = values[..., :half_dim]
    second_half = values[..., half_dim:]
    cos_wide = cosine[:, None, :]
    sin_wide = sine_tab[:, None, :]
    return jnp.concatenate(
        [
            first_half * cos_wide + second_half * sin_wide,
            second_half * cos_wide - first_half * sin_wide,
        ],
        axis=-1,
    )


def norm_scale(values):
    return lax.rsqrt(jnp.mean(values * values, axis=-1, keepdims=True) + epsilon)


def block_scores(queries, key_block, offset, positions, length):
    score_scale = 1.0 / math.sqrt(HD)
    raw_scores = (
        jnp.einsum("tkgd,skd->kgts", queries, key_block, preferred_element_type=jnp.float32)
        * score_scale
    )
    key_pos = offset + jnp.arange(key_block.shape[0], dtype=jnp.int32)
    allowed = (key_pos[None, :] <= positions[:, None]) & (key_pos[None, :] < length)
    return jnp.where(allowed[None, None], raw_scores, neg_big)


def block_needed(offset, positions, length):
    return (offset <= positions[-1]) & (offset < length)


def attend_forward(queries, key_blocks, value_blocks, positions, length):
    tok_count = queries.shape[0]
    group_size = queries.shape[2]
    offsets = jnp.arange(key_blocks.shape[0], dtype=jnp.int32) * KBLK

    def stat_step(carried, element):
        key_block, offset = element

        def stat_update(state):
            running_max, running_total = state
            scores = block_scores(queries, key_block, offset, positions, length)
            new_max = jnp.maximum(running_max, jnp.max(scores, axis=-1))
            new_total = running_total * jnp.exp(running_max - new_max) + jnp.sum(
                jnp.exp(scores - new_max[..., None]), axis=-1
            )
            return (new_max, new_total)

        return (
            lax.cond(
                block_needed(offset, positions, length), stat_update, lambda state: state, carried
            ),
            None,
        )

    start_max = jnp.full((KVH, group_size, tok_count), neg_big, jnp.float32)
    start_total = jnp.zeros((KVH, group_size, tok_count), jnp.float32)
    (row_max, row_total), unused = lax.scan(
        stat_step, (start_max, start_total), (key_blocks, offsets)
    )
    log_total = row_max + jnp.log(row_total)

    def value_step(carried, element):
        key_block, value_block, offset = element

        def value_update(state):
            accumulated, exact_sum = state
            scores = block_scores(queries, key_block, offset, positions, length)
            probs = jnp.exp(scores - log_total[..., None])
            weights = probs.astype(jnp.bfloat16)
            accumulated = accumulated + jnp.einsum(
                "kgts,skd->tkgd", weights, value_block, preferred_element_type=jnp.float32
            )
            exact_sum = exact_sum + jnp.einsum(
                "kgts,skd->tkgd",
                probs,
                value_block.astype(jnp.float32),
                preferred_element_type=jnp.float32,
            )
            return (accumulated, exact_sum)

        return (
            lax.cond(
                block_needed(offset, positions, length), value_update, lambda state: state, carried
            ),
            None,
        )

    start_acc = jnp.zeros((tok_count, KVH, group_size, HD), jnp.float32)
    (attended, exact_out), unused = lax.scan(
        value_step, (start_acc, start_acc), (key_blocks, value_blocks, offsets)
    )
    return (attended, exact_out, log_total)


def attend_backward(
    queries, key_blocks, value_blocks, attn_back, exact_out, log_total, positions, length
):
    tok_count = queries.shape[0]
    group_size = queries.shape[2]
    block_keys = key_blocks.shape[1]
    score_scale = 1.0 / math.sqrt(HD)
    offsets = jnp.arange(key_blocks.shape[0], dtype=jnp.int32) * KBLK
    delta = jnp.einsum("tkgd,tkgd->kgt", attn_back.astype(jnp.float32), exact_out)

    def grad_step(query_acc, element):
        key_block, value_block, offset = element

        def compute(acc):
            scores = block_scores(queries, key_block, offset, positions, length)
            probs = jnp.exp(scores - log_total[..., None])
            weights = probs.astype(jnp.bfloat16)
            dprobs = jnp.einsum(
                "tkgd,skd->kgts", attn_back, value_block, preferred_element_type=jnp.float32
            )
            score_back = (probs * (dprobs - delta[..., None])).astype(jnp.bfloat16)
            acc = acc + score_scale * jnp.einsum(
                "kgts,skd->tkgd", score_back, key_block, preferred_element_type=jnp.float32
            )
            key_part = score_scale * jnp.einsum(
                "kgts,tkgd->skd", score_back, queries, preferred_element_type=jnp.float32
            )
            value_part = jnp.einsum(
                "kgts,tkgd->skd", weights, attn_back, preferred_element_type=jnp.float32
            )
            return (acc, key_part, value_part)

        def skip(acc):
            empty = jnp.zeros((block_keys, KVH, HD), jnp.float32)
            return (acc, empty, empty)

        acc, key_part, value_part = lax.cond(
            block_needed(offset, positions, length), compute, skip, query_acc
        )
        return (acc, (key_part, value_part))

    start_query = jnp.zeros((tok_count, KVH, group_size, HD), jnp.float32)
    query_grad, (key_parts, value_parts) = lax.scan(
        grad_step, start_query, (key_blocks, value_blocks, offsets)
    )
    return (query_grad, key_parts.reshape(-1, KVH * HD), value_parts.reshape(-1, KVH * HD))


def split_rows(values, groups_count, seq_count):
    return values.reshape(
        (groups_count, seq_count, values.shape[0] // (groups_count * seq_count)) + values.shape[1:]
    )


def per_device(
    hidden_in,
    lengths,
    attn_gain,
    w_query,
    w_key,
    w_value,
    w_out,
    mlp_gain,
    w_gate,
    w_up,
    w_down,
    out_grad,
):
    tok_count = hidden_in.shape[1]
    group_size = H // KVH
    groups_count = lax.axis_size("grp")
    seq_count = lax.axis_size("seq")
    positions = lax.axis_index("seq") * tok_count + jnp.arange(tok_count, dtype=jnp.int32)
    length = lengths[0]
    valid_rows = (positions < length).astype(jnp.float32)[:, None]
    cosine, sine_tab = rope_tables(positions)
    front_weights = (
        lax.all_gather(attn_gain, ("grp", "seq"), axis=0, tiled=True),
        lax.all_gather(w_query, ("grp", "seq"), axis=0, tiled=True),
        lax.all_gather(w_key, ("grp", "seq"), axis=0, tiled=True),
        lax.all_gather(w_value, ("grp", "seq"), axis=0, tiled=True),
        lax.all_gather(w_out, ("grp", "seq"), axis=0, tiled=True),
        lax.all_gather(mlp_gain, ("grp", "seq"), axis=0, tiled=True),
        lax.all_gather(w_gate, ("grp", "seq"), axis=0, tiled=True),
        lax.all_gather(w_up, ("grp", "seq"), axis=0, tiled=True),
        lax.all_gather(w_down, ("grp", "seq"), axis=0, tiled=True),
    )
    gain_one, query_w, key_w, value_w, out_w, gain_two, gate_w, up_w, down_w = front_weights
    tokens_in = hidden_in[0].astype(jnp.float32)
    scale_one = norm_scale(tokens_in)
    normed = (tokens_in * scale_one * gain_one.astype(jnp.float32)).astype(jnp.bfloat16)
    query_lin = jnp.dot(normed, query_w, preferred_element_type=jnp.float32)
    key_lin = jnp.dot(normed, key_w, preferred_element_type=jnp.float32)
    value_lin = jnp.dot(normed, value_w, preferred_element_type=jnp.float32)
    queries = (
        rotate(query_lin.reshape(tok_count, H, HD), cosine, sine_tab)
        .astype(jnp.bfloat16)
        .reshape(tok_count, KVH, group_size, HD)
    )
    key_rot = (
        rotate(key_lin.reshape(tok_count, KVH, HD), cosine, sine_tab)
        .astype(jnp.bfloat16)
        .reshape(tok_count, KVH * HD)
    )
    value_low = value_lin.astype(jnp.bfloat16)
    keys_all, values_all = (
        lax.all_gather(key_rot, "seq", axis=0, tiled=True),
        lax.all_gather(value_low, "seq", axis=0, tiled=True),
    )
    key_blocks = keys_all.reshape(-1, KBLK, KVH, HD)
    value_blocks = values_all.reshape(-1, KBLK, KVH, HD)
    attended, exact_out, log_total = attend_forward(
        queries, key_blocks, value_blocks, positions, length
    )
    attn_mix = attended.reshape(tok_count, H * HD).astype(jnp.bfloat16)
    hidden = tokens_in + jnp.dot(attn_mix, out_w, preferred_element_type=jnp.float32)
    scale_two = norm_scale(hidden)
    normed_mlp = (hidden * scale_two * gain_two.astype(jnp.float32)).astype(jnp.bfloat16)
    gate_lin = jnp.dot(normed_mlp, gate_w, preferred_element_type=jnp.float32)
    up_lin = jnp.dot(normed_mlp, up_w, preferred_element_type=jnp.float32)
    silu_act = jax.nn.silu(gate_lin)
    inner_act = (silu_act * up_lin).astype(jnp.bfloat16)
    branch = jnp.dot(inner_act, down_w, preferred_element_type=jnp.float32)
    result = (valid_rows * (hidden + branch)).astype(jnp.bfloat16)[None]
    gain_one, query_w, key_w, value_w, out_w, gain_two, gate_w, up_w, down_w = front_weights
    cotangent = out_grad[0].astype(jnp.float32)
    branch_grad = valid_rows * cotangent
    branch_low = branch_grad.astype(jnp.bfloat16)
    down_grad = jnp.einsum("tf,td->fd", inner_act, branch_low, preferred_element_type=jnp.float32)
    inner_grad = jnp.einsum("td,fd->tf", branch_low, down_w, preferred_element_type=jnp.float32)
    sigma = jax.nn.sigmoid(gate_lin)
    gate_back = (inner_grad * up_lin * (sigma + gate_lin * sigma * (1.0 - sigma))).astype(
        jnp.bfloat16
    )
    up_back = (inner_grad * silu_act).astype(jnp.bfloat16)
    gate_grad = jnp.einsum("td,tf->df", normed_mlp, gate_back, preferred_element_type=jnp.float32)
    up_grad = jnp.einsum("td,tf->df", normed_mlp, up_back, preferred_element_type=jnp.float32)
    mlp_norm_grad = jnp.einsum(
        "tf,df->td", gate_back, gate_w, preferred_element_type=jnp.float32
    ) + jnp.einsum("tf,df->td", up_back, up_w, preferred_element_type=jnp.float32)
    gain_two_grad = jnp.sum(mlp_norm_grad * hidden * scale_two, axis=0)
    weighted_two = mlp_norm_grad * gain_two.astype(jnp.float32)
    hidden_grad = (
        branch_grad
        + scale_two * weighted_two
        - hidden
        * (scale_two * scale_two * scale_two)
        * jnp.mean(weighted_two * hidden, axis=-1, keepdims=True)
    )
    mlp_seq = (
        lax.psum_scatter(
            split_rows(gain_two_grad, groups_count, seq_count).astype(jnp.bfloat16),
            "seq",
            scatter_dimension=1,
            tiled=True,
        ).astype(jnp.float32),
        lax.psum_scatter(
            split_rows(gate_grad, groups_count, seq_count).astype(jnp.bfloat16),
            "seq",
            scatter_dimension=1,
            tiled=True,
        ).astype(jnp.float32),
        lax.psum_scatter(
            split_rows(up_grad, groups_count, seq_count).astype(jnp.bfloat16),
            "seq",
            scatter_dimension=1,
            tiled=True,
        ).astype(jnp.float32),
        lax.psum_scatter(
            split_rows(down_grad, groups_count, seq_count).astype(jnp.bfloat16),
            "seq",
            scatter_dimension=1,
            tiled=True,
        ).astype(jnp.float32),
    )
    mlp_grp = (
        lax.psum_scatter(
            mlp_seq[0].astype(jnp.bfloat16), "grp", scatter_dimension=0, tiled=True
        ).astype(jnp.float32),
        lax.psum_scatter(
            mlp_seq[1].astype(jnp.bfloat16), "grp", scatter_dimension=0, tiled=True
        ).astype(jnp.float32),
        lax.psum_scatter(
            mlp_seq[2].astype(jnp.bfloat16), "grp", scatter_dimension=0, tiled=True
        ).astype(jnp.float32),
        lax.psum_scatter(
            mlp_seq[3].astype(jnp.bfloat16), "grp", scatter_dimension=0, tiled=True
        ).astype(jnp.float32),
    )
    mlp_grads = tuple((piece.reshape(piece.shape[2:]) for piece in mlp_grp))
    mix_back = hidden_grad.astype(jnp.bfloat16)
    out_w_grad = jnp.einsum("td,te->de", attn_mix, mix_back, preferred_element_type=jnp.float32)
    attn_back = (
        jnp.einsum("te,de->td", mix_back, out_w, preferred_element_type=jnp.float32)
        .astype(jnp.bfloat16)
        .reshape(tok_count, KVH, group_size, HD)
    )
    query_grad, key_grad_all, value_grad_all = attend_backward(
        queries, key_blocks, value_blocks, attn_back, exact_out, log_total, positions, length
    )
    key_grad, value_grad = (
        lax.psum_scatter(
            key_grad_all.astype(jnp.bfloat16), "seq", scatter_dimension=0, tiled=True
        ).astype(jnp.float32),
        lax.psum_scatter(
            value_grad_all.astype(jnp.bfloat16), "seq", scatter_dimension=0, tiled=True
        ).astype(jnp.float32),
    )
    query_back = (
        unrotate(query_grad.reshape(tok_count, H, HD), cosine, sine_tab)
        .astype(jnp.bfloat16)
        .reshape(tok_count, H * HD)
    )
    key_back = (
        unrotate(key_grad.reshape(tok_count, KVH, HD), cosine, sine_tab)
        .astype(jnp.bfloat16)
        .reshape(tok_count, KVH * HD)
    )
    value_back = value_grad.astype(jnp.bfloat16)
    query_w_grad = jnp.einsum("td,te->de", normed, query_back, preferred_element_type=jnp.float32)
    key_w_grad = jnp.einsum("td,te->de", normed, key_back, preferred_element_type=jnp.float32)
    value_w_grad = jnp.einsum("td,te->de", normed, value_back, preferred_element_type=jnp.float32)
    attn_norm_grad = (
        jnp.einsum("te,de->td", query_back, query_w, preferred_element_type=jnp.float32)
        + jnp.einsum("te,de->td", key_back, key_w, preferred_element_type=jnp.float32)
        + jnp.einsum("te,de->td", value_back, value_w, preferred_element_type=jnp.float32)
    )
    gain_one_grad = jnp.sum(attn_norm_grad * tokens_in * scale_one, axis=0)
    weighted_one = attn_norm_grad * gain_one.astype(jnp.float32)
    input_back = (
        hidden_grad
        + scale_one * weighted_one
        - tokens_in
        * (scale_one * scale_one * scale_one)
        * jnp.mean(weighted_one * tokens_in, axis=-1, keepdims=True)
    )
    attn_seq = (
        lax.psum_scatter(
            split_rows(gain_one_grad, groups_count, seq_count).astype(jnp.bfloat16),
            "seq",
            scatter_dimension=1,
            tiled=True,
        ).astype(jnp.float32),
        lax.psum_scatter(
            split_rows(query_w_grad, groups_count, seq_count).astype(jnp.bfloat16),
            "seq",
            scatter_dimension=1,
            tiled=True,
        ).astype(jnp.float32),
        lax.psum_scatter(
            split_rows(key_w_grad, groups_count, seq_count).astype(jnp.bfloat16),
            "seq",
            scatter_dimension=1,
            tiled=True,
        ).astype(jnp.float32),
        lax.psum_scatter(
            split_rows(value_w_grad, groups_count, seq_count).astype(jnp.bfloat16),
            "seq",
            scatter_dimension=1,
            tiled=True,
        ).astype(jnp.float32),
        lax.psum_scatter(
            split_rows(out_w_grad, groups_count, seq_count).astype(jnp.bfloat16),
            "seq",
            scatter_dimension=1,
            tiled=True,
        ).astype(jnp.float32),
    )
    attn_grp = (
        lax.psum_scatter(
            attn_seq[0].astype(jnp.bfloat16), "grp", scatter_dimension=0, tiled=True
        ).astype(jnp.float32),
        lax.psum_scatter(
            attn_seq[1].astype(jnp.bfloat16), "grp", scatter_dimension=0, tiled=True
        ).astype(jnp.float32),
        lax.psum_scatter(
            attn_seq[2].astype(jnp.bfloat16), "grp", scatter_dimension=0, tiled=True
        ).astype(jnp.float32),
        lax.psum_scatter(
            attn_seq[3].astype(jnp.bfloat16), "grp", scatter_dimension=0, tiled=True
        ).astype(jnp.float32),
        lax.psum_scatter(
            attn_seq[4].astype(jnp.bfloat16), "grp", scatter_dimension=0, tiled=True
        ).astype(jnp.float32),
    )
    attn_grads = tuple((piece.reshape(piece.shape[2:]) for piece in attn_grp))
    return (
        result,
        input_back.astype(jnp.bfloat16)[None],
        attn_grads[0],
        attn_grads[1],
        attn_grads[2],
        attn_grads[3],
        attn_grads[4],
        mlp_grads[0],
        mlp_grads[1],
        mlp_grads[2],
        mlp_grads[3],
    )


MESH_ID = pl.DeviceIdType.MESH
VMEM = pltpu.VMEM
LINE = 4
CHIPS = 8
TOK = 128
PAD = 128
CHUNKS = 4
ROWS = TOK // CHUNKS
BF = jnp.bfloat16
F32 = jnp.float32
VSPEC = pl.BlockSpec(memory_space=pltpu.VMEM)


def ring_of(chip):
    z = chip // 2
    x = chip % 2
    return x * LINE + z + x * (LINE - 1 - 2 * z)


def chip_of(ring):
    x = ring // LINE
    q = ring % LINE
    return (q + x * (LINE - 1 - 2 * q)) * 2 + x


class Place:
    def __init__(self):
        self.g = lax.axis_index("grp")
        self.s = lax.axis_index("seq")
        self.core = self.s % 2
        self.chip = self.s // 2
        self.x = self.chip % 2
        self.ring = ring_of(self.chip)
        self.step = 1 - 2 * self.core
        self.next = {"seq": self.at(self.step) * 2 + self.core}
        self.prev = {"seq": self.at(-self.step) * 2 + self.core}
        self.sib = {"seq": self.s + 1 - 2 * self.core}
        self.ynb = {"grp": 1 - self.g}
        self.xnb = {"seq": self.s + 2 - 4 * self.x}

    def at(self, offset):
        return chip_of((self.ring + offset + 8 * CHIPS) % CHIPS)

    def behind(self, t):
        return self.at(-t * self.step)

    def off(self, i):
        return {"seq": ((self.chip + i + CHIPS) % CHIPS) * 2 + self.core}

    def src(self, i):
        return (self.chip - i + CHIPS) % CHIPS


def greet(devices):
    barrier = pltpu.get_barrier_semaphore()
    for device in devices:
        pl.semaphore_signal(barrier, inc=1, device_id=device, device_id_type=MESH_ID)
    pl.semaphore_wait(barrier, len(devices))


def remote(src, dst, send, recv, device):
    return pltpu.make_async_remote_copy(
        src_ref=src, dst_ref=dst, send_sem=send, recv_sem=recv, device_id=device,
        device_id_type=MESH_ID,
    )


class RingGather:
    sems = [pltpu.SemaphoreType.DMA((CHIPS, CHUNKS)), pltpu.SemaphoreType.DMA((CHIPS, CHUNKS))]

    def __init__(self, place, all_ref, send, recv):
        self.place, self.all, self.send, self.recv = place, all_ref, send, recv

    def copy(self, t, k):
        part = self.all.at[self.place.behind(t), pl.ds(k * ROWS, ROWS)]
        return remote(part, part, self.send.at[t, k], self.recv.at[t, k], self.place.next)

    def start(self, k=None):
        for k in range(CHUNKS) if k is None else (k,):
            self.copy(0, k).start()

    def pump(self, t):
        for k in range(CHUNKS):
            self.pass_on(t, k)

    def pass_on(self, t, k):
        self.copy(t - 1, k).wait_recv()
        if t < CHIPS - 1:
            self.copy(t, k).start()

    def pump_some(self, first, last):
        for n in range(first, last):
            self.pass_on(1 + n // CHUNKS, n % CHUNKS)

    def finish(self):
        for t in range(CHIPS - 1):
            for k in range(CHUNKS):
                self.copy(t, k).wait_send()


class RingScatter:
    sems = [pltpu.SemaphoreType.DMA((CHIPS, CHUNKS)), pltpu.SemaphoreType.DMA((CHIPS, CHUNKS))]
    bufs = [VMEM((CHIPS - 1, TOK, 1536), BF), VMEM((CHIPS - 1, TOK, 1536), BF)]

    def __init__(self, place, out, held, send, recv):
        self.place, self.out, self.held, self.send, self.recv = place, out, held, send, recv

    def copy(self, t, k):
        rows = pl.ds(k * ROWS, ROWS)
        return remote(self.out.at[t, rows], self.held.at[t, rows], self.send.at[t, k],
                      self.recv.at[t, k], self.place.next)

    def dest(self, t):
        return self.place.behind(t + 1)

    def push(self, t, term):
        for k in range(CHUNKS):
            rows = pl.ds(k * ROWS, ROWS)
            value = term(k)
            if t > 0:
                self.copy(t - 1, k).wait_recv()
                value = value + self.held[t - 1, rows].astype(F32)
            self.out[t, rows] = value.astype(BF)
            self.copy(t, k).start()

    def last(self, k):
        self.copy(CHIPS - 2, k).wait_recv()
        return self.held[CHIPS - 2, pl.ds(k * ROWS, ROWS)].astype(F32)

    def finish(self):
        for t in range(CHIPS - 1):
            for k in range(CHUNKS):
                self.copy(t, k).wait_send()


class Spread:
    sems = [pltpu.SemaphoreType.DMA((CHIPS,)), pltpu.SemaphoreType.DMA((CHIPS,)),
            pltpu.SemaphoreType.DMA((CHIPS,)), pltpu.SemaphoreType.DMA((CHIPS,)),
            pltpu.SemaphoreType.DMA((2 * CHIPS,)), pltpu.SemaphoreType.DMA((2 * CHIPS,))]

    def __init__(self, place, slab, all_ref, local, *sems):
        self.place, self.slab, self.all, self.local = place, slab, all_ref, local
        self.s1, self.r1, self.s2, self.r2, self.s3, self.r3 = sems

    def block(self, g, chip):
        return self.all.at[g * 16 + chip * 2 + self.place.core]

    def across(self, i):
        p = self.place
        return remote(self.slab.at[(p.chip + i) % CHIPS], self.block(p.g, p.chip), self.s1.at[i],
                      self.r1.at[i], p.off(i))

    def arrived(self, i):
        p = self.place
        return remote(self.slab.at[0], self.block(p.g, p.src(i)), self.s1.at[i], self.r1.at[i],
                      p.off(i))

    def to_y(self, i):
        p = self.place
        part = self.block(p.g, p.src(i))
        return remote(part, part, self.s2.at[i], self.r2.at[i], p.ynb)

    def from_y(self, i):
        p = self.place
        part = self.block(1 - p.g, p.src(i))
        return remote(part, part, self.s2.at[i], self.r2.at[i], p.ynb)

    def to_sib(self, i, other):
        p = self.place
        part = self.block((1 - p.g) if other else p.g, p.src(i))
        n = i + CHIPS * other
        return remote(part, part, self.s3.at[n], self.r3.at[n], p.sib)

    def from_sib(self, i, other):
        p = self.place
        g = (1 - p.g) if other else p.g
        part = self.all.at[g * 16 + p.src(i) * 2 + 1 - p.core]
        n = i + CHIPS * other
        return remote(part, part, self.s3.at[n], self.r3.at[n], p.sib)

    def start(self):
        p = self.place
        own = pltpu.make_async_copy(self.slab.at[p.chip], self.block(p.g, p.chip), self.local)
        own.start()
        for i in range(1, CHIPS):
            self.across(i).start()
        own.wait()
        self.to_y(0).start()
        self.to_sib(0, 0).start()

    def pump(self, i):
        self.arrived(i).wait_recv()
        self.to_y(i).start()
        self.to_sib(i, 0).start()
        self.from_y(i - 1).wait_recv()
        self.to_sib(i - 1, 1).start()

    def finish(self):
        self.from_y(CHIPS - 1).wait_recv()
        self.to_sib(CHIPS - 1, 1).start()
        for i in range(CHIPS):
            self.from_sib(i, 0).wait_recv()
            self.from_sib(i, 1).wait_recv()
        for i in range(CHIPS):
            if i > 0:
                self.across(i).wait_send()
            self.to_y(i).wait_send()
            self.to_sib(i, 0).wait_send()
            self.to_sib(i, 1).wait_send()


class Collect:
    order = tuple(range(1, CHIPS)) + (0,)
    sems = [pltpu.SemaphoreType.DMA((CHIPS,))] * 6

    @staticmethod
    def bufs(rows, columns):
        return [VMEM((CHIPS, 2, rows, columns), BF), VMEM((CHIPS, 2, rows, columns), BF),
                VMEM((CHIPS, rows, columns), BF), VMEM((CHIPS, rows, columns), BF)]

    def __init__(self, place, grads, own, got, bufs, sems):
        self.place, self.grads, self.own, self.got = place, grads, own, got
        self.sib_in, self.pair, self.y_in, self.total = bufs
        self.s1, self.r1, self.s2, self.r2, self.s3, self.r3 = sems

    def sib(self, n):
        p = self.place
        return remote(self.grads.at[:, (p.chip + n) % CHIPS, 1 - p.core], self.sib_in.at[n],
                      self.s1.at[n], self.r1.at[n], p.sib)

    def y(self, n):
        p = self.place
        return remote(self.pair.at[n, 1 - p.g], self.y_in.at[n], self.s2.at[n], self.r2.at[n], p.ynb)

    def across(self, n):
        p = self.place
        return remote(self.total.at[n], self.got.at[p.chip], self.s3.at[n], self.r3.at[n], p.off(n))

    def arrived(self, n):
        p = self.place
        return remote(self.total.at[n], self.got.at[p.src(n)], self.s3.at[n], self.r3.at[n], p.off(n))

    def start(self):
        for n in self.order:
            self.sib(n).start()

    def pair_up(self, m):
        p, n = self.place, self.order[m]
        self.sib(n).wait_recv()
        for g in range(2):
            self.pair[n, g] = (self.own(g, (p.chip + n) % CHIPS).astype(F32)
                               + self.sib_in[n, g].astype(F32)).astype(BF)
        self.y(n).start()

    def send(self, m):
        p, n = self.place, self.order[m]
        self.y(n).wait_recv()
        value = (self.pair[n, p.g].astype(F32) + self.y_in[n].astype(F32)).astype(BF)
        if n == 0:
            self.got[p.chip] = value
        else:
            self.total[n] = value
            self.across(n).start()

    def receive(self):
        for n in range(1, CHIPS):
            self.arrived(n).wait_recv()

    def finish(self):
        for n in range(CHIPS):
            self.sib(n).wait_send()
            self.y(n).wait_send()
            if n > 0:
                self.across(n).wait_send()


def dot(a, b):
    return lax.dot_general(a, b, (((1,), (0,)), ((), ())), preferred_element_type=F32)


def dot_nt(a, b):
    return lax.dot_general(a, b, (((1,), (1,)), ((), ())), preferred_element_type=F32)


def all_to_all_devices(place):
    return [place.off(i) for i in range(1, CHIPS)]


def call(body, outs, ins, scratch, collective_id, far_ins=(), far_outs=(), flops=0, nbytes=0):
    kwargs = {}
    if collective_id is not None:
        kwargs = dict(collective_id=collective_id, has_side_effects=True)
    far = pl.BlockSpec(memory_space=pl.ANY)
    return pl.pallas_call(
        body,
        out_shape=outs,
        in_specs=[far if n in far_ins else VSPEC for n in range(len(ins))],
        out_specs=tuple(far if n in far_outs else VSPEC for n in range(len(outs))),
        scratch_shapes=scratch,
        compiler_params=pltpu.CompilerParams(vmem_limit_bytes=60 << 20, **kwargs),
        cost_estimate=pl.CostEstimate(flops=flops, bytes_accessed=nbytes, transcendentals=0),
    )(*ins)


class Moves:
    def __init__(self, sems, *pairs):
        self.copies = [pltpu.make_async_copy(a, b, sems.at[n]) for n, (a, b) in enumerate(pairs)]

    def start(self, *which):
        for n in which or range(len(self.copies)):
            self.copies[n].start()

    def wait(self, *which):
        for n in which or range(len(self.copies)):
            self.copies[n].wait()


def sds(*shape, dtype=BF):
    return jax.ShapeDtypeStruct(shape, dtype)


def rope(u, cosine, sine):
    return u * cosine + pltpu.roll(u, 64, 1) * sine


def tables(rows, starts, i):
    c_row, s_row = rows[0], rows[1]
    c_start, s_start = starts[0, i], starts[1, i]
    return c_start * c_row - s_start * s_row, s_start * c_row + c_start * s_row


def limit_of(p, i, length):
    lane = lax.broadcasted_iota(jnp.int32, (1, 2 * TOK), 1)
    slot = jnp.where(lane < TOK, lane, lane - TOK) + (2 * i + p.core) * TOK
    return jnp.minimum(slot.astype(F32), length - 1.0)


def valid_of(p, first, rows, length):
    slot = lax.broadcasted_iota(jnp.int32, (rows, 1), 0) + p.s * TOK + first
    return jnp.where(slot.astype(F32) < length, 1.0, 0.0)


def spacing():
    r = lax.broadcasted_iota(jnp.int32, (384, 512), 0)
    c = lax.broadcasted_iota(jnp.int32, (384, 512), 1)
    target = r
    for n in range(1, 8):
        target = target + jnp.where(r >= 48 * n, 16, 0)
    return jnp.where(target == c, 1.0, 0.0).astype(BF)


def chip_of_head(j):
    return 2 * (j % LINE) + j // LINE


def diagonal(n):
    return lax.broadcasted_iota(jnp.int32, (n, n), 0) == lax.broadcasted_iota(jnp.int32, (n, n), 1)


def to_column(row):
    n = row.shape[1]
    return jnp.sum(jnp.where(diagonal(n), jnp.broadcast_to(row, (n, n)), 0.0), axis=1, keepdims=True)


def to_row(column):
    n = column.shape[0]
    return jnp.sum(jnp.where(diagonal(n), jnp.broadcast_to(column, (n, n)), 0.0), axis=0, keepdims=True)


def norm_column(h):
    return lax.rsqrt(jnp.mean(h * h, axis=-1, keepdims=True) + epsilon)


def whole(ref):
    value = ref[...]
    return value.reshape(value.shape[0] * value.shape[1], value.shape[2])


LOG2E = 1.4426950408889634
SCALE = 1.0 / math.sqrt(96)
SCALE2 = SCALE * LOG2E


def scores_of(keys, query, limit, j):
    s = dot_nt(keys[j], query) * SCALE2
    pos = lax.broadcasted_iota(jnp.int32, s.shape, 0) + j * 256
    return jnp.where(pos.astype(F32) <= limit, s, neg_big)


def front_kernel(tokens, wq, wk, wv, wo, gain_one, rope_rows, rope_starts, length_row, out_grad, wg, wu, gain_two, wd,
                 xg_out, wqkv_out, wpad_out, q_out, keys_out, values_out, mix_out, mix_t_out, stat_out,
                 bgg, wgu, wdown,
                 xg, wqkv, wpad, q, keys, values, mix, mix_t, stat,
                 slab, slab_gu, bg, wout, wo2, vt,
                 ag_s, ag_r, s1, r1, s2, r2, s3, r3, bg_s, bg_r, g1, h1, g2, h2, g3, h3,
                 ws, wr, ks, kr, vs, vr, ds, dr, local, move_s):
    p = Place()
    gather = RingGather(p, xg, ag_s, ag_r)
    spread = Spread(p, slab, wqkv, local, s1, r1, s2, r2, s3, r3)
    gather_bg = RingGather(p, bgg, bg_s, bg_r)
    spread_gu = Spread(p, slab_gu, wgu, local, g1, h1, g2, h2, g3, h3)
    here = p.g * 2 + p.core
    there = (1 - p.g) * 2 + p.core
    moves = Moves(move_s, (xg, xg_out), (wqkv, wqkv_out), (wpad, wpad_out), (q, q_out), (keys, keys_out),
                  (values, values_out), (mix, mix_out), (mix_t, mix_t_out), (stat, stat_out),
                  (bg, bgg.at[p.chip]), (wd, wdown.at[here]))
    moves.start(10)
    length = length_row[:, pl.ds(0, 1)]
    h = tokens[...].astype(F32)
    xg[p.chip] = (h * norm_column(h)).astype(BF)
    greet(all_to_all_devices(p) + [p.sib, p.ynb])
    gather.start()
    wo2[p.g] = wo[...]
    swap = remote(wo2.at[p.g], wo2.at[p.g], ws.at[0], wr.at[0], p.ynb)
    swap.start()
    space = spacing()
    gain_column = to_column(gain_one[...].astype(F32))
    gain_column2 = to_column(gain_two[...].astype(F32))
    for n in range(4):
        cols = pl.ds(n * 384, 384)
        wide = dot((wq[:, cols].astype(F32) * gain_column).astype(BF), space).astype(BF)
        for m in range(2):
            slab[chip_of_head(2 * n + m), :, pl.ds(0, 256)] = wide[:, m * 256:m * 256 + 256]
    for n in range(2):
        for source, place in ((wk, 256), (wv, 384)):
            wide = dot((source[:, pl.ds(n * 384, 384)].astype(F32) * gain_column).astype(BF), space).astype(BF)
            for m in range(4):
                slab[chip_of_head(4 * n + m), :, pl.ds(place, 128)] = wide[:, m * 128:m * 128 + 128]
    spread.start()
    bg[...] = (out_grad[...].astype(F32) * valid_of(p, 0, TOK, length)).astype(BF)
    moves.start(9)
    d_swap = remote(wdown.at[here], wdown.at[here], ds.at[0], dr.at[0], p.ynb)
    d_sib = remote(wdown.at[here], wdown.at[here], ds.at[1], dr.at[1], p.sib)
    d_sib2 = remote(wdown.at[there], wdown.at[there], ds.at[2], dr.at[2], p.sib)
    gather.pump(1)
    for chip in range(CHIPS):
        for n, source in enumerate((wg, wu)):
            for g in range(2):
                slab_gu[chip, :, pl.ds(n * 512 + g * 256, 256)] = (
                    source[:, pl.ds(g * 2048 + chip * 256, 256)].astype(F32) * gain_column2).astype(BF)
    remote(wo2.at[1 - p.g], wo2.at[1 - p.g], ws.at[0], wr.at[0], p.ynb).wait_recv()
    mine = p.x * 2 + p.core
    theirs = (1 - p.x) * 2 + p.core
    wout[mine] = wo2[p.x]
    to_x = remote(wo2.at[1 - p.x], wout.at[mine], ws.at[1], wr.at[1], p.xnb)
    to_x.start()
    to_s = remote(wout.at[mine], wout.at[mine], ws.at[2], wr.at[2], p.sib)
    to_s.start()
    spread.pump(1)
    gather.pump(2)
    remote(wo2.at[0], wout.at[theirs], ws.at[1], wr.at[1], p.xnb).wait_recv()
    to_s2 = remote(wout.at[theirs], wout.at[theirs], ws.at[3], wr.at[3], p.sib)
    to_s2.start()
    spread.pump(2)
    for t in range(3, CHIPS):
        gather.pump(t)
        spread.pump(t)
    moves.start(0)
    moves.wait(9, 10)
    gather_bg.start()
    spread_gu.start()
    d_swap.start()
    d_sib.start()
    spread.finish()
    moves.start(1)

    def kv_copy(i, n):
        ref, send, recv = ((keys, ks, kr), (values, vs, vr))[n]
        part = ref.at[i, pl.ds(pl.multiple_of(p.core * TOK, TOK), TOK)]
        return remote(part, part, send.at[i], recv.at[i], p.sib)

    def kv_in(i, n):
        ref, send, recv = ((keys, ks, kr), (values, vs, vr))[n]
        part = ref.at[i, pl.ds(pl.multiple_of((1 - p.core) * TOK, TOK), TOK)]
        return remote(part, part, send.at[i], recv.at[i], p.sib)

    def project(i):
        lin = dot(xg[i], whole(wqkv))
        cosine, sine = tables(rope_rows, rope_starts, i)
        q[i, pl.ds(0, TOK)] = rope(lin[:, 0:128], cosine, sine).astype(BF)
        q[i, pl.ds(TOK, TOK)] = rope(lin[:, 128:256], cosine, sine).astype(BF)
        own = pl.ds(pl.multiple_of(p.core * TOK, TOK), TOK)
        keys[i, own] = rope(lin[:, 256:384], cosine, sine).astype(BF)
        values[i, own] = lin[:, 384:512].astype(BF)
        kv_copy(i, 0).start()
        kv_copy(i, 1).start()

    def attend(i):
        query = q[i]
        limit = limit_of(p, i, length)

        def chunk(j, state):
            top, total, acc = state
            s = scores_of(keys, query, limit, j)
            new_top = jnp.maximum(top, jnp.max(s, axis=0, keepdims=True))
            fade = jnp.exp2(top - new_top)
            w = jnp.exp2(s - new_top)
            total = total * fade + jnp.sum(w, axis=0, keepdims=True)
            acc = acc * fade + dot(vt[j], w.astype(BF))
            return new_top, total, acc

        start = (jnp.full((1, 256), neg_big, F32), jnp.zeros((1, 256), F32),
                 jnp.zeros((PAD, 256), F32))
        top, total, acc = lax.fori_loop(0, i + 1, chunk, start)
        acc = acc / total
        mix_t[i] = acc
        stat[i] = top + jnp.log2(total)
        out = acc.T.astype(BF)
        mix[i, :, pl.ds(0, PAD)] = out[:TOK]
        mix[i, :, pl.ds(PAD, PAD)] = out[TOK:]

    for i in range(CHIPS):
        project(i)
        gather_bg.pump_some(i, i + 1)
    spread_gu.pump(1)
    for i in range(CHIPS):
        for n in range(2):
            kv_in(i, n).wait_recv()
        vt[i] = values[i].astype(F32).T.astype(BF)
    moves.start(3, 4, 5)
    done = CHIPS
    for i in range(CHIPS):
        attend(i)
        gather_bg.pump_some(done, done + (2 if i < 4 else 3))
        done += 2 if i < 4 else 3
        if 1 <= i < CHIPS - 1:
            spread_gu.pump(i + 1)
        if i == 3:
            remote(wdown.at[there], wdown.at[there], ds.at[0], dr.at[0], p.ynb).wait_recv()
            d_sib2.start()
    for n, slot in ((2, p.x), (3, 1 - p.x)):
        rest = slot * 2 + 1 - p.core
        remote(wout.at[rest], wout.at[rest], ws.at[n], wr.at[n], p.sib).wait_recv()
    wpad[...] = jnp.zeros_like(wpad)
    for n in range(4):
        wpad[n, pl.ds(0, 48)] = wout[n]
    moves.start(2, 6, 7, 8)
    spread_gu.finish()
    gather.finish()
    gather_bg.finish()
    for copy in (swap, to_x, to_s, to_s2, d_swap, d_sib, d_sib2):
        copy.wait_send()
    for n, slot in ((1, p.g), (2, 1 - p.g)):
        rest = slot * 2 + 1 - p.core
        remote(wdown.at[rest], wdown.at[rest], ds.at[n], dr.at[n], p.sib).wait_recv()
    for i in range(CHIPS):
        for n in range(2):
            kv_copy(i, n).wait_send()
    moves.wait(*range(9))


def front(*ins):
    dma = pltpu.SemaphoreType.DMA
    shapes = (((CHIPS, TOK, 1536), BF), ((32, 48, 512), BF), ((4, 64, 1536), BF), ((CHIPS, 2 * TOK, PAD), BF),
              ((CHIPS, 2 * TOK, PAD), BF), ((CHIPS, 2 * TOK, PAD), BF), ((CHIPS, TOK, 2 * PAD), BF),
              ((CHIPS, PAD, 256), F32), ((CHIPS, 1, 256), F32))
    return call(
        front_kernel,
        tuple(sds(*shape, dtype=kind) for shape, kind in shapes)
        + (sds(CHIPS, TOK, 1536), sds(32, 48, 1024), sds(4, 128, 1536)),
        ins,
        [VMEM(shape, kind) for shape, kind in shapes]
        + [VMEM((CHIPS, 48, 512), BF), VMEM((CHIPS, 48, 1024), BF), VMEM((TOK, 1536), BF),
           VMEM((4, 48, 1536), BF), VMEM((2, 48, 1536), BF), VMEM((CHIPS, PAD, 256), BF)]
        + RingGather.sems + Spread.sems + RingGather.sems + Spread.sems
        + [dma((4,)), dma((4,))] + [dma((CHIPS,))] * 4 + [dma((3,)), dma((3,)), dma, dma((11,))],
        1, far_ins=(13,), far_outs=range(12), flops=5 * 10**9, nbytes=20 << 20,
    )


def dot_tn(a, b):
    return lax.dot_general(a, b, (((0,), (0,)), ((), ())), preferred_element_type=F32)


def rows_of(k):
    return pl.ds(k * ROWS, ROWS)


def mid_kernel(mix, wout, tokens, wgu_in, wdown_in, bgg_in, hidden_out, grad_out, inner_out, dgu_out, dwd_out, rows_out, dout,
               hidden, grad, inner, dgu, dwd, grad_rows, wgu, wdown, bgg,
               x2, gub, low, part, own, scale, out, held, out2, held2,
               rs_s, rs_r, ag_s, ag_r, rs2_s, rs2_r, ag2_s, ag2_r, move_s):
    p = Place()
    moves = Moves(move_s, (wgu_in, wgu), (wdown_in, wdown), (bgg_in, bgg), (hidden, hidden_out), (grad, grad_out),
                  (inner, inner_out), (dgu, dgu_out), (dwd, dwd_out), (grad_rows, rows_out))
    moves.start(0, 1, 2)
    greet([p.next, p.prev])
    scatter = RingScatter(p, out, held, rs_s, rs_r)
    gather = RingGather(p, x2, ag_s, ag_r)
    scatter2 = RingScatter(p, out2, held2, rs2_s, rs2_r)
    gather2 = RingGather(p, low, ag2_s, ag2_r)
    for t in range(CHIPS):
        part[...] = dot(mix[scatter.dest(t)], wout[...])
        if t < CHIPS - 1:
            scatter.push(t, lambda k: part[rows_of(k)])
    for k in range(CHUNKS):
        rows = rows_of(k)
        h = tokens[rows].astype(F32) + part[rows] + scatter.last(k)
        r = lax.rsqrt(jnp.mean(h * h, axis=-1, keepdims=True) + epsilon)
        hidden[rows] = h
        scale[rows] = jnp.broadcast_to(r, (ROWS, 128))
        x2[p.chip, rows] = (h * r).astype(BF)
        gather.start(k)

    def feed(b, target):
        lin = dot(x2[b], wgu[...])
        gate, up = lin[:, :512], lin[:, 512:]
        sigma = jax.nn.sigmoid(gate)
        act = gate * sigma
        inner[b] = (act * up).astype(BF)
        back = dot_nt(bgg[b], wdown[...])
        gub[b, :, pl.ds(0, 512)] = (back * up * (sigma + act * (1.0 - sigma))).astype(BF)
        gub[b, :, pl.ds(512, 512)] = (back * act).astype(BF)
        target[...] = dot_nt(gub[b], wgu[...])

    moves.start(3)
    moves.wait(0, 1, 2)
    feed(p.chip, own)
    for t in range(1, CHIPS):
        gather.pump(t)
        feed(p.behind(t), part)
        scatter2.push(t - 1, lambda k: part[rows_of(k)])
    for k in range(CHUNKS):
        rows = rows_of(k)
        a = own[rows] + scatter2.last(k)
        h = hidden[rows]
        r = scale[rows, pl.ds(0, 1)]
        value = (bgg[p.chip, rows].astype(F32) + r * a
                 - h * (r * r * r) * jnp.mean(a * h, axis=-1, keepdims=True))
        grad[rows] = value
        low[p.chip, rows] = value.astype(BF)
        gather2.start(k)

    def weight_part(n):
        if n < 12:
            cols = pl.ds(n * 128, 128)
            dgu[cols] = dot_tn(whole(x2.at[:, :, cols]), whole(gub)).astype(BF)
        else:
            cols = pl.ds((n - 12) * 128, 128)
            dwd[cols] = dot_tn(whole(inner.at[:, :, cols]), whole(bgg)).astype(BF)

    def head_part(b):
        rows = dot_nt(low[b], wout[...]).astype(BF)
        grad_rows[b, pl.ds(0, TOK)] = rows[:, :PAD]
        grad_rows[b, pl.ds(TOK, TOK)] = rows[:, PAD:]

    moves.start(4, 5)
    head_part(p.chip)
    for t in range(1, CHIPS):
        for n in range(2 * t - 2, 2 * t):
            weight_part(n)
        gather2.pump(t)
        head_part(p.behind(t))
    moves.start(8)
    weight_part(14)
    weight_part(15)
    moves.start(6, 7)
    for n in range(2):
        value = dot_tn(whole(mix.at[:, :, pl.ds(n * 128, 128)]), whole(low)).astype(BF)
        dout[2 * n] = value[:48]
        dout[2 * n + 1] = value[64:112]
    moves.wait(*range(3, 9))
    scatter.finish()
    gather.finish()
    scatter2.finish()
    gather2.finish()


def middle(*ins):
    shapes = (((TOK, 1536), F32), ((TOK, 1536), F32), ((CHIPS, TOK, 512), BF), ((1536, 1024), BF), ((512, 1536), BF),
              ((CHIPS, 2 * TOK, PAD), BF))
    return call(
        mid_kernel,
        tuple(sds(*shape, dtype=kind) for shape, kind in shapes) + (sds(4, 48, 1536),),
        ins,
        [VMEM(shape, kind) for shape, kind in shapes]
        + [VMEM((1536, 1024), BF), VMEM((512, 1536), BF), VMEM((CHIPS, TOK, 1536), BF),
           VMEM((CHIPS, TOK, 1536), BF), VMEM((CHIPS, TOK, 1024), BF), VMEM((CHIPS, TOK, 1536), BF),
           VMEM((TOK, 1536), F32), VMEM((TOK, 1536), F32), VMEM((TOK, 128), F32)]
        + RingScatter.bufs * 2 + RingScatter.sems + RingGather.sems + RingScatter.sems + RingGather.sems
        + [pltpu.SemaphoreType.DMA((9,))],
        3, far_ins=(3, 4, 5), far_outs=range(6), flops=15 * 10**9, nbytes=20 << 20,
    )


def tail_kernel(q_in, keys_in, values_in, rows_in, mix_t_in, stat_in, inner_in, wdown_in, hidden_in, dgu_far, dwd_far,
                xg_in, wqkv_in, grad_in, rope_rows, rope_starts, length_row, dout, tokens,
                result, input_back, got_gu, got_qkv, dout_sum, dwd_sum,
                q, keys, values, grad_rows, mix_t, stat, inner, wdown, hidden, dgu, dwd, xg, wqkv, grad,
                kt, dk, dv, dkv_low, dkv_in, back_out, dqkv, part, out, held, out2, held2,
                gu1, gu2, gu3, gu4, qk1, qk2, qk3, qk4, d_in, d_pair, d_y, o_in, o_pair, o_two, o_y,
                rs_s, rs_r, rs2_s, rs2_r, a1, a2, a3, a4, a5, a6, c1, c2, c3, c4, c5, c6,
                ds, dr, xs, xr, os, orr, move_s):
    p = Place()
    moves = Moves(move_s, (inner_in, inner), (wdown_in, wdown), (q_in, q), (keys_in, keys), (values_in, values),
                  (rows_in, grad_rows), (mix_t_in, mix_t), (stat_in, stat), (dgu_far.at[:, :, p.core], dgu),
                  (dwd_far.at[:, p.core], dwd), (hidden_in, hidden), (xg_in, xg), (wqkv_in, wqkv), (grad_in, grad))
    moves.start()
    length = length_row[:, pl.ds(0, 1)]
    greet(all_to_all_devices(p) + [p.sib, p.ynb])
    scatter = RingScatter(p, out, held, rs_s, rs_r)
    scatter2 = RingScatter(p, out2, held2, rs2_s, rs2_r)
    collect = Collect(p, dgu_far, lambda g, chip: dgu[g, chip], got_gu, (gu1, gu2, gu3, gu4), (a1, a2, a3, a4, a5, a6))
    collect2 = Collect(p, dqkv, lambda g, chip: dqkv[g, chip, p.core], got_qkv, (qk1, qk2, qk3, qk4),
                       (c1, c2, c3, c4, c5, c6))
    collect.start()
    fold = remote(dwd_far.at[:, 1 - p.core], d_in, ds.at[0], dr.at[0], p.sib)
    fold.start()
    y_fold = remote(d_pair.at[1 - p.g], d_y, ds.at[1], dr.at[1], p.ynb)
    o_fold = remote(dout.at[:, 1 - p.core], o_in, os.at[0], orr.at[0], p.sib)
    o_fold.start()
    x_fold = remote(o_pair.at[1 - p.x], o_two.at[p.x], os.at[1], orr.at[1], p.xnb)
    x_here = remote(o_pair.at[0], o_two.at[1 - p.x], os.at[1], orr.at[1], p.xnb)
    oy_fold = remote(o_two.at[1 - p.g], o_y, os.at[2], orr.at[2], p.ynb)

    def branch(t):
        part[...] = dot(inner[scatter.dest(t)], wdown[...])
        if t < CHIPS - 1:
            scatter.push(t, lambda k: part[rows_of(k)])

    moves.wait(0, 1)
    branch(0)
    moves.wait(*range(2, 10))

    def turn(n, carry):
        kt[n] = keys[n].astype(F32).T.astype(BF)
        dk[n] = jnp.zeros((256, PAD), F32)
        dv[n] = jnp.zeros((256, PAD), F32)
        return carry

    lax.fori_loop(0, CHIPS, turn, 0)

    def attend(i):
        query = q[i]
        limit = limit_of(p, i, length)
        do = grad_rows[i]
        lse = stat[i]
        delta = jnp.sum(do.astype(F32).T * mix_t[i], axis=0, keepdims=True)

        def chunk(j, acc):
            w = jnp.exp2(scores_of(keys, query, limit, j) - lse)
            dp = dot_nt(values[j], do)
            ds_low = (w * (dp - delta)).astype(BF)
            dk[j] += dot(ds_low, query)
            dv[j] += dot(w.astype(BF), do)
            return acc + dot(kt[j], ds_low)

        acc = lax.fori_loop(0, i + 1, chunk, jnp.zeros((PAD, 256), F32))
        dq = acc.T * SCALE
        cosine, sine = tables(rope_rows, rope_starts, i)
        sine = -sine
        back_out[i, :, pl.ds(0, PAD)] = rope(dq[:TOK], cosine, sine).astype(BF)
        back_out[i, :, pl.ds(PAD, PAD)] = rope(dq[TOK:], cosine, sine).astype(BF)

    def fold_pairs():
        fold.wait_recv()
        for n in range(2):
            d_pair[n] = (dwd[n].astype(F32) + d_in[n].astype(F32)).astype(BF)
        y_fold.start()
        o_fold.wait_recv()
        for n in range(2):
            o_pair[n] = (dout[n, p.core].astype(F32) + o_in[n].astype(F32)).astype(BF)
        x_fold.start()

    for m in range(3):
        collect.pair_up(m)
    for i in range(CHIPS):
        attend(i)
        if i < 5:
            collect.pair_up(i + 3)
        if 0 < i < CHIPS - 1:
            branch(i)
            collect.send(i - 1)
        if i == 5:
            fold_pairs()
    collect.send(6)
    collect.send(7)
    for n in range(CHIPS):
        for c in range(2):
            rows = pl.ds(c * TOK, TOK)
            dkv_low[0, n, c] = dk[n, rows].astype(BF)
            dkv_low[1, n, c] = dv[n, rows].astype(BF)
    swap = remote(dkv_low.at[:, :, 1 - p.core], dkv_in, xs, xr, p.sib)
    swap.start()
    branch(CHIPS - 1)
    moves.wait(*range(10, 14))
    for k in range(CHUNKS):
        rows = rows_of(k)
        result[rows] = (valid_of(p, k * ROWS, ROWS, length)
                        * (hidden[rows] + part[rows] + scatter.last(k))).astype(BF)
    o_two[p.x] = o_pair[p.x]
    x_here.wait_recv()
    oy_fold.start()
    swap.wait_recv()

    def keys_back(n, carry):
        own = pl.ds(pl.multiple_of(p.core * TOK, TOK), TOK)
        cosine, sine = tables(rope_rows, rope_starts, n)
        back_out[n, :, pl.ds(2 * PAD, PAD)] = rope(
            (dk[n, own] + dkv_in[0, n].astype(F32)) * SCALE, cosine, -sine).astype(BF)
        back_out[n, :, pl.ds(3 * PAD, PAD)] = (dv[n, own] + dkv_in[1, n].astype(F32)).astype(BF)
        return carry

    lax.fori_loop(0, CHIPS, keys_back, 0)

    def weight_part(n):
        value = dot_tn(whole(xg.at[:, :, pl.ds(n * 384, 384)]), whole(back_out)).astype(BF)
        dqkv[n // 2, pl.ds((n % 2) * 4, 4)] = value.reshape(4, 2, 48, 512)

    for t in range(CHIPS):
        part[...] = dot_nt(back_out[scatter2.dest(t)], whole(wqkv))
        if t < CHIPS - 1:
            scatter2.push(t, lambda k: part[rows_of(k)])
        if t == 0:
            for n in range(4):
                weight_part(n)
            collect2.start()
        if 1 <= t <= 4:
            collect2.pair_up(2 * t - 2)
            collect2.pair_up(2 * t - 1)
        if 2 <= t <= 5:
            collect2.send(2 * t - 4)
            collect2.send(2 * t - 3)
        if t == 5:
            y_fold.wait_recv()
            dwd_sum[...] = (d_pair[p.g].astype(F32) + d_y[...].astype(F32)).astype(BF)
            oy_fold.wait_recv()
            dout_sum[...] = (o_two[p.g].astype(F32) + o_y[...].astype(F32)).astype(BF)
        if t == 6:
            collect.receive()
    for k in range(CHUNKS):
        rows = rows_of(k)
        c = part[rows] + scatter2.last(k)
        h = tokens[rows].astype(F32)
        r = norm_column(h)
        input_back[rows] = (grad[rows] + r * c
                            - h * (r * r * r) * jnp.mean(c * h, axis=-1, keepdims=True)).astype(BF)
    collect2.receive()
    collect.finish()
    collect2.finish()
    scatter.finish()
    scatter2.finish()
    for copy in (fold, y_fold, swap, o_fold, x_fold, oy_fold):
        copy.wait_send()


def tail(*ins):
    dma = pltpu.SemaphoreType.DMA
    heads = (CHIPS, 2 * TOK, PAD)
    near = [VMEM(heads, BF)] * 4 + [
        VMEM((CHIPS, PAD, 256), F32), VMEM((CHIPS, 1, 256), F32), VMEM((CHIPS, TOK, 512), BF), VMEM((512, 1536), BF),
        VMEM((TOK, 1536), F32), VMEM((2, CHIPS, 48, 1024), BF), VMEM((2, TOK, 1536), BF), VMEM((CHIPS, TOK, 1536), BF),
        VMEM((32, 48, 512), BF), VMEM((TOK, 1536), F32)]
    return call(
        tail_kernel,
        (sds(TOK, 1536), sds(TOK, 1536), sds(CHIPS, 48, 1024), sds(CHIPS, 48, 512), sds(48, 1536), sds(TOK, 1536)),
        ins,
        near + [VMEM((CHIPS, PAD, 256), BF), VMEM((CHIPS, 256, PAD), F32), VMEM((CHIPS, 256, PAD), F32),
         VMEM((2, CHIPS, 2, TOK, PAD), BF), VMEM((2, CHIPS, TOK, PAD), BF), VMEM((CHIPS, TOK, 4 * PAD), BF),
         VMEM((2, CHIPS, 2, 48, 512), BF), VMEM((TOK, 1536), F32)]
        + RingScatter.bufs * 2 + Collect.bufs(48, 1024) + Collect.bufs(48, 512)
        + [VMEM((2, TOK, 1536), BF), VMEM((2, TOK, 1536), BF), VMEM((TOK, 1536), BF),
           VMEM((2, 48, 1536), BF), VMEM((2, 48, 1536), BF), VMEM((2, 48, 1536), BF), VMEM((48, 1536), BF)]
        + RingScatter.sems * 2 + Collect.sems * 2 + [dma((2,)), dma((2,)), dma, dma, dma((3,)), dma((3,)), dma((14,))],
        5, far_ins=range(14), flops=10 * 10**9, nbytes=20 << 20,
    )


def place_kernel(got_gu, got_qkv, dout, dwd, block, back, wq, wk, wv, wg, wu, gain_one, gain_two,
                 block_out, back_out, d_gain_one, d_q, d_k, d_v, d_out, d_gain_two, d_gate, d_up, d_down):
    block_out[...] = block[...]
    back_out[...] = back[...]
    d_out[...] = dout[...].astype(F32)
    d_down[...] = dwd[...].astype(F32)
    space = spacing()
    gain_column = to_column(gain_one[...].astype(F32))
    gain_column2 = to_column(gain_two[...].astype(F32))
    lanes = lambda v: jnp.sum(v, axis=-1, keepdims=True)
    total = jnp.zeros((48, 1), F32)
    for n in range(4):
        cols = pl.ds(n * 384, 384)
        wide = jnp.concatenate([got_qkv[chip_of_head(2 * n + m), :, pl.ds(0, 256)] for m in range(2)], axis=-1)
        value = dot_nt(wide, space)
        total = total + lanes(value * wq[:, cols].astype(F32))
        d_q[:, cols] = value * gain_column
    for n in range(2):
        cols = pl.ds(n * 384, 384)
        for source, target, place in ((wk, d_k, 256), (wv, d_v, 384)):
            wide = jnp.concatenate([got_qkv[chip_of_head(4 * n + m), :, pl.ds(place, 128)] for m in range(4)], axis=-1)
            value = dot_nt(wide, space)
            total = total + lanes(value * source[:, cols].astype(F32))
            target[:, cols] = value * gain_column
    d_gain_one[...] = to_row(total)
    total = jnp.zeros((48, 256), F32)
    for chip in range(CHIPS):
        for g in range(2):
            cols = pl.ds(g * 2048 + chip * 256, 256)
            for n, (target, weight) in enumerate(((d_gate, wg), (d_up, wu))):
                piece = got_gu[chip, :, pl.ds(n * 512 + g * 256, 256)].astype(F32)
                target[:, cols] = piece * gain_column2
                total = total + piece * weight[:, cols].astype(F32)
    d_gain_two[...] = to_row(lanes(total))


def place_all(*ins):
    f = lambda *shape: sds(*shape, dtype=F32)
    return call(
        place_kernel,
        (sds(TOK, 1536), sds(TOK, 1536), f(1, 48), f(48, 1536), f(48, 768), f(48, 768), f(48, 1536), f(1, 48), f(48, 4096),
         f(48, 4096), f(TOK, 1536)),
        ins, [], None, nbytes=10 << 20,
    )


def plane_device(hidden_in, lengths, attn_gain, w_query, w_key, w_value, w_out, mlp_gain, w_gate, w_up,
                 w_down, out_grad):
    core = lax.axis_index("seq") % 2
    gain_one = attn_gain[None]
    gain_two = mlp_gain[None]
    tokens = hidden_in[0]
    length_row = jnp.broadcast_to(lengths.astype(F32)[:, None], (1, 128))

    entry = jnp.arange(PAD, dtype=jnp.int32) % 64
    used = entry < HD // 2
    frequency = jnp.where(used, jnp.exp(-math.log(rope_base) * (2.0 * entry.astype(F32) / HD)), 0.0)
    sign = jnp.where(jnp.arange(PAD) < 64, -1.0, 1.0)

    def both(slots):
        angles = slots.astype(F32)[:, None] * frequency[None, :]
        return jnp.stack([jnp.cos(angles), jnp.sin(angles) * sign])

    rope_rows = both(jnp.arange(TOK, dtype=jnp.int32))
    rope_starts = both((2 * jnp.arange(CHIPS, dtype=jnp.int32) + core) * TOK)[:, :, None]

    xg, wqkv, wpad, q, keys, values, mix, mix_t, stat, bgg, wgu, wdown = front(
        tokens, w_query, w_key, w_value, w_out, gain_one, rope_rows, rope_starts, length_row, out_grad[0],
        w_gate, w_up, gain_two, w_down)
    hidden, grad, inner, dgu, dwd, grad_rows, dout = middle(
        mix, wpad.reshape(256, 1536), tokens, wgu.reshape(1536, 1024), wdown.reshape(512, 1536), bgg)
    block, back, got_gu, got_qkv, dout_sum, dwd_sum = tail(
        q, keys, values, grad_rows, mix_t, stat, inner, wdown.reshape(512, 1536), hidden,
        dgu.reshape(2, CHIPS, 2, 48, 1024), dwd.reshape(2, 2, TOK, 1536), xg, wqkv, grad,
        rope_rows, rope_starts, length_row, dout.reshape(2, 2, 48, 1536), tokens)
    block, back, d_gain_one, d_q, d_k, d_v, d_out, d_gain_two, d_gate, d_up, d_down = place_all(
        got_gu, got_qkv, dout_sum, dwd_sum, block, back, w_query, w_key, w_value, w_gate, w_up, gain_one, gain_two)
    return (block[None], back[None], d_gain_one[0], d_q, d_k, d_v, d_out, d_gain_two[0], d_gate, d_up, d_down)


def solution(mesh):
    placed = (
        P("grp", "seq", None),
        P("grp"),
        P(("grp", "seq")),
        P(("grp", "seq"), None),
        P(("grp", "seq"), None),
        P(("grp", "seq"), None),
        P(("grp", "seq"), None),
        P(("grp", "seq")),
        P(("grp", "seq"), None),
        P(("grp", "seq"), None),
        P(("grp", "seq"), None),
        P("grp", "seq", None),
    )
    small = mesh.shape["grp"] == 2 and mesh.shape["seq"] == 2 * CHIPS
    return jax.shard_map(
        plane_device if small else per_device,
        mesh=mesh,
        in_specs=placed,
        out_specs=(
            P("grp", "seq", None),
            P("grp", "seq", None),
            P(("grp", "seq")),
            P(("grp", "seq"), None),
            P(("grp", "seq"), None),
            P(("grp", "seq"), None),
            P(("grp", "seq"), None),
            P(("grp", "seq")),
            P(("grp", "seq"), None),
            P(("grp", "seq"), None),
            P(("grp", "seq"), None),
        ),
        check_vma=False,
    )
```

```python
import math

import jax
import jax.numpy as jnp
from jax import lax
from jax.experimental import pallas as pl
from jax.experimental.pallas import tpu as pltpu
from jax.sharding import PartitionSpec as P

H = 16
KVH = 8
HD = 96
KBLK = 256


epsilon = 1e-05
rope_base = 100000.0
neg_big = -1e30


def rope_tables(positions):
    half_dim = HD // 2
    frequency = jnp.exp(-math.log(rope_base) * (2.0 * jnp.arange(half_dim, dtype=jnp.float32) / HD))
    angles = positions.astype(jnp.float32)[:, None] * frequency[None, :]
    return (jnp.cos(angles), jnp.sin(angles))


def rotate(values, cosine, sine_tab):
    half_dim = values.shape[-1] // 2
    first_half = values[..., :half_dim]
    second_half = values[..., half_dim:]
    cos_wide = cosine[:, None, :]
    sin_wide = sine_tab[:, None, :]
    return jnp.concatenate(
        [
            first_half * cos_wide - second_half * sin_wide,
            second_half * cos_wide + first_half * sin_wide,
        ],
        axis=-1,
    )


def unrotate(values, cosine, sine_tab):
    half_dim = values.shape[-1] // 2
    first_half = values[..., :half_dim]
    second_half = values[..., half_dim:]
    cos_wide = cosine[:, None, :]
    sin_wide = sine_tab[:, None, :]
    return jnp.concatenate(
        [
            first_half * cos_wide + second_half * sin_wide,
            second_half * cos_wide - first_half * sin_wide,
        ],
        axis=-1,
    )


def norm_scale(values):
    return lax.rsqrt(jnp.mean(values * values, axis=-1, keepdims=True) + epsilon)


def block_scores(queries, key_block, offset, positions, length):
    score_scale = 1.0 / math.sqrt(HD)
    raw_scores = (
        jnp.einsum("tkgd,skd->kgts", queries, key_block, preferred_element_type=jnp.float32)
        * score_scale
    )
    key_pos = offset + jnp.arange(key_block.shape[0], dtype=jnp.int32)
    allowed = (key_pos[None, :] <= positions[:, None]) & (key_pos[None, :] < length)
    return jnp.where(allowed[None, None], raw_scores, neg_big)


def block_needed(offset, positions, length):
    return (offset <= positions[-1]) & (offset < length)


def attend_forward(queries, key_blocks, value_blocks, positions, length):
    tok_count = queries.shape[0]
    group_size = queries.shape[2]
    offsets = jnp.arange(key_blocks.shape[0], dtype=jnp.int32) * KBLK

    def stat_step(carried, element):
        key_block, offset = element

        def stat_update(state):
            running_max, running_total = state
            scores = block_scores(queries, key_block, offset, positions, length)
            new_max = jnp.maximum(running_max, jnp.max(scores, axis=-1))
            new_total = running_total * jnp.exp(running_max - new_max) + jnp.sum(
                jnp.exp(scores - new_max[..., None]), axis=-1
            )
            return (new_max, new_total)

        return (
            lax.cond(
                block_needed(offset, positions, length), stat_update, lambda state: state, carried
            ),
            None,
        )

    start_max = jnp.full((KVH, group_size, tok_count), neg_big, jnp.float32)
    start_total = jnp.zeros((KVH, group_size, tok_count), jnp.float32)
    (row_max, row_total), unused = lax.scan(
        stat_step, (start_max, start_total), (key_blocks, offsets)
    )
    log_total = row_max + jnp.log(row_total)

    def value_step(carried, element):
        key_block, value_block, offset = element

        def value_update(state):
            accumulated, exact_sum = state
            scores = block_scores(queries, key_block, offset, positions, length)
            probs = jnp.exp(scores - log_total[..., None])
            weights = probs.astype(jnp.bfloat16)
            accumulated = accumulated + jnp.einsum(
                "kgts,skd->tkgd", weights, value_block, preferred_element_type=jnp.float32
            )
            exact_sum = exact_sum + jnp.einsum(
                "kgts,skd->tkgd",
                probs,
                value_block.astype(jnp.float32),
                preferred_element_type=jnp.float32,
            )
            return (accumulated, exact_sum)

        return (
            lax.cond(
                block_needed(offset, positions, length), value_update, lambda state: state, carried
            ),
            None,
        )

    start_acc = jnp.zeros((tok_count, KVH, group_size, HD), jnp.float32)
    (attended, exact_out), unused = lax.scan(
        value_step, (start_acc, start_acc), (key_blocks, value_blocks, offsets)
    )
    return (attended, exact_out, log_total)


def attend_backward(
    queries, key_blocks, value_blocks, attn_back, exact_out, log_total, positions, length
):
    tok_count = queries.shape[0]
    group_size = queries.shape[2]
    block_keys = key_blocks.shape[1]
    score_scale = 1.0 / math.sqrt(HD)
    offsets = jnp.arange(key_blocks.shape[0], dtype=jnp.int32) * KBLK
    delta = jnp.einsum("tkgd,tkgd->kgt", attn_back.astype(jnp.float32), exact_out)

    def grad_step(query_acc, element):
        key_block, value_block, offset = element

        def compute(acc):
            scores = block_scores(queries, key_block, offset, positions, length)
            probs = jnp.exp(scores - log_total[..., None])
            weights = probs.astype(jnp.bfloat16)
            dprobs = jnp.einsum(
                "tkgd,skd->kgts", attn_back, value_block, preferred_element_type=jnp.float32
            )
            score_back = (probs * (dprobs - delta[..., None])).astype(jnp.bfloat16)
            acc = acc + score_scale * jnp.einsum(
                "kgts,skd->tkgd", score_back, key_block, preferred_element_type=jnp.float32
            )
            key_part = score_scale * jnp.einsum(
                "kgts,tkgd->skd", score_back, queries, preferred_element_type=jnp.float32
            )
            value_part = jnp.einsum(
                "kgts,tkgd->skd", weights, attn_back, preferred_element_type=jnp.float32
            )
            return (acc, key_part, value_part)

        def skip(acc):
            empty = jnp.zeros((block_keys, KVH, HD), jnp.float32)
            return (acc, empty, empty)

        acc, key_part, value_part = lax.cond(
            block_needed(offset, positions, length), compute, skip, query_acc
        )
        return (acc, (key_part, value_part))

    start_query = jnp.zeros((tok_count, KVH, group_size, HD), jnp.float32)
    query_grad, (key_parts, value_parts) = lax.scan(
        grad_step, start_query, (key_blocks, value_blocks, offsets)
    )
    return (query_grad, key_parts.reshape(-1, KVH * HD), value_parts.reshape(-1, KVH * HD))


def split_rows(values, groups_count, seq_count):
    return values.reshape(
        (groups_count, seq_count, values.shape[0] // (groups_count * seq_count)) + values.shape[1:]
    )


def per_device(
    hidden_in,
    lengths,
    attn_gain,
    w_query,
    w_key,
    w_value,
    w_out,
    mlp_gain,
    w_gate,
    w_up,
    w_down,
    out_grad,
):
    tok_count = hidden_in.shape[1]
    group_size = H // KVH
    groups_count = lax.axis_size("grp")
    seq_count = lax.axis_size("seq")
    positions = lax.axis_index("seq") * tok_count + jnp.arange(tok_count, dtype=jnp.int32)
    length = lengths[0]
    valid_rows = (positions < length).astype(jnp.float32)[:, None]
    cosine, sine_tab = rope_tables(positions)
    front_weights = (
        lax.all_gather(attn_gain, ("grp", "seq"), axis=0, tiled=True),
        lax.all_gather(w_query, ("grp", "seq"), axis=0, tiled=True),
        lax.all_gather(w_key, ("grp", "seq"), axis=0, tiled=True),
        lax.all_gather(w_value, ("grp", "seq"), axis=0, tiled=True),
        lax.all_gather(w_out, ("grp", "seq"), axis=0, tiled=True),
        lax.all_gather(mlp_gain, ("grp", "seq"), axis=0, tiled=True),
        lax.all_gather(w_gate, ("grp", "seq"), axis=0, tiled=True),
        lax.all_gather(w_up, ("grp", "seq"), axis=0, tiled=True),
        lax.all_gather(w_down, ("grp", "seq"), axis=0, tiled=True),
    )
    gain_one, query_w, key_w, value_w, out_w, gain_two, gate_w, up_w, down_w = front_weights
    tokens_in = hidden_in[0].astype(jnp.float32)
    scale_one = norm_scale(tokens_in)
    normed = (tokens_in * scale_one * gain_one.astype(jnp.float32)).astype(jnp.bfloat16)
    query_lin = jnp.dot(normed, query_w, preferred_element_type=jnp.float32)
    key_lin = jnp.dot(normed, key_w, preferred_element_type=jnp.float32)
    value_lin = jnp.dot(normed, value_w, preferred_element_type=jnp.float32)
    queries = (
        rotate(query_lin.reshape(tok_count, H, HD), cosine, sine_tab)
        .astype(jnp.bfloat16)
        .reshape(tok_count, KVH, group_size, HD)
    )
    key_rot = (
        rotate(key_lin.reshape(tok_count, KVH, HD), cosine, sine_tab)
        .astype(jnp.bfloat16)
        .reshape(tok_count, KVH * HD)
    )
    value_low = value_lin.astype(jnp.bfloat16)
    keys_all, values_all = (
        lax.all_gather(key_rot, "seq", axis=0, tiled=True),
        lax.all_gather(value_low, "seq", axis=0, tiled=True),
    )
    key_blocks = keys_all.reshape(-1, KBLK, KVH, HD)
    value_blocks = values_all.reshape(-1, KBLK, KVH, HD)
    attended, exact_out, log_total = attend_forward(
        queries, key_blocks, value_blocks, positions, length
    )
    attn_mix = attended.reshape(tok_count, H * HD).astype(jnp.bfloat16)
    hidden = tokens_in + jnp.dot(attn_mix, out_w, preferred_element_type=jnp.float32)
    scale_two = norm_scale(hidden)
    normed_mlp = (hidden * scale_two * gain_two.astype(jnp.float32)).astype(jnp.bfloat16)
    gate_lin = jnp.dot(normed_mlp, gate_w, preferred_element_type=jnp.float32)
    up_lin = jnp.dot(normed_mlp, up_w, preferred_element_type=jnp.float32)
    silu_act = jax.nn.silu(gate_lin)
    inner_act = (silu_act * up_lin).astype(jnp.bfloat16)
    branch = jnp.dot(inner_act, down_w, preferred_element_type=jnp.float32)
    result = (valid_rows * (hidden + branch)).astype(jnp.bfloat16)[None]
    gain_one, query_w, key_w, value_w, out_w, gain_two, gate_w, up_w, down_w = front_weights
    cotangent = out_grad[0].astype(jnp.float32)
    branch_grad = valid_rows * cotangent
    branch_low = branch_grad.astype(jnp.bfloat16)
    down_grad = jnp.einsum("tf,td->fd", inner_act, branch_low, preferred_element_type=jnp.float32)
    inner_grad = jnp.einsum("td,fd->tf", branch_low, down_w, preferred_element_type=jnp.float32)
    sigma = jax.nn.sigmoid(gate_lin)
    gate_back = (inner_grad * up_lin * (sigma + gate_lin * sigma * (1.0 - sigma))).astype(
        jnp.bfloat16
    )
    up_back = (inner_grad * silu_act).astype(jnp.bfloat16)
    gate_grad = jnp.einsum("td,tf->df", normed_mlp, gate_back, preferred_element_type=jnp.float32)
    up_grad = jnp.einsum("td,tf->df", normed_mlp, up_back, preferred_element_type=jnp.float32)
    mlp_norm_grad = jnp.einsum(
        "tf,df->td", gate_back, gate_w, preferred_element_type=jnp.float32
    ) + jnp.einsum("tf,df->td", up_back, up_w, preferred_element_type=jnp.float32)
    gain_two_grad = jnp.sum(mlp_norm_grad * hidden * scale_two, axis=0)
    weighted_two = mlp_norm_grad * gain_two.astype(jnp.float32)
    hidden_grad = (
        branch_grad
        + scale_two * weighted_two
        - hidden
        * (scale_two * scale_two * scale_two)
        * jnp.mean(weighted_two * hidden, axis=-1, keepdims=True)
    )
    mlp_seq = (
        lax.psum_scatter(
            split_rows(gain_two_grad, groups_count, seq_count).astype(jnp.bfloat16),
            "seq",
            scatter_dimension=1,
            tiled=True,
        ).astype(jnp.float32),
        lax.psum_scatter(
            split_rows(gate_grad, groups_count, seq_count).astype(jnp.bfloat16),
            "seq",
            scatter_dimension=1,
            tiled=True,
        ).astype(jnp.float32),
        lax.psum_scatter(
            split_rows(up_grad, groups_count, seq_count).astype(jnp.bfloat16),
            "seq",
            scatter_dimension=1,
            tiled=True,
        ).astype(jnp.float32),
        lax.psum_scatter(
            split_rows(down_grad, groups_count, seq_count).astype(jnp.bfloat16),
            "seq",
            scatter_dimension=1,
            tiled=True,
        ).astype(jnp.float32),
    )
    mlp_grp = (
        lax.psum_scatter(
            mlp_seq[0].astype(jnp.bfloat16), "grp", scatter_dimension=0, tiled=True
        ).astype(jnp.float32),
        lax.psum_scatter(
            mlp_seq[1].astype(jnp.bfloat16), "grp", scatter_dimension=0, tiled=True
        ).astype(jnp.float32),
        lax.psum_scatter(
            mlp_seq[2].astype(jnp.bfloat16), "grp", scatter_dimension=0, tiled=True
        ).astype(jnp.float32),
        lax.psum_scatter(
            mlp_seq[3].astype(jnp.bfloat16), "grp", scatter_dimension=0, tiled=True
        ).astype(jnp.float32),
    )
    mlp_grads = tuple((piece.reshape(piece.shape[2:]) for piece in mlp_grp))
    mix_back = hidden_grad.astype(jnp.bfloat16)
    out_w_grad = jnp.einsum("td,te->de", attn_mix, mix_back, preferred_element_type=jnp.float32)
    attn_back = (
        jnp.einsum("te,de->td", mix_back, out_w, preferred_element_type=jnp.float32)
        .astype(jnp.bfloat16)
        .reshape(tok_count, KVH, group_size, HD)
    )
    query_grad, key_grad_all, value_grad_all = attend_backward(
        queries, key_blocks, value_blocks, attn_back, exact_out, log_total, positions, length
    )
    key_grad, value_grad = (
        lax.psum_scatter(
            key_grad_all.astype(jnp.bfloat16), "seq", scatter_dimension=0, tiled=True
        ).astype(jnp.float32),
        lax.psum_scatter(
            value_grad_all.astype(jnp.bfloat16), "seq", scatter_dimension=0, tiled=True
        ).astype(jnp.float32),
    )
    query_back = (
        unrotate(query_grad.reshape(tok_count, H, HD), cosine, sine_tab)
        .astype(jnp.bfloat16)
        .reshape(tok_count, H * HD)
    )
    key_back = (
        unrotate(key_grad.reshape(tok_count, KVH, HD), cosine, sine_tab)
        .astype(jnp.bfloat16)
        .reshape(tok_count, KVH * HD)
    )
    value_back = value_grad.astype(jnp.bfloat16)
    query_w_grad = jnp.einsum("td,te->de", normed, query_back, preferred_element_type=jnp.float32)
    key_w_grad = jnp.einsum("td,te->de", normed, key_back, preferred_element_type=jnp.float32)
    value_w_grad = jnp.einsum("td,te->de", normed, value_back, preferred_element_type=jnp.float32)
    attn_norm_grad = (
        jnp.einsum("te,de->td", query_back, query_w, preferred_element_type=jnp.float32)
        + jnp.einsum("te,de->td", key_back, key_w, preferred_element_type=jnp.float32)
        + jnp.einsum("te,de->td", value_back, value_w, preferred_element_type=jnp.float32)
    )
    gain_one_grad = jnp.sum(attn_norm_grad * tokens_in * scale_one, axis=0)
    weighted_one = attn_norm_grad * gain_one.astype(jnp.float32)
    input_back = (
        hidden_grad
        + scale_one * weighted_one
        - tokens_in
        * (scale_one * scale_one * scale_one)
        * jnp.mean(weighted_one * tokens_in, axis=-1, keepdims=True)
    )
    attn_seq = (
        lax.psum_scatter(
            split_rows(gain_one_grad, groups_count, seq_count).astype(jnp.bfloat16),
            "seq",
            scatter_dimension=1,
            tiled=True,
        ).astype(jnp.float32),
        lax.psum_scatter(
            split_rows(query_w_grad, groups_count, seq_count).astype(jnp.bfloat16),
            "seq",
            scatter_dimension=1,
            tiled=True,
        ).astype(jnp.float32),
        lax.psum_scatter(
            split_rows(key_w_grad, groups_count, seq_count).astype(jnp.bfloat16),
            "seq",
            scatter_dimension=1,
            tiled=True,
        ).astype(jnp.float32),
        lax.psum_scatter(
            split_rows(value_w_grad, groups_count, seq_count).astype(jnp.bfloat16),
            "seq",
            scatter_dimension=1,
            tiled=True,
        ).astype(jnp.float32),
        lax.psum_scatter(
            split_rows(out_w_grad, groups_count, seq_count).astype(jnp.bfloat16),
            "seq",
            scatter_dimension=1,
            tiled=True,
        ).astype(jnp.float32),
    )
    attn_grp = (
        lax.psum_scatter(
            attn_seq[0].astype(jnp.bfloat16), "grp", scatter_dimension=0, tiled=True
        ).astype(jnp.float32),
        lax.psum_scatter(
            attn_seq[1].astype(jnp.bfloat16), "grp", scatter_dimension=0, tiled=True
        ).astype(jnp.float32),
        lax.psum_scatter(
            attn_seq[2].astype(jnp.bfloat16), "grp", scatter_dimension=0, tiled=True
        ).astype(jnp.float32),
        lax.psum_scatter(
            attn_seq[3].astype(jnp.bfloat16), "grp", scatter_dimension=0, tiled=True
        ).astype(jnp.float32),
        lax.psum_scatter(
            attn_seq[4].astype(jnp.bfloat16), "grp", scatter_dimension=0, tiled=True
        ).astype(jnp.float32),
    )
    attn_grads = tuple((piece.reshape(piece.shape[2:]) for piece in attn_grp))
    return (
        result,
        input_back.astype(jnp.bfloat16)[None],
        attn_grads[0],
        attn_grads[1],
        attn_grads[2],
        attn_grads[3],
        attn_grads[4],
        mlp_grads[0],
        mlp_grads[1],
        mlp_grads[2],
        mlp_grads[3],
    )


MESH_ID = pl.DeviceIdType.MESH
VMEM = pltpu.VMEM
LINE = 4
CHIPS = 8
TOK = 128
PAD = 128
CHUNKS = 4
ROWS = TOK // CHUNKS
BF = jnp.bfloat16
F32 = jnp.float32
VSPEC = pl.BlockSpec(memory_space=pltpu.VMEM)


def ring_of(chip):
    z = chip // 2
    x = chip % 2
    return x * LINE + z + x * (LINE - 1 - 2 * z)


def chip_of(ring):
    x = ring // LINE
    q = ring % LINE
    return (q + x * (LINE - 1 - 2 * q)) * 2 + x


class Place:
    def __init__(self):
        self.g = lax.axis_index("grp")
        self.s = lax.axis_index("seq")
        self.core = self.s % 2
        self.chip = self.s // 2
        self.x = self.chip % 2
        self.ring = ring_of(self.chip)
        self.step = 1 - 2 * self.core
        self.next = {"seq": self.at(self.step) * 2 + self.core}
        self.prev = {"seq": self.at(-self.step) * 2 + self.core}
        self.sib = {"seq": self.s + 1 - 2 * self.core}
        self.ynb = {"grp": 1 - self.g}
        self.xnb = {"seq": self.s + 2 - 4 * self.x}

    def at(self, offset):
        return chip_of((self.ring + offset + 8 * CHIPS) % CHIPS)

    def behind(self, t):
        return self.at(-t * self.step)

    def off(self, i):
        return {"seq": ((self.chip + i + CHIPS) % CHIPS) * 2 + self.core}

    def src(self, i):
        return (self.chip - i + CHIPS) % CHIPS


def greet(devices):
    barrier = pltpu.get_barrier_semaphore()
    for device in devices:
        pl.semaphore_signal(barrier, inc=1, device_id=device, device_id_type=MESH_ID)
    pl.semaphore_wait(barrier, len(devices))


def remote(src, dst, send, recv, device):
    return pltpu.make_async_remote_copy(
        src_ref=src, dst_ref=dst, send_sem=send, recv_sem=recv, device_id=device,
        device_id_type=MESH_ID,
    )


class RingGather:
    sems = [pltpu.SemaphoreType.DMA((CHIPS, CHUNKS)), pltpu.SemaphoreType.DMA((CHIPS, CHUNKS))]

    def __init__(self, place, all_ref, send, recv):
        self.place, self.all, self.send, self.recv = place, all_ref, send, recv
        self.rows = all_ref.shape[1] // CHUNKS

    def copy(self, t, k):
        part = self.all.at[self.place.behind(t), pl.ds(k * self.rows, self.rows)]
        return remote(part, part, self.send.at[t, k], self.recv.at[t, k], self.place.next)

    def start(self, k=None):
        for k in range(CHUNKS) if k is None else (k,):
            self.copy(0, k).start()

    def pump(self, t):
        for k in range(CHUNKS):
            self.pass_on(t, k)

    def pass_on(self, t, k):
        self.copy(t - 1, k).wait_recv()
        if t < CHIPS - 1:
            self.copy(t, k).start()

    def pump_some(self, first, last):
        for n in range(first, last):
            self.pass_on(1 + n // CHUNKS, n % CHUNKS)

    def finish(self):
        for t in range(CHIPS - 1):
            for k in range(CHUNKS):
                self.copy(t, k).wait_send()


class RingScatter:
    sems = [pltpu.SemaphoreType.DMA((CHIPS, CHUNKS)), pltpu.SemaphoreType.DMA((CHIPS, CHUNKS))]
    bufs = [VMEM((CHIPS - 1, TOK, 1536), BF), VMEM((CHIPS - 1, TOK, 1536), BF)]

    def __init__(self, place, out, held, send, recv):
        self.place, self.out, self.held, self.send, self.recv = place, out, held, send, recv

    def copy(self, t, k):
        rows = pl.ds(k * ROWS, ROWS)
        return remote(self.out.at[t, rows], self.held.at[t, rows], self.send.at[t, k],
                      self.recv.at[t, k], self.place.next)

    def dest(self, t):
        return self.place.behind(t + 1)

    def push(self, t, term):
        for k in range(CHUNKS):
            rows = pl.ds(k * ROWS, ROWS)
            value = term(k)
            if t > 0:
                self.copy(t - 1, k).wait_recv()
                value = value + self.held[t - 1, rows].astype(F32)
            self.out[t, rows] = value.astype(BF)
            self.copy(t, k).start()

    def last(self, k):
        self.copy(CHIPS - 2, k).wait_recv()
        return self.held[CHIPS - 2, pl.ds(k * ROWS, ROWS)].astype(F32)

    def finish(self):
        for t in range(CHIPS - 1):
            for k in range(CHUNKS):
                self.copy(t, k).wait_send()


class Spread:
    sems = [pltpu.SemaphoreType.DMA((CHIPS,)), pltpu.SemaphoreType.DMA((CHIPS,)),
            pltpu.SemaphoreType.DMA((CHIPS,)), pltpu.SemaphoreType.DMA((CHIPS,)),
            pltpu.SemaphoreType.DMA((2 * CHIPS,)), pltpu.SemaphoreType.DMA((2 * CHIPS,))]

    def __init__(self, place, slab, all_ref, local, *sems):
        self.place, self.slab, self.all, self.local = place, slab, all_ref, local
        self.s1, self.r1, self.s2, self.r2, self.s3, self.r3 = sems

    def block(self, g, chip):
        return self.all.at[g * 16 + chip * 2 + self.place.core]

    def across(self, i):
        p = self.place
        return remote(self.slab.at[(p.chip + i) % CHIPS], self.block(p.g, p.chip), self.s1.at[i],
                      self.r1.at[i], p.off(i))

    def arrived(self, i):
        p = self.place
        return remote(self.slab.at[0], self.block(p.g, p.src(i)), self.s1.at[i], self.r1.at[i],
                      p.off(i))

    def to_y(self, i):
        p = self.place
        part = self.block(p.g, p.src(i))
        return remote(part, part, self.s2.at[i], self.r2.at[i], p.ynb)

    def from_y(self, i):
        p = self.place
        part = self.block(1 - p.g, p.src(i))
        return remote(part, part, self.s2.at[i], self.r2.at[i], p.ynb)

    def to_sib(self, i, other):
        p = self.place
        part = self.block((1 - p.g) if other else p.g, p.src(i))
        n = i + CHIPS * other
        return remote(part, part, self.s3.at[n], self.r3.at[n], p.sib)

    def from_sib(self, i, other):
        p = self.place
        g = (1 - p.g) if other else p.g
        part = self.all.at[g * 16 + p.src(i) * 2 + 1 - p.core]
        n = i + CHIPS * other
        return remote(part, part, self.s3.at[n], self.r3.at[n], p.sib)

    def start(self):
        p = self.place
        own = pltpu.make_async_copy(self.slab.at[p.chip], self.block(p.g, p.chip), self.local)
        own.start()
        for i in range(1, CHIPS):
            self.across(i).start()
        own.wait()
        self.to_y(0).start()
        self.to_sib(0, 0).start()

    def pump(self, i):
        self.arrived(i).wait_recv()
        self.to_y(i).start()
        self.to_sib(i, 0).start()
        self.from_y(i - 1).wait_recv()
        self.to_sib(i - 1, 1).start()

    def finish(self):
        self.from_y(CHIPS - 1).wait_recv()
        self.to_sib(CHIPS - 1, 1).start()
        for i in range(CHIPS):
            self.from_sib(i, 0).wait_recv()
            self.from_sib(i, 1).wait_recv()
        for i in range(CHIPS):
            if i > 0:
                self.across(i).wait_send()
            self.to_y(i).wait_send()
            self.to_sib(i, 0).wait_send()
            self.to_sib(i, 1).wait_send()


class Across:
    sems = [pltpu.SemaphoreType.DMA((CHIPS,)), pltpu.SemaphoreType.DMA((CHIPS,))]

    def __init__(self, place, slab, got, local, send, recv):
        self.place, self.slab, self.got, self.send, self.recv = place, slab, got, send, recv
        self.own = pltpu.make_async_copy(slab.at[place.chip], got.at[place.chip], local)

    def to(self, i):
        p = self.place
        return remote(self.slab.at[(p.chip + i) % CHIPS], self.got.at[p.chip], self.send.at[i], self.recv.at[i], p.off(i))

    def arrived(self, i):
        p = self.place
        return remote(self.slab.at[0], self.got.at[p.src(i)], self.send.at[i], self.recv.at[i], p.off(i))

    def start(self):
        self.own.start()
        for i in range(1, CHIPS):
            self.to(i).start()

    def land(self):
        self.own.wait()
        for i in range(1, CHIPS):
            self.arrived(i).wait_recv()

    def sent(self):
        for i in range(1, CHIPS):
            self.to(i).wait_send()


class Quarters:
    sems = [pltpu.SemaphoreType.DMA((3,)), pltpu.SemaphoreType.DMA((3,))]

    def __init__(self, place, view, send, recv):
        p = place
        here, over = view(p.g, p.core), view(1 - p.g, p.core)
        self.y = remote(here, here, send.at[0], recv.at[0], p.ynb)
        self.sib = remote(here, here, send.at[1], recv.at[1], p.sib)
        self.sib2 = remote(over, over, send.at[2], recv.at[2], p.sib)

    def start(self):
        self.y.start()
        self.sib.start()

    def pass_on(self):
        self.y.wait_recv()
        self.sib2.start()

    def arrive(self):
        self.sib.wait_recv()
        self.sib2.wait_recv()

    def finish(self):
        for copy in (self.y, self.sib, self.sib2):
            copy.wait_send()


class Share:
    sems = [pltpu.SemaphoreType.DMA((CHIPS,))] * 4 + [pltpu.SemaphoreType.DMA((2 * CHIPS,))] * 2

    def __init__(self, place, all_ref, *sems):
        self.place, self.all = place, all_ref
        self.s1, self.r1, self.s2, self.r2, self.s3, self.r3 = sems

    def slot(self, t, other):
        p = self.place
        return self.all.at[((1 - p.g) if other else p.g) * 16 + p.behind(t) * 2 + p.core]

    def ring(self, t):
        part = self.slot(t, 0)
        return remote(part, part, self.s1.at[t], self.r1.at[t], self.place.next)

    def y(self, t, back):
        part = self.slot(t, back)
        return remote(part, part, self.s2.at[t], self.r2.at[t], self.place.ynb)

    def to_sib(self, t, other):
        part = self.slot(t, other)
        n = t + CHIPS * other
        return remote(part, part, self.s3.at[n], self.r3.at[n], self.place.sib)

    def from_sib(self, t, other):
        p = self.place
        part = self.all.at[((1 - p.g) if other else p.g) * 16 + p.behind(-t) * 2 + 1 - p.core]
        n = t + CHIPS * other
        return remote(part, part, self.s3.at[n], self.r3.at[n], p.sib)

    def start(self):
        self.ring(0).start()
        self.y(0, 0).start()
        self.to_sib(0, 0).start()

    def pump(self, t):
        self.ring(t - 1).wait_recv()
        if t < CHIPS - 1:
            self.ring(t).start()
        self.y(t, 0).start()
        self.to_sib(t, 0).start()
        self.y(t - 1, 1).wait_recv()
        self.to_sib(t - 1, 1).start()

    def finish(self):
        self.y(CHIPS - 1, 1).wait_recv()
        self.to_sib(CHIPS - 1, 1).start()
        for t in range(CHIPS):
            for other in range(2):
                self.from_sib(t, other).wait_recv()
                self.to_sib(t, other).wait_send()
            self.y(t, 0).wait_send()
            if t < CHIPS - 1:
                self.ring(t).wait_send()


class Collect:
    order = tuple(range(1, CHIPS)) + (0,)
    sems = [pltpu.SemaphoreType.DMA((CHIPS,))] * 6

    @staticmethod
    def bufs(rows, columns):
        return [VMEM((CHIPS, 2, rows, columns), BF), VMEM((CHIPS, 2, rows, columns), BF),
                VMEM((CHIPS, rows, columns), BF), VMEM((CHIPS, rows, columns), BF)]

    def __init__(self, place, grads, own, got, bufs, sems):
        self.place, self.grads, self.own, self.got = place, grads, own, got
        self.sib_in, self.pair, self.y_in, self.total = bufs
        self.s1, self.r1, self.s2, self.r2, self.s3, self.r3 = sems

    def sib(self, n):
        p = self.place
        return remote(self.grads.at[:, (p.chip + n) % CHIPS, 1 - p.core], self.sib_in.at[n],
                      self.s1.at[n], self.r1.at[n], p.sib)

    def y(self, n):
        p = self.place
        return remote(self.pair.at[n, 1 - p.g], self.y_in.at[n], self.s2.at[n], self.r2.at[n], p.ynb)

    def across(self, n):
        p = self.place
        return remote(self.total.at[n], self.got.at[p.chip], self.s3.at[n], self.r3.at[n], p.off(n))

    def arrived(self, n):
        p = self.place
        return remote(self.total.at[n], self.got.at[p.src(n)], self.s3.at[n], self.r3.at[n], p.off(n))

    def start(self):
        for n in self.order:
            self.sib(n).start()

    def pair_up(self, m):
        p, n = self.place, self.order[m]
        self.sib(n).wait_recv()
        for g in range(2):
            self.pair[n, g] = (self.own(g, (p.chip + n) % CHIPS).astype(F32)
                               + self.sib_in[n, g].astype(F32)).astype(BF)
        self.y(n).start()

    def send(self, m):
        p, n = self.place, self.order[m]
        self.y(n).wait_recv()
        value = (self.pair[n, p.g].astype(F32) + self.y_in[n].astype(F32)).astype(BF)
        if n == 0:
            self.got[p.chip] = value
        else:
            self.total[n] = value
            self.across(n).start()

    def receive(self):
        for n in range(1, CHIPS):
            self.arrived(n).wait_recv()

    def finish(self):
        for n in range(CHIPS):
            self.sib(n).wait_send()
            self.y(n).wait_send()
            if n > 0:
                self.across(n).wait_send()


def dot(a, b):
    return lax.dot_general(a, b, (((1,), (0,)), ((), ())), preferred_element_type=F32)


def dot_nt(a, b):
    return lax.dot_general(a, b, (((1,), (1,)), ((), ())), preferred_element_type=F32)


def all_to_all_devices(place):
    return [place.off(i) for i in range(1, CHIPS)]


def call(body, outs, ins, scratch, collective_id, far_ins=(), far_outs=(), flops=0, nbytes=0):
    kwargs = {}
    if collective_id is not None:
        kwargs = dict(collective_id=collective_id, has_side_effects=True)
    far = pl.BlockSpec(memory_space=pl.ANY)
    return pl.pallas_call(
        body,
        out_shape=outs,
        in_specs=[far if n in far_ins else VSPEC for n in range(len(ins))],
        out_specs=tuple(far if n in far_outs else VSPEC for n in range(len(outs))),
        scratch_shapes=scratch,
        compiler_params=pltpu.CompilerParams(vmem_limit_bytes=60 << 20, **kwargs),
        cost_estimate=pl.CostEstimate(flops=flops, bytes_accessed=nbytes, transcendentals=0),
    )(*ins)


class Moves:
    def __init__(self, sems, *pairs):
        self.copies = [pltpu.make_async_copy(a, b, sems.at[n]) for n, (a, b) in enumerate(pairs)]

    def start(self, *which):
        for n in which or range(len(self.copies)):
            self.copies[n].start()

    def wait(self, *which):
        for n in which or range(len(self.copies)):
            self.copies[n].wait()


def sds(*shape, dtype=BF):
    return jax.ShapeDtypeStruct(shape, dtype)


def rope(u, cosine, sine):
    return u * cosine + pltpu.roll(u, 64, 1) * sine


def tables(rows, starts, i):
    c_row, s_row = rows[0], rows[1]
    c_start, s_start = starts[0, i], starts[1, i]
    return c_start * c_row - s_start * s_row, s_start * c_row + c_start * s_row


def limit_of(p, i, length):
    lane = lax.broadcasted_iota(jnp.int32, (1, 2 * TOK), 1)
    slot = jnp.where(lane < TOK, lane, lane - TOK) + (2 * i + p.core) * TOK
    return jnp.minimum(slot.astype(F32), length - 1.0)


def valid_of(p, first, rows, length):
    slot = lax.broadcasted_iota(jnp.int32, (rows, 1), 0) + p.s * TOK + first
    return jnp.where(slot.astype(F32) < length, 1.0, 0.0)


def spacing():
    r = lax.broadcasted_iota(jnp.int32, (384, 512), 0)
    c = lax.broadcasted_iota(jnp.int32, (384, 512), 1)
    target = r
    for n in range(1, 8):
        target = target + jnp.where(r >= 48 * n, 16, 0)
    return jnp.where(target == c, 1.0, 0.0).astype(BF)


def chip_of_head(j):
    return 2 * (j % LINE) + j // LINE


def diagonal(n):
    return lax.broadcasted_iota(jnp.int32, (n, n), 0) == lax.broadcasted_iota(jnp.int32, (n, n), 1)


def to_column(row):
    n = row.shape[1]
    return jnp.sum(jnp.where(diagonal(n), jnp.broadcast_to(row, (n, n)), 0.0), axis=1, keepdims=True)


def to_row(column):
    n = column.shape[0]
    return jnp.sum(jnp.where(diagonal(n), jnp.broadcast_to(column, (n, n)), 0.0), axis=0, keepdims=True)


def norm_column(h):
    return lax.rsqrt(jnp.mean(h * h, axis=-1, keepdims=True) + epsilon)


def whole(ref):
    value = ref[...]
    return value.reshape(value.shape[0] * value.shape[1], value.shape[2])


LOG2E = 1.4426950408889634
SCALE = 1.0 / math.sqrt(96)
SCALE2 = SCALE * LOG2E


def scores_of(keys, query, limit, j):
    s = dot_nt(keys[j], query) * SCALE2
    pos = lax.broadcasted_iota(jnp.int32, s.shape, 0) + j * 256
    return jnp.where(pos.astype(F32) <= limit, s, neg_big)


def dot_tn(a, b):
    return lax.dot_general(a, b, (((0,), (0,)), ((), ())), preferred_element_type=F32)


def rows_of(k):
    return pl.ds(k * ROWS, ROWS)


def main_kernel(tokens, wq, wk, wv, gain_one, rope_rows, rope_starts, length_row, out_grad, wg, wu, gain_two, wo, wd,
                tg_out, wqkv_out, q_out, keys_out, values_out, mix_t_out, stat_out,
                hidden_out, grad_out, inner_out, dgu_out, dwd_out, rows_out, wdown_out, dout,
                tg, wqkv, q, keys, values, mix_t, stat, grad, inner, dgu, dwd, grad_rows,
                slab, slab_gu, mix, vt, bgg, wall, wgu, wdown, mx, wpad, hid, x2, gub, low, part, scale, out2, held2,
                ag_s, ag_r, s1, r1, s2, r2, s3, r3, bg_s, bg_r, g1, h1, o1, p1, o2, p2, o3, p3,
                mx_s, mx_r, rs2_s, rs2_r, ag2_s, ag2_r, ks, kr, vs, vr, q1, q2, q3, q4, local, local2, move_s):
    p = Place()
    gather = RingGather(p, tg, ag_s, ag_r)
    spread = Spread(p, slab, wqkv, local, s1, r1, s2, r2, s3, r3)
    gather_bg = RingGather(p, bgg, bg_s, bg_r)
    across = Across(p, slab_gu, wgu.at[p.g, :, p.core], local2, g1, h1)
    share = Share(p, wall, o1, p1, o2, p2, o3, p3)
    gather_mix = RingGather(p, mx, mx_s, mx_r)
    scatter2 = RingScatter(p, out2, held2, rs2_s, rs2_r)
    gather2 = RingGather(p, low, ag2_s, ag2_r)
    quarters = Quarters(p, lambda g, core: wgu.at[g, :, core], q1, q2)
    quarters2 = Quarters(p, lambda g, core: wdown.at[g, core], q3, q4)
    moves = Moves(move_s, (tg, tg_out), (wqkv, wqkv_out), (q, q_out), (keys, keys_out),
                  (values, values_out), (mix_t, mix_t_out), (stat, stat_out),
                  (hid.at[p.chip], hidden_out), (grad, grad_out), (inner, inner_out), (dgu, dgu_out), (dwd, dwd_out),
                  (grad_rows, rows_out), (wdown, wdown_out),
                  (wo, wall.at[p.g * 16 + p.s]), (wd, wdown.at[p.g, p.core]))
    moves.start(14, 15)
    length = length_row[:, pl.ds(0, 1)]
    tg[p.chip] = tokens[...]
    greet(all_to_all_devices(p) + [p.sib, p.ynb])
    gather.start()
    space = spacing()
    gain_column = to_column(gain_one[...].astype(F32))
    gain_column2 = to_column(gain_two[...].astype(F32))
    for n in range(4):
        cols = pl.ds(n * 384, 384)
        wide = dot((wq[:, cols].astype(F32) * gain_column).astype(BF), space).astype(BF)
        for m in range(2):
            slab[chip_of_head(2 * n + m), :, pl.ds(0, 256)] = wide[:, m * 256:m * 256 + 256]
    for n in range(2):
        for source, place in ((wk, 256), (wv, 384)):
            wide = dot((source[:, pl.ds(n * 384, 384)].astype(F32) * gain_column).astype(BF), space).astype(BF)
            for m in range(4):
                slab[chip_of_head(4 * n + m), :, pl.ds(place, 128)] = wide[:, m * 128:m * 128 + 128]
    spread.start()
    bgg[p.chip] = (out_grad[...].astype(F32) * valid_of(p, 0, TOK, length)).astype(BF)
    gather.pump(1)
    for chip in range(CHIPS):
        for n, source in enumerate((wg, wu)):
            for g in range(2):
                slab_gu[chip, :, pl.ds(n * 512 + g * 256, 256)] = (
                    source[:, pl.ds(g * 2048 + chip * 256, 256)].astype(F32) * gain_column2).astype(BF)
    spread.pump(1)
    for t in range(2, CHIPS):
        gather.pump(t)
        spread.pump(t)
    moves.start(0)
    moves.wait(14, 15)
    gather_bg.start()
    share.start()
    across.start()
    quarters2.start()
    spread.finish()
    moves.start(1)

    def kv_copy(i, n):
        ref, send, recv = ((keys, ks, kr), (values, vs, vr))[n]
        part = ref.at[i, pl.ds(pl.multiple_of(p.core * TOK, TOK), TOK)]
        return remote(part, part, send.at[i], recv.at[i], p.sib)

    def kv_in(i, n):
        ref, send, recv = ((keys, ks, kr), (values, vs, vr))[n]
        part = ref.at[i, pl.ds(pl.multiple_of((1 - p.core) * TOK, TOK), TOK)]
        return remote(part, part, send.at[i], recv.at[i], p.sib)

    def project(i):
        h = tg[i].astype(F32)
        lin = dot((h * norm_column(h)).astype(BF), whole(wqkv))
        cosine, sine = tables(rope_rows, rope_starts, i)
        q[i, pl.ds(0, TOK)] = rope(lin[:, 0:128], cosine, sine).astype(BF)
        q[i, pl.ds(TOK, TOK)] = rope(lin[:, 128:256], cosine, sine).astype(BF)
        own = pl.ds(pl.multiple_of(p.core * TOK, TOK), TOK)
        keys[i, own] = rope(lin[:, 256:384], cosine, sine).astype(BF)
        values[i, own] = lin[:, 384:512].astype(BF)
        kv_copy(i, 0).start()
        kv_copy(i, 1).start()

    def attend(i):
        query = q[i]
        limit = limit_of(p, i, length)

        def chunk(j, state):
            top, total, acc = state
            s = scores_of(keys, query, limit, j)
            new_top = jnp.maximum(top, jnp.max(s, axis=0, keepdims=True))
            fade = jnp.exp2(top - new_top)
            w = jnp.exp2(s - new_top)
            total = total * fade + jnp.sum(w, axis=0, keepdims=True)
            acc = acc * fade + dot(vt[j], w.astype(BF))
            return new_top, total, acc

        start = (jnp.full((1, 256), neg_big, F32), jnp.zeros((1, 256), F32),
                 jnp.zeros((PAD, 256), F32))
        top, total, acc = lax.fori_loop(0, i + 1, chunk, start)
        acc = acc / total
        mix_t[i] = acc
        stat[i] = top + jnp.log2(total)
        low = acc.astype(BF)
        for n in range(4):
            mix[pl.ds(n * 48, 48), pl.ds(i * TOK, TOK)] = low[(n % 2) * 64:(n % 2) * 64 + 48,
                                                              (n // 2) * TOK:(n // 2) * TOK + TOK]

    for i in range(CHIPS):
        project(i)
        gather_bg.pump_some(i, i + 1)
    share.pump(1)
    for i in range(CHIPS):
        for n in range(2):
            kv_in(i, n).wait_recv()
        vt[i] = values[i].astype(F32).T.astype(BF)
    moves.start(2, 3, 4)
    done = CHIPS
    for i in range(CHIPS):
        attend(i)
        gather_bg.pump_some(done, done + (2 if i < 4 else 3))
        done += 2 if i < 4 else 3
        if 1 <= i < CHIPS - 1:
            share.pump(i + 1)
    moves.start(5, 6)
    mx[p.chip] = mix[...]
    gather_mix.start()
    across.land()
    quarters.start()
    wpad[...] = jnp.zeros_like(wpad)
    share.finish()
    quarters2.pass_on()
    def head_of(chip):
        return chip // 2 + LINE * (chip % 2)

    def out_rows(chip):
        return whole(wall.at[pl.ds(4 * head_of(chip), 4)])

    def mixed(chip, b):
        lanes = pl.ds(pl.multiple_of(b * TOK, TOK), TOK)
        return dot_tn(mx[chip, :, lanes], out_rows(chip))

    def first(b, carry):
        hid[b] = tg[b].astype(F32) + mixed(p.chip, b)
        return carry

    lax.fori_loop(0, CHIPS, first, 0)
    for n in range(4):
        wpad[pl.ds(n * 64, 48)] = wall[4 * head_of(p.chip) + n]
    for t in range(1, CHIPS - 1):
        gather_mix.pump(t)

        def more(b, carry):
            hid[b] += mixed(p.behind(t), b)
            return carry

        lax.fori_loop(0, CHIPS, more, 0)
        if t == 5:
            quarters.pass_on()

    def feed(b):
        h = hid[b] + mixed(p.behind(CHIPS - 1), b)
        hid[b] = h
        r = norm_column(h)
        scale[...] = jnp.broadcast_to(r, (TOK, 128))
        x2[b] = (h * r).astype(BF)
        lin = dot(x2[b], wgu[...].reshape(1536, 1024))
        gate, up = lin[:, :512], lin[:, 512:]
        sigma = jax.nn.sigmoid(gate)
        act = gate * sigma
        inner[b] = (act * up).astype(BF)
        back = dot_nt(bgg[b], wdown[...].reshape(512, 1536))
        gub[b, :, pl.ds(0, 512)] = (back * up * (sigma + act * (1.0 - sigma))).astype(BF)
        gub[b, :, pl.ds(512, 512)] = (back * act).astype(BF)
        part[...] = dot_nt(gub[b], wgu[...].reshape(1536, 1024))

    gather_mix.pump(CHIPS - 1)
    quarters.arrive()
    quarters2.arrive()
    moves.start(13)
    for t in range(CHIPS):
        feed(scatter2.dest(t))
        if t < CHIPS - 1:
            scatter2.push(t, lambda k: part[rows_of(k)])
    moves.start(7)
    for k in range(CHUNKS):
        rows = rows_of(k)
        a = part[rows] + scatter2.last(k)
        h = hid[p.chip, rows]
        r = scale[rows, pl.ds(0, 1)]
        value = (bgg[p.chip, rows].astype(F32) + r * a
                 - h * (r * r * r) * jnp.mean(a * h, axis=-1, keepdims=True))
        grad[rows] = value
        low[p.chip, rows] = value.astype(BF)
        gather2.start(k)

    def weight_part(n):
        if n < 12:
            cols = pl.ds(n * 128, 128)
            dgu[cols] = dot_tn(whole(x2.at[:, :, cols]), whole(gub)).astype(BF)
        else:
            cols = pl.ds((n - 12) * 128, 128)
            dwd[cols] = dot_tn(whole(inner.at[:, :, cols]), whole(bgg)).astype(BF)

    def head_part(b):
        rows = dot_nt(low[b], wpad[...]).astype(BF)
        grad_rows[b, pl.ds(0, TOK)] = rows[:, :PAD]
        grad_rows[b, pl.ds(TOK, TOK)] = rows[:, PAD:]

    moves.start(8, 9)
    head_part(p.chip)
    for t in range(1, CHIPS):
        for n in range(2 * t - 2, 2 * t):
            weight_part(n)
        gather2.pump(t)
        head_part(p.behind(t))
    moves.start(12)
    weight_part(14)
    weight_part(15)
    moves.start(10, 11)
    value = dot(mix[...], whole(low)).astype(BF)
    for n in range(4):
        dout[n] = value[48 * n:48 * n + 48]
    moves.wait(*range(14))
    for one in (gather, gather_bg, gather_mix, gather2, scatter2, quarters, quarters2):
        one.finish()
    across.sent()
    for i in range(CHIPS):
        for n in range(2):
            kv_copy(i, n).wait_send()


def main(*ins):
    dma = pltpu.SemaphoreType.DMA
    block = ((CHIPS, TOK, 1536), BF)
    heads = ((CHIPS, 2 * TOK, PAD), BF)
    shapes = (block, ((32, 48, 512), BF), heads, heads, heads, ((CHIPS, PAD, 256), F32), ((CHIPS, 1, 256), F32))
    shapes2 = (((TOK, 1536), F32), ((CHIPS, TOK, 512), BF), ((1536, 1024), BF), ((512, 1536), BF), heads)
    outs = shapes + (((TOK, 1536), F32),) + shapes2 + (((2, 2, TOK, 1536), BF), ((4, 48, 1536), BF))
    near = shapes + shapes2 + (
        ((CHIPS, 48, 512), BF), ((CHIPS, 48, 1024), BF), ((192, 1024), BF), ((CHIPS, PAD, 256), BF), block,
        ((32, 48, 1536), BF), ((2, CHIPS, 2, 48, 1024), BF), ((2, 2, TOK, 1536), BF), ((CHIPS, 192, 1024), BF),
        ((256, 1536), BF), ((CHIPS, TOK, 1536), F32), block, ((CHIPS, TOK, 1024), BF), block, ((TOK, 1536), F32),
        ((TOK, 128), F32))
    return call(
        main_kernel,
        tuple(sds(*shape, dtype=kind) for shape, kind in outs),
        ins,
        [VMEM(shape, kind) for shape, kind in near] + RingScatter.bufs
        + RingGather.sems + Spread.sems + RingGather.sems + Across.sems + Share.sems + RingGather.sems + RingScatter.sems
        + RingGather.sems + [dma((CHIPS,))] * 4 + Quarters.sems * 2 + [dma, dma, dma((16,))],
        1, far_ins=(12, 13), far_outs=range(14), flops=20 * 10**9, nbytes=40 << 20,
    )


def tail_kernel(q_in, keys_in, values_in, rows_in, mix_t_in, stat_in, inner_in, wdown_in, hidden_in, dgu_far, dwd_far,
                xg_in, wqkv_in, grad_in, rope_rows, rope_starts, length_row, dout, tokens,
                result, input_back, got_gu, got_qkv, dout_sum, dwd_sum,
                q, keys, values, grad_rows, mix_t, stat, inner, wdown, hidden, dgu, dwd, xg, wqkv, grad,
                kt, dk, dv, dkv_low, dkv_in, back_out, dqkv, part, out, held, out2, held2,
                gu1, gu2, gu3, gu4, qk1, qk2, qk3, qk4, d_in, d_pair, d_y, o_in, o_pair, o_two, o_y,
                rs_s, rs_r, rs2_s, rs2_r, a1, a2, a3, a4, a5, a6, c1, c2, c3, c4, c5, c6,
                ds, dr, xs, xr, os, orr, move_s):
    p = Place()
    moves = Moves(move_s, (inner_in, inner), (wdown_in, wdown), (q_in, q), (keys_in, keys), (values_in, values),
                  (rows_in, grad_rows), (mix_t_in, mix_t), (stat_in, stat), (dgu_far.at[:, :, p.core], dgu),
                  (dwd_far.at[:, p.core], dwd), (hidden_in, hidden), (xg_in, xg), (wqkv_in, wqkv), (grad_in, grad))
    moves.start()
    length = length_row[:, pl.ds(0, 1)]
    greet(all_to_all_devices(p) + [p.sib, p.ynb])
    scatter = RingScatter(p, out, held, rs_s, rs_r)
    scatter2 = RingScatter(p, out2, held2, rs2_s, rs2_r)
    collect = Collect(p, dgu_far, lambda g, chip: dgu[g, chip], got_gu, (gu1, gu2, gu3, gu4), (a1, a2, a3, a4, a5, a6))
    collect2 = Collect(p, dqkv, lambda g, chip: dqkv[g, chip, p.core], got_qkv, (qk1, qk2, qk3, qk4),
                       (c1, c2, c3, c4, c5, c6))
    collect.start()
    fold = remote(dwd_far.at[:, 1 - p.core], d_in, ds.at[0], dr.at[0], p.sib)
    fold.start()
    y_fold = remote(d_pair.at[1 - p.g], d_y, ds.at[1], dr.at[1], p.ynb)
    o_fold = remote(dout.at[:, 1 - p.core], o_in, os.at[0], orr.at[0], p.sib)
    o_fold.start()
    x_fold = remote(o_pair.at[1 - p.x], o_two.at[p.x], os.at[1], orr.at[1], p.xnb)
    x_here = remote(o_pair.at[0], o_two.at[1 - p.x], os.at[1], orr.at[1], p.xnb)
    oy_fold = remote(o_two.at[1 - p.g], o_y, os.at[2], orr.at[2], p.ynb)

    def branch(t):
        part[...] = dot(inner[scatter.dest(t)], wdown[...])
        if t < CHIPS - 1:
            scatter.push(t, lambda k: part[rows_of(k)])

    moves.wait(0, 1)
    branch(0)
    moves.wait(*range(2, 10))

    def turn(n, carry):
        kt[n] = keys[n].astype(F32).T.astype(BF)
        dk[n] = jnp.zeros((256, PAD), F32)
        dv[n] = jnp.zeros((256, PAD), F32)
        return carry

    lax.fori_loop(0, CHIPS, turn, 0)

    def attend(i):
        query = q[i]
        limit = limit_of(p, i, length)
        do = grad_rows[i]
        lse = stat[i]
        delta = jnp.sum(do.astype(F32).T * mix_t[i], axis=0, keepdims=True)

        def chunk(j, acc):
            w = jnp.exp2(scores_of(keys, query, limit, j) - lse)
            dp = dot_nt(values[j], do)
            ds_low = (w * (dp - delta)).astype(BF)
            dk[j] += dot(ds_low, query)
            dv[j] += dot(w.astype(BF), do)
            return acc + dot(kt[j], ds_low)

        acc = lax.fori_loop(0, i + 1, chunk, jnp.zeros((PAD, 256), F32))
        dq = acc.T * SCALE
        cosine, sine = tables(rope_rows, rope_starts, i)
        sine = -sine
        back_out[i, :, pl.ds(0, PAD)] = rope(dq[:TOK], cosine, sine).astype(BF)
        back_out[i, :, pl.ds(PAD, PAD)] = rope(dq[TOK:], cosine, sine).astype(BF)

    def fold_pairs():
        fold.wait_recv()
        for n in range(2):
            d_pair[n] = (dwd[n].astype(F32) + d_in[n].astype(F32)).astype(BF)
        y_fold.start()
        o_fold.wait_recv()
        for n in range(2):
            o_pair[n] = (dout[n, p.core].astype(F32) + o_in[n].astype(F32)).astype(BF)
        x_fold.start()

    for m in range(3):
        collect.pair_up(m)
    for i in range(CHIPS):
        attend(i)
        if i < 5:
            collect.pair_up(i + 3)
        if 0 < i < CHIPS - 1:
            branch(i)
            collect.send(i - 1)
        if i == 5:
            fold_pairs()
    collect.send(6)
    collect.send(7)
    for n in range(CHIPS):
        for c in range(2):
            rows = pl.ds(c * TOK, TOK)
            dkv_low[0, n, c] = dk[n, rows].astype(BF)
            dkv_low[1, n, c] = dv[n, rows].astype(BF)
    swap = remote(dkv_low.at[:, :, 1 - p.core], dkv_in, xs, xr, p.sib)
    swap.start()
    branch(CHIPS - 1)
    moves.wait(*range(10, 14))
    for k in range(CHUNKS):
        rows = rows_of(k)
        result[rows] = (valid_of(p, k * ROWS, ROWS, length)
                        * (hidden[rows] + part[rows] + scatter.last(k))).astype(BF)
    o_two[p.x] = o_pair[p.x]
    x_here.wait_recv()
    oy_fold.start()
    swap.wait_recv()

    def keys_back(n, carry):
        own = pl.ds(pl.multiple_of(p.core * TOK, TOK), TOK)
        cosine, sine = tables(rope_rows, rope_starts, n)
        back_out[n, :, pl.ds(2 * PAD, PAD)] = rope(
            (dk[n, own] + dkv_in[0, n].astype(F32)) * SCALE, cosine, -sine).astype(BF)
        back_out[n, :, pl.ds(3 * PAD, PAD)] = (dv[n, own] + dkv_in[1, n].astype(F32)).astype(BF)
        return carry

    lax.fori_loop(0, CHIPS, keys_back, 0)

    def again(b, carry):
        h = xg[b].astype(F32)
        xg[b] = (h * norm_column(h)).astype(BF)
        return carry

    lax.fori_loop(0, CHIPS, again, 0)

    def weight_part(n):
        value = dot_tn(whole(xg.at[:, :, pl.ds(n * 384, 384)]), whole(back_out)).astype(BF)
        dqkv[n // 2, pl.ds((n % 2) * 4, 4)] = value.reshape(4, 2, 48, 512)

    for t in range(CHIPS):
        part[...] = dot_nt(back_out[scatter2.dest(t)], whole(wqkv))
        if t < CHIPS - 1:
            scatter2.push(t, lambda k: part[rows_of(k)])
        if t == 0:
            for n in range(4):
                weight_part(n)
            collect2.start()
        if 1 <= t <= 4:
            collect2.pair_up(2 * t - 2)
            collect2.pair_up(2 * t - 1)
        if 2 <= t <= 5:
            collect2.send(2 * t - 4)
            collect2.send(2 * t - 3)
        if t == 5:
            y_fold.wait_recv()
            dwd_sum[...] = (d_pair[p.g].astype(F32) + d_y[...].astype(F32)).astype(BF)
            oy_fold.wait_recv()
            dout_sum[...] = (o_two[p.g].astype(F32) + o_y[...].astype(F32)).astype(BF)
        if t == 6:
            collect.receive()
    for k in range(CHUNKS):
        rows = rows_of(k)
        c = part[rows] + scatter2.last(k)
        h = tokens[rows].astype(F32)
        r = norm_column(h)
        input_back[rows] = (grad[rows] + r * c
                            - h * (r * r * r) * jnp.mean(c * h, axis=-1, keepdims=True)).astype(BF)
    collect2.receive()
    collect.finish()
    collect2.finish()
    scatter.finish()
    scatter2.finish()
    for copy in (fold, y_fold, swap, o_fold, x_fold, oy_fold):
        copy.wait_send()


def tail(*ins):
    dma = pltpu.SemaphoreType.DMA
    heads = (CHIPS, 2 * TOK, PAD)
    near = [VMEM(heads, BF)] * 4 + [
        VMEM((CHIPS, PAD, 256), F32), VMEM((CHIPS, 1, 256), F32), VMEM((CHIPS, TOK, 512), BF), VMEM((512, 1536), BF),
        VMEM((TOK, 1536), F32), VMEM((2, CHIPS, 48, 1024), BF), VMEM((2, TOK, 1536), BF), VMEM((CHIPS, TOK, 1536), BF),
        VMEM((32, 48, 512), BF), VMEM((TOK, 1536), F32)]
    return call(
        tail_kernel,
        (sds(TOK, 1536), sds(TOK, 1536), sds(CHIPS, 48, 1024), sds(CHIPS, 48, 512), sds(48, 1536), sds(TOK, 1536)),
        ins,
        near + [VMEM((CHIPS, PAD, 256), BF), VMEM((CHIPS, 256, PAD), F32), VMEM((CHIPS, 256, PAD), F32),
         VMEM((2, CHIPS, 2, TOK, PAD), BF), VMEM((2, CHIPS, TOK, PAD), BF), VMEM((CHIPS, TOK, 4 * PAD), BF),
         VMEM((2, CHIPS, 2, 48, 512), BF), VMEM((TOK, 1536), F32)]
        + RingScatter.bufs * 2 + Collect.bufs(48, 1024) + Collect.bufs(48, 512)
        + [VMEM((2, TOK, 1536), BF), VMEM((2, TOK, 1536), BF), VMEM((TOK, 1536), BF),
           VMEM((2, 48, 1536), BF), VMEM((2, 48, 1536), BF), VMEM((2, 48, 1536), BF), VMEM((48, 1536), BF)]
        + RingScatter.sems * 2 + Collect.sems * 2 + [dma((2,)), dma((2,)), dma, dma, dma((3,)), dma((3,)), dma((14,))],
        5, far_ins=range(14), flops=10 * 10**9, nbytes=20 << 20,
    )


def place_kernel(got_gu, got_qkv, dout, dwd, block, back, wq, wk, wv, wg, wu, gain_one, gain_two,
                 block_out, back_out, d_gain_one, d_q, d_k, d_v, d_out, d_gain_two, d_gate, d_up, d_down):
    block_out[...] = block[...]
    back_out[...] = back[...]
    d_out[...] = dout[...].astype(F32)
    d_down[...] = dwd[...].astype(F32)
    space = spacing()
    gain_column = to_column(gain_one[...].astype(F32))
    gain_column2 = to_column(gain_two[...].astype(F32))
    lanes = lambda v: jnp.sum(v, axis=-1, keepdims=True)
    total = jnp.zeros((48, 1), F32)
    for n in range(4):
        cols = pl.ds(n * 384, 384)
        wide = jnp.concatenate([got_qkv[chip_of_head(2 * n + m), :, pl.ds(0, 256)] for m in range(2)], axis=-1)
        value = dot_nt(wide, space)
        total = total + lanes(value * wq[:, cols].astype(F32))
        d_q[:, cols] = value * gain_column
    for n in range(2):
        cols = pl.ds(n * 384, 384)
        for source, target, place in ((wk, d_k, 256), (wv, d_v, 384)):
            wide = jnp.concatenate([got_qkv[chip_of_head(4 * n + m), :, pl.ds(place, 128)] for m in range(4)], axis=-1)
            value = dot_nt(wide, space)
            total = total + lanes(value * source[:, cols].astype(F32))
            target[:, cols] = value * gain_column
    d_gain_one[...] = to_row(total)
    total = jnp.zeros((48, 256), F32)
    for chip in range(CHIPS):
        for g in range(2):
            cols = pl.ds(g * 2048 + chip * 256, 256)
            for n, (target, weight) in enumerate(((d_gate, wg), (d_up, wu))):
                piece = got_gu[chip, :, pl.ds(n * 512 + g * 256, 256)].astype(F32)
                target[:, cols] = piece * gain_column2
                total = total + piece * weight[:, cols].astype(F32)
    d_gain_two[...] = to_row(lanes(total))


def place_all(*ins):
    f = lambda *shape: sds(*shape, dtype=F32)
    return call(
        place_kernel,
        (sds(TOK, 1536), sds(TOK, 1536), f(1, 48), f(48, 1536), f(48, 768), f(48, 768), f(48, 1536), f(1, 48), f(48, 4096),
         f(48, 4096), f(TOK, 1536)),
        ins, [], None, nbytes=10 << 20,
    )


def plane_device(hidden_in, lengths, attn_gain, w_query, w_key, w_value, w_out, mlp_gain, w_gate, w_up,
                 w_down, out_grad):
    core = lax.axis_index("seq") % 2
    gain_one = attn_gain[None]
    gain_two = mlp_gain[None]
    tokens = hidden_in[0]
    length_row = jnp.broadcast_to(lengths.astype(F32)[:, None], (1, 128))

    entry = jnp.arange(PAD, dtype=jnp.int32) % 64
    used = entry < HD // 2
    frequency = jnp.where(used, jnp.exp(-math.log(rope_base) * (2.0 * entry.astype(F32) / HD)), 0.0)
    sign = jnp.where(jnp.arange(PAD) < 64, -1.0, 1.0)

    def both(slots):
        angles = slots.astype(F32)[:, None] * frequency[None, :]
        return jnp.stack([jnp.cos(angles), jnp.sin(angles) * sign])

    rope_rows = both(jnp.arange(TOK, dtype=jnp.int32))
    rope_starts = both((2 * jnp.arange(CHIPS, dtype=jnp.int32) + core) * TOK)[:, :, None]

    tg, wqkv, q, keys, values, mix_t, stat, hidden, grad, inner, dgu, dwd, grad_rows, wdown, dout = main(
        tokens, w_query, w_key, w_value, gain_one, rope_rows, rope_starts, length_row, out_grad[0],
        w_gate, w_up, gain_two, w_out, w_down)
    block, back, got_gu, got_qkv, dout_sum, dwd_sum = tail(
        q, keys, values, grad_rows, mix_t, stat, inner, wdown.reshape(512, 1536), hidden,
        dgu.reshape(2, CHIPS, 2, 48, 1024), dwd.reshape(2, 2, TOK, 1536), tg, wqkv, grad,
        rope_rows, rope_starts, length_row, dout.reshape(2, 2, 48, 1536), tokens)
    block, back, d_gain_one, d_q, d_k, d_v, d_out, d_gain_two, d_gate, d_up, d_down = place_all(
        got_gu, got_qkv, dout_sum, dwd_sum, block, back, w_query, w_key, w_value, w_gate, w_up, gain_one, gain_two)
    return (block[None], back[None], d_gain_one[0], d_q, d_k, d_v, d_out, d_gain_two[0], d_gate, d_up, d_down)


def solution(mesh):
    placed = (
        P("grp", "seq", None),
        P("grp"),
        P(("grp", "seq")),
        P(("grp", "seq"), None),
        P(("grp", "seq"), None),
        P(("grp", "seq"), None),
        P(("grp", "seq"), None),
        P(("grp", "seq")),
        P(("grp", "seq"), None),
        P(("grp", "seq"), None),
        P(("grp", "seq"), None),
        P("grp", "seq", None),
    )
    small = mesh.shape["grp"] == 2 and mesh.shape["seq"] == 2 * CHIPS
    return jax.shard_map(
        plane_device if small else per_device,
        mesh=mesh,
        in_specs=placed,
        out_specs=(
            P("grp", "seq", None),
            P("grp", "seq", None),
            P(("grp", "seq")),
            P(("grp", "seq"), None),
            P(("grp", "seq"), None),
            P(("grp", "seq"), None),
            P(("grp", "seq"), None),
            P(("grp", "seq")),
            P(("grp", "seq"), None),
            P(("grp", "seq"), None),
            P(("grp", "seq"), None),
        ),
        check_vma=False,
    )
```

```python
import math

import jax
import jax.numpy as jnp
from jax import lax
from jax.experimental import pallas as pl
from jax.experimental.pallas import tpu as pltpu
from jax.sharding import PartitionSpec as P

H = 16
KVH = 8
HD = 96
KBLK = 256


epsilon = 1e-05
rope_base = 100000.0
neg_big = -1e30


def rope_tables(positions):
    half_dim = HD // 2
    frequency = jnp.exp(-math.log(rope_base) * (2.0 * jnp.arange(half_dim, dtype=jnp.float32) / HD))
    angles = positions.astype(jnp.float32)[:, None] * frequency[None, :]
    return (jnp.cos(angles), jnp.sin(angles))


def rotate(values, cosine, sine_tab):
    half_dim = values.shape[-1] // 2
    first_half = values[..., :half_dim]
    second_half = values[..., half_dim:]
    cos_wide = cosine[:, None, :]
    sin_wide = sine_tab[:, None, :]
    return jnp.concatenate(
        [
            first_half * cos_wide - second_half * sin_wide,
            second_half * cos_wide + first_half * sin_wide,
        ],
        axis=-1,
    )


def unrotate(values, cosine, sine_tab):
    half_dim = values.shape[-1] // 2
    first_half = values[..., :half_dim]
    second_half = values[..., half_dim:]
    cos_wide = cosine[:, None, :]
    sin_wide = sine_tab[:, None, :]
    return jnp.concatenate(
        [
            first_half * cos_wide + second_half * sin_wide,
            second_half * cos_wide - first_half * sin_wide,
        ],
        axis=-1,
    )


def norm_scale(values):
    return lax.rsqrt(jnp.mean(values * values, axis=-1, keepdims=True) + epsilon)


def block_scores(queries, key_block, offset, positions, length):
    score_scale = 1.0 / math.sqrt(HD)
    raw_scores = (
        jnp.einsum("tkgd,skd->kgts", queries, key_block, preferred_element_type=jnp.float32)
        * score_scale
    )
    key_pos = offset + jnp.arange(key_block.shape[0], dtype=jnp.int32)
    allowed = (key_pos[None, :] <= positions[:, None]) & (key_pos[None, :] < length)
    return jnp.where(allowed[None, None], raw_scores, neg_big)


def block_needed(offset, positions, length):
    return (offset <= positions[-1]) & (offset < length)


def attend_forward(queries, key_blocks, value_blocks, positions, length):
    tok_count = queries.shape[0]
    group_size = queries.shape[2]
    offsets = jnp.arange(key_blocks.shape[0], dtype=jnp.int32) * KBLK

    def stat_step(carried, element):
        key_block, offset = element

        def stat_update(state):
            running_max, running_total = state
            scores = block_scores(queries, key_block, offset, positions, length)
            new_max = jnp.maximum(running_max, jnp.max(scores, axis=-1))
            new_total = running_total * jnp.exp(running_max - new_max) + jnp.sum(
                jnp.exp(scores - new_max[..., None]), axis=-1
            )
            return (new_max, new_total)

        return (
            lax.cond(
                block_needed(offset, positions, length), stat_update, lambda state: state, carried
            ),
            None,
        )

    start_max = jnp.full((KVH, group_size, tok_count), neg_big, jnp.float32)
    start_total = jnp.zeros((KVH, group_size, tok_count), jnp.float32)
    (row_max, row_total), unused = lax.scan(
        stat_step, (start_max, start_total), (key_blocks, offsets)
    )
    log_total = row_max + jnp.log(row_total)

    def value_step(carried, element):
        key_block, value_block, offset = element

        def value_update(state):
            accumulated, exact_sum = state
            scores = block_scores(queries, key_block, offset, positions, length)
            probs = jnp.exp(scores - log_total[..., None])
            weights = probs.astype(jnp.bfloat16)
            accumulated = accumulated + jnp.einsum(
                "kgts,skd->tkgd", weights, value_block, preferred_element_type=jnp.float32
            )
            exact_sum = exact_sum + jnp.einsum(
                "kgts,skd->tkgd",
                probs,
                value_block.astype(jnp.float32),
                preferred_element_type=jnp.float32,
            )
            return (accumulated, exact_sum)

        return (
            lax.cond(
                block_needed(offset, positions, length), value_update, lambda state: state, carried
            ),
            None,
        )

    start_acc = jnp.zeros((tok_count, KVH, group_size, HD), jnp.float32)
    (attended, exact_out), unused = lax.scan(
        value_step, (start_acc, start_acc), (key_blocks, value_blocks, offsets)
    )
    return (attended, exact_out, log_total)


def attend_backward(
    queries, key_blocks, value_blocks, attn_back, exact_out, log_total, positions, length
):
    tok_count = queries.shape[0]
    group_size = queries.shape[2]
    block_keys = key_blocks.shape[1]
    score_scale = 1.0 / math.sqrt(HD)
    offsets = jnp.arange(key_blocks.shape[0], dtype=jnp.int32) * KBLK
    delta = jnp.einsum("tkgd,tkgd->kgt", attn_back.astype(jnp.float32), exact_out)

    def grad_step(query_acc, element):
        key_block, value_block, offset = element

        def compute(acc):
            scores = block_scores(queries, key_block, offset, positions, length)
            probs = jnp.exp(scores - log_total[..., None])
            weights = probs.astype(jnp.bfloat16)
            dprobs = jnp.einsum(
                "tkgd,skd->kgts", attn_back, value_block, preferred_element_type=jnp.float32
            )
            score_back = (probs * (dprobs - delta[..., None])).astype(jnp.bfloat16)
            acc = acc + score_scale * jnp.einsum(
                "kgts,skd->tkgd", score_back, key_block, preferred_element_type=jnp.float32
            )
            key_part = score_scale * jnp.einsum(
                "kgts,tkgd->skd", score_back, queries, preferred_element_type=jnp.float32
            )
            value_part = jnp.einsum(
                "kgts,tkgd->skd", weights, attn_back, preferred_element_type=jnp.float32
            )
            return (acc, key_part, value_part)

        def skip(acc):
            empty = jnp.zeros((block_keys, KVH, HD), jnp.float32)
            return (acc, empty, empty)

        acc, key_part, value_part = lax.cond(
            block_needed(offset, positions, length), compute, skip, query_acc
        )
        return (acc, (key_part, value_part))

    start_query = jnp.zeros((tok_count, KVH, group_size, HD), jnp.float32)
    query_grad, (key_parts, value_parts) = lax.scan(
        grad_step, start_query, (key_blocks, value_blocks, offsets)
    )
    return (query_grad, key_parts.reshape(-1, KVH * HD), value_parts.reshape(-1, KVH * HD))


def split_rows(values, groups_count, seq_count):
    return values.reshape(
        (groups_count, seq_count, values.shape[0] // (groups_count * seq_count)) + values.shape[1:]
    )


def per_device(
    hidden_in,
    lengths,
    attn_gain,
    w_query,
    w_key,
    w_value,
    w_out,
    mlp_gain,
    w_gate,
    w_up,
    w_down,
    out_grad,
):
    tok_count = hidden_in.shape[1]
    group_size = H // KVH
    groups_count = lax.axis_size("grp")
    seq_count = lax.axis_size("seq")
    positions = lax.axis_index("seq") * tok_count + jnp.arange(tok_count, dtype=jnp.int32)
    length = lengths[0]
    valid_rows = (positions < length).astype(jnp.float32)[:, None]
    cosine, sine_tab = rope_tables(positions)
    front_weights = (
        lax.all_gather(attn_gain, ("grp", "seq"), axis=0, tiled=True),
        lax.all_gather(w_query, ("grp", "seq"), axis=0, tiled=True),
        lax.all_gather(w_key, ("grp", "seq"), axis=0, tiled=True),
        lax.all_gather(w_value, ("grp", "seq"), axis=0, tiled=True),
        lax.all_gather(w_out, ("grp", "seq"), axis=0, tiled=True),
        lax.all_gather(mlp_gain, ("grp", "seq"), axis=0, tiled=True),
        lax.all_gather(w_gate, ("grp", "seq"), axis=0, tiled=True),
        lax.all_gather(w_up, ("grp", "seq"), axis=0, tiled=True),
        lax.all_gather(w_down, ("grp", "seq"), axis=0, tiled=True),
    )
    gain_one, query_w, key_w, value_w, out_w, gain_two, gate_w, up_w, down_w = front_weights
    tokens_in = hidden_in[0].astype(jnp.float32)
    scale_one = norm_scale(tokens_in)
    normed = (tokens_in * scale_one * gain_one.astype(jnp.float32)).astype(jnp.bfloat16)
    query_lin = jnp.dot(normed, query_w, preferred_element_type=jnp.float32)
    key_lin = jnp.dot(normed, key_w, preferred_element_type=jnp.float32)
    value_lin = jnp.dot(normed, value_w, preferred_element_type=jnp.float32)
    queries = (
        rotate(query_lin.reshape(tok_count, H, HD), cosine, sine_tab)
        .astype(jnp.bfloat16)
        .reshape(tok_count, KVH, group_size, HD)
    )
    key_rot = (
        rotate(key_lin.reshape(tok_count, KVH, HD), cosine, sine_tab)
        .astype(jnp.bfloat16)
        .reshape(tok_count, KVH * HD)
    )
    value_low = value_lin.astype(jnp.bfloat16)
    keys_all, values_all = (
        lax.all_gather(key_rot, "seq", axis=0, tiled=True),
        lax.all_gather(value_low, "seq", axis=0, tiled=True),
    )
    key_blocks = keys_all.reshape(-1, KBLK, KVH, HD)
    value_blocks = values_all.reshape(-1, KBLK, KVH, HD)
    attended, exact_out, log_total = attend_forward(
        queries, key_blocks, value_blocks, positions, length
    )
    attn_mix = attended.reshape(tok_count, H * HD).astype(jnp.bfloat16)
    hidden = tokens_in + jnp.dot(attn_mix, out_w, preferred_element_type=jnp.float32)
    scale_two = norm_scale(hidden)
    normed_mlp = (hidden * scale_two * gain_two.astype(jnp.float32)).astype(jnp.bfloat16)
    gate_lin = jnp.dot(normed_mlp, gate_w, preferred_element_type=jnp.float32)
    up_lin = jnp.dot(normed_mlp, up_w, preferred_element_type=jnp.float32)
    silu_act = jax.nn.silu(gate_lin)
    inner_act = (silu_act * up_lin).astype(jnp.bfloat16)
    branch = jnp.dot(inner_act, down_w, preferred_element_type=jnp.float32)
    result = (valid_rows * (hidden + branch)).astype(jnp.bfloat16)[None]
    gain_one, query_w, key_w, value_w, out_w, gain_two, gate_w, up_w, down_w = front_weights
    cotangent = out_grad[0].astype(jnp.float32)
    branch_grad = valid_rows * cotangent
    branch_low = branch_grad.astype(jnp.bfloat16)
    down_grad = jnp.einsum("tf,td->fd", inner_act, branch_low, preferred_element_type=jnp.float32)
    inner_grad = jnp.einsum("td,fd->tf", branch_low, down_w, preferred_element_type=jnp.float32)
    sigma = jax.nn.sigmoid(gate_lin)
    gate_back = (inner_grad * up_lin * (sigma + gate_lin * sigma * (1.0 - sigma))).astype(
        jnp.bfloat16
    )
    up_back = (inner_grad * silu_act).astype(jnp.bfloat16)
    gate_grad = jnp.einsum("td,tf->df", normed_mlp, gate_back, preferred_element_type=jnp.float32)
    up_grad = jnp.einsum("td,tf->df", normed_mlp, up_back, preferred_element_type=jnp.float32)
    mlp_norm_grad = jnp.einsum(
        "tf,df->td", gate_back, gate_w, preferred_element_type=jnp.float32
    ) + jnp.einsum("tf,df->td", up_back, up_w, preferred_element_type=jnp.float32)
    gain_two_grad = jnp.sum(mlp_norm_grad * hidden * scale_two, axis=0)
    weighted_two = mlp_norm_grad * gain_two.astype(jnp.float32)
    hidden_grad = (
        branch_grad
        + scale_two * weighted_two
        - hidden
        * (scale_two * scale_two * scale_two)
        * jnp.mean(weighted_two * hidden, axis=-1, keepdims=True)
    )
    mlp_seq = (
        lax.psum_scatter(
            split_rows(gain_two_grad, groups_count, seq_count).astype(jnp.bfloat16),
            "seq",
            scatter_dimension=1,
            tiled=True,
        ).astype(jnp.float32),
        lax.psum_scatter(
            split_rows(gate_grad, groups_count, seq_count).astype(jnp.bfloat16),
            "seq",
            scatter_dimension=1,
            tiled=True,
        ).astype(jnp.float32),
        lax.psum_scatter(
            split_rows(up_grad, groups_count, seq_count).astype(jnp.bfloat16),
            "seq",
            scatter_dimension=1,
            tiled=True,
        ).astype(jnp.float32),
        lax.psum_scatter(
            split_rows(down_grad, groups_count, seq_count).astype(jnp.bfloat16),
            "seq",
            scatter_dimension=1,
            tiled=True,
        ).astype(jnp.float32),
    )
    mlp_grp = (
        lax.psum_scatter(
            mlp_seq[0].astype(jnp.bfloat16), "grp", scatter_dimension=0, tiled=True
        ).astype(jnp.float32),
        lax.psum_scatter(
            mlp_seq[1].astype(jnp.bfloat16), "grp", scatter_dimension=0, tiled=True
        ).astype(jnp.float32),
        lax.psum_scatter(
            mlp_seq[2].astype(jnp.bfloat16), "grp", scatter_dimension=0, tiled=True
        ).astype(jnp.float32),
        lax.psum_scatter(
            mlp_seq[3].astype(jnp.bfloat16), "grp", scatter_dimension=0, tiled=True
        ).astype(jnp.float32),
    )
    mlp_grads = tuple((piece.reshape(piece.shape[2:]) for piece in mlp_grp))
    mix_back = hidden_grad.astype(jnp.bfloat16)
    out_w_grad = jnp.einsum("td,te->de", attn_mix, mix_back, preferred_element_type=jnp.float32)
    attn_back = (
        jnp.einsum("te,de->td", mix_back, out_w, preferred_element_type=jnp.float32)
        .astype(jnp.bfloat16)
        .reshape(tok_count, KVH, group_size, HD)
    )
    query_grad, key_grad_all, value_grad_all = attend_backward(
        queries, key_blocks, value_blocks, attn_back, exact_out, log_total, positions, length
    )
    key_grad, value_grad = (
        lax.psum_scatter(
            key_grad_all.astype(jnp.bfloat16), "seq", scatter_dimension=0, tiled=True
        ).astype(jnp.float32),
        lax.psum_scatter(
            value_grad_all.astype(jnp.bfloat16), "seq", scatter_dimension=0, tiled=True
        ).astype(jnp.float32),
    )
    query_back = (
        unrotate(query_grad.reshape(tok_count, H, HD), cosine, sine_tab)
        .astype(jnp.bfloat16)
        .reshape(tok_count, H * HD)
    )
    key_back = (
        unrotate(key_grad.reshape(tok_count, KVH, HD), cosine, sine_tab)
        .astype(jnp.bfloat16)
        .reshape(tok_count, KVH * HD)
    )
    value_back = value_grad.astype(jnp.bfloat16)
    query_w_grad = jnp.einsum("td,te->de", normed, query_back, preferred_element_type=jnp.float32)
    key_w_grad = jnp.einsum("td,te->de", normed, key_back, preferred_element_type=jnp.float32)
    value_w_grad = jnp.einsum("td,te->de", normed, value_back, preferred_element_type=jnp.float32)
    attn_norm_grad = (
        jnp.einsum("te,de->td", query_back, query_w, preferred_element_type=jnp.float32)
        + jnp.einsum("te,de->td", key_back, key_w, preferred_element_type=jnp.float32)
        + jnp.einsum("te,de->td", value_back, value_w, preferred_element_type=jnp.float32)
    )
    gain_one_grad = jnp.sum(attn_norm_grad * tokens_in * scale_one, axis=0)
    weighted_one = attn_norm_grad * gain_one.astype(jnp.float32)
    input_back = (
        hidden_grad
        + scale_one * weighted_one
        - tokens_in
        * (scale_one * scale_one * scale_one)
        * jnp.mean(weighted_one * tokens_in, axis=-1, keepdims=True)
    )
    attn_seq = (
        lax.psum_scatter(
            split_rows(gain_one_grad, groups_count, seq_count).astype(jnp.bfloat16),
            "seq",
            scatter_dimension=1,
            tiled=True,
        ).astype(jnp.float32),
        lax.psum_scatter(
            split_rows(query_w_grad, groups_count, seq_count).astype(jnp.bfloat16),
            "seq",
            scatter_dimension=1,
            tiled=True,
        ).astype(jnp.float32),
        lax.psum_scatter(
            split_rows(key_w_grad, groups_count, seq_count).astype(jnp.bfloat16),
            "seq",
            scatter_dimension=1,
            tiled=True,
        ).astype(jnp.float32),
        lax.psum_scatter(
            split_rows(value_w_grad, groups_count, seq_count).astype(jnp.bfloat16),
            "seq",
            scatter_dimension=1,
            tiled=True,
        ).astype(jnp.float32),
        lax.psum_scatter(
            split_rows(out_w_grad, groups_count, seq_count).astype(jnp.bfloat16),
            "seq",
            scatter_dimension=1,
            tiled=True,
        ).astype(jnp.float32),
    )
    attn_grp = (
        lax.psum_scatter(
            attn_seq[0].astype(jnp.bfloat16), "grp", scatter_dimension=0, tiled=True
        ).astype(jnp.float32),
        lax.psum_scatter(
            attn_seq[1].astype(jnp.bfloat16), "grp", scatter_dimension=0, tiled=True
        ).astype(jnp.float32),
        lax.psum_scatter(
            attn_seq[2].astype(jnp.bfloat16), "grp", scatter_dimension=0, tiled=True
        ).astype(jnp.float32),
        lax.psum_scatter(
            attn_seq[3].astype(jnp.bfloat16), "grp", scatter_dimension=0, tiled=True
        ).astype(jnp.float32),
        lax.psum_scatter(
            attn_seq[4].astype(jnp.bfloat16), "grp", scatter_dimension=0, tiled=True
        ).astype(jnp.float32),
    )
    attn_grads = tuple((piece.reshape(piece.shape[2:]) for piece in attn_grp))
    return (
        result,
        input_back.astype(jnp.bfloat16)[None],
        attn_grads[0],
        attn_grads[1],
        attn_grads[2],
        attn_grads[3],
        attn_grads[4],
        mlp_grads[0],
        mlp_grads[1],
        mlp_grads[2],
        mlp_grads[3],
    )


MESH_ID = pl.DeviceIdType.MESH
VMEM = pltpu.VMEM
LINE = 4
CHIPS = 8
TOK = 128
PAD = 128
CHUNKS = 4
ROWS = TOK // CHUNKS
BF = jnp.bfloat16
F32 = jnp.float32
VSPEC = pl.BlockSpec(memory_space=pltpu.VMEM)


def ring_of(chip):
    z = chip // 2
    x = chip % 2
    return x * LINE + z + x * (LINE - 1 - 2 * z)


def chip_of(ring):
    x = ring // LINE
    q = ring % LINE
    return (q + x * (LINE - 1 - 2 * q)) * 2 + x


class Place:
    def __init__(self):
        self.g = lax.axis_index("grp")
        self.s = lax.axis_index("seq")
        self.core = self.s % 2
        self.chip = self.s // 2
        self.x = self.chip % 2
        self.ring = ring_of(self.chip)
        self.step = 1 - 2 * self.core
        self.next = {"seq": self.at(self.step) * 2 + self.core}
        self.prev = {"seq": self.at(-self.step) * 2 + self.core}
        self.sib = {"seq": self.s + 1 - 2 * self.core}
        self.ynb = {"grp": 1 - self.g}
        self.xnb = {"seq": self.s + 2 - 4 * self.x}

    def at(self, offset):
        return chip_of((self.ring + offset + 8 * CHIPS) % CHIPS)

    def behind(self, t):
        return self.at(-t * self.step)

    def off(self, i):
        return {"seq": ((self.chip + i + CHIPS) % CHIPS) * 2 + self.core}

    def src(self, i):
        return (self.chip - i + CHIPS) % CHIPS


def greet(devices):
    barrier = pltpu.get_barrier_semaphore()
    for device in devices:
        pl.semaphore_signal(barrier, inc=1, device_id=device, device_id_type=MESH_ID)
    pl.semaphore_wait(barrier, len(devices))


def remote(src, dst, send, recv, device):
    return pltpu.make_async_remote_copy(
        src_ref=src, dst_ref=dst, send_sem=send, recv_sem=recv, device_id=device,
        device_id_type=MESH_ID,
    )


class RingGather:
    sems = [pltpu.SemaphoreType.DMA((CHIPS, CHUNKS)), pltpu.SemaphoreType.DMA((CHIPS, CHUNKS))]

    def __init__(self, place, all_ref, send, recv):
        self.place, self.all, self.send, self.recv = place, all_ref, send, recv
        self.rows = all_ref.shape[1] // CHUNKS

    def copy(self, t, k):
        part = self.all.at[self.place.behind(t), pl.ds(k * self.rows, self.rows)]
        return remote(part, part, self.send.at[t, k], self.recv.at[t, k], self.place.next)

    def start(self, k=None):
        for k in range(CHUNKS) if k is None else (k,):
            self.copy(0, k).start()

    def pump(self, t):
        for k in range(CHUNKS):
            self.pass_on(t, k)

    def pass_on(self, t, k):
        self.copy(t - 1, k).wait_recv()
        if t < CHIPS - 1:
            self.copy(t, k).start()

    def pump_some(self, first, last):
        for n in range(first, last):
            self.pass_on(1 + n // CHUNKS, n % CHUNKS)

    def finish(self):
        for t in range(CHIPS - 1):
            for k in range(CHUNKS):
                self.copy(t, k).wait_send()


class RingScatter:
    sems = [pltpu.SemaphoreType.DMA((CHIPS, CHUNKS)), pltpu.SemaphoreType.DMA((CHIPS, CHUNKS))]
    bufs = [VMEM((CHIPS - 1, TOK, 1536), BF), VMEM((CHIPS - 1, TOK, 1536), BF)]

    def __init__(self, place, out, held, send, recv):
        self.place, self.out, self.held, self.send, self.recv = place, out, held, send, recv

    def copy(self, t, k):
        rows = pl.ds(k * ROWS, ROWS)
        return remote(self.out.at[t, rows], self.held.at[t, rows], self.send.at[t, k],
                      self.recv.at[t, k], self.place.next)

    def dest(self, t):
        return self.place.behind(t + 1)

    def push(self, t, term):
        for k in range(CHUNKS):
            rows = pl.ds(k * ROWS, ROWS)
            value = term(k)
            if t > 0:
                self.copy(t - 1, k).wait_recv()
                value = value + self.held[t - 1, rows].astype(F32)
            self.out[t, rows] = value.astype(BF)
            self.copy(t, k).start()

    def last(self, k):
        self.copy(CHIPS - 2, k).wait_recv()
        return self.held[CHIPS - 2, pl.ds(k * ROWS, ROWS)].astype(F32)

    def finish(self):
        for t in range(CHIPS - 1):
            for k in range(CHUNKS):
                self.copy(t, k).wait_send()


class Spread:
    sems = [pltpu.SemaphoreType.DMA((CHIPS,)), pltpu.SemaphoreType.DMA((CHIPS,)),
            pltpu.SemaphoreType.DMA((CHIPS,)), pltpu.SemaphoreType.DMA((CHIPS,)),
            pltpu.SemaphoreType.DMA((2 * CHIPS,)), pltpu.SemaphoreType.DMA((2 * CHIPS,))]

    def __init__(self, place, slab, all_ref, local, *sems):
        self.place, self.slab, self.all, self.local = place, slab, all_ref, local
        self.s1, self.r1, self.s2, self.r2, self.s3, self.r3 = sems

    def block(self, g, chip):
        return self.all.at[g * 16 + chip * 2 + self.place.core]

    def across(self, i):
        p = self.place
        return remote(self.slab.at[(p.chip + i) % CHIPS], self.block(p.g, p.chip), self.s1.at[i],
                      self.r1.at[i], p.off(i))

    def arrived(self, i):
        p = self.place
        return remote(self.slab.at[0], self.block(p.g, p.src(i)), self.s1.at[i], self.r1.at[i],
                      p.off(i))

    def to_y(self, i):
        p = self.place
        part = self.block(p.g, p.src(i))
        return remote(part, part, self.s2.at[i], self.r2.at[i], p.ynb)

    def from_y(self, i):
        p = self.place
        part = self.block(1 - p.g, p.src(i))
        return remote(part, part, self.s2.at[i], self.r2.at[i], p.ynb)

    def to_sib(self, i, other):
        p = self.place
        part = self.block((1 - p.g) if other else p.g, p.src(i))
        n = i + CHIPS * other
        return remote(part, part, self.s3.at[n], self.r3.at[n], p.sib)

    def from_sib(self, i, other):
        p = self.place
        g = (1 - p.g) if other else p.g
        part = self.all.at[g * 16 + p.src(i) * 2 + 1 - p.core]
        n = i + CHIPS * other
        return remote(part, part, self.s3.at[n], self.r3.at[n], p.sib)

    def start(self):
        p = self.place
        own = pltpu.make_async_copy(self.slab.at[p.chip], self.block(p.g, p.chip), self.local)
        own.start()
        for i in range(1, CHIPS):
            self.across(i).start()
        own.wait()
        self.to_y(0).start()
        self.to_sib(0, 0).start()

    def pump(self, i):
        self.arrived(i).wait_recv()
        self.to_y(i).start()
        self.to_sib(i, 0).start()
        self.from_y(i - 1).wait_recv()
        self.to_sib(i - 1, 1).start()

    def finish(self):
        self.from_y(CHIPS - 1).wait_recv()
        self.to_sib(CHIPS - 1, 1).start()
        for i in range(CHIPS):
            self.from_sib(i, 0).wait_recv()
            self.from_sib(i, 1).wait_recv()
        for i in range(CHIPS):
            if i > 0:
                self.across(i).wait_send()
            self.to_y(i).wait_send()
            self.to_sib(i, 0).wait_send()
            self.to_sib(i, 1).wait_send()


class Across:
    sems = [pltpu.SemaphoreType.DMA((CHIPS,)), pltpu.SemaphoreType.DMA((CHIPS,))]

    def __init__(self, place, slab, got, local, send, recv):
        self.place, self.slab, self.got, self.send, self.recv = place, slab, got, send, recv
        self.own = pltpu.make_async_copy(slab.at[place.chip], got.at[place.chip], local)

    def to(self, i):
        p = self.place
        return remote(self.slab.at[(p.chip + i) % CHIPS], self.got.at[p.chip], self.send.at[i], self.recv.at[i], p.off(i))

    def arrived(self, i):
        p = self.place
        return remote(self.slab.at[0], self.got.at[p.src(i)], self.send.at[i], self.recv.at[i], p.off(i))

    def start(self):
        self.own.start()
        for i in range(1, CHIPS):
            self.to(i).start()

    def land(self):
        self.own.wait()
        for i in range(1, CHIPS):
            self.arrived(i).wait_recv()

    def sent(self):
        for i in range(1, CHIPS):
            self.to(i).wait_send()


class Quarters:
    sems = [pltpu.SemaphoreType.DMA((3,)), pltpu.SemaphoreType.DMA((3,))]

    def __init__(self, place, view, send, recv):
        p = place
        here, over = view(p.g, p.core), view(1 - p.g, p.core)
        self.y = remote(here, here, send.at[0], recv.at[0], p.ynb)
        self.sib = remote(here, here, send.at[1], recv.at[1], p.sib)
        self.sib2 = remote(over, over, send.at[2], recv.at[2], p.sib)

    def start(self):
        self.y.start()
        self.sib.start()

    def pass_on(self):
        self.y.wait_recv()
        self.sib2.start()

    def arrive(self):
        self.sib.wait_recv()
        self.sib2.wait_recv()

    def finish(self):
        for copy in (self.y, self.sib, self.sib2):
            copy.wait_send()


class Share:
    sems = [pltpu.SemaphoreType.DMA((CHIPS,))] * 4 + [pltpu.SemaphoreType.DMA((2 * CHIPS,))] * 2

    def __init__(self, place, all_ref, *sems):
        self.place, self.all = place, all_ref
        self.s1, self.r1, self.s2, self.r2, self.s3, self.r3 = sems

    def slot(self, t, other):
        p = self.place
        return self.all.at[((1 - p.g) if other else p.g) * 16 + p.behind(t) * 2 + p.core]

    def ring(self, t):
        part = self.slot(t, 0)
        return remote(part, part, self.s1.at[t], self.r1.at[t], self.place.next)

    def y(self, t, back):
        part = self.slot(t, back)
        return remote(part, part, self.s2.at[t], self.r2.at[t], self.place.ynb)

    def to_sib(self, t, other):
        part = self.slot(t, other)
        n = t + CHIPS * other
        return remote(part, part, self.s3.at[n], self.r3.at[n], self.place.sib)

    def from_sib(self, t, other):
        p = self.place
        part = self.all.at[((1 - p.g) if other else p.g) * 16 + p.behind(-t) * 2 + 1 - p.core]
        n = t + CHIPS * other
        return remote(part, part, self.s3.at[n], self.r3.at[n], p.sib)

    def start(self):
        self.ring(0).start()
        self.y(0, 0).start()
        self.to_sib(0, 0).start()

    def pump(self, t):
        self.ring(t - 1).wait_recv()
        if t < CHIPS - 1:
            self.ring(t).start()
        self.y(t, 0).start()
        self.to_sib(t, 0).start()
        self.y(t - 1, 1).wait_recv()
        self.to_sib(t - 1, 1).start()

    def finish(self):
        self.y(CHIPS - 1, 1).wait_recv()
        self.to_sib(CHIPS - 1, 1).start()
        for t in range(CHIPS):
            for other in range(2):
                self.from_sib(t, other).wait_recv()
                self.to_sib(t, other).wait_send()
            self.y(t, 0).wait_send()
            if t < CHIPS - 1:
                self.ring(t).wait_send()


class Collect:
    order = tuple(range(1, CHIPS)) + (0,)
    sems = [pltpu.SemaphoreType.DMA((CHIPS,))] * 6

    @staticmethod
    def bufs(rows, columns):
        return [VMEM((CHIPS, 2, rows, columns), BF), VMEM((CHIPS, 2, rows, columns), BF),
                VMEM((CHIPS, rows, columns), BF), VMEM((CHIPS, rows, columns), BF)]

    def __init__(self, place, grads, own, got, bufs, sems):
        self.place, self.grads, self.own, self.got = place, grads, own, got
        self.sib_in, self.pair, self.y_in, self.total = bufs
        self.s1, self.r1, self.s2, self.r2, self.s3, self.r3 = sems

    def sib(self, n):
        p = self.place
        return remote(self.grads.at[:, (p.chip + n) % CHIPS, 1 - p.core], self.sib_in.at[n],
                      self.s1.at[n], self.r1.at[n], p.sib)

    def y(self, n):
        p = self.place
        return remote(self.pair.at[n, 1 - p.g], self.y_in.at[n], self.s2.at[n], self.r2.at[n], p.ynb)

    def across(self, n):
        p = self.place
        return remote(self.total.at[n], self.got.at[p.chip], self.s3.at[n], self.r3.at[n], p.off(n))

    def arrived(self, n):
        p = self.place
        return remote(self.total.at[n], self.got.at[p.src(n)], self.s3.at[n], self.r3.at[n], p.off(n))

    def start(self):
        for n in self.order:
            self.sib(n).start()

    def pair_up(self, m):
        p, n = self.place, self.order[m]
        self.sib(n).wait_recv()
        for g in range(2):
            self.pair[n, g] = (self.own(g, (p.chip + n) % CHIPS).astype(F32)
                               + self.sib_in[n, g].astype(F32)).astype(BF)
        self.y(n).start()

    def send(self, m):
        p, n = self.place, self.order[m]
        self.y(n).wait_recv()
        value = (self.pair[n, p.g].astype(F32) + self.y_in[n].astype(F32)).astype(BF)
        if n == 0:
            self.got[p.chip] = value
        else:
            self.total[n] = value
            self.across(n).start()

    def receive(self):
        for n in range(1, CHIPS):
            self.arrived(n).wait_recv()

    def finish(self):
        for n in range(CHIPS):
            self.sib(n).wait_send()
            self.y(n).wait_send()
            if n > 0:
                self.across(n).wait_send()


def dot(a, b):
    return lax.dot_general(a, b, (((1,), (0,)), ((), ())), preferred_element_type=F32)


def dot_nt(a, b):
    return lax.dot_general(a, b, (((1,), (1,)), ((), ())), preferred_element_type=F32)


def all_to_all_devices(place):
    return [place.off(i) for i in range(1, CHIPS)]


def call(body, outs, ins, scratch, collective_id, far_ins=(), far_outs=(), scalar_ins=(), flops=0, nbytes=0):
    kwargs = {}
    if collective_id is not None:
        kwargs = dict(collective_id=collective_id, has_side_effects=True)
    far = pl.BlockSpec(memory_space=pl.ANY)
    scalar = pl.BlockSpec(memory_space=pltpu.SMEM)
    return pl.pallas_call(
        body,
        out_shape=outs,
        in_specs=[far if n in far_ins else scalar if n in scalar_ins else VSPEC for n in range(len(ins))],
        out_specs=tuple(far if n in far_outs else VSPEC for n in range(len(outs))),
        scratch_shapes=scratch,
        compiler_params=pltpu.CompilerParams(vmem_limit_bytes=60 << 20, **kwargs),
        cost_estimate=pl.CostEstimate(flops=flops, bytes_accessed=nbytes, transcendentals=0),
    )(*ins)


class Moves:
    def __init__(self, sems, *pairs):
        self.copies = [pltpu.make_async_copy(a, b, sems.at[n]) for n, (a, b) in enumerate(pairs)]

    def start(self, *which):
        for n in which or range(len(self.copies)):
            self.copies[n].start()

    def wait(self, *which):
        for n in which or range(len(self.copies)):
            self.copies[n].wait()


def sds(*shape, dtype=BF):
    return jax.ShapeDtypeStruct(shape, dtype)


def rope(u, cosine, sine):
    return u * cosine + pltpu.roll(u, 64, 1) * sine


def make_tables(p, rows, starts):
    def fill(target, slots):
        entry = lax.broadcasted_iota(jnp.int32, slots.shape, 1)
        upper = entry >= 64
        entry = jnp.where(upper, entry - 64, entry)
        frequency = jnp.where(entry < HD // 2, jnp.exp(-math.log(rope_base) * (2.0 * entry.astype(F32) / HD)), 0.0)
        angles = slots.astype(F32) * frequency
        target[0] = jnp.cos(angles)
        target[1] = jnp.where(upper, 1.0, -1.0) * jnp.sin(angles)

    fill(rows, lax.broadcasted_iota(jnp.int32, (TOK, PAD), 0))
    fill(starts, (2 * lax.broadcasted_iota(jnp.int32, (CHIPS, PAD), 0) + p.core) * TOK)


def tables(rows, starts, i):
    c_row, s_row = rows[0], rows[1]
    c_start, s_start = starts[0, pl.ds(i, 1)], starts[1, pl.ds(i, 1)]
    return c_start * c_row - s_start * s_row, s_start * c_row + c_start * s_row


def limit_of(p, i, length):
    lane = lax.broadcasted_iota(jnp.int32, (1, 2 * TOK), 1)
    slot = jnp.where(lane < TOK, lane, lane - TOK) + (2 * i + p.core) * TOK
    return jnp.minimum(slot.astype(F32), length - 1.0)


def valid_of(p, first, rows, length):
    slot = lax.broadcasted_iota(jnp.int32, (rows, 1), 0) + p.s * TOK + first
    return jnp.where(slot.astype(F32) < length, 1.0, 0.0)


def spacing():
    r = lax.broadcasted_iota(jnp.int32, (384, 512), 0)
    c = lax.broadcasted_iota(jnp.int32, (384, 512), 1)
    target = r
    for n in range(1, 8):
        target = target + jnp.where(r >= 48 * n, 16, 0)
    return jnp.where(target == c, 1.0, 0.0).astype(BF)


def chip_of_head(j):
    return 2 * (j % LINE) + j // LINE


def diagonal(n):
    return lax.broadcasted_iota(jnp.int32, (n, n), 0) == lax.broadcasted_iota(jnp.int32, (n, n), 1)


def to_column(row):
    n = row.shape[1]
    return jnp.sum(jnp.where(diagonal(n), jnp.broadcast_to(row, (n, n)), 0.0), axis=1, keepdims=True)


def to_row(column):
    n = column.shape[0]
    return jnp.sum(jnp.where(diagonal(n), jnp.broadcast_to(column, (n, n)), 0.0), axis=0, keepdims=True)


def norm_column(h):
    return lax.rsqrt(jnp.mean(h * h, axis=-1, keepdims=True) + epsilon)


def whole(ref):
    value = ref[...]
    return value.reshape(value.shape[0] * value.shape[1], value.shape[2])


LOG2E = 1.4426950408889634
SCALE = 1.0 / math.sqrt(96)
SCALE2 = SCALE * LOG2E


def scores_of(keys, query, limit, j):
    s = dot_nt(keys[j], query) * SCALE2
    pos = lax.broadcasted_iota(jnp.int32, s.shape, 0) + j * 256
    return jnp.where(pos.astype(F32) <= limit, s, neg_big)


def dot_tn(a, b):
    return lax.dot_general(a, b, (((0,), (0,)), ((), ())), preferred_element_type=F32)


def rows_of(k):
    return pl.ds(k * ROWS, ROWS)


def main_kernel(lengths, tokens, wq, wk, wv, gain_one, out_grad, wg, wu, gain_two, wo, wd,
                tg_out, wqkv_out, q_out, keys_out, values_out, mix_t_out, stat_out,
                hidden_out, grad_out, inner_out, dgu_out, dwd_out, rows_out, wdown_out, dout,
                tg, wqkv, q, keys, values, mix_t, stat, grad, inner, dgu, dwd, grad_rows,
                rope_rows, rope_starts, slab, slab_gu, mix, vt, bgg, wall, wgu, wdown, mx, wpad, hid, x2, gub, low, part, scale, out2, held2,
                ag_s, ag_r, s1, r1, s2, r2, s3, r3, bg_s, bg_r, g1, h1, o1, p1, o2, p2, o3, p3,
                mx_s, mx_r, rs2_s, rs2_r, ag2_s, ag2_r, ks, kr, vs, vr, q1, q2, q3, q4, local, local2, move_s):
    p = Place()
    gather = RingGather(p, tg, ag_s, ag_r)
    spread = Spread(p, slab, wqkv, local, s1, r1, s2, r2, s3, r3)
    gather_bg = RingGather(p, bgg, bg_s, bg_r)
    across = Across(p, slab_gu, wgu.at[p.g, :, p.core], local2, g1, h1)
    share = Share(p, wall, o1, p1, o2, p2, o3, p3)
    gather_mix = RingGather(p, mx, mx_s, mx_r)
    scatter2 = RingScatter(p, out2, held2, rs2_s, rs2_r)
    gather2 = RingGather(p, low, ag2_s, ag2_r)
    quarters = Quarters(p, lambda g, core: wgu.at[g, :, core], q1, q2)
    quarters2 = Quarters(p, lambda g, core: wdown.at[g, core], q3, q4)
    moves = Moves(move_s, (tg, tg_out), (wqkv, wqkv_out), (q, q_out), (keys, keys_out),
                  (values, values_out), (mix_t, mix_t_out), (stat, stat_out),
                  (hid.at[p.chip], hidden_out), (grad, grad_out), (inner, inner_out), (dgu, dgu_out), (dwd, dwd_out),
                  (grad_rows, rows_out), (wdown, wdown_out),
                  (wo, wall.at[p.g * 16 + p.s]), (wd, wdown.at[p.g, p.core]))
    moves.start(14, 15)
    length = lengths[0].astype(F32)
    tg[p.chip] = tokens[...]
    greet(all_to_all_devices(p) + [p.sib, p.ynb])
    gather.start()
    make_tables(p, rope_rows, rope_starts)
    space = spacing()
    gain_column = to_column(gain_one[...].astype(F32))
    gain_column2 = to_column(gain_two[...].astype(F32))
    for n in range(4):
        cols = pl.ds(n * 384, 384)
        wide = dot((wq[:, cols].astype(F32) * gain_column).astype(BF), space).astype(BF)
        for m in range(2):
            slab[chip_of_head(2 * n + m), :, pl.ds(0, 256)] = wide[:, m * 256:m * 256 + 256]
    for n in range(2):
        for source, place in ((wk, 256), (wv, 384)):
            wide = dot((source[:, pl.ds(n * 384, 384)].astype(F32) * gain_column).astype(BF), space).astype(BF)
            for m in range(4):
                slab[chip_of_head(4 * n + m), :, pl.ds(place, 128)] = wide[:, m * 128:m * 128 + 128]
    spread.start()
    bgg[p.chip] = (out_grad[...].astype(F32) * valid_of(p, 0, TOK, length)).astype(BF)
    gather.pump(1)
    for chip in range(CHIPS):
        for n, source in enumerate((wg, wu)):
            for g in range(2):
                slab_gu[chip, :, pl.ds(n * 512 + g * 256, 256)] = (
                    source[:, pl.ds(g * 2048 + chip * 256, 256)].astype(F32) * gain_column2).astype(BF)
    spread.pump(1)
    for t in range(2, CHIPS):
        gather.pump(t)
        spread.pump(t)
    moves.start(0)
    moves.wait(14, 15)
    gather_bg.start()
    share.start()
    across.start()
    quarters2.start()
    spread.finish()
    moves.start(1)

    def kv_copy(i, n):
        ref, send, recv = ((keys, ks, kr), (values, vs, vr))[n]
        part = ref.at[i, pl.ds(pl.multiple_of(p.core * TOK, TOK), TOK)]
        return remote(part, part, send.at[i], recv.at[i], p.sib)

    def kv_in(i, n):
        ref, send, recv = ((keys, ks, kr), (values, vs, vr))[n]
        part = ref.at[i, pl.ds(pl.multiple_of((1 - p.core) * TOK, TOK), TOK)]
        return remote(part, part, send.at[i], recv.at[i], p.sib)

    def project(i):
        h = tg[i].astype(F32)
        lin = dot((h * norm_column(h)).astype(BF), whole(wqkv))
        cosine, sine = tables(rope_rows, rope_starts, i)
        q[i, pl.ds(0, TOK)] = rope(lin[:, 0:128], cosine, sine).astype(BF)
        q[i, pl.ds(TOK, TOK)] = rope(lin[:, 128:256], cosine, sine).astype(BF)
        own = pl.ds(pl.multiple_of(p.core * TOK, TOK), TOK)
        keys[i, own] = rope(lin[:, 256:384], cosine, sine).astype(BF)
        values[i, own] = lin[:, 384:512].astype(BF)
        kv_copy(i, 0).start()
        kv_copy(i, 1).start()

    def attend(i):
        query = q[i]
        limit = limit_of(p, i, length)

        def chunk(j, state):
            top, total, acc = state
            s = scores_of(keys, query, limit, j)
            new_top = jnp.maximum(top, jnp.max(s, axis=0, keepdims=True))
            fade = jnp.exp2(top - new_top)
            w = jnp.exp2(s - new_top)
            total = total * fade + jnp.sum(w, axis=0, keepdims=True)
            acc = acc * fade + dot(vt[j], w.astype(BF))
            return new_top, total, acc

        start = (jnp.full((1, 256), neg_big, F32), jnp.zeros((1, 256), F32),
                 jnp.zeros((PAD, 256), F32))
        top, total, acc = lax.fori_loop(0, i + 1, chunk, start)
        acc = acc / total
        mix_t[i] = acc
        stat[i] = top + jnp.log2(total)
        low = acc.astype(BF)
        for n in range(4):
            mix[pl.ds(n * 48, 48), pl.ds(i * TOK, TOK)] = low[(n % 2) * 64:(n % 2) * 64 + 48,
                                                              (n // 2) * TOK:(n // 2) * TOK + TOK]

    for i in range(CHIPS):
        project(i)
        gather_bg.pump_some(i, i + 1)
    share.pump(1)
    for i in range(CHIPS):
        for n in range(2):
            kv_in(i, n).wait_recv()
        vt[i] = values[i].astype(F32).T.astype(BF)
    moves.start(2, 3, 4)
    done = CHIPS
    for i in range(CHIPS):
        attend(i)
        gather_bg.pump_some(done, done + (2 if i < 4 else 3))
        done += 2 if i < 4 else 3
        if 1 <= i < CHIPS - 1:
            share.pump(i + 1)
    moves.start(5, 6)
    mx[p.chip] = mix[...]
    gather_mix.start()
    across.land()
    quarters.start()
    wpad[...] = jnp.zeros_like(wpad)
    share.finish()
    quarters2.pass_on()
    def head_of(chip):
        return chip // 2 + LINE * (chip % 2)

    def out_rows(chip):
        return whole(wall.at[pl.ds(4 * head_of(chip), 4)])

    def mixed(chip, b):
        lanes = pl.ds(pl.multiple_of(b * TOK, TOK), TOK)
        return dot_tn(mx[chip, :, lanes], out_rows(chip))

    def first(b, carry):
        hid[b] = tg[b].astype(F32) + mixed(p.chip, b)
        return carry

    lax.fori_loop(0, CHIPS, first, 0)
    for n in range(4):
        wpad[pl.ds(n * 64, 48)] = wall[4 * head_of(p.chip) + n]
    for t in range(1, CHIPS - 1):
        gather_mix.pump(t)

        def more(b, carry):
            hid[b] += mixed(p.behind(t), b)
            return carry

        lax.fori_loop(0, CHIPS, more, 0)
        if t == 5:
            quarters.pass_on()

    def feed(b):
        h = hid[b] + mixed(p.behind(CHIPS - 1), b)
        hid[b] = h
        r = norm_column(h)
        scale[...] = jnp.broadcast_to(r, (TOK, 128))
        x2[b] = (h * r).astype(BF)
        lin = dot(x2[b], wgu[...].reshape(1536, 1024))
        gate, up = lin[:, :512], lin[:, 512:]
        sigma = jax.nn.sigmoid(gate)
        act = gate * sigma
        inner[b] = (act * up).astype(BF)
        back = dot_nt(bgg[b], wdown[...].reshape(512, 1536))
        gub[b, :, pl.ds(0, 512)] = (back * up * (sigma + act * (1.0 - sigma))).astype(BF)
        gub[b, :, pl.ds(512, 512)] = (back * act).astype(BF)
        part[...] = dot_nt(gub[b], wgu[...].reshape(1536, 1024))

    gather_mix.pump(CHIPS - 1)
    quarters.arrive()
    quarters2.arrive()
    moves.start(13)
    for t in range(CHIPS):
        feed(scatter2.dest(t))
        if t < CHIPS - 1:
            scatter2.push(t, lambda k: part[rows_of(k)])
    moves.start(7)
    for k in range(CHUNKS):
        rows = rows_of(k)
        a = part[rows] + scatter2.last(k)
        h = hid[p.chip, rows]
        r = scale[rows, pl.ds(0, 1)]
        value = (bgg[p.chip, rows].astype(F32) + r * a
                 - h * (r * r * r) * jnp.mean(a * h, axis=-1, keepdims=True))
        grad[rows] = value
        low[p.chip, rows] = value.astype(BF)
        gather2.start(k)

    def weight_part(n):
        if n < 12:
            cols = pl.ds(n * 128, 128)
            dgu[cols] = dot_tn(whole(x2.at[:, :, cols]), whole(gub)).astype(BF)
        else:
            cols = pl.ds((n - 12) * 128, 128)
            dwd[cols] = dot_tn(whole(inner.at[:, :, cols]), whole(bgg)).astype(BF)

    def head_part(b):
        rows = dot_nt(low[b], wpad[...]).astype(BF)
        grad_rows[b, pl.ds(0, TOK)] = rows[:, :PAD]
        grad_rows[b, pl.ds(TOK, TOK)] = rows[:, PAD:]

    moves.start(8, 9)
    head_part(p.chip)
    for t in range(1, CHIPS):
        for n in range(2 * t - 2, 2 * t):
            weight_part(n)
        gather2.pump(t)
        head_part(p.behind(t))
    moves.start(12)
    weight_part(14)
    weight_part(15)
    moves.start(10, 11)
    value = dot(mix[...], whole(low)).astype(BF)
    for n in range(4):
        dout[n] = value[48 * n:48 * n + 48]
    moves.wait(*range(14))
    for one in (gather, gather_bg, gather_mix, gather2, scatter2, quarters, quarters2):
        one.finish()
    across.sent()
    for i in range(CHIPS):
        for n in range(2):
            kv_copy(i, n).wait_send()


def main(*ins):
    dma = pltpu.SemaphoreType.DMA
    block = ((CHIPS, TOK, 1536), BF)
    heads = ((CHIPS, 2 * TOK, PAD), BF)
    shapes = (block, ((32, 48, 512), BF), heads, heads, heads, ((CHIPS, PAD, 256), F32), ((CHIPS, 1, 256), F32))
    shapes2 = (((TOK, 1536), F32), ((CHIPS, TOK, 512), BF), ((1536, 1024), BF), ((512, 1536), BF), heads)
    outs = shapes + (((TOK, 1536), F32),) + shapes2 + (((2, 2, TOK, 1536), BF), ((4, 48, 1536), BF))
    near = shapes + shapes2 + (
        ((2, TOK, PAD), F32), ((2, CHIPS, PAD), F32),
        ((CHIPS, 48, 512), BF), ((CHIPS, 48, 1024), BF), ((192, 1024), BF), ((CHIPS, PAD, 256), BF), block,
        ((32, 48, 1536), BF), ((2, CHIPS, 2, 48, 1024), BF), ((2, 2, TOK, 1536), BF), ((CHIPS, 192, 1024), BF),
        ((256, 1536), BF), ((CHIPS, TOK, 1536), F32), block, ((CHIPS, TOK, 1024), BF), block, ((TOK, 1536), F32),
        ((TOK, 128), F32))
    return call(
        main_kernel,
        tuple(sds(*shape, dtype=kind) for shape, kind in outs),
        ins,
        [VMEM(shape, kind) for shape, kind in near] + RingScatter.bufs
        + RingGather.sems + Spread.sems + RingGather.sems + Across.sems + Share.sems + RingGather.sems + RingScatter.sems
        + RingGather.sems + [dma((CHIPS,))] * 4 + Quarters.sems * 2 + [dma, dma, dma((16,))],
        1, far_ins=(10, 11), far_outs=range(14), scalar_ins=(0,), flops=20 * 10**9, nbytes=40 << 20,
    )


def tail_kernel(q_in, keys_in, values_in, rows_in, mix_t_in, stat_in, inner_in, wdown_in, hidden_in, dgu_far, dwd_far,
                xg_in, wqkv_in, grad_in, lengths, dout, tokens,
                result, input_back, got_gu, got_qkv, dout_sum, dwd_sum,
                rope_rows, rope_starts, q, keys, values, grad_rows, mix_t, stat, inner, wdown, hidden, dgu, dwd, xg, wqkv, grad,
                kt, dk, dv, dkv_low, dkv_in, back_out, dqkv, part, out, held, out2, held2,
                gu1, gu2, gu3, gu4, qk1, qk2, qk3, qk4, d_in, d_pair, d_y, o_in, o_pair, o_two, o_y,
                rs_s, rs_r, rs2_s, rs2_r, a1, a2, a3, a4, a5, a6, c1, c2, c3, c4, c5, c6,
                ds, dr, xs, xr, os, orr, move_s):
    p = Place()
    moves = Moves(move_s, (inner_in, inner), (wdown_in, wdown), (q_in, q), (keys_in, keys), (values_in, values),
                  (rows_in, grad_rows), (mix_t_in, mix_t), (stat_in, stat), (dgu_far.at[:, :, p.core], dgu),
                  (dwd_far.at[:, p.core], dwd), (hidden_in, hidden), (xg_in, xg), (wqkv_in, wqkv), (grad_in, grad))
    moves.start()
    length = lengths[0].astype(F32)
    greet(all_to_all_devices(p) + [p.sib, p.ynb])
    scatter = RingScatter(p, out, held, rs_s, rs_r)
    scatter2 = RingScatter(p, out2, held2, rs2_s, rs2_r)
    collect = Collect(p, dgu_far, lambda g, chip: dgu[g, chip], got_gu, (gu1, gu2, gu3, gu4), (a1, a2, a3, a4, a5, a6))
    collect2 = Collect(p, dqkv, lambda g, chip: dqkv[g, chip, p.core], got_qkv, (qk1, qk2, qk3, qk4),
                       (c1, c2, c3, c4, c5, c6))
    collect.start()
    fold = remote(dwd_far.at[:, 1 - p.core], d_in, ds.at[0], dr.at[0], p.sib)
    fold.start()
    y_fold = remote(d_pair.at[1 - p.g], d_y, ds.at[1], dr.at[1], p.ynb)
    o_fold = remote(dout.at[:, 1 - p.core], o_in, os.at[0], orr.at[0], p.sib)
    o_fold.start()
    x_fold = remote(o_pair.at[1 - p.x], o_two.at[p.x], os.at[1], orr.at[1], p.xnb)
    x_here = remote(o_pair.at[0], o_two.at[1 - p.x], os.at[1], orr.at[1], p.xnb)
    oy_fold = remote(o_two.at[1 - p.g], o_y, os.at[2], orr.at[2], p.ynb)

    def branch(t):
        part[...] = dot(inner[scatter.dest(t)], wdown[...])
        if t < CHIPS - 1:
            scatter.push(t, lambda k: part[rows_of(k)])

    make_tables(p, rope_rows, rope_starts)
    moves.wait(0, 1)
    branch(0)
    moves.wait(*range(2, 10))

    def turn(n, carry):
        kt[n] = keys[n].astype(F32).T.astype(BF)
        dk[n] = jnp.zeros((256, PAD), F32)
        dv[n] = jnp.zeros((256, PAD), F32)
        return carry

    lax.fori_loop(0, CHIPS, turn, 0)

    def attend(i):
        query = q[i]
        limit = limit_of(p, i, length)
        do = grad_rows[i]
        lse = stat[i]
        delta = jnp.sum(do.astype(F32).T * mix_t[i], axis=0, keepdims=True)

        def chunk(j, acc):
            w = jnp.exp2(scores_of(keys, query, limit, j) - lse)
            dp = dot_nt(values[j], do)
            ds_low = (w * (dp - delta)).astype(BF)
            dk[j] += dot(ds_low, query)
            dv[j] += dot(w.astype(BF), do)
            return acc + dot(kt[j], ds_low)

        acc = lax.fori_loop(0, i + 1, chunk, jnp.zeros((PAD, 256), F32))
        dq = acc.T * SCALE
        cosine, sine = tables(rope_rows, rope_starts, i)
        sine = -sine
        back_out[i, :, pl.ds(0, PAD)] = rope(dq[:TOK], cosine, sine).astype(BF)
        back_out[i, :, pl.ds(PAD, PAD)] = rope(dq[TOK:], cosine, sine).astype(BF)

    def fold_pairs():
        fold.wait_recv()
        for n in range(2):
            d_pair[n] = (dwd[n].astype(F32) + d_in[n].astype(F32)).astype(BF)
        y_fold.start()
        o_fold.wait_recv()
        for n in range(2):
            o_pair[n] = (dout[n, p.core].astype(F32) + o_in[n].astype(F32)).astype(BF)
        x_fold.start()

    for m in range(3):
        collect.pair_up(m)
    def again(b):
        h = xg[b].astype(F32)
        xg[b] = (h * norm_column(h)).astype(BF)

    moves.wait(11)
    for i in range(CHIPS):
        attend(i)
        again(i)
        if i < 5:
            collect.pair_up(i + 3)
        if 0 < i < CHIPS - 1:
            branch(i)
            collect.send(i - 1)
        if i == 5:
            fold_pairs()
    collect.send(6)
    collect.send(7)
    for n in range(CHIPS):
        for c in range(2):
            rows = pl.ds(c * TOK, TOK)
            dkv_low[0, n, c] = dk[n, rows].astype(BF)
            dkv_low[1, n, c] = dv[n, rows].astype(BF)
    swap = remote(dkv_low.at[:, :, 1 - p.core], dkv_in, xs, xr, p.sib)
    swap.start()
    branch(CHIPS - 1)
    moves.wait(10, 12, 13)
    for k in range(CHUNKS):
        rows = rows_of(k)
        result[rows] = (valid_of(p, k * ROWS, ROWS, length)
                        * (hidden[rows] + part[rows] + scatter.last(k))).astype(BF)
    o_two[p.x] = o_pair[p.x]
    x_here.wait_recv()
    oy_fold.start()
    swap.wait_recv()

    def keys_back(n, carry):
        own = pl.ds(pl.multiple_of(p.core * TOK, TOK), TOK)
        cosine, sine = tables(rope_rows, rope_starts, n)
        back_out[n, :, pl.ds(2 * PAD, PAD)] = rope(
            (dk[n, own] + dkv_in[0, n].astype(F32)) * SCALE, cosine, -sine).astype(BF)
        back_out[n, :, pl.ds(3 * PAD, PAD)] = (dv[n, own] + dkv_in[1, n].astype(F32)).astype(BF)
        return carry

    lax.fori_loop(0, CHIPS, keys_back, 0)

    def weight_part(n):
        value = dot_tn(whole(xg.at[:, :, pl.ds(n * 384, 384)]), whole(back_out)).astype(BF)
        dqkv[n // 2, pl.ds((n % 2) * 4, 4)] = value.reshape(4, 2, 48, 512)

    for t in range(CHIPS):
        part[...] = dot_nt(back_out[scatter2.dest(t)], whole(wqkv))
        if t < CHIPS - 1:
            scatter2.push(t, lambda k: part[rows_of(k)])
        if t == 0:
            for n in range(4):
                weight_part(n)
            collect2.start()
        if 1 <= t <= 4:
            collect2.pair_up(2 * t - 2)
            collect2.pair_up(2 * t - 1)
        if 2 <= t <= 5:
            collect2.send(2 * t - 4)
            collect2.send(2 * t - 3)
        if t == 5:
            y_fold.wait_recv()
            dwd_sum[...] = (d_pair[p.g].astype(F32) + d_y[...].astype(F32)).astype(BF)
            oy_fold.wait_recv()
            dout_sum[...] = (o_two[p.g].astype(F32) + o_y[...].astype(F32)).astype(BF)
        if t == 6:
            collect.receive()
    for k in range(CHUNKS):
        rows = rows_of(k)
        c = part[rows] + scatter2.last(k)
        h = tokens[rows].astype(F32)
        r = norm_column(h)
        input_back[rows] = (grad[rows] + r * c
                            - h * (r * r * r) * jnp.mean(c * h, axis=-1, keepdims=True)).astype(BF)
    collect2.receive()
    collect.finish()
    collect2.finish()
    scatter.finish()
    scatter2.finish()
    for copy in (fold, y_fold, swap, o_fold, x_fold, oy_fold):
        copy.wait_send()


def tail(*ins):
    dma = pltpu.SemaphoreType.DMA
    heads = (CHIPS, 2 * TOK, PAD)
    near = [VMEM((2, TOK, PAD), F32), VMEM((2, CHIPS, PAD), F32)] + [VMEM(heads, BF)] * 4 + [
        VMEM((CHIPS, PAD, 256), F32), VMEM((CHIPS, 1, 256), F32), VMEM((CHIPS, TOK, 512), BF), VMEM((512, 1536), BF),
        VMEM((TOK, 1536), F32), VMEM((2, CHIPS, 48, 1024), BF), VMEM((2, TOK, 1536), BF), VMEM((CHIPS, TOK, 1536), BF),
        VMEM((32, 48, 512), BF), VMEM((TOK, 1536), F32)]
    return call(
        tail_kernel,
        (sds(TOK, 1536), sds(TOK, 1536), sds(CHIPS, 48, 1024), sds(CHIPS, 48, 512), sds(48, 1536), sds(TOK, 1536)),
        ins,
        near + [VMEM((CHIPS, PAD, 256), BF), VMEM((CHIPS, 256, PAD), F32), VMEM((CHIPS, 256, PAD), F32),
         VMEM((2, CHIPS, 2, TOK, PAD), BF), VMEM((2, CHIPS, TOK, PAD), BF), VMEM((CHIPS, TOK, 4 * PAD), BF),
         VMEM((2, CHIPS, 2, 48, 512), BF), VMEM((TOK, 1536), F32)]
        + RingScatter.bufs * 2 + Collect.bufs(48, 1024) + Collect.bufs(48, 512)
        + [VMEM((2, TOK, 1536), BF), VMEM((2, TOK, 1536), BF), VMEM((TOK, 1536), BF),
           VMEM((2, 48, 1536), BF), VMEM((2, 48, 1536), BF), VMEM((2, 48, 1536), BF), VMEM((48, 1536), BF)]
        + RingScatter.sems * 2 + Collect.sems * 2 + [dma((2,)), dma((2,)), dma, dma, dma((3,)), dma((3,)), dma((14,))],
        5, far_ins=range(14), scalar_ins=(14,), flops=10 * 10**9, nbytes=20 << 20,
    )


def place_kernel(got_gu_in, got_qkv_in, dout_in, dwd_in, block_in, back_in, wq_in, wk_in, wv_in, wg_in, wu_in, gain_one, gain_two,
                 block_out, back_out, d_gain_one, d_q_out, d_k_out, d_v_out, d_out_out, d_gain_two, d_gate_out, d_up_out,
                 d_down_out,
                 got_gu, got_qkv, dout, dwd, wq, wk, wv, wg, wu, d_q, d_k, d_v, d_out, d_gate, d_up, d_down, block, back, move_s):
    moves = Moves(move_s, (wg_in, wg), (wu_in, wu), (got_gu_in, got_gu), (dwd_in, dwd), (dout_in, dout),
                  (got_qkv_in, got_qkv), (wq_in, wq), (wk_in, wk), (wv_in, wv), (block_in, block), (back_in, back),
                  (d_gate, d_gate_out), (d_up, d_up_out), (d_down, d_down_out), (d_out, d_out_out), (d_q, d_q_out),
                  (d_k, d_k_out), (d_v, d_v_out), (block, block_out), (back, back_out))
    moves.start(*range(11))
    space = spacing()
    gain_column = to_column(gain_one[...].astype(F32))
    gain_column2 = to_column(gain_two[...].astype(F32))
    lanes = lambda v: jnp.sum(v, axis=-1, keepdims=True)
    moves.wait(0, 1, 2)
    total = jnp.zeros((48, 256), F32)
    for n, (target, weight) in enumerate(((d_gate, wg), (d_up, wu))):
        for chip in range(CHIPS):
            for g in range(2):
                cols = pl.ds(g * 2048 + chip * 256, 256)
                piece = got_gu[chip, :, pl.ds(n * 512 + g * 256, 256)].astype(F32)
                target[:, cols] = piece * gain_column2
                total = total + piece * weight[:, cols].astype(F32)
        moves.start(11 + n)
    d_gain_two[...] = to_row(lanes(total))
    moves.wait(3, 4)
    d_down[...] = dwd[...].astype(F32)
    moves.start(13)
    d_out[...] = dout[...].astype(F32)
    moves.start(14)
    moves.wait(9, 10)
    moves.start(18, 19)
    moves.wait(5, 6, 7, 8)
    total = jnp.zeros((48, 1), F32)
    for n in range(4):
        cols = pl.ds(n * 384, 384)
        wide = jnp.concatenate([got_qkv[chip_of_head(2 * n + m), :, pl.ds(0, 256)] for m in range(2)], axis=-1)
        value = dot_nt(wide, space)
        total = total + lanes(value * wq[:, cols].astype(F32))
        d_q[:, cols] = value * gain_column
    moves.start(15)
    for n in range(2):
        cols = pl.ds(n * 384, 384)
        for source, target, place in ((wk, d_k, 256), (wv, d_v, 384)):
            wide = jnp.concatenate([got_qkv[chip_of_head(4 * n + m), :, pl.ds(place, 128)] for m in range(4)], axis=-1)
            value = dot_nt(wide, space)
            total = total + lanes(value * source[:, cols].astype(F32))
            target[:, cols] = value * gain_column
    moves.start(16, 17)
    d_gain_one[...] = to_row(total)
    moves.wait(*range(11, 20))


def place_all(*ins):
    f = lambda *shape: sds(*shape, dtype=F32)
    near = (((CHIPS, 48, 1024), BF), ((CHIPS, 48, 512), BF), ((48, 1536), BF), ((TOK, 1536), BF), ((48, 1536), BF),
            ((48, 768), BF), ((48, 768), BF), ((48, 4096), BF), ((48, 4096), BF), ((48, 1536), F32), ((48, 768), F32),
            ((48, 768), F32), ((48, 1536), F32), ((48, 4096), F32), ((48, 4096), F32), ((TOK, 1536), F32), ((TOK, 1536), BF), ((TOK, 1536), BF))
    return call(
        place_kernel,
        (sds(TOK, 1536), sds(TOK, 1536), f(1, 48), f(48, 1536), f(48, 768), f(48, 768), f(48, 1536), f(1, 48), f(48, 4096),
         f(48, 4096), f(TOK, 1536)),
        ins, [VMEM(shape, kind) for shape, kind in near] + [pltpu.SemaphoreType.DMA((20,))], None,
        far_ins=range(11), far_outs=(0, 1, 3, 4, 5, 6, 8, 9, 10), nbytes=10 << 20,
    )


def plane_device(hidden_in, lengths, attn_gain, w_query, w_key, w_value, w_out, mlp_gain, w_gate, w_up,
                 w_down, out_grad):
    gain_one = attn_gain[None]
    gain_two = mlp_gain[None]
    tokens = hidden_in[0]
    tg, wqkv, q, keys, values, mix_t, stat, hidden, grad, inner, dgu, dwd, grad_rows, wdown, dout = main(
        lengths, tokens, w_query, w_key, w_value, gain_one, out_grad[0],
        w_gate, w_up, gain_two, w_out, w_down)
    block, back, got_gu, got_qkv, dout_sum, dwd_sum = tail(
        q, keys, values, grad_rows, mix_t, stat, inner, wdown.reshape(512, 1536), hidden,
        dgu.reshape(2, CHIPS, 2, 48, 1024), dwd.reshape(2, 2, TOK, 1536), tg, wqkv, grad,
        lengths, dout.reshape(2, 2, 48, 1536), tokens)
    block, back, d_gain_one, d_q, d_k, d_v, d_out, d_gain_two, d_gate, d_up, d_down = place_all(
        got_gu, got_qkv, dout_sum, dwd_sum, block, back, w_query, w_key, w_value, w_gate, w_up, gain_one, gain_two)
    return (block[None], back[None], d_gain_one[0], d_q, d_k, d_v, d_out, d_gain_two[0], d_gate, d_up, d_down)


def solution(mesh):
    placed = (
        P("grp", "seq", None),
        P("grp"),
        P(("grp", "seq")),
        P(("grp", "seq"), None),
        P(("grp", "seq"), None),
        P(("grp", "seq"), None),
        P(("grp", "seq"), None),
        P(("grp", "seq")),
        P(("grp", "seq"), None),
        P(("grp", "seq"), None),
        P(("grp", "seq"), None),
        P("grp", "seq", None),
    )
    small = mesh.shape["grp"] == 2 and mesh.shape["seq"] == 2 * CHIPS
    return jax.shard_map(
        plane_device if small else per_device,
        mesh=mesh,
        in_specs=placed,
        out_specs=(
            P("grp", "seq", None),
            P("grp", "seq", None),
            P(("grp", "seq")),
            P(("grp", "seq"), None),
            P(("grp", "seq"), None),
            P(("grp", "seq"), None),
            P(("grp", "seq"), None),
            P(("grp", "seq")),
            P(("grp", "seq"), None),
            P(("grp", "seq"), None),
            P(("grp", "seq"), None),
        ),
        check_vma=False,
    )
```

```python
import math

import jax
import jax.numpy as jnp
from jax import lax
from jax.experimental import pallas as pl
from jax.experimental.pallas import tpu as pltpu
from jax.sharding import PartitionSpec as P

H = 16
KVH = 8
HD = 96
KBLK = 256


epsilon = 1e-05
rope_base = 100000.0
neg_big = -1e30


def rope_tables(positions):
    half_dim = HD // 2
    frequency = jnp.exp(-math.log(rope_base) * (2.0 * jnp.arange(half_dim, dtype=jnp.float32) / HD))
    angles = positions.astype(jnp.float32)[:, None] * frequency[None, :]
    return (jnp.cos(angles), jnp.sin(angles))


def rotate(values, cosine, sine_tab):
    half_dim = values.shape[-1] // 2
    first_half = values[..., :half_dim]
    second_half = values[..., half_dim:]
    cos_wide = cosine[:, None, :]
    sin_wide = sine_tab[:, None, :]
    return jnp.concatenate(
        [
            first_half * cos_wide - second_half * sin_wide,
            second_half * cos_wide + first_half * sin_wide,
        ],
        axis=-1,
    )


def unrotate(values, cosine, sine_tab):
    half_dim = values.shape[-1] // 2
    first_half = values[..., :half_dim]
    second_half = values[..., half_dim:]
    cos_wide = cosine[:, None, :]
    sin_wide = sine_tab[:, None, :]
    return jnp.concatenate(
        [
            first_half * cos_wide + second_half * sin_wide,
            second_half * cos_wide - first_half * sin_wide,
        ],
        axis=-1,
    )


def norm_scale(values):
    return lax.rsqrt(jnp.mean(values * values, axis=-1, keepdims=True) + epsilon)


def block_scores(queries, key_block, offset, positions, length):
    score_scale = 1.0 / math.sqrt(HD)
    raw_scores = (
        jnp.einsum("tkgd,skd->kgts", queries, key_block, preferred_element_type=jnp.float32)
        * score_scale
    )
    key_pos = offset + jnp.arange(key_block.shape[0], dtype=jnp.int32)
    allowed = (key_pos[None, :] <= positions[:, None]) & (key_pos[None, :] < length)
    return jnp.where(allowed[None, None], raw_scores, neg_big)


def block_needed(offset, positions, length):
    return (offset <= positions[-1]) & (offset < length)


def attend_forward(queries, key_blocks, value_blocks, positions, length):
    tok_count = queries.shape[0]
    group_size = queries.shape[2]
    offsets = jnp.arange(key_blocks.shape[0], dtype=jnp.int32) * KBLK

    def stat_step(carried, element):
        key_block, offset = element

        def stat_update(state):
            running_max, running_total = state
            scores = block_scores(queries, key_block, offset, positions, length)
            new_max = jnp.maximum(running_max, jnp.max(scores, axis=-1))
            new_total = running_total * jnp.exp(running_max - new_max) + jnp.sum(
                jnp.exp(scores - new_max[..., None]), axis=-1
            )
            return (new_max, new_total)

        return (
            lax.cond(
                block_needed(offset, positions, length), stat_update, lambda state: state, carried
            ),
            None,
        )

    start_max = jnp.full((KVH, group_size, tok_count), neg_big, jnp.float32)
    start_total = jnp.zeros((KVH, group_size, tok_count), jnp.float32)
    (row_max, row_total), unused = lax.scan(
        stat_step, (start_max, start_total), (key_blocks, offsets)
    )
    log_total = row_max + jnp.log(row_total)

    def value_step(carried, element):
        key_block, value_block, offset = element

        def value_update(state):
            accumulated, exact_sum = state
            scores = block_scores(queries, key_block, offset, positions, length)
            probs = jnp.exp(scores - log_total[..., None])
            weights = probs.astype(jnp.bfloat16)
            accumulated = accumulated + jnp.einsum(
                "kgts,skd->tkgd", weights, value_block, preferred_element_type=jnp.float32
            )
            exact_sum = exact_sum + jnp.einsum(
                "kgts,skd->tkgd",
                probs,
                value_block.astype(jnp.float32),
                preferred_element_type=jnp.float32,
            )
            return (accumulated, exact_sum)

        return (
            lax.cond(
                block_needed(offset, positions, length), value_update, lambda state: state, carried
            ),
            None,
        )

    start_acc = jnp.zeros((tok_count, KVH, group_size, HD), jnp.float32)
    (attended, exact_out), unused = lax.scan(
        value_step, (start_acc, start_acc), (key_blocks, value_blocks, offsets)
    )
    return (attended, exact_out, log_total)


def attend_backward(
    queries, key_blocks, value_blocks, attn_back, exact_out, log_total, positions, length
):
    tok_count = queries.shape[0]
    group_size = queries.shape[2]
    block_keys = key_blocks.shape[1]
    score_scale = 1.0 / math.sqrt(HD)
    offsets = jnp.arange(key_blocks.shape[0], dtype=jnp.int32) * KBLK
    delta = jnp.einsum("tkgd,tkgd->kgt", attn_back.astype(jnp.float32), exact_out)

    def grad_step(query_acc, element):
        key_block, value_block, offset = element

        def compute(acc):
            scores = block_scores(queries, key_block, offset, positions, length)
            probs = jnp.exp(scores - log_total[..., None])
            weights = probs.astype(jnp.bfloat16)
            dprobs = jnp.einsum(
                "tkgd,skd->kgts", attn_back, value_block, preferred_element_type=jnp.float32
            )
            score_back = (probs * (dprobs - delta[..., None])).astype(jnp.bfloat16)
            acc = acc + score_scale * jnp.einsum(
                "kgts,skd->tkgd", score_back, key_block, preferred_element_type=jnp.float32
            )
            key_part = score_scale * jnp.einsum(
                "kgts,tkgd->skd", score_back, queries, preferred_element_type=jnp.float32
            )
            value_part = jnp.einsum(
                "kgts,tkgd->skd", weights, attn_back, preferred_element_type=jnp.float32
            )
            return (acc, key_part, value_part)

        def skip(acc):
            empty = jnp.zeros((block_keys, KVH, HD), jnp.float32)
            return (acc, empty, empty)

        acc, key_part, value_part = lax.cond(
            block_needed(offset, positions, length), compute, skip, query_acc
        )
        return (acc, (key_part, value_part))

    start_query = jnp.zeros((tok_count, KVH, group_size, HD), jnp.float32)
    query_grad, (key_parts, value_parts) = lax.scan(
        grad_step, start_query, (key_blocks, value_blocks, offsets)
    )
    return (query_grad, key_parts.reshape(-1, KVH * HD), value_parts.reshape(-1, KVH * HD))


def split_rows(values, groups_count, seq_count):
    return values.reshape(
        (groups_count, seq_count, values.shape[0] // (groups_count * seq_count)) + values.shape[1:]
    )


def per_device(
    hidden_in,
    lengths,
    attn_gain,
    w_query,
    w_key,
    w_value,
    w_out,
    mlp_gain,
    w_gate,
    w_up,
    w_down,
    out_grad,
):
    tok_count = hidden_in.shape[1]
    group_size = H // KVH
    groups_count = lax.axis_size("grp")
    seq_count = lax.axis_size("seq")
    positions = lax.axis_index("seq") * tok_count + jnp.arange(tok_count, dtype=jnp.int32)
    length = lengths[0]
    valid_rows = (positions < length).astype(jnp.float32)[:, None]
    cosine, sine_tab = rope_tables(positions)
    front_weights = (
        lax.all_gather(attn_gain, ("grp", "seq"), axis=0, tiled=True),
        lax.all_gather(w_query, ("grp", "seq"), axis=0, tiled=True),
        lax.all_gather(w_key, ("grp", "seq"), axis=0, tiled=True),
        lax.all_gather(w_value, ("grp", "seq"), axis=0, tiled=True),
        lax.all_gather(w_out, ("grp", "seq"), axis=0, tiled=True),
        lax.all_gather(mlp_gain, ("grp", "seq"), axis=0, tiled=True),
        lax.all_gather(w_gate, ("grp", "seq"), axis=0, tiled=True),
        lax.all_gather(w_up, ("grp", "seq"), axis=0, tiled=True),
        lax.all_gather(w_down, ("grp", "seq"), axis=0, tiled=True),
    )
    gain_one, query_w, key_w, value_w, out_w, gain_two, gate_w, up_w, down_w = front_weights
    tokens_in = hidden_in[0].astype(jnp.float32)
    scale_one = norm_scale(tokens_in)
    normed = (tokens_in * scale_one * gain_one.astype(jnp.float32)).astype(jnp.bfloat16)
    query_lin = jnp.dot(normed, query_w, preferred_element_type=jnp.float32)
    key_lin = jnp.dot(normed, key_w, preferred_element_type=jnp.float32)
    value_lin = jnp.dot(normed, value_w, preferred_element_type=jnp.float32)
    queries = (
        rotate(query_lin.reshape(tok_count, H, HD), cosine, sine_tab)
        .astype(jnp.bfloat16)
        .reshape(tok_count, KVH, group_size, HD)
    )
    key_rot = (
        rotate(key_lin.reshape(tok_count, KVH, HD), cosine, sine_tab)
        .astype(jnp.bfloat16)
        .reshape(tok_count, KVH * HD)
    )
    value_low = value_lin.astype(jnp.bfloat16)
    keys_all, values_all = (
        lax.all_gather(key_rot, "seq", axis=0, tiled=True),
        lax.all_gather(value_low, "seq", axis=0, tiled=True),
    )
    key_blocks = keys_all.reshape(-1, KBLK, KVH, HD)
    value_blocks = values_all.reshape(-1, KBLK, KVH, HD)
    attended, exact_out, log_total = attend_forward(
        queries, key_blocks, value_blocks, positions, length
    )
    attn_mix = attended.reshape(tok_count, H * HD).astype(jnp.bfloat16)
    hidden = tokens_in + jnp.dot(attn_mix, out_w, preferred_element_type=jnp.float32)
    scale_two = norm_scale(hidden)
    normed_mlp = (hidden * scale_two * gain_two.astype(jnp.float32)).astype(jnp.bfloat16)
    gate_lin = jnp.dot(normed_mlp, gate_w, preferred_element_type=jnp.float32)
    up_lin = jnp.dot(normed_mlp, up_w, preferred_element_type=jnp.float32)
    silu_act = jax.nn.silu(gate_lin)
    inner_act = (silu_act * up_lin).astype(jnp.bfloat16)
    branch = jnp.dot(inner_act, down_w, preferred_element_type=jnp.float32)
    result = (valid_rows * (hidden + branch)).astype(jnp.bfloat16)[None]
    gain_one, query_w, key_w, value_w, out_w, gain_two, gate_w, up_w, down_w = front_weights
    cotangent = out_grad[0].astype(jnp.float32)
    branch_grad = valid_rows * cotangent
    branch_low = branch_grad.astype(jnp.bfloat16)
    down_grad = jnp.einsum("tf,td->fd", inner_act, branch_low, preferred_element_type=jnp.float32)
    inner_grad = jnp.einsum("td,fd->tf", branch_low, down_w, preferred_element_type=jnp.float32)
    sigma = jax.nn.sigmoid(gate_lin)
    gate_back = (inner_grad * up_lin * (sigma + gate_lin * sigma * (1.0 - sigma))).astype(
        jnp.bfloat16
    )
    up_back = (inner_grad * silu_act).astype(jnp.bfloat16)
    gate_grad = jnp.einsum("td,tf->df", normed_mlp, gate_back, preferred_element_type=jnp.float32)
    up_grad = jnp.einsum("td,tf->df", normed_mlp, up_back, preferred_element_type=jnp.float32)
    mlp_norm_grad = jnp.einsum(
        "tf,df->td", gate_back, gate_w, preferred_element_type=jnp.float32
    ) + jnp.einsum("tf,df->td", up_back, up_w, preferred_element_type=jnp.float32)
    gain_two_grad = jnp.sum(mlp_norm_grad * hidden * scale_two, axis=0)
    weighted_two = mlp_norm_grad * gain_two.astype(jnp.float32)
    hidden_grad = (
        branch_grad
        + scale_two * weighted_two
        - hidden
        * (scale_two * scale_two * scale_two)
        * jnp.mean(weighted_two * hidden, axis=-1, keepdims=True)
    )
    mlp_seq = (
        lax.psum_scatter(
            split_rows(gain_two_grad, groups_count, seq_count).astype(jnp.bfloat16),
            "seq",
            scatter_dimension=1,
            tiled=True,
        ).astype(jnp.float32),
        lax.psum_scatter(
            split_rows(gate_grad, groups_count, seq_count).astype(jnp.bfloat16),
            "seq",
            scatter_dimension=1,
            tiled=True,
        ).astype(jnp.float32),
        lax.psum_scatter(
            split_rows(up_grad, groups_count, seq_count).astype(jnp.bfloat16),
            "seq",
            scatter_dimension=1,
            tiled=True,
        ).astype(jnp.float32),
        lax.psum_scatter(
            split_rows(down_grad, groups_count, seq_count).astype(jnp.bfloat16),
            "seq",
            scatter_dimension=1,
            tiled=True,
        ).astype(jnp.float32),
    )
    mlp_grp = (
        lax.psum_scatter(
            mlp_seq[0].astype(jnp.bfloat16), "grp", scatter_dimension=0, tiled=True
        ).astype(jnp.float32),
        lax.psum_scatter(
            mlp_seq[1].astype(jnp.bfloat16), "grp", scatter_dimension=0, tiled=True
        ).astype(jnp.float32),
        lax.psum_scatter(
            mlp_seq[2].astype(jnp.bfloat16), "grp", scatter_dimension=0, tiled=True
        ).astype(jnp.float32),
        lax.psum_scatter(
            mlp_seq[3].astype(jnp.bfloat16), "grp", scatter_dimension=0, tiled=True
        ).astype(jnp.float32),
    )
    mlp_grads = tuple((piece.reshape(piece.shape[2:]) for piece in mlp_grp))
    mix_back = hidden_grad.astype(jnp.bfloat16)
    out_w_grad = jnp.einsum("td,te->de", attn_mix, mix_back, preferred_element_type=jnp.float32)
    attn_back = (
        jnp.einsum("te,de->td", mix_back, out_w, preferred_element_type=jnp.float32)
        .astype(jnp.bfloat16)
        .reshape(tok_count, KVH, group_size, HD)
    )
    query_grad, key_grad_all, value_grad_all = attend_backward(
        queries, key_blocks, value_blocks, attn_back, exact_out, log_total, positions, length
    )
    key_grad, value_grad = (
        lax.psum_scatter(
            key_grad_all.astype(jnp.bfloat16), "seq", scatter_dimension=0, tiled=True
        ).astype(jnp.float32),
        lax.psum_scatter(
            value_grad_all.astype(jnp.bfloat16), "seq", scatter_dimension=0, tiled=True
        ).astype(jnp.float32),
    )
    query_back = (
        unrotate(query_grad.reshape(tok_count, H, HD), cosine, sine_tab)
        .astype(jnp.bfloat16)
        .reshape(tok_count, H * HD)
    )
    key_back = (
        unrotate(key_grad.reshape(tok_count, KVH, HD), cosine, sine_tab)
        .astype(jnp.bfloat16)
        .reshape(tok_count, KVH * HD)
    )
    value_back = value_grad.astype(jnp.bfloat16)
    query_w_grad = jnp.einsum("td,te->de", normed, query_back, preferred_element_type=jnp.float32)
    key_w_grad = jnp.einsum("td,te->de", normed, key_back, preferred_element_type=jnp.float32)
    value_w_grad = jnp.einsum("td,te->de", normed, value_back, preferred_element_type=jnp.float32)
    attn_norm_grad = (
        jnp.einsum("te,de->td", query_back, query_w, preferred_element_type=jnp.float32)
        + jnp.einsum("te,de->td", key_back, key_w, preferred_element_type=jnp.float32)
        + jnp.einsum("te,de->td", value_back, value_w, preferred_element_type=jnp.float32)
    )
    gain_one_grad = jnp.sum(attn_norm_grad * tokens_in * scale_one, axis=0)
    weighted_one = attn_norm_grad * gain_one.astype(jnp.float32)
    input_back = (
        hidden_grad
        + scale_one * weighted_one
        - tokens_in
        * (scale_one * scale_one * scale_one)
        * jnp.mean(weighted_one * tokens_in, axis=-1, keepdims=True)
    )
    attn_seq = (
        lax.psum_scatter(
            split_rows(gain_one_grad, groups_count, seq_count).astype(jnp.bfloat16),
            "seq",
            scatter_dimension=1,
            tiled=True,
        ).astype(jnp.float32),
        lax.psum_scatter(
            split_rows(query_w_grad, groups_count, seq_count).astype(jnp.bfloat16),
            "seq",
            scatter_dimension=1,
            tiled=True,
        ).astype(jnp.float32),
        lax.psum_scatter(
            split_rows(key_w_grad, groups_count, seq_count).astype(jnp.bfloat16),
            "seq",
            scatter_dimension=1,
            tiled=True,
        ).astype(jnp.float32),
        lax.psum_scatter(
            split_rows(value_w_grad, groups_count, seq_count).astype(jnp.bfloat16),
            "seq",
            scatter_dimension=1,
            tiled=True,
        ).astype(jnp.float32),
        lax.psum_scatter(
            split_rows(out_w_grad, groups_count, seq_count).astype(jnp.bfloat16),
            "seq",
            scatter_dimension=1,
            tiled=True,
        ).astype(jnp.float32),
    )
    attn_grp = (
        lax.psum_scatter(
            attn_seq[0].astype(jnp.bfloat16), "grp", scatter_dimension=0, tiled=True
        ).astype(jnp.float32),
        lax.psum_scatter(
            attn_seq[1].astype(jnp.bfloat16), "grp", scatter_dimension=0, tiled=True
        ).astype(jnp.float32),
        lax.psum_scatter(
            attn_seq[2].astype(jnp.bfloat16), "grp", scatter_dimension=0, tiled=True
        ).astype(jnp.float32),
        lax.psum_scatter(
            attn_seq[3].astype(jnp.bfloat16), "grp", scatter_dimension=0, tiled=True
        ).astype(jnp.float32),
        lax.psum_scatter(
            attn_seq[4].astype(jnp.bfloat16), "grp", scatter_dimension=0, tiled=True
        ).astype(jnp.float32),
    )
    attn_grads = tuple((piece.reshape(piece.shape[2:]) for piece in attn_grp))
    return (
        result,
        input_back.astype(jnp.bfloat16)[None],
        attn_grads[0],
        attn_grads[1],
        attn_grads[2],
        attn_grads[3],
        attn_grads[4],
        mlp_grads[0],
        mlp_grads[1],
        mlp_grads[2],
        mlp_grads[3],
    )


MESH_ID = pl.DeviceIdType.MESH
VMEM = pltpu.VMEM
LINE = 4
CHIPS = 8
TOK = 128
PAD = 128
CHUNKS = 4
ROWS = TOK // CHUNKS
BF = jnp.bfloat16
F32 = jnp.float32
VSPEC = pl.BlockSpec(memory_space=pltpu.VMEM)


def ring_of(chip):
    z = chip // 2
    x = chip % 2
    return x * LINE + z + x * (LINE - 1 - 2 * z)


def chip_of(ring):
    x = ring // LINE
    q = ring % LINE
    return (q + x * (LINE - 1 - 2 * q)) * 2 + x


class Place:
    def __init__(self):
        self.g = lax.axis_index("grp")
        self.s = lax.axis_index("seq")
        self.core = self.s % 2
        self.chip = self.s // 2
        self.x = self.chip % 2
        self.ring = ring_of(self.chip)
        self.step = 1 - 2 * self.core
        self.next = {"seq": self.at(self.step) * 2 + self.core}
        self.prev = {"seq": self.at(-self.step) * 2 + self.core}
        self.sib = {"seq": self.s + 1 - 2 * self.core}
        self.ynb = {"grp": 1 - self.g}
        self.xnb = {"seq": self.s + 2 - 4 * self.x}

    def at(self, offset):
        return chip_of((self.ring + offset + 8 * CHIPS) % CHIPS)

    def behind(self, t):
        return self.at(-t * self.step)

    def off(self, i):
        return {"seq": ((self.chip + i + CHIPS) % CHIPS) * 2 + self.core}

    def src(self, i):
        return (self.chip - i + CHIPS) % CHIPS


def greet(devices):
    barrier = pltpu.get_barrier_semaphore()
    for device in devices:
        pl.semaphore_signal(barrier, inc=1, device_id=device, device_id_type=MESH_ID)
    pl.semaphore_wait(barrier, len(devices))


def remote(src, dst, send, recv, device):
    return pltpu.make_async_remote_copy(
        src_ref=src, dst_ref=dst, send_sem=send, recv_sem=recv, device_id=device,
        device_id_type=MESH_ID,
    )


class RingGather:
    sems = [pltpu.SemaphoreType.DMA((CHIPS, CHUNKS)), pltpu.SemaphoreType.DMA((CHIPS, CHUNKS))]

    def __init__(self, place, all_ref, send, recv):
        self.place, self.all, self.send, self.recv = place, all_ref, send, recv
        self.rows = all_ref.shape[1] // CHUNKS

    def copy(self, t, k):
        part = self.all.at[self.place.behind(t), pl.ds(k * self.rows, self.rows)]
        return remote(part, part, self.send.at[t, k], self.recv.at[t, k], self.place.next)

    def start(self, k=None):
        for k in range(CHUNKS) if k is None else (k,):
            self.copy(0, k).start()

    def pump(self, t):
        for k in range(CHUNKS):
            self.pass_on(t, k)

    def pass_on(self, t, k):
        self.copy(t - 1, k).wait_recv()
        if t < CHIPS - 1:
            self.copy(t, k).start()

    def pump_some(self, first, last):
        for n in range(first, last):
            self.pass_on(1 + n // CHUNKS, n % CHUNKS)

    def finish(self):
        for t in range(CHIPS - 1):
            for k in range(CHUNKS):
                self.copy(t, k).wait_send()


class RingScatter:
    sems = [pltpu.SemaphoreType.DMA((CHIPS, CHUNKS)), pltpu.SemaphoreType.DMA((CHIPS, CHUNKS))]
    bufs = [VMEM((CHIPS - 1, TOK, 1536), BF), VMEM((CHIPS - 1, TOK, 1536), BF)]

    def __init__(self, place, out, held, send, recv):
        self.place, self.out, self.held, self.send, self.recv = place, out, held, send, recv

    def copy(self, t, k):
        rows = pl.ds(k * ROWS, ROWS)
        return remote(self.out.at[t, rows], self.held.at[t, rows], self.send.at[t, k],
                      self.recv.at[t, k], self.place.next)

    def dest(self, t):
        return self.place.behind(t + 1)

    def push(self, t, term):
        for k in range(CHUNKS):
            rows = pl.ds(k * ROWS, ROWS)
            value = term(k)
            if t > 0:
                self.copy(t - 1, k).wait_recv()
                value = value + self.held[t - 1, rows].astype(F32)
            self.out[t, rows] = value.astype(BF)
            self.copy(t, k).start()

    def last(self, k):
        self.copy(CHIPS - 2, k).wait_recv()
        return self.held[CHIPS - 2, pl.ds(k * ROWS, ROWS)].astype(F32)

    def finish(self):
        for t in range(CHIPS - 1):
            for k in range(CHUNKS):
                self.copy(t, k).wait_send()


class Spread:
    sems = [pltpu.SemaphoreType.DMA((CHIPS,)), pltpu.SemaphoreType.DMA((CHIPS,)),
            pltpu.SemaphoreType.DMA((CHIPS,)), pltpu.SemaphoreType.DMA((CHIPS,)),
            pltpu.SemaphoreType.DMA((2 * CHIPS,)), pltpu.SemaphoreType.DMA((2 * CHIPS,))]

    def __init__(self, place, slab, all_ref, local, *sems):
        self.place, self.slab, self.all, self.local = place, slab, all_ref, local
        self.s1, self.r1, self.s2, self.r2, self.s3, self.r3 = sems

    def block(self, g, chip):
        return self.all.at[g * 16 + chip * 2 + self.place.core]

    def across(self, i):
        p = self.place
        return remote(self.slab.at[(p.chip + i) % CHIPS], self.block(p.g, p.chip), self.s1.at[i],
                      self.r1.at[i], p.off(i))

    def arrived(self, i):
        p = self.place
        return remote(self.slab.at[0], self.block(p.g, p.src(i)), self.s1.at[i], self.r1.at[i],
                      p.off(i))

    def to_y(self, i):
        p = self.place
        part = self.block(p.g, p.src(i))
        return remote(part, part, self.s2.at[i], self.r2.at[i], p.ynb)

    def from_y(self, i):
        p = self.place
        part = self.block(1 - p.g, p.src(i))
        return remote(part, part, self.s2.at[i], self.r2.at[i], p.ynb)

    def to_sib(self, i, other):
        p = self.place
        part = self.block((1 - p.g) if other else p.g, p.src(i))
        n = i + CHIPS * other
        return remote(part, part, self.s3.at[n], self.r3.at[n], p.sib)

    def from_sib(self, i, other):
        p = self.place
        g = (1 - p.g) if other else p.g
        part = self.all.at[g * 16 + p.src(i) * 2 + 1 - p.core]
        n = i + CHIPS * other
        return remote(part, part, self.s3.at[n], self.r3.at[n], p.sib)

    def start(self):
        p = self.place
        own = pltpu.make_async_copy(self.slab.at[p.chip], self.block(p.g, p.chip), self.local)
        own.start()
        for i in range(1, CHIPS):
            self.across(i).start()
        own.wait()
        self.to_y(0).start()
        self.to_sib(0, 0).start()

    def pump(self, i):
        self.arrived(i).wait_recv()
        self.to_y(i).start()
        self.to_sib(i, 0).start()
        self.from_y(i - 1).wait_recv()
        self.to_sib(i - 1, 1).start()

    def finish(self):
        self.from_y(CHIPS - 1).wait_recv()
        self.to_sib(CHIPS - 1, 1).start()
        for i in range(CHIPS):
            self.from_sib(i, 0).wait_recv()
            self.from_sib(i, 1).wait_recv()
        for i in range(CHIPS):
            if i > 0:
                self.across(i).wait_send()
            self.to_y(i).wait_send()
            self.to_sib(i, 0).wait_send()
            self.to_sib(i, 1).wait_send()


class Across:
    sems = [pltpu.SemaphoreType.DMA((CHIPS,)), pltpu.SemaphoreType.DMA((CHIPS,))]

    def __init__(self, place, slab, got, local, send, recv):
        self.place, self.slab, self.got, self.send, self.recv = place, slab, got, send, recv
        self.own = pltpu.make_async_copy(slab.at[place.chip], got.at[place.chip], local)

    def to(self, i):
        p = self.place
        return remote(self.slab.at[(p.chip + i) % CHIPS], self.got.at[p.chip], self.send.at[i], self.recv.at[i], p.off(i))

    def arrived(self, i):
        p = self.place
        return remote(self.slab.at[0], self.got.at[p.src(i)], self.send.at[i], self.recv.at[i], p.off(i))

    def start(self):
        self.own.start()
        for i in range(1, CHIPS):
            self.to(i).start()

    def land(self):
        self.own.wait()
        for i in range(1, CHIPS):
            self.arrived(i).wait_recv()

    def sent(self):
        for i in range(1, CHIPS):
            self.to(i).wait_send()


class Quarters:
    sems = [pltpu.SemaphoreType.DMA((3,)), pltpu.SemaphoreType.DMA((3,))]

    def __init__(self, place, view, send, recv):
        p = place
        here, over = view(p.g, p.core), view(1 - p.g, p.core)
        self.y = remote(here, here, send.at[0], recv.at[0], p.ynb)
        self.sib = remote(here, here, send.at[1], recv.at[1], p.sib)
        self.sib2 = remote(over, over, send.at[2], recv.at[2], p.sib)

    def start(self):
        self.y.start()
        self.sib.start()

    def pass_on(self):
        self.y.wait_recv()
        self.sib2.start()

    def arrive(self):
        self.sib.wait_recv()
        self.sib2.wait_recv()

    def finish(self):
        for copy in (self.y, self.sib, self.sib2):
            copy.wait_send()


class Share:
    sems = [pltpu.SemaphoreType.DMA((CHIPS,))] * 4 + [pltpu.SemaphoreType.DMA((2 * CHIPS,))] * 2

    def __init__(self, place, all_ref, *sems):
        self.place, self.all = place, all_ref
        self.s1, self.r1, self.s2, self.r2, self.s3, self.r3 = sems

    def slot(self, t, other):
        p = self.place
        return self.all.at[((1 - p.g) if other else p.g) * 16 + p.behind(t) * 2 + p.core]

    def ring(self, t):
        part = self.slot(t, 0)
        return remote(part, part, self.s1.at[t], self.r1.at[t], self.place.next)

    def y(self, t, back):
        part = self.slot(t, back)
        return remote(part, part, self.s2.at[t], self.r2.at[t], self.place.ynb)

    def to_sib(self, t, other):
        part = self.slot(t, other)
        n = t + CHIPS * other
        return remote(part, part, self.s3.at[n], self.r3.at[n], self.place.sib)

    def from_sib(self, t, other):
        p = self.place
        part = self.all.at[((1 - p.g) if other else p.g) * 16 + p.behind(-t) * 2 + 1 - p.core]
        n = t + CHIPS * other
        return remote(part, part, self.s3.at[n], self.r3.at[n], p.sib)

    def start(self):
        self.ring(0).start()
        self.y(0, 0).start()
        self.to_sib(0, 0).start()

    def pump(self, t):
        self.ring(t - 1).wait_recv()
        if t < CHIPS - 1:
            self.ring(t).start()
        self.y(t, 0).start()
        self.to_sib(t, 0).start()
        self.y(t - 1, 1).wait_recv()
        self.to_sib(t - 1, 1).start()

    def finish(self):
        self.y(CHIPS - 1, 1).wait_recv()
        self.to_sib(CHIPS - 1, 1).start()
        for t in range(CHIPS):
            for other in range(2):
                self.from_sib(t, other).wait_recv()
                self.to_sib(t, other).wait_send()
            self.y(t, 0).wait_send()
            if t < CHIPS - 1:
                self.ring(t).wait_send()


class Reduce:
    sems = [pltpu.SemaphoreType.DMA((CHIPS,))] * 6

    @staticmethod
    def bufs(rows, columns):
        return [VMEM((2, CHIPS, rows, columns), BF), VMEM((CHIPS, 2, rows, columns), BF)] + [
            VMEM((CHIPS, rows, columns), BF)] * 4

    def __init__(self, place, grads, bufs, sems):
        self.place, self.grads = place, grads
        self.own, self.sib_in, self.pair, self.y_in, self.out, self.held = bufs
        self.s1, self.r1, self.s2, self.r2, self.s3, self.r3 = sems

    def sib(self, chip):
        p = self.place
        return remote(self.grads.at[:, chip, 1 - p.core], self.sib_in.at[chip], self.s1.at[chip], self.r1.at[chip], p.sib)

    def y(self, chip):
        return remote(self.pair.at[chip], self.y_in.at[chip], self.s2.at[chip], self.r2.at[chip], self.place.ynb)

    def ring(self, t):
        return remote(self.out.at[t], self.held.at[t], self.s3.at[t], self.r3.at[t], self.place.next)

    def start(self):
        for chip in range(CHIPS):
            self.sib(chip).start()

    def pair_up(self, chip):
        other = 1 - self.place.g
        self.sib(chip).wait_recv()
        self.pair[chip] = (self.own[other, chip].astype(F32) + self.sib_in[chip, other].astype(F32)).astype(BF)
        self.y(chip).start()

    def term(self, t):
        p = self.place
        chip = p.behind(t + 1)
        self.y(chip).wait_recv()
        value = (self.own[p.g, chip].astype(F32) + self.sib_in[chip, p.g].astype(F32)) + self.y_in[chip].astype(F32)
        if t > 0:
            self.ring(t - 1).wait_recv()
            value = value + self.held[t - 1].astype(F32)
        return value

    def push(self, t):
        self.out[t] = self.term(t).astype(BF)
        self.ring(t).start()

    def finish(self):
        for chip in range(CHIPS):
            self.sib(chip).wait_send()
            self.y(chip).wait_send()
        for t in range(CHIPS - 1):
            self.ring(t).wait_send()


class Collect:
    order = tuple(range(1, CHIPS)) + (0,)
    sems = [pltpu.SemaphoreType.DMA((CHIPS,))] * 6

    @staticmethod
    def bufs(rows, columns):
        return [VMEM((CHIPS, 2, rows, columns), BF), VMEM((CHIPS, 2, rows, columns), BF),
                VMEM((CHIPS, rows, columns), BF), VMEM((CHIPS, rows, columns), BF)]

    def __init__(self, place, grads, own, got, bufs, sems):
        self.place, self.grads, self.own, self.got = place, grads, own, got
        self.sib_in, self.pair, self.y_in, self.total = bufs
        self.s1, self.r1, self.s2, self.r2, self.s3, self.r3 = sems

    def sib(self, n):
        p = self.place
        return remote(self.grads.at[:, (p.chip + n) % CHIPS, 1 - p.core], self.sib_in.at[n],
                      self.s1.at[n], self.r1.at[n], p.sib)

    def y(self, n):
        p = self.place
        return remote(self.pair.at[n, 1 - p.g], self.y_in.at[n], self.s2.at[n], self.r2.at[n], p.ynb)

    def across(self, n):
        p = self.place
        return remote(self.total.at[n], self.got.at[p.chip], self.s3.at[n], self.r3.at[n], p.off(n))

    def arrived(self, n):
        p = self.place
        return remote(self.total.at[n], self.got.at[p.src(n)], self.s3.at[n], self.r3.at[n], p.off(n))

    def start(self):
        for n in self.order:
            self.sib(n).start()

    def pair_up(self, m):
        p, n = self.place, self.order[m]
        self.sib(n).wait_recv()
        for g in range(2):
            self.pair[n, g] = (self.own(g, (p.chip + n) % CHIPS).astype(F32)
                               + self.sib_in[n, g].astype(F32)).astype(BF)
        self.y(n).start()

    def send(self, m):
        p, n = self.place, self.order[m]
        self.y(n).wait_recv()
        value = (self.pair[n, p.g].astype(F32) + self.y_in[n].astype(F32)).astype(BF)
        if n == 0:
            self.got[p.chip] = value
        else:
            self.total[n] = value
            self.across(n).start()

    def receive(self):
        for n in range(1, CHIPS):
            self.arrived(n).wait_recv()

    def finish(self):
        for n in range(CHIPS):
            self.sib(n).wait_send()
            self.y(n).wait_send()
            if n > 0:
                self.across(n).wait_send()


def dot(a, b):
    return lax.dot_general(a, b, (((1,), (0,)), ((), ())), preferred_element_type=F32)


def dot_nt(a, b):
    return lax.dot_general(a, b, (((1,), (1,)), ((), ())), preferred_element_type=F32)


def all_to_all_devices(place):
    return [place.off(i) for i in range(1, CHIPS)]


def call(body, outs, ins, scratch, collective_id, far_ins=(), far_outs=(), scalar_ins=(), flops=0, nbytes=0):
    kwargs = {}
    if collective_id is not None:
        kwargs = dict(collective_id=collective_id, has_side_effects=True)
    far = pl.BlockSpec(memory_space=pl.ANY)
    scalar = pl.BlockSpec(memory_space=pltpu.SMEM)
    return pl.pallas_call(
        body,
        out_shape=outs,
        in_specs=[far if n in far_ins else scalar if n in scalar_ins else VSPEC for n in range(len(ins))],
        out_specs=tuple(far if n in far_outs else VSPEC for n in range(len(outs))),
        scratch_shapes=scratch,
        compiler_params=pltpu.CompilerParams(vmem_limit_bytes=60 << 20, **kwargs),
        cost_estimate=pl.CostEstimate(flops=flops, bytes_accessed=nbytes, transcendentals=0),
    )(*ins)


class Moves:
    def __init__(self, sems, *pairs):
        self.copies = [pltpu.make_async_copy(a, b, sems.at[n]) for n, (a, b) in enumerate(pairs)]

    def start(self, *which):
        for n in which or range(len(self.copies)):
            self.copies[n].start()

    def wait(self, *which):
        for n in which or range(len(self.copies)):
            self.copies[n].wait()


def sds(*shape, dtype=BF):
    return jax.ShapeDtypeStruct(shape, dtype)


def rope(u, cosine, sine):
    return u * cosine + pltpu.roll(u, 64, 1) * sine


def make_tables(p, rows, starts):
    def fill(target, slots):
        entry = lax.broadcasted_iota(jnp.int32, slots.shape, 1)
        upper = entry >= 64
        entry = jnp.where(upper, entry - 64, entry)
        frequency = jnp.where(entry < HD // 2, jnp.exp(-math.log(rope_base) * (2.0 * entry.astype(F32) / HD)), 0.0)
        angles = slots.astype(F32) * frequency
        target[0] = jnp.cos(angles)
        target[1] = jnp.where(upper, 1.0, -1.0) * jnp.sin(angles)

    fill(rows, lax.broadcasted_iota(jnp.int32, (TOK, PAD), 0))
    fill(starts, (2 * lax.broadcasted_iota(jnp.int32, (CHIPS, PAD), 0) + p.core) * TOK)


def tables(rows, starts, i):
    c_row, s_row = rows[0], rows[1]
    c_start, s_start = starts[0, pl.ds(i, 1)], starts[1, pl.ds(i, 1)]
    return c_start * c_row - s_start * s_row, s_start * c_row + c_start * s_row


def limit_of(p, i, length):
    lane = lax.broadcasted_iota(jnp.int32, (1, 2 * TOK), 1)
    slot = jnp.where(lane < TOK, lane, lane - TOK) + (2 * i + p.core) * TOK
    return jnp.minimum(slot.astype(F32), length - 1.0)


def valid_of(p, first, rows, length):
    slot = lax.broadcasted_iota(jnp.int32, (rows, 1), 0) + p.s * TOK + first
    return jnp.where(slot.astype(F32) < length, 1.0, 0.0)


def spacing(heads=4):
    r = lax.broadcasted_iota(jnp.int32, (96 * heads, 128 * heads), 0)
    c = lax.broadcasted_iota(jnp.int32, (96 * heads, 128 * heads), 1)
    target = r
    for n in range(1, 2 * heads):
        target = target + jnp.where(r >= 48 * n, 16, 0)
    return jnp.where(target == c, 1.0, 0.0).astype(BF)


def chip_of_head(j):
    return 2 * (j % LINE) + j // LINE


def diagonal(n):
    return lax.broadcasted_iota(jnp.int32, (n, n), 0) == lax.broadcasted_iota(jnp.int32, (n, n), 1)


def to_column(row):
    n = row.shape[1]
    return jnp.sum(jnp.where(diagonal(n), jnp.broadcast_to(row, (n, n)), 0.0), axis=1, keepdims=True)


def to_row(column):
    n = column.shape[0]
    return jnp.sum(jnp.where(diagonal(n), jnp.broadcast_to(column, (n, n)), 0.0), axis=0, keepdims=True)


def norm_column(h):
    return lax.rsqrt(jnp.mean(h * h, axis=-1, keepdims=True) + epsilon)


def whole(ref):
    value = ref[...]
    return value.reshape(value.shape[0] * value.shape[1], value.shape[2])


LOG2E = 1.4426950408889634
SCALE = 1.0 / math.sqrt(96)
SCALE2 = SCALE * LOG2E


def scores_of(keys, query, limit, j):
    s = dot_nt(keys[j], query) * SCALE2
    pos = lax.broadcasted_iota(jnp.int32, s.shape, 0) + j * 256
    return jnp.where(pos.astype(F32) <= limit, s, neg_big)


def dot_tn(a, b):
    return lax.dot_general(a, b, (((0,), (0,)), ((), ())), preferred_element_type=F32)


def rows_of(k):
    return pl.ds(k * ROWS, ROWS)


def main_kernel(lengths, tokens, wq, wk, wv, gain_one, out_grad, wg, wu, gain_two, wo, wd,
                tg_out, wqkv_out, q_out, keys_out, values_out, mix_t_out, stat_out,
                hidden_out, grad_out, inner_out, dgu_out, dwd_out, rows_out, wdown_out, dwo_out,
                tg, wqkv, q, keys, values, mix_t, stat, grad, inner, dgu, dwd, grad_rows,
                rope_rows, rope_starts, slab, slab_gu, mix, vt, bgg, wall, wgu, wdown, mx, hid, x2, gub, low, rows_away, part, scale, out2, held2,
                ag_s, ag_r, s1, r1, s2, r2, s3, r3, bg_s, bg_r, g1, h1, o1, p1, o2, p2, o3, p3,
                mx_s, mx_r, rs2_s, rs2_r, away_s, away_r, ks, kr, vs, vr, q1, q2, q3, q4, local, local2, move_s):
    p = Place()
    gather = RingGather(p, tg, ag_s, ag_r)
    spread = Spread(p, slab, wqkv, local, s1, r1, s2, r2, s3, r3)
    gather_bg = RingGather(p, bgg, bg_s, bg_r)
    across = Across(p, slab_gu, wgu.at[p.g, :, p.core], local2, g1, h1)
    share = Share(p, wall, o1, p1, o2, p2, o3, p3)
    gather_mix = RingGather(p, mx, mx_s, mx_r)
    scatter2 = RingScatter(p, out2, held2, rs2_s, rs2_r)
    quarters = Quarters(p, lambda g, core: wgu.at[g, :, core], q1, q2)
    quarters2 = Quarters(p, lambda g, core: wdown.at[g, core], q3, q4)
    moves = Moves(move_s, (tg, tg_out), (wqkv, wqkv_out), (q, q_out), (keys, keys_out),
                  (values, values_out), (mix_t, mix_t_out), (stat, stat_out),
                  (hid.at[p.chip], hidden_out), (grad, grad_out), (inner, inner_out), (dgu, dgu_out), (dwd, dwd_out),
                  (grad_rows, rows_out), (wdown, wdown_out),
                  (wo, wall.at[p.g * 16 + p.s]), (wd, wdown.at[p.g, p.core]), (wall, dwo_out))
    moves.start(14, 15)
    length = lengths[0].astype(F32)
    tg[p.chip] = tokens[...]
    greet(all_to_all_devices(p) + [p.sib, p.ynb])
    gather.start()
    make_tables(p, rope_rows, rope_starts)
    space = spacing()
    gain_column = to_column(gain_one[...].astype(F32))
    gain_column2 = to_column(gain_two[...].astype(F32))
    for n in range(4):
        cols = pl.ds(n * 384, 384)
        wide = dot((wq[:, cols].astype(F32) * gain_column).astype(BF), space).astype(BF)
        for m in range(2):
            slab[chip_of_head(2 * n + m), :, pl.ds(0, 256)] = wide[:, m * 256:m * 256 + 256]
    for n in range(2):
        for source, place in ((wk, 256), (wv, 384)):
            wide = dot((source[:, pl.ds(n * 384, 384)].astype(F32) * gain_column).astype(BF), space).astype(BF)
            for m in range(4):
                slab[chip_of_head(4 * n + m), :, pl.ds(place, 128)] = wide[:, m * 128:m * 128 + 128]
    spread.start()
    bgg[p.chip] = (out_grad[...].astype(F32) * valid_of(p, 0, TOK, length)).astype(BF)
    gather.pump(1)
    for chip in range(CHIPS):
        for n, source in enumerate((wg, wu)):
            for g in range(2):
                slab_gu[chip, :, pl.ds(n * 512 + g * 256, 256)] = (
                    source[:, pl.ds(g * 2048 + chip * 256, 256)].astype(F32) * gain_column2).astype(BF)
    spread.pump(1)
    for t in range(2, CHIPS):
        gather.pump(t)
        spread.pump(t)
    moves.start(0)
    moves.wait(14, 15)
    gather_bg.start()
    share.start()
    across.start()
    quarters2.start()
    spread.finish()
    moves.start(1)

    def kv_copy(i, n):
        ref, send, recv = ((keys, ks, kr), (values, vs, vr))[n]
        part = ref.at[i, pl.ds(pl.multiple_of(p.core * TOK, TOK), TOK)]
        return remote(part, part, send.at[i], recv.at[i], p.sib)

    def kv_in(i, n):
        ref, send, recv = ((keys, ks, kr), (values, vs, vr))[n]
        part = ref.at[i, pl.ds(pl.multiple_of((1 - p.core) * TOK, TOK), TOK)]
        return remote(part, part, send.at[i], recv.at[i], p.sib)

    def project(i):
        h = tg[i].astype(F32)
        lin = dot((h * norm_column(h)).astype(BF), whole(wqkv))
        cosine, sine = tables(rope_rows, rope_starts, i)
        q[i, pl.ds(0, TOK)] = rope(lin[:, 0:128], cosine, sine).astype(BF)
        q[i, pl.ds(TOK, TOK)] = rope(lin[:, 128:256], cosine, sine).astype(BF)
        own = pl.ds(pl.multiple_of(p.core * TOK, TOK), TOK)
        keys[i, own] = rope(lin[:, 256:384], cosine, sine).astype(BF)
        values[i, own] = lin[:, 384:512].astype(BF)
        kv_copy(i, 0).start()
        kv_copy(i, 1).start()

    def attend(i):
        query = q[i]
        limit = limit_of(p, i, length)

        def chunk(j, state):
            top, total, acc = state
            s = scores_of(keys, query, limit, j)
            new_top = jnp.maximum(top, jnp.max(s, axis=0, keepdims=True))
            fade = jnp.exp2(top - new_top)
            w = jnp.exp2(s - new_top)
            total = total * fade + jnp.sum(w, axis=0, keepdims=True)
            acc = acc * fade + dot(vt[j], w.astype(BF))
            return new_top, total, acc

        start = (jnp.full((1, 256), neg_big, F32), jnp.zeros((1, 256), F32),
                 jnp.zeros((PAD, 256), F32))
        top, total, acc = lax.fori_loop(0, i + 1, chunk, start)
        acc = acc / total
        mix_t[i] = acc
        stat[i] = top + jnp.log2(total)
        low = acc.astype(BF)
        for n in range(4):
            mix[pl.ds(n * 48, 48), pl.ds(i * TOK, TOK)] = low[(n % 2) * 64:(n % 2) * 64 + 48,
                                                              (n // 2) * TOK:(n // 2) * TOK + TOK]

    for i in range(CHIPS):
        project(i)
        gather_bg.pump_some(i, i + 1)
    share.pump(1)
    for i in range(CHIPS):
        for n in range(2):
            kv_in(i, n).wait_recv()
        vt[i] = values[i].astype(F32).T.astype(BF)
    moves.start(2, 3, 4)
    done = CHIPS
    for i in range(CHIPS):
        attend(i)
        gather_bg.pump_some(done, done + (2 if i < 4 else 3))
        done += 2 if i < 4 else 3
        if 1 <= i < CHIPS - 1:
            share.pump(i + 1)
    moves.start(5, 6)
    mx[p.chip] = mix[...]
    gather_mix.start()
    across.land()
    quarters.start()
    share.finish()
    quarters2.pass_on()
    def head_of(chip):
        return chip // 2 + LINE * (chip % 2)

    def out_rows(chip):
        return whole(wall.at[pl.ds(4 * head_of(chip), 4)])

    def mixed(chip, b):
        lanes = pl.ds(pl.multiple_of(b * TOK, TOK), TOK)
        return dot_tn(mx[chip, :, lanes], out_rows(chip))

    def first(b, carry):
        hid[b] = tg[b].astype(F32) + mixed(p.chip, b)
        return carry

    lax.fori_loop(0, CHIPS, first, 0)
    for t in range(1, CHIPS - 1):
        gather_mix.pump(t)

        def more(b, carry):
            hid[b] += mixed(p.behind(t), b)
            return carry

        lax.fori_loop(0, CHIPS, more, 0)
        if t == 5:
            quarters.pass_on()

    def feed(b):
        h = hid[b] + mixed(p.behind(CHIPS - 1), b)
        hid[b] = h
        r = norm_column(h)
        scale[...] = jnp.broadcast_to(r, (TOK, 128))
        x2[b] = (h * r).astype(BF)
        lin = dot(x2[b], wgu[...].reshape(1536, 1024))
        gate, up = lin[:, :512], lin[:, 512:]
        sigma = jax.nn.sigmoid(gate)
        act = gate * sigma
        inner[b] = (act * up).astype(BF)
        back = dot_nt(bgg[b], wdown[...].reshape(512, 1536))
        gub[b, :, pl.ds(0, 512)] = (back * up * (sigma + act * (1.0 - sigma))).astype(BF)
        gub[b, :, pl.ds(512, 512)] = (back * act).astype(BF)
        part[...] = dot_nt(gub[b], wgu[...].reshape(1536, 1024))

    gather_mix.pump(CHIPS - 1)
    quarters.arrive()
    quarters2.arrive()
    moves.start(13)
    for t in range(CHIPS):
        feed(scatter2.dest(t))
        if t < CHIPS - 1:
            scatter2.push(t, lambda k: part[rows_of(k)])
    moves.start(7)
    for k in range(CHUNKS):
        rows = rows_of(k)
        a = part[rows] + scatter2.last(k)
        h = hid[p.chip, rows]
        r = scale[rows, pl.ds(0, 1)]
        value = (bgg[p.chip, rows].astype(F32) + r * a
                 - h * (r * r * r) * jnp.mean(a * h, axis=-1, keepdims=True))
        grad[rows] = value
        low[rows] = value.astype(BF)

    def weight_part(n):
        if n < 12:
            cols = pl.ds(n * 128, 128)
            dgu[cols] = dot_tn(whole(x2.at[:, :, cols]), whole(gub)).astype(BF)
        else:
            cols = pl.ds((n - 12) * 128, 128)
            dwd[cols] = dot_tn(whole(inner.at[:, :, cols]), whole(bgg)).astype(BF)

    def away(i):
        return remote(rows_away.at[i], grad_rows.at[p.chip], away_s.at[i], away_r.at[i], p.off(i))

    def from_away(i):
        return remote(rows_away.at[i], grad_rows.at[p.src(i)], away_s.at[i], away_r.at[i], p.off(i))

    moves.start(8, 9)
    space2 = spacing(2)
    for i in tuple(range(1, CHIPS)) + (0,):
        rows = dot_nt(low[...], out_rows((p.chip + i) % CHIPS)).astype(BF)
        wide = dot(rows, space2).astype(BF)
        rows_away[i, pl.ds(0, TOK)] = wide[:, :PAD]
        rows_away[i, pl.ds(TOK, TOK)] = wide[:, PAD:]
        if i > 0:
            away(i).start()
    grad_rows[p.chip] = rows_away[0]
    lanes = pl.ds(pl.multiple_of(p.chip * TOK, TOK), TOK)
    for chip in range(CHIPS):
        value = dot(mx[chip, :, lanes], low[...]).astype(BF)
        for n in range(4):
            wall[4 * head_of(chip) + n] = value[48 * n:48 * n + 48]
    moves.start(16)
    for n in range(12):
        weight_part(n)
    moves.start(10)
    for n in range(12, 16):
        weight_part(n)
    moves.start(11)
    for i in range(1, CHIPS):
        from_away(i).wait_recv()
    moves.start(12)
    for i in range(1, CHIPS):
        away(i).wait_send()
    moves.wait(16)
    moves.wait(*range(14))
    for one in (gather, gather_bg, gather_mix, scatter2, quarters, quarters2):
        one.finish()
    across.sent()
    for i in range(CHIPS):
        for n in range(2):
            kv_copy(i, n).wait_send()


def main(*ins):
    dma = pltpu.SemaphoreType.DMA
    block = ((CHIPS, TOK, 1536), BF)
    heads = ((CHIPS, 2 * TOK, PAD), BF)
    shapes = (block, ((32, 48, 512), BF), heads, heads, heads, ((CHIPS, PAD, 256), F32), ((CHIPS, 1, 256), F32))
    shapes2 = (((TOK, 1536), F32), ((CHIPS, TOK, 512), BF), ((1536, 1024), BF), ((512, 1536), BF), heads)
    outs = shapes + (((TOK, 1536), F32),) + shapes2 + (((2, 2, TOK, 1536), BF), ((32, 48, 1536), BF))
    near = shapes + shapes2 + (
        ((2, TOK, PAD), F32), ((2, CHIPS, PAD), F32),
        ((CHIPS, 48, 512), BF), ((CHIPS, 48, 1024), BF), ((192, 1024), BF), ((CHIPS, PAD, 256), BF), block,
        ((32, 48, 1536), BF), ((2, CHIPS, 2, 48, 1024), BF), ((2, 2, TOK, 1536), BF), ((CHIPS, 192, 1024), BF),
        ((CHIPS, TOK, 1536), F32), block, ((CHIPS, TOK, 1024), BF), ((TOK, 1536), BF), heads, ((TOK, 1536), F32),
        ((TOK, 128), F32))
    return call(
        main_kernel,
        tuple(sds(*shape, dtype=kind) for shape, kind in outs),
        ins,
        [VMEM(shape, kind) for shape, kind in near] + RingScatter.bufs
        + RingGather.sems + Spread.sems + RingGather.sems + Across.sems + Share.sems + RingGather.sems + RingScatter.sems
        + [dma((CHIPS,))] * 6 + Quarters.sems * 2 + [dma, dma, dma((17,))],
        1, far_ins=(10, 11), far_outs=range(15), scalar_ins=(0,), flops=20 * 10**9, nbytes=40 << 20,
    )


def tail_kernel(q_in, keys_in, values_in, rows_in, mix_t_in, stat_in, inner_in, wdown_in, hidden_in, dgu_far, dwd_far,
                xg_in, wqkv_in, grad_in, lengths, dwo_far, tokens,
                result, input_back, got_gu, got_qkv, dout_sum, dwd_sum,
                rope_rows, rope_starts, q, keys, values, grad_rows, mix_t, stat, inner, wdown, hidden, dgu, dwd, xg, wqkv, grad,
                kt, dk, dv, dkv_low, dkv_in, back_out, dqkv, part, out, held, out2, held2,
                gu1, gu2, gu3, gu4, qk1, qk2, qk3, qk4, d_in, d_pair, d_y, wo1, wo2, wo3, wo4, wo5, wo6,
                rs_s, rs_r, rs2_s, rs2_r, a1, a2, a3, a4, a5, a6, c1, c2, c3, c4, c5, c6,
                ds, dr, xs, xr, o1, o2, o3, o4, o5, o6, move_s):
    p = Place()
    moves = Moves(move_s, (inner_in, inner), (wdown_in, wdown), (q_in, q), (keys_in, keys), (values_in, values),
                  (rows_in, grad_rows), (mix_t_in, mix_t), (stat_in, stat), (dgu_far.at[:, :, p.core], dgu),
                  (dwd_far.at[:, p.core], dwd), (hidden_in, hidden), (xg_in, xg), (wqkv_in, wqkv), (grad_in, grad),
                  (dwo_far.at[:, :, p.core], wo1))
    moves.start()
    length = lengths[0].astype(F32)
    greet(all_to_all_devices(p) + [p.sib, p.ynb])
    scatter = RingScatter(p, out, held, rs_s, rs_r)
    scatter2 = RingScatter(p, out2, held2, rs2_s, rs2_r)
    collect = Collect(p, dgu_far, lambda g, chip: dgu[g, chip], got_gu, (gu1, gu2, gu3, gu4), (a1, a2, a3, a4, a5, a6))
    collect2 = Collect(p, dqkv, lambda g, chip: dqkv[g, chip, p.core], got_qkv, (qk1, qk2, qk3, qk4),
                       (c1, c2, c3, c4, c5, c6))
    collect.start()
    fold = remote(dwd_far.at[:, 1 - p.core], d_in, ds.at[0], dr.at[0], p.sib)
    fold.start()
    y_fold = remote(d_pair.at[1 - p.g], d_y, ds.at[1], dr.at[1], p.ynb)
    reduce = Reduce(p, dwo_far, (wo1, wo2, wo3, wo4, wo5, wo6), (o1, o2, o3, o4, o5, o6))
    reduce.start()

    def branch(t):
        part[...] = dot(inner[scatter.dest(t)], wdown[...])
        if t < CHIPS - 1:
            scatter.push(t, lambda k: part[rows_of(k)])

    make_tables(p, rope_rows, rope_starts)
    moves.wait(0, 1)
    branch(0)
    moves.wait(*range(2, 10))

    def turn(n, carry):
        kt[n] = keys[n].astype(F32).T.astype(BF)
        dk[n] = jnp.zeros((256, PAD), F32)
        dv[n] = jnp.zeros((256, PAD), F32)
        return carry

    lax.fori_loop(0, CHIPS, turn, 0)

    def attend(i):
        query = q[i]
        limit = limit_of(p, i, length)
        do = grad_rows[i]
        lse = stat[i]
        delta = jnp.sum(do.astype(F32).T * mix_t[i], axis=0, keepdims=True)

        def chunk(j, acc):
            w = jnp.exp2(scores_of(keys, query, limit, j) - lse)
            dp = dot_nt(values[j], do)
            ds_low = (w * (dp - delta)).astype(BF)
            dk[j] += dot(ds_low, query)
            dv[j] += dot(w.astype(BF), do)
            return acc + dot(kt[j], ds_low)

        acc = lax.fori_loop(0, i + 1, chunk, jnp.zeros((PAD, 256), F32))
        dq = acc.T * SCALE
        cosine, sine = tables(rope_rows, rope_starts, i)
        sine = -sine
        back_out[i, :, pl.ds(0, PAD)] = rope(dq[:TOK], cosine, sine).astype(BF)
        back_out[i, :, pl.ds(PAD, PAD)] = rope(dq[TOK:], cosine, sine).astype(BF)

    def fold_pairs():
        fold.wait_recv()
        for n in range(2):
            d_pair[n] = (dwd[n].astype(F32) + d_in[n].astype(F32)).astype(BF)
        y_fold.start()

    for m in range(3):
        collect.pair_up(m)

    def again(b):
        h = xg[b].astype(F32)
        xg[b] = (h * norm_column(h)).astype(BF)

    moves.wait(11)
    for i in range(CHIPS):
        attend(i)
        again(i)
        if i < 5:
            collect.pair_up(i + 3)
        if 0 < i < CHIPS - 1:
            branch(i)
            collect.send(i - 1)
        if i == 4:
            fold_pairs()
            moves.wait(14)
        if i >= 4:
            reduce.pair_up(p.behind(2 * i - 7))
            reduce.pair_up(p.behind(2 * i - 6))
    collect.send(6)
    collect.send(7)
    for n in range(CHIPS):
        for c in range(2):
            rows = pl.ds(c * TOK, TOK)
            dkv_low[0, n, c] = dk[n, rows].astype(BF)
            dkv_low[1, n, c] = dv[n, rows].astype(BF)
    swap = remote(dkv_low.at[:, :, 1 - p.core], dkv_in, xs, xr, p.sib)
    swap.start()
    branch(CHIPS - 1)
    moves.wait(10, 12, 13)
    for k in range(CHUNKS):
        rows = rows_of(k)
        result[rows] = (valid_of(p, k * ROWS, ROWS, length)
                        * (hidden[rows] + part[rows] + scatter.last(k))).astype(BF)
    swap.wait_recv()

    def keys_back(n, carry):
        own = pl.ds(pl.multiple_of(p.core * TOK, TOK), TOK)
        cosine, sine = tables(rope_rows, rope_starts, n)
        back_out[n, :, pl.ds(2 * PAD, PAD)] = rope(
            (dk[n, own] + dkv_in[0, n].astype(F32)) * SCALE, cosine, -sine).astype(BF)
        back_out[n, :, pl.ds(3 * PAD, PAD)] = (dv[n, own] + dkv_in[1, n].astype(F32)).astype(BF)
        return carry

    lax.fori_loop(0, CHIPS, keys_back, 0)

    def weight_part(n):
        value = dot_tn(whole(xg.at[:, :, pl.ds(n * 384, 384)]), whole(back_out)).astype(BF)
        dqkv[n // 2, pl.ds((n % 2) * 4, 4)] = value.reshape(4, 2, 48, 512)

    for t in range(CHIPS):
        part[...] = dot_nt(back_out[scatter2.dest(t)], whole(wqkv))
        if t < CHIPS - 1:
            scatter2.push(t, lambda k: part[rows_of(k)])
        if t == 0:
            for n in range(4):
                weight_part(n)
            collect2.start()
        if 1 <= t <= 4:
            collect2.pair_up(2 * t - 2)
            collect2.pair_up(2 * t - 1)
        if 2 <= t <= 5:
            collect2.send(2 * t - 4)
            collect2.send(2 * t - 3)
        if t == 5:
            y_fold.wait_recv()
            dwd_sum[...] = (d_pair[p.g].astype(F32) + d_y[...].astype(F32)).astype(BF)
        if t == 6:
            collect.receive()
        if t < CHIPS - 1:
            reduce.push(t)
    dout_sum[...] = reduce.term(CHIPS - 1).astype(BF)
    for k in range(CHUNKS):
        rows = rows_of(k)
        c = part[rows] + scatter2.last(k)
        h = tokens[rows].astype(F32)
        r = norm_column(h)
        input_back[rows] = (grad[rows] + r * c
                            - h * (r * r * r) * jnp.mean(c * h, axis=-1, keepdims=True)).astype(BF)
    collect2.receive()
    collect.finish()
    collect2.finish()
    scatter.finish()
    scatter2.finish()
    reduce.finish()
    for copy in (fold, y_fold, swap):
        copy.wait_send()


def tail(*ins):
    dma = pltpu.SemaphoreType.DMA
    heads = (CHIPS, 2 * TOK, PAD)
    near = [VMEM((2, TOK, PAD), F32), VMEM((2, CHIPS, PAD), F32)] + [VMEM(heads, BF)] * 4 + [
        VMEM((CHIPS, PAD, 256), F32), VMEM((CHIPS, 1, 256), F32), VMEM((CHIPS, TOK, 512), BF), VMEM((512, 1536), BF),
        VMEM((TOK, 1536), F32), VMEM((2, CHIPS, 48, 1024), BF), VMEM((2, TOK, 1536), BF), VMEM((CHIPS, TOK, 1536), BF),
        VMEM((32, 48, 512), BF), VMEM((TOK, 1536), F32)]
    return call(
        tail_kernel,
        (sds(TOK, 1536), sds(TOK, 1536), sds(CHIPS, 48, 1024), sds(CHIPS, 48, 512), sds(48, 1536), sds(TOK, 1536)),
        ins,
        near + [VMEM((CHIPS, PAD, 256), BF), VMEM((CHIPS, 256, PAD), F32), VMEM((CHIPS, 256, PAD), F32),
         VMEM((2, CHIPS, 2, TOK, PAD), BF), VMEM((2, CHIPS, TOK, PAD), BF), VMEM((CHIPS, TOK, 4 * PAD), BF),
         VMEM((2, CHIPS, 2, 48, 512), BF), VMEM((TOK, 1536), F32)]
        + RingScatter.bufs * 2 + Collect.bufs(48, 1024) + Collect.bufs(48, 512)
        + [VMEM((2, TOK, 1536), BF), VMEM((2, TOK, 1536), BF), VMEM((TOK, 1536), BF)]
        + Reduce.bufs(48, 1536)
        + RingScatter.sems * 2 + Collect.sems * 2 + [dma((2,)), dma((2,)), dma, dma] + Reduce.sems + [dma((15,))],
        5, far_ins=tuple(range(14)) + (15,), scalar_ins=(14,), flops=10 * 10**9, nbytes=20 << 20,
    )


def place_kernel(got_gu_in, got_qkv_in, dout_in, dwd_in, block_in, back_in, wq_in, wk_in, wv_in, wg_in, wu_in, gain_one, gain_two,
                 block_out, back_out, d_gain_one, d_q_out, d_k_out, d_v_out, d_out_out, d_gain_two, d_gate_out, d_up_out,
                 d_down_out,
                 got_gu, got_qkv, dout, dwd, wq, wk, wv, wg, wu, d_q, d_k, d_v, d_out, d_gate, d_up, d_down, block, back, move_s):
    moves = Moves(move_s, (wg_in, wg), (wu_in, wu), (got_gu_in, got_gu), (dwd_in, dwd), (dout_in, dout),
                  (got_qkv_in, got_qkv), (wq_in, wq), (wk_in, wk), (wv_in, wv), (block_in, block), (back_in, back),
                  (d_gate, d_gate_out), (d_up, d_up_out), (d_down, d_down_out), (d_out, d_out_out), (d_q, d_q_out),
                  (d_k, d_k_out), (d_v, d_v_out), (block, block_out), (back, back_out))
    moves.start(*range(11))
    space = spacing()
    gain_column = to_column(gain_one[...].astype(F32))
    gain_column2 = to_column(gain_two[...].astype(F32))
    lanes = lambda v: jnp.sum(v, axis=-1, keepdims=True)
    moves.wait(0, 1, 2)
    total = jnp.zeros((48, 256), F32)
    for n, (target, weight) in enumerate(((d_gate, wg), (d_up, wu))):
        for chip in range(CHIPS):
            for g in range(2):
                cols = pl.ds(g * 2048 + chip * 256, 256)
                piece = got_gu[chip, :, pl.ds(n * 512 + g * 256, 256)].astype(F32)
                target[:, cols] = piece * gain_column2
                total = total + piece * weight[:, cols].astype(F32)
        moves.start(11 + n)
    d_gain_two[...] = to_row(lanes(total))
    moves.wait(3, 4)
    d_down[...] = dwd[...].astype(F32)
    moves.start(13)
    d_out[...] = dout[...].astype(F32)
    moves.start(14)
    moves.wait(9, 10)
    moves.start(18, 19)
    moves.wait(5, 6, 7, 8)
    total = jnp.zeros((48, 1), F32)
    for n in range(4):
        cols = pl.ds(n * 384, 384)
        wide = jnp.concatenate([got_qkv[chip_of_head(2 * n + m), :, pl.ds(0, 256)] for m in range(2)], axis=-1)
        value = dot_nt(wide, space)
        total = total + lanes(value * wq[:, cols].astype(F32))
        d_q[:, cols] = value * gain_column
    moves.start(15)
    for n in range(2):
        cols = pl.ds(n * 384, 384)
        for source, target, place in ((wk, d_k, 256), (wv, d_v, 384)):
            wide = jnp.concatenate([got_qkv[chip_of_head(4 * n + m), :, pl.ds(place, 128)] for m in range(4)], axis=-1)
            value = dot_nt(wide, space)
            total = total + lanes(value * source[:, cols].astype(F32))
            target[:, cols] = value * gain_column
    moves.start(16, 17)
    d_gain_one[...] = to_row(total)
    moves.wait(*range(11, 20))


def place_all(*ins):
    f = lambda *shape: sds(*shape, dtype=F32)
    near = (((CHIPS, 48, 1024), BF), ((CHIPS, 48, 512), BF), ((48, 1536), BF), ((TOK, 1536), BF), ((48, 1536), BF),
            ((48, 768), BF), ((48, 768), BF), ((48, 4096), BF), ((48, 4096), BF), ((48, 1536), F32), ((48, 768), F32),
            ((48, 768), F32), ((48, 1536), F32), ((48, 4096), F32), ((48, 4096), F32), ((TOK, 1536), F32), ((TOK, 1536), BF), ((TOK, 1536), BF))
    return call(
        place_kernel,
        (sds(TOK, 1536), sds(TOK, 1536), f(1, 48), f(48, 1536), f(48, 768), f(48, 768), f(48, 1536), f(1, 48), f(48, 4096),
         f(48, 4096), f(TOK, 1536)),
        ins, [VMEM(shape, kind) for shape, kind in near] + [pltpu.SemaphoreType.DMA((20,))], None,
        far_ins=range(11), far_outs=(0, 1, 3, 4, 5, 6, 8, 9, 10), nbytes=10 << 20,
    )


def plane_device(hidden_in, lengths, attn_gain, w_query, w_key, w_value, w_out, mlp_gain, w_gate, w_up,
                 w_down, out_grad):
    gain_one = attn_gain[None]
    gain_two = mlp_gain[None]
    tokens = hidden_in[0]
    tg, wqkv, q, keys, values, mix_t, stat, hidden, grad, inner, dgu, dwd, grad_rows, wdown, dwo = main(
        lengths, tokens, w_query, w_key, w_value, gain_one, out_grad[0],
        w_gate, w_up, gain_two, w_out, w_down)
    block, back, got_gu, got_qkv, dout_sum, dwd_sum = tail(
        q, keys, values, grad_rows, mix_t, stat, inner, wdown.reshape(512, 1536), hidden,
        dgu.reshape(2, CHIPS, 2, 48, 1024), dwd.reshape(2, 2, TOK, 1536), tg, wqkv, grad,
        lengths, dwo.reshape(2, CHIPS, 2, 48, 1536), tokens)
    block, back, d_gain_one, d_q, d_k, d_v, d_out, d_gain_two, d_gate, d_up, d_down = place_all(
        got_gu, got_qkv, dout_sum, dwd_sum, block, back, w_query, w_key, w_value, w_gate, w_up, gain_one, gain_two)
    return (block[None], back[None], d_gain_one[0], d_q, d_k, d_v, d_out, d_gain_two[0], d_gate, d_up, d_down)


def solution(mesh):
    placed = (
        P("grp", "seq", None),
        P("grp"),
        P(("grp", "seq")),
        P(("grp", "seq"), None),
        P(("grp", "seq"), None),
        P(("grp", "seq"), None),
        P(("grp", "seq"), None),
        P(("grp", "seq")),
        P(("grp", "seq"), None),
        P(("grp", "seq"), None),
        P(("grp", "seq"), None),
        P("grp", "seq", None),
    )
    small = mesh.shape["grp"] == 2 and mesh.shape["seq"] == 2 * CHIPS
    return jax.shard_map(
        plane_device if small else per_device,
        mesh=mesh,
        in_specs=placed,
        out_specs=(
            P("grp", "seq", None),
            P("grp", "seq", None),
            P(("grp", "seq")),
            P(("grp", "seq"), None),
            P(("grp", "seq"), None),
            P(("grp", "seq"), None),
            P(("grp", "seq"), None),
            P(("grp", "seq")),
            P(("grp", "seq"), None),
            P(("grp", "seq"), None),
            P(("grp", "seq"), None),
        ),
        check_vma=False,
    )
```

```python
import math

import jax
import jax.numpy as jnp
from jax import lax
from jax.experimental import pallas as pl
from jax.experimental.pallas import tpu as pltpu
from jax.sharding import PartitionSpec as P

H = 16
KVH = 8
HD = 96
KBLK = 256


epsilon = 1e-05
rope_base = 100000.0
neg_big = -1e30


def rope_tables(positions):
    half_dim = HD // 2
    frequency = jnp.exp(-math.log(rope_base) * (2.0 * jnp.arange(half_dim, dtype=jnp.float32) / HD))
    angles = positions.astype(jnp.float32)[:, None] * frequency[None, :]
    return (jnp.cos(angles), jnp.sin(angles))


def rotate(values, cosine, sine_tab):
    half_dim = values.shape[-1] // 2
    first_half = values[..., :half_dim]
    second_half = values[..., half_dim:]
    cos_wide = cosine[:, None, :]
    sin_wide = sine_tab[:, None, :]
    return jnp.concatenate(
        [
            first_half * cos_wide - second_half * sin_wide,
            second_half * cos_wide + first_half * sin_wide,
        ],
        axis=-1,
    )


def unrotate(values, cosine, sine_tab):
    half_dim = values.shape[-1] // 2
    first_half = values[..., :half_dim]
    second_half = values[..., half_dim:]
    cos_wide = cosine[:, None, :]
    sin_wide = sine_tab[:, None, :]
    return jnp.concatenate(
        [
            first_half * cos_wide + second_half * sin_wide,
            second_half * cos_wide - first_half * sin_wide,
        ],
        axis=-1,
    )


def norm_scale(values):
    return lax.rsqrt(jnp.mean(values * values, axis=-1, keepdims=True) + epsilon)


def block_scores(queries, key_block, offset, positions, length):
    score_scale = 1.0 / math.sqrt(HD)
    raw_scores = (
        jnp.einsum("tkgd,skd->kgts", queries, key_block, preferred_element_type=jnp.float32)
        * score_scale
    )
    key_pos = offset + jnp.arange(key_block.shape[0], dtype=jnp.int32)
    allowed = (key_pos[None, :] <= positions[:, None]) & (key_pos[None, :] < length)
    return jnp.where(allowed[None, None], raw_scores, neg_big)


def block_needed(offset, positions, length):
    return (offset <= positions[-1]) & (offset < length)


def attend_forward(queries, key_blocks, value_blocks, positions, length):
    tok_count = queries.shape[0]
    group_size = queries.shape[2]
    offsets = jnp.arange(key_blocks.shape[0], dtype=jnp.int32) * KBLK

    def stat_step(carried, element):
        key_block, offset = element

        def stat_update(state):
            running_max, running_total = state
            scores = block_scores(queries, key_block, offset, positions, length)
            new_max = jnp.maximum(running_max, jnp.max(scores, axis=-1))
            new_total = running_total * jnp.exp(running_max - new_max) + jnp.sum(
                jnp.exp(scores - new_max[..., None]), axis=-1
            )
            return (new_max, new_total)

        return (
            lax.cond(
                block_needed(offset, positions, length), stat_update, lambda state: state, carried
            ),
            None,
        )

    start_max = jnp.full((KVH, group_size, tok_count), neg_big, jnp.float32)
    start_total = jnp.zeros((KVH, group_size, tok_count), jnp.float32)
    (row_max, row_total), unused = lax.scan(
        stat_step, (start_max, start_total), (key_blocks, offsets)
    )
    log_total = row_max + jnp.log(row_total)

    def value_step(carried, element):
        key_block, value_block, offset = element

        def value_update(state):
            accumulated, exact_sum = state
            scores = block_scores(queries, key_block, offset, positions, length)
            probs = jnp.exp(scores - log_total[..., None])
            weights = probs.astype(jnp.bfloat16)
            accumulated = accumulated + jnp.einsum(
                "kgts,skd->tkgd", weights, value_block, preferred_element_type=jnp.float32
            )
            exact_sum = exact_sum + jnp.einsum(
                "kgts,skd->tkgd",
                probs,
                value_block.astype(jnp.float32),
                preferred_element_type=jnp.float32,
            )
            return (accumulated, exact_sum)

        return (
            lax.cond(
                block_needed(offset, positions, length), value_update, lambda state: state, carried
            ),
            None,
        )

    start_acc = jnp.zeros((tok_count, KVH, group_size, HD), jnp.float32)
    (attended, exact_out), unused = lax.scan(
        value_step, (start_acc, start_acc), (key_blocks, value_blocks, offsets)
    )
    return (attended, exact_out, log_total)


def attend_backward(
    queries, key_blocks, value_blocks, attn_back, exact_out, log_total, positions, length
):
    tok_count = queries.shape[0]
    group_size = queries.shape[2]
    block_keys = key_blocks.shape[1]
    score_scale = 1.0 / math.sqrt(HD)
    offsets = jnp.arange(key_blocks.shape[0], dtype=jnp.int32) * KBLK
    delta = jnp.einsum("tkgd,tkgd->kgt", attn_back.astype(jnp.float32), exact_out)

    def grad_step(query_acc, element):
        key_block, value_block, offset = element

        def compute(acc):
            scores = block_scores(queries, key_block, offset, positions, length)
            probs = jnp.exp(scores - log_total[..., None])
            weights = probs.astype(jnp.bfloat16)
            dprobs = jnp.einsum(
                "tkgd,skd->kgts", attn_back, value_block, preferred_element_type=jnp.float32
            )
            score_back = (probs * (dprobs - delta[..., None])).astype(jnp.bfloat16)
            acc = acc + score_scale * jnp.einsum(
                "kgts,skd->tkgd", score_back, key_block, preferred_element_type=jnp.float32
            )
            key_part = score_scale * jnp.einsum(
                "kgts,tkgd->skd", score_back, queries, preferred_element_type=jnp.float32
            )
            value_part = jnp.einsum(
                "kgts,tkgd->skd", weights, attn_back, preferred_element_type=jnp.float32
            )
            return (acc, key_part, value_part)

        def skip(acc):
            empty = jnp.zeros((block_keys, KVH, HD), jnp.float32)
            return (acc, empty, empty)

        acc, key_part, value_part = lax.cond(
            block_needed(offset, positions, length), compute, skip, query_acc
        )
        return (acc, (key_part, value_part))

    start_query = jnp.zeros((tok_count, KVH, group_size, HD), jnp.float32)
    query_grad, (key_parts, value_parts) = lax.scan(
        grad_step, start_query, (key_blocks, value_blocks, offsets)
    )
    return (query_grad, key_parts.reshape(-1, KVH * HD), value_parts.reshape(-1, KVH * HD))


def split_rows(values, groups_count, seq_count):
    return values.reshape(
        (groups_count, seq_count, values.shape[0] // (groups_count * seq_count)) + values.shape[1:]
    )


def per_device(
    hidden_in,
    lengths,
    attn_gain,
    w_query,
    w_key,
    w_value,
    w_out,
    mlp_gain,
    w_gate,
    w_up,
    w_down,
    out_grad,
):
    tok_count = hidden_in.shape[1]
    group_size = H // KVH
    groups_count = lax.axis_size("grp")
    seq_count = lax.axis_size("seq")
    positions = lax.axis_index("seq") * tok_count + jnp.arange(tok_count, dtype=jnp.int32)
    length = lengths[0]
    valid_rows = (positions < length).astype(jnp.float32)[:, None]
    cosine, sine_tab = rope_tables(positions)
    front_weights = (
        lax.all_gather(attn_gain, ("grp", "seq"), axis=0, tiled=True),
        lax.all_gather(w_query, ("grp", "seq"), axis=0, tiled=True),
        lax.all_gather(w_key, ("grp", "seq"), axis=0, tiled=True),
        lax.all_gather(w_value, ("grp", "seq"), axis=0, tiled=True),
        lax.all_gather(w_out, ("grp", "seq"), axis=0, tiled=True),
        lax.all_gather(mlp_gain, ("grp", "seq"), axis=0, tiled=True),
        lax.all_gather(w_gate, ("grp", "seq"), axis=0, tiled=True),
        lax.all_gather(w_up, ("grp", "seq"), axis=0, tiled=True),
        lax.all_gather(w_down, ("grp", "seq"), axis=0, tiled=True),
    )
    gain_one, query_w, key_w, value_w, out_w, gain_two, gate_w, up_w, down_w = front_weights
    tokens_in = hidden_in[0].astype(jnp.float32)
    scale_one = norm_scale(tokens_in)
    normed = (tokens_in * scale_one * gain_one.astype(jnp.float32)).astype(jnp.bfloat16)
    query_lin = jnp.dot(normed, query_w, preferred_element_type=jnp.float32)
    key_lin = jnp.dot(normed, key_w, preferred_element_type=jnp.float32)
    value_lin = jnp.dot(normed, value_w, preferred_element_type=jnp.float32)
    queries = (
        rotate(query_lin.reshape(tok_count, H, HD), cosine, sine_tab)
        .astype(jnp.bfloat16)
        .reshape(tok_count, KVH, group_size, HD)
    )
    key_rot = (
        rotate(key_lin.reshape(tok_count, KVH, HD), cosine, sine_tab)
        .astype(jnp.bfloat16)
        .reshape(tok_count, KVH * HD)
    )
    value_low = value_lin.astype(jnp.bfloat16)
    keys_all, values_all = (
        lax.all_gather(key_rot, "seq", axis=0, tiled=True),
        lax.all_gather(value_low, "seq", axis=0, tiled=True),
    )
    key_blocks = keys_all.reshape(-1, KBLK, KVH, HD)
    value_blocks = values_all.reshape(-1, KBLK, KVH, HD)
    attended, exact_out, log_total = attend_forward(
        queries, key_blocks, value_blocks, positions, length
    )
    attn_mix = attended.reshape(tok_count, H * HD).astype(jnp.bfloat16)
    hidden = tokens_in + jnp.dot(attn_mix, out_w, preferred_element_type=jnp.float32)
    scale_two = norm_scale(hidden)
    normed_mlp = (hidden * scale_two * gain_two.astype(jnp.float32)).astype(jnp.bfloat16)
    gate_lin = jnp.dot(normed_mlp, gate_w, preferred_element_type=jnp.float32)
    up_lin = jnp.dot(normed_mlp, up_w, preferred_element_type=jnp.float32)
    silu_act = jax.nn.silu(gate_lin)
    inner_act = (silu_act * up_lin).astype(jnp.bfloat16)
    branch = jnp.dot(inner_act, down_w, preferred_element_type=jnp.float32)
    result = (valid_rows * (hidden + branch)).astype(jnp.bfloat16)[None]
    gain_one, query_w, key_w, value_w, out_w, gain_two, gate_w, up_w, down_w = front_weights
    cotangent = out_grad[0].astype(jnp.float32)
    branch_grad = valid_rows * cotangent
    branch_low = branch_grad.astype(jnp.bfloat16)
    down_grad = jnp.einsum("tf,td->fd", inner_act, branch_low, preferred_element_type=jnp.float32)
    inner_grad = jnp.einsum("td,fd->tf", branch_low, down_w, preferred_element_type=jnp.float32)
    sigma = jax.nn.sigmoid(gate_lin)
    gate_back = (inner_grad * up_lin * (sigma + gate_lin * sigma * (1.0 - sigma))).astype(
        jnp.bfloat16
    )
    up_back = (inner_grad * silu_act).astype(jnp.bfloat16)
    gate_grad = jnp.einsum("td,tf->df", normed_mlp, gate_back, preferred_element_type=jnp.float32)
    up_grad = jnp.einsum("td,tf->df", normed_mlp, up_back, preferred_element_type=jnp.float32)
    mlp_norm_grad = jnp.einsum(
        "tf,df->td", gate_back, gate_w, preferred_element_type=jnp.float32
    ) + jnp.einsum("tf,df->td", up_back, up_w, preferred_element_type=jnp.float32)
    gain_two_grad = jnp.sum(mlp_norm_grad * hidden * scale_two, axis=0)
    weighted_two = mlp_norm_grad * gain_two.astype(jnp.float32)
    hidden_grad = (
        branch_grad
        + scale_two * weighted_two
        - hidden
        * (scale_two * scale_two * scale_two)
        * jnp.mean(weighted_two * hidden, axis=-1, keepdims=True)
    )
    mlp_seq = (
        lax.psum_scatter(
            split_rows(gain_two_grad, groups_count, seq_count).astype(jnp.bfloat16),
            "seq",
            scatter_dimension=1,
            tiled=True,
        ).astype(jnp.float32),
        lax.psum_scatter(
            split_rows(gate_grad, groups_count, seq_count).astype(jnp.bfloat16),
            "seq",
            scatter_dimension=1,
            tiled=True,
        ).astype(jnp.float32),
        lax.psum_scatter(
            split_rows(up_grad, groups_count, seq_count).astype(jnp.bfloat16),
            "seq",
            scatter_dimension=1,
            tiled=True,
        ).astype(jnp.float32),
        lax.psum_scatter(
            split_rows(down_grad, groups_count, seq_count).astype(jnp.bfloat16),
            "seq",
            scatter_dimension=1,
            tiled=True,
        ).astype(jnp.float32),
    )
    mlp_grp = (
        lax.psum_scatter(
            mlp_seq[0].astype(jnp.bfloat16), "grp", scatter_dimension=0, tiled=True
        ).astype(jnp.float32),
        lax.psum_scatter(
            mlp_seq[1].astype(jnp.bfloat16), "grp", scatter_dimension=0, tiled=True
        ).astype(jnp.float32),
        lax.psum_scatter(
            mlp_seq[2].astype(jnp.bfloat16), "grp", scatter_dimension=0, tiled=True
        ).astype(jnp.float32),
        lax.psum_scatter(
            mlp_seq[3].astype(jnp.bfloat16), "grp", scatter_dimension=0, tiled=True
        ).astype(jnp.float32),
    )
    mlp_grads = tuple((piece.reshape(piece.shape[2:]) for piece in mlp_grp))
    mix_back = hidden_grad.astype(jnp.bfloat16)
    out_w_grad = jnp.einsum("td,te->de", attn_mix, mix_back, preferred_element_type=jnp.float32)
    attn_back = (
        jnp.einsum("te,de->td", mix_back, out_w, preferred_element_type=jnp.float32)
        .astype(jnp.bfloat16)
        .reshape(tok_count, KVH, group_size, HD)
    )
    query_grad, key_grad_all, value_grad_all = attend_backward(
        queries, key_blocks, value_blocks, attn_back, exact_out, log_total, positions, length
    )
    key_grad, value_grad = (
        lax.psum_scatter(
            key_grad_all.astype(jnp.bfloat16), "seq", scatter_dimension=0, tiled=True
        ).astype(jnp.float32),
        lax.psum_scatter(
            value_grad_all.astype(jnp.bfloat16), "seq", scatter_dimension=0, tiled=True
        ).astype(jnp.float32),
    )
    query_back = (
        unrotate(query_grad.reshape(tok_count, H, HD), cosine, sine_tab)
        .astype(jnp.bfloat16)
        .reshape(tok_count, H * HD)
    )
    key_back = (
        unrotate(key_grad.reshape(tok_count, KVH, HD), cosine, sine_tab)
        .astype(jnp.bfloat16)
        .reshape(tok_count, KVH * HD)
    )
    value_back = value_grad.astype(jnp.bfloat16)
    query_w_grad = jnp.einsum("td,te->de", normed, query_back, preferred_element_type=jnp.float32)
    key_w_grad = jnp.einsum("td,te->de", normed, key_back, preferred_element_type=jnp.float32)
    value_w_grad = jnp.einsum("td,te->de", normed, value_back, preferred_element_type=jnp.float32)
    attn_norm_grad = (
        jnp.einsum("te,de->td", query_back, query_w, preferred_element_type=jnp.float32)
        + jnp.einsum("te,de->td", key_back, key_w, preferred_element_type=jnp.float32)
        + jnp.einsum("te,de->td", value_back, value_w, preferred_element_type=jnp.float32)
    )
    gain_one_grad = jnp.sum(attn_norm_grad * tokens_in * scale_one, axis=0)
    weighted_one = attn_norm_grad * gain_one.astype(jnp.float32)
    input_back = (
        hidden_grad
        + scale_one * weighted_one
        - tokens_in
        * (scale_one * scale_one * scale_one)
        * jnp.mean(weighted_one * tokens_in, axis=-1, keepdims=True)
    )
    attn_seq = (
        lax.psum_scatter(
            split_rows(gain_one_grad, groups_count, seq_count).astype(jnp.bfloat16),
            "seq",
            scatter_dimension=1,
            tiled=True,
        ).astype(jnp.float32),
        lax.psum_scatter(
            split_rows(query_w_grad, groups_count, seq_count).astype(jnp.bfloat16),
            "seq",
            scatter_dimension=1,
            tiled=True,
        ).astype(jnp.float32),
        lax.psum_scatter(
            split_rows(key_w_grad, groups_count, seq_count).astype(jnp.bfloat16),
            "seq",
            scatter_dimension=1,
            tiled=True,
        ).astype(jnp.float32),
        lax.psum_scatter(
            split_rows(value_w_grad, groups_count, seq_count).astype(jnp.bfloat16),
            "seq",
            scatter_dimension=1,
            tiled=True,
        ).astype(jnp.float32),
        lax.psum_scatter(
            split_rows(out_w_grad, groups_count, seq_count).astype(jnp.bfloat16),
            "seq",
            scatter_dimension=1,
            tiled=True,
        ).astype(jnp.float32),
    )
    attn_grp = (
        lax.psum_scatter(
            attn_seq[0].astype(jnp.bfloat16), "grp", scatter_dimension=0, tiled=True
        ).astype(jnp.float32),
        lax.psum_scatter(
            attn_seq[1].astype(jnp.bfloat16), "grp", scatter_dimension=0, tiled=True
        ).astype(jnp.float32),
        lax.psum_scatter(
            attn_seq[2].astype(jnp.bfloat16), "grp", scatter_dimension=0, tiled=True
        ).astype(jnp.float32),
        lax.psum_scatter(
            attn_seq[3].astype(jnp.bfloat16), "grp", scatter_dimension=0, tiled=True
        ).astype(jnp.float32),
        lax.psum_scatter(
            attn_seq[4].astype(jnp.bfloat16), "grp", scatter_dimension=0, tiled=True
        ).astype(jnp.float32),
    )
    attn_grads = tuple((piece.reshape(piece.shape[2:]) for piece in attn_grp))
    return (
        result,
        input_back.astype(jnp.bfloat16)[None],
        attn_grads[0],
        attn_grads[1],
        attn_grads[2],
        attn_grads[3],
        attn_grads[4],
        mlp_grads[0],
        mlp_grads[1],
        mlp_grads[2],
        mlp_grads[3],
    )


MESH_ID = pl.DeviceIdType.MESH
VMEM = pltpu.VMEM
LINE = 4
CHIPS = 8
TOK = 128
PAD = 128
CHUNKS = 4
ROWS = TOK // CHUNKS
BF = jnp.bfloat16
F32 = jnp.float32
VSPEC = pl.BlockSpec(memory_space=pltpu.VMEM)


def ring_of(chip):
    z = chip // 2
    x = chip % 2
    return x * LINE + z + x * (LINE - 1 - 2 * z)


def chip_of(ring):
    x = ring // LINE
    q = ring % LINE
    return (q + x * (LINE - 1 - 2 * q)) * 2 + x


class Place:
    def __init__(self):
        self.g = lax.axis_index("grp")
        self.s = lax.axis_index("seq")
        self.core = self.s % 2
        self.chip = self.s // 2
        self.x = self.chip % 2
        self.ring = ring_of(self.chip)
        self.step = 1 - 2 * self.core
        self.next = {"seq": self.at(self.step) * 2 + self.core}
        self.prev = {"seq": self.at(-self.step) * 2 + self.core}
        self.sib = {"seq": self.s + 1 - 2 * self.core}
        self.ynb = {"grp": 1 - self.g}
        self.xnb = {"seq": self.s + 2 - 4 * self.x}

    def at(self, offset):
        return chip_of((self.ring + offset + 8 * CHIPS) % CHIPS)

    def behind(self, t):
        return self.at(-t * self.step)

    def off(self, i):
        return {"seq": ((self.chip + i + CHIPS) % CHIPS) * 2 + self.core}

    def src(self, i):
        return (self.chip - i + CHIPS) % CHIPS


def greet(devices):
    barrier = pltpu.get_barrier_semaphore()
    for device in devices:
        pl.semaphore_signal(barrier, inc=1, device_id=device, device_id_type=MESH_ID)
    pl.semaphore_wait(barrier, len(devices))


def remote(src, dst, send, recv, device):
    return pltpu.make_async_remote_copy(
        src_ref=src, dst_ref=dst, send_sem=send, recv_sem=recv, device_id=device,
        device_id_type=MESH_ID,
    )


class RingGather:
    sems = [pltpu.SemaphoreType.DMA((CHIPS, CHUNKS)), pltpu.SemaphoreType.DMA((CHIPS, CHUNKS))]

    def __init__(self, place, all_ref, send, recv):
        self.place, self.all, self.send, self.recv = place, all_ref, send, recv
        self.rows = all_ref.shape[1] // CHUNKS

    def copy(self, t, k):
        part = self.all.at[self.place.behind(t), pl.ds(k * self.rows, self.rows)]
        return remote(part, part, self.send.at[t, k], self.recv.at[t, k], self.place.next)

    def start(self, k=None):
        for k in range(CHUNKS) if k is None else (k,):
            self.copy(0, k).start()

    def pump(self, t):
        for k in range(CHUNKS):
            self.pass_on(t, k)

    def pass_on(self, t, k):
        self.copy(t - 1, k).wait_recv()
        if t < CHIPS - 1:
            self.copy(t, k).start()

    def pump_some(self, first, last):
        for n in range(first, last):
            self.pass_on(1 + n // CHUNKS, n % CHUNKS)

    def finish(self):
        for t in range(CHIPS - 1):
            for k in range(CHUNKS):
                self.copy(t, k).wait_send()


class RingScatter:
    sems = [pltpu.SemaphoreType.DMA((CHIPS, CHUNKS)), pltpu.SemaphoreType.DMA((CHIPS, CHUNKS))]
    bufs = [VMEM((CHIPS - 1, TOK, 1536), BF), VMEM((CHIPS - 1, TOK, 1536), BF)]

    def __init__(self, place, out, held, send, recv):
        self.place, self.out, self.held, self.send, self.recv = place, out, held, send, recv

    def copy(self, t, k):
        rows = pl.ds(k * ROWS, ROWS)
        return remote(self.out.at[t, rows], self.held.at[t, rows], self.send.at[t, k],
                      self.recv.at[t, k], self.place.next)

    def dest(self, t):
        return self.place.behind(t + 1)

    def push(self, t, term):
        for k in range(CHUNKS):
            rows = pl.ds(k * ROWS, ROWS)
            value = term(k)
            if t > 0:
                self.copy(t - 1, k).wait_recv()
                value = value + self.held[t - 1, rows].astype(F32)
            self.out[t, rows] = value.astype(BF)
            self.copy(t, k).start()

    def last(self, k):
        self.copy(CHIPS - 2, k).wait_recv()
        return self.held[CHIPS - 2, pl.ds(k * ROWS, ROWS)].astype(F32)

    def finish(self):
        for t in range(CHIPS - 1):
            for k in range(CHUNKS):
                self.copy(t, k).wait_send()


class Spread:
    sems = [pltpu.SemaphoreType.DMA((CHIPS,)), pltpu.SemaphoreType.DMA((CHIPS,)),
            pltpu.SemaphoreType.DMA((CHIPS,)), pltpu.SemaphoreType.DMA((CHIPS,)),
            pltpu.SemaphoreType.DMA((2 * CHIPS,)), pltpu.SemaphoreType.DMA((2 * CHIPS,))]

    def __init__(self, place, slab, all_ref, local, *sems):
        self.place, self.slab, self.all, self.local = place, slab, all_ref, local
        self.s1, self.r1, self.s2, self.r2, self.s3, self.r3 = sems

    def block(self, g, chip):
        return self.all.at[g * 16 + chip * 2 + self.place.core]

    def across(self, i):
        p = self.place
        return remote(self.slab.at[(p.chip + i) % CHIPS], self.block(p.g, p.chip), self.s1.at[i],
                      self.r1.at[i], p.off(i))

    def arrived(self, i):
        p = self.place
        return remote(self.slab.at[0], self.block(p.g, p.src(i)), self.s1.at[i], self.r1.at[i],
                      p.off(i))

    def to_y(self, i):
        p = self.place
        part = self.block(p.g, p.src(i))
        return remote(part, part, self.s2.at[i], self.r2.at[i], p.ynb)

    def from_y(self, i):
        p = self.place
        part = self.block(1 - p.g, p.src(i))
        return remote(part, part, self.s2.at[i], self.r2.at[i], p.ynb)

    def to_sib(self, i, other):
        p = self.place
        part = self.block((1 - p.g) if other else p.g, p.src(i))
        n = i + CHIPS * other
        return remote(part, part, self.s3.at[n], self.r3.at[n], p.sib)

    def from_sib(self, i, other):
        p = self.place
        g = (1 - p.g) if other else p.g
        part = self.all.at[g * 16 + p.src(i) * 2 + 1 - p.core]
        n = i + CHIPS * other
        return remote(part, part, self.s3.at[n], self.r3.at[n], p.sib)

    def start(self):
        p = self.place
        own = pltpu.make_async_copy(self.slab.at[p.chip], self.block(p.g, p.chip), self.local)
        own.start()
        for i in range(1, CHIPS):
            self.across(i).start()
        own.wait()
        self.to_y(0).start()
        self.to_sib(0, 0).start()

    def pump(self, i):
        self.arrived(i).wait_recv()
        self.to_y(i).start()
        self.to_sib(i, 0).start()
        self.from_y(i - 1).wait_recv()
        self.to_sib(i - 1, 1).start()

    def finish(self):
        self.from_y(CHIPS - 1).wait_recv()
        self.to_sib(CHIPS - 1, 1).start()
        for i in range(CHIPS):
            self.from_sib(i, 0).wait_recv()
            self.from_sib(i, 1).wait_recv()
        for i in range(CHIPS):
            if i > 0:
                self.across(i).wait_send()
            self.to_y(i).wait_send()
            self.to_sib(i, 0).wait_send()
            self.to_sib(i, 1).wait_send()


class Across:
    sems = [pltpu.SemaphoreType.DMA((CHIPS,)), pltpu.SemaphoreType.DMA((CHIPS,))]

    def __init__(self, place, slab, got, local, send, recv):
        self.place, self.slab, self.got, self.send, self.recv = place, slab, got, send, recv
        self.own = pltpu.make_async_copy(slab.at[place.chip], got.at[place.chip], local)

    def to(self, i):
        p = self.place
        return remote(self.slab.at[(p.chip + i) % CHIPS], self.got.at[p.chip], self.send.at[i], self.recv.at[i], p.off(i))

    def arrived(self, i):
        p = self.place
        return remote(self.slab.at[0], self.got.at[p.src(i)], self.send.at[i], self.recv.at[i], p.off(i))

    def start(self):
        self.own.start()
        for i in range(1, CHIPS):
            self.to(i).start()

    def land(self):
        self.own.wait()
        for i in range(1, CHIPS):
            self.arrived(i).wait_recv()

    def sent(self):
        for i in range(1, CHIPS):
            self.to(i).wait_send()


class Quarters:
    sems = [pltpu.SemaphoreType.DMA((3,)), pltpu.SemaphoreType.DMA((3,))]

    def __init__(self, place, view, send, recv):
        p = place
        here, over = view(p.g, p.core), view(1 - p.g, p.core)
        self.y = remote(here, here, send.at[0], recv.at[0], p.ynb)
        self.sib = remote(here, here, send.at[1], recv.at[1], p.sib)
        self.sib2 = remote(over, over, send.at[2], recv.at[2], p.sib)

    def start(self):
        self.y.start()
        self.sib.start()

    def pass_on(self):
        self.y.wait_recv()
        self.sib2.start()

    def arrive(self):
        self.sib.wait_recv()
        self.sib2.wait_recv()

    def finish(self):
        for copy in (self.y, self.sib, self.sib2):
            copy.wait_send()


class Share:
    sems = [pltpu.SemaphoreType.DMA((CHIPS,))] * 4 + [pltpu.SemaphoreType.DMA((2 * CHIPS,))] * 2

    def __init__(self, place, all_ref, *sems):
        self.place, self.all = place, all_ref
        self.s1, self.r1, self.s2, self.r2, self.s3, self.r3 = sems

    def slot(self, t, other):
        p = self.place
        return self.all.at[((1 - p.g) if other else p.g) * 16 + p.behind(t) * 2 + p.core]

    def ring(self, t):
        part = self.slot(t, 0)
        return remote(part, part, self.s1.at[t], self.r1.at[t], self.place.next)

    def y(self, t, back):
        part = self.slot(t, back)
        return remote(part, part, self.s2.at[t], self.r2.at[t], self.place.ynb)

    def to_sib(self, t, other):
        part = self.slot(t, other)
        n = t + CHIPS * other
        return remote(part, part, self.s3.at[n], self.r3.at[n], self.place.sib)

    def from_sib(self, t, other):
        p = self.place
        part = self.all.at[((1 - p.g) if other else p.g) * 16 + p.behind(-t) * 2 + 1 - p.core]
        n = t + CHIPS * other
        return remote(part, part, self.s3.at[n], self.r3.at[n], p.sib)

    def start(self):
        self.ring(0).start()
        self.y(0, 0).start()
        self.to_sib(0, 0).start()

    def pump(self, t):
        self.ring(t - 1).wait_recv()
        if t < CHIPS - 1:
            self.ring(t).start()
        self.y(t, 0).start()
        self.to_sib(t, 0).start()
        self.y(t - 1, 1).wait_recv()
        self.to_sib(t - 1, 1).start()

    def finish(self):
        self.y(CHIPS - 1, 1).wait_recv()
        self.to_sib(CHIPS - 1, 1).start()
        for t in range(CHIPS):
            for other in range(2):
                self.from_sib(t, other).wait_recv()
                self.to_sib(t, other).wait_send()
            self.y(t, 0).wait_send()
            if t < CHIPS - 1:
                self.ring(t).wait_send()


class Reduce:
    sems = [pltpu.SemaphoreType.DMA((CHIPS,))] * 6

    @staticmethod
    def bufs(rows, columns):
        return [VMEM((2, CHIPS, rows, columns), BF), VMEM((CHIPS, 2, rows, columns), BF)] + [
            VMEM((CHIPS, rows, columns), BF)] * 4

    def __init__(self, place, grads, bufs, sems):
        self.place, self.grads = place, grads
        self.own, self.sib_in, self.pair, self.y_in, self.out, self.held = bufs
        self.s1, self.r1, self.s2, self.r2, self.s3, self.r3 = sems

    def sib(self, chip):
        p = self.place
        return remote(self.grads.at[:, chip, 1 - p.core], self.sib_in.at[chip], self.s1.at[chip], self.r1.at[chip], p.sib)

    def y(self, chip):
        return remote(self.pair.at[chip], self.y_in.at[chip], self.s2.at[chip], self.r2.at[chip], self.place.ynb)

    def ring(self, t):
        return remote(self.out.at[t], self.held.at[t], self.s3.at[t], self.r3.at[t], self.place.next)

    def start(self):
        for chip in range(CHIPS):
            self.sib(chip).start()

    def pair_up(self, chip):
        other = 1 - self.place.g
        self.sib(chip).wait_recv()
        self.pair[chip] = (self.own[other, chip].astype(F32) + self.sib_in[chip, other].astype(F32)).astype(BF)
        self.y(chip).start()

    def term(self, t):
        p = self.place
        chip = p.behind(t + 1)
        self.y(chip).wait_recv()
        value = (self.own[p.g, chip].astype(F32) + self.sib_in[chip, p.g].astype(F32)) + self.y_in[chip].astype(F32)
        if t > 0:
            self.ring(t - 1).wait_recv()
            value = value + self.held[t - 1].astype(F32)
        return value

    def push(self, t):
        self.out[t] = self.term(t).astype(BF)
        self.ring(t).start()

    def finish(self):
        for chip in range(CHIPS):
            self.sib(chip).wait_send()
            self.y(chip).wait_send()
        for t in range(CHIPS - 1):
            self.ring(t).wait_send()


class Collect:
    order = tuple(range(1, CHIPS)) + (0,)
    sems = [pltpu.SemaphoreType.DMA((CHIPS,))] * 6

    @staticmethod
    def bufs(rows, columns):
        return [VMEM((CHIPS, 2, rows, columns), BF), VMEM((CHIPS, 2, rows, columns), BF),
                VMEM((CHIPS, rows, columns), BF), VMEM((CHIPS, rows, columns), BF)]

    def __init__(self, place, grads, own, got, bufs, sems):
        self.place, self.grads, self.own, self.got = place, grads, own, got
        self.sib_in, self.pair, self.y_in, self.total = bufs
        self.s1, self.r1, self.s2, self.r2, self.s3, self.r3 = sems

    def sib(self, n):
        p = self.place
        return remote(self.grads.at[:, (p.chip + n) % CHIPS, 1 - p.core], self.sib_in.at[n],
                      self.s1.at[n], self.r1.at[n], p.sib)

    def y(self, n):
        p = self.place
        return remote(self.pair.at[n, 1 - p.g], self.y_in.at[n], self.s2.at[n], self.r2.at[n], p.ynb)

    def across(self, n):
        p = self.place
        return remote(self.total.at[n], self.got.at[p.chip], self.s3.at[n], self.r3.at[n], p.off(n))

    def arrived(self, n):
        p = self.place
        return remote(self.total.at[n], self.got.at[p.src(n)], self.s3.at[n], self.r3.at[n], p.off(n))

    def start(self):
        for n in self.order:
            self.sib(n).start()

    def pair_up(self, m):
        p, n = self.place, self.order[m]
        self.sib(n).wait_recv()
        for g in range(2):
            self.pair[n, g] = (self.own(g, (p.chip + n) % CHIPS).astype(F32)
                               + self.sib_in[n, g].astype(F32)).astype(BF)
        self.y(n).start()

    def send(self, m):
        p, n = self.place, self.order[m]
        self.y(n).wait_recv()
        value = (self.pair[n, p.g].astype(F32) + self.y_in[n].astype(F32)).astype(BF)
        if n == 0:
            self.got[p.chip] = value
        else:
            self.total[n] = value
            self.across(n).start()

    def receive(self):
        for n in range(1, CHIPS):
            self.arrived(n).wait_recv()

    def finish(self):
        for n in range(CHIPS):
            self.sib(n).wait_send()
            self.y(n).wait_send()
            if n > 0:
                self.across(n).wait_send()


def dot(a, b):
    return lax.dot_general(a, b, (((1,), (0,)), ((), ())), preferred_element_type=F32)


def dot_nt(a, b):
    return lax.dot_general(a, b, (((1,), (1,)), ((), ())), preferred_element_type=F32)


def all_to_all_devices(place):
    return [place.off(i) for i in range(1, CHIPS)]


def call(body, outs, ins, scratch, collective_id, far_ins=(), far_outs=(), scalar_ins=(), flops=0, nbytes=0):
    kwargs = {}
    if collective_id is not None:
        kwargs = dict(collective_id=collective_id, has_side_effects=True)
    far = pl.BlockSpec(memory_space=pl.ANY)
    scalar = pl.BlockSpec(memory_space=pltpu.SMEM)
    return pl.pallas_call(
        body,
        out_shape=outs,
        in_specs=[far if n in far_ins else scalar if n in scalar_ins else VSPEC for n in range(len(ins))],
        out_specs=tuple(far if n in far_outs else VSPEC for n in range(len(outs))),
        scratch_shapes=scratch,
        compiler_params=pltpu.CompilerParams(vmem_limit_bytes=60 << 20, **kwargs),
        cost_estimate=pl.CostEstimate(flops=flops, bytes_accessed=nbytes, transcendentals=0),
    )(*ins)


class Moves:
    def __init__(self, sems, *pairs):
        self.copies = [pltpu.make_async_copy(a, b, sems.at[n]) for n, (a, b) in enumerate(pairs)]

    def start(self, *which):
        for n in which or range(len(self.copies)):
            self.copies[n].start()

    def wait(self, *which):
        for n in which or range(len(self.copies)):
            self.copies[n].wait()


def sds(*shape, dtype=BF):
    return jax.ShapeDtypeStruct(shape, dtype)


def rope(u, cosine, sine):
    return u * cosine + pltpu.roll(u, 64, 1) * sine


def make_tables(p, rows, starts):
    def fill(target, slots):
        entry = lax.broadcasted_iota(jnp.int32, slots.shape, 1)
        upper = entry >= 64
        entry = jnp.where(upper, entry - 64, entry)
        frequency = jnp.where(entry < HD // 2, jnp.exp(-math.log(rope_base) * (2.0 * entry.astype(F32) / HD)), 0.0)
        angles = slots.astype(F32) * frequency
        target[0] = jnp.cos(angles)
        target[1] = jnp.where(upper, 1.0, -1.0) * jnp.sin(angles)

    fill(rows, lax.broadcasted_iota(jnp.int32, (TOK, PAD), 0))
    fill(starts, (2 * lax.broadcasted_iota(jnp.int32, (CHIPS, PAD), 0) + p.core) * TOK)


def tables(rows, starts, i):
    c_row, s_row = rows[0], rows[1]
    c_start, s_start = starts[0, pl.ds(i, 1)], starts[1, pl.ds(i, 1)]
    return c_start * c_row - s_start * s_row, s_start * c_row + c_start * s_row


def limit_of(p, i, length):
    lane = lax.broadcasted_iota(jnp.int32, (1, 2 * TOK), 1)
    slot = jnp.where(lane < TOK, lane, lane - TOK) + (2 * i + p.core) * TOK
    return jnp.minimum(slot.astype(F32), length - 1.0)


def valid_of(p, first, rows, length):
    slot = lax.broadcasted_iota(jnp.int32, (rows, 1), 0) + p.s * TOK + first
    return jnp.where(slot.astype(F32) < length, 1.0, 0.0)


def spacing(heads=4):
    r = lax.broadcasted_iota(jnp.int32, (96 * heads, 128 * heads), 0)
    c = lax.broadcasted_iota(jnp.int32, (96 * heads, 128 * heads), 1)
    target = r
    for n in range(1, 2 * heads):
        target = target + jnp.where(r >= 48 * n, 16, 0)
    return jnp.where(target == c, 1.0, 0.0).astype(BF)


def chip_of_head(j):
    return 2 * (j % LINE) + j // LINE


def diagonal(n):
    return lax.broadcasted_iota(jnp.int32, (n, n), 0) == lax.broadcasted_iota(jnp.int32, (n, n), 1)


def to_column(row):
    n = row.shape[1]
    return jnp.sum(jnp.where(diagonal(n), jnp.broadcast_to(row, (n, n)), 0.0), axis=1, keepdims=True)


def to_row(column):
    n = column.shape[0]
    return jnp.sum(jnp.where(diagonal(n), jnp.broadcast_to(column, (n, n)), 0.0), axis=0, keepdims=True)


def norm_column(h):
    return lax.rsqrt(jnp.mean(h * h, axis=-1, keepdims=True) + epsilon)


def whole(ref):
    value = ref[...]
    return value.reshape(value.shape[0] * value.shape[1], value.shape[2])


LOG2E = 1.4426950408889634
SCALE = 1.0 / math.sqrt(96)
SCALE2 = SCALE * LOG2E


def scores_of(keys, query, limit, j):
    s = dot_nt(keys[j], query) * SCALE2
    pos = lax.broadcasted_iota(jnp.int32, s.shape, 0) + j * 256
    return jnp.where(pos.astype(F32) <= limit, s, neg_big)


def dot_tn(a, b):
    return lax.dot_general(a, b, (((0,), (0,)), ((), ())), preferred_element_type=F32)


def rows_of(k):
    return pl.ds(k * ROWS, ROWS)


def main_kernel(lengths, tokens, wq, wk, wv, gain_one, out_grad, wg, wu, gain_two, wo, wd,
                tg_out, wqkv_out, q_out, keys_out, values_out, mix_t_out, stat_out,
                hidden_out, grad_out, inner_out, dgu_out, dwd_out, rows_out, wdown_out, dwo_out,
                tg, wqkv, q, keys, values, mix_t, stat, grad, inner, dgu, dwd, grad_rows,
                rope_rows, rope_starts, slab, slab_gu, mix, vt, bgg, wall, wgu, wdown, mx, hid, x2, gub, low, rows_away, part, scale, out2, held2,
                ag_s, ag_r, s1, r1, s2, r2, s3, r3, bg_s, bg_r, g1, h1, o1, p1, o2, p2, o3, p3,
                mx_s, mx_r, rs2_s, rs2_r, away_s, away_r, ks, kr, vs, vr, q1, q2, q3, q4, local, local2, move_s):
    p = Place()
    gather = RingGather(p, tg, ag_s, ag_r)
    spread = Spread(p, slab, wqkv, local, s1, r1, s2, r2, s3, r3)
    gather_bg = RingGather(p, bgg, bg_s, bg_r)
    across = Across(p, slab_gu, wgu.at[p.g, :, p.core], local2, g1, h1)
    share = Share(p, wall, o1, p1, o2, p2, o3, p3)
    gather_mix = RingGather(p, mx, mx_s, mx_r)
    scatter2 = RingScatter(p, out2, held2, rs2_s, rs2_r)
    quarters = Quarters(p, lambda g, core: wgu.at[g, :, core], q1, q2)
    quarters2 = Quarters(p, lambda g, core: wdown.at[g, core], q3, q4)
    moves = Moves(move_s, (tg, tg_out), (wqkv, wqkv_out), (q, q_out), (keys, keys_out),
                  (values, values_out), (mix_t, mix_t_out), (stat, stat_out),
                  (hid.at[p.chip], hidden_out), (grad, grad_out), (inner, inner_out), (dgu, dgu_out), (dwd, dwd_out),
                  (grad_rows, rows_out), (wdown, wdown_out),
                  (wo, wall.at[p.g * 16 + p.s]), (wd, wdown.at[p.g, p.core]), (wall, dwo_out))
    moves.start(14, 15)
    length = lengths[0].astype(F32)
    tg[p.chip] = tokens[...]
    greet(all_to_all_devices(p) + [p.sib, p.ynb])
    gather.start()
    make_tables(p, rope_rows, rope_starts)
    space = spacing()
    gain_column = to_column(gain_one[...].astype(F32))
    gain_column2 = to_column(gain_two[...].astype(F32))
    for n in range(4):
        cols = pl.ds(n * 384, 384)
        wide = dot((wq[:, cols].astype(F32) * gain_column).astype(BF), space).astype(BF)
        for m in range(2):
            slab[chip_of_head(2 * n + m), :, pl.ds(0, 256)] = wide[:, m * 256:m * 256 + 256]
    for n in range(2):
        for source, place in ((wk, 256), (wv, 384)):
            wide = dot((source[:, pl.ds(n * 384, 384)].astype(F32) * gain_column).astype(BF), space).astype(BF)
            for m in range(4):
                slab[chip_of_head(4 * n + m), :, pl.ds(place, 128)] = wide[:, m * 128:m * 128 + 128]
    spread.start()
    bgg[p.chip] = (out_grad[...].astype(F32) * valid_of(p, 0, TOK, length)).astype(BF)
    gather.pump(1)
    for chip in range(CHIPS):
        for n, source in enumerate((wg, wu)):
            for g in range(2):
                slab_gu[chip, :, pl.ds(n * 512 + g * 256, 256)] = (
                    source[:, pl.ds(g * 2048 + chip * 256, 256)].astype(F32) * gain_column2).astype(BF)
    spread.pump(1)
    for t in range(2, CHIPS):
        gather.pump(t)
        spread.pump(t)
    moves.start(0)
    moves.wait(14, 15)
    gather_bg.start()
    share.start()
    across.start()
    quarters2.start()
    spread.finish()
    moves.start(1)

    def kv_copy(i, n):
        ref, send, recv = ((keys, ks, kr), (values, vs, vr))[n]
        part = ref.at[i, pl.ds(pl.multiple_of(p.core * TOK, TOK), TOK)]
        return remote(part, part, send.at[i], recv.at[i], p.sib)

    def kv_in(i, n):
        ref, send, recv = ((keys, ks, kr), (values, vs, vr))[n]
        part = ref.at[i, pl.ds(pl.multiple_of((1 - p.core) * TOK, TOK), TOK)]
        return remote(part, part, send.at[i], recv.at[i], p.sib)

    def project(i):
        h = tg[i].astype(F32)
        lin = dot((h * norm_column(h)).astype(BF), whole(wqkv))
        cosine, sine = tables(rope_rows, rope_starts, i)
        q[i, pl.ds(0, TOK)] = rope(lin[:, 0:128], cosine, sine).astype(BF)
        q[i, pl.ds(TOK, TOK)] = rope(lin[:, 128:256], cosine, sine).astype(BF)
        own = pl.ds(pl.multiple_of(p.core * TOK, TOK), TOK)
        keys[i, own] = rope(lin[:, 256:384], cosine, sine).astype(BF)
        values[i, own] = lin[:, 384:512].astype(BF)
        kv_copy(i, 0).start()
        kv_copy(i, 1).start()

    def attend(i):
        query = q[i]
        limit = limit_of(p, i, length)

        def chunk(j, state):
            top, total, acc = state
            s = scores_of(keys, query, limit, j)
            new_top = jnp.maximum(top, jnp.max(s, axis=0, keepdims=True))
            fade = jnp.exp2(top - new_top)
            w = jnp.exp2(s - new_top)
            total = total * fade + jnp.sum(w, axis=0, keepdims=True)
            acc = acc * fade + dot(vt[j], w.astype(BF))
            return new_top, total, acc

        start = (jnp.full((1, 256), neg_big, F32), jnp.zeros((1, 256), F32),
                 jnp.zeros((PAD, 256), F32))
        top, total, acc = lax.fori_loop(0, i + 1, chunk, start)
        acc = acc / total
        mix_t[i] = acc
        stat[i] = top + jnp.log2(total)
        low = acc.astype(BF)
        for n in range(4):
            mix[pl.ds(n * 48, 48), pl.ds(i * TOK, TOK)] = low[(n % 2) * 64:(n % 2) * 64 + 48,
                                                              (n // 2) * TOK:(n // 2) * TOK + TOK]

    for i in range(CHIPS):
        project(i)
        gather_bg.pump_some(i, i + 1)
    share.pump(1)
    for i in range(CHIPS):
        for n in range(2):
            kv_in(i, n).wait_recv()
        vt[i] = values[i].astype(F32).T.astype(BF)
    moves.start(2, 3, 4)
    done = CHIPS
    for i in range(CHIPS):
        attend(i)
        gather_bg.pump_some(done, done + (2 if i < 4 else 3))
        done += 2 if i < 4 else 3
        if 1 <= i < CHIPS - 1:
            share.pump(i + 1)
    moves.start(5, 6)
    mx[p.chip] = mix[...]
    gather_mix.start()
    across.land()
    quarters.start()
    share.finish()
    quarters2.pass_on()
    def head_of(chip):
        return chip // 2 + LINE * (chip % 2)

    def out_rows(chip):
        return whole(wall.at[pl.ds(4 * head_of(chip), 4)])

    def mixed(chip, b):
        lanes = pl.ds(pl.multiple_of(b * TOK, TOK), TOK)
        return dot_tn(mx[chip, :, lanes], out_rows(chip))

    def first(b, carry):
        hid[b] = tg[b].astype(F32) + mixed(p.chip, b)
        return carry

    lax.fori_loop(0, CHIPS, first, 0)
    def more(t, begin):
        def step(b, carry):
            hid[b] += mixed(p.behind(t), b)
            return carry

        lax.fori_loop(begin, begin + 2, step, 0)

    for t in range(1, CHIPS):
        for k in range(CHUNKS):
            gather_mix.pass_on(t, k)
            if t > 1:
                more(t - 1, 2 * k)
        if t == 5:
            quarters.pass_on()

    def feed(b):
        h = hid[b] + mixed(p.behind(CHIPS - 1), b)
        hid[b] = h
        r = norm_column(h)
        scale[...] = jnp.broadcast_to(r, (TOK, 128))
        x2[b] = (h * r).astype(BF)
        lin = dot(x2[b], wgu[...].reshape(1536, 1024))
        gate, up = lin[:, :512], lin[:, 512:]
        sigma = jax.nn.sigmoid(gate)
        act = gate * sigma
        inner[b] = (act * up).astype(BF)
        back = dot_nt(bgg[b], wdown[...].reshape(512, 1536))
        gub[b, :, pl.ds(0, 512)] = (back * up * (sigma + act * (1.0 - sigma))).astype(BF)
        gub[b, :, pl.ds(512, 512)] = (back * act).astype(BF)
        part[...] = dot_nt(gub[b], wgu[...].reshape(1536, 1024))

    quarters.arrive()
    quarters2.arrive()
    moves.start(13)
    for t in range(CHIPS):
        feed(scatter2.dest(t))
        if t < CHIPS - 1:
            scatter2.push(t, lambda k: part[rows_of(k)])
    moves.start(7)
    for k in range(CHUNKS):
        rows = rows_of(k)
        a = part[rows] + scatter2.last(k)
        h = hid[p.chip, rows]
        r = scale[rows, pl.ds(0, 1)]
        value = (bgg[p.chip, rows].astype(F32) + r * a
                 - h * (r * r * r) * jnp.mean(a * h, axis=-1, keepdims=True))
        grad[rows] = value
        low[rows] = value.astype(BF)

    def weight_part(n):
        if n < 12:
            cols = pl.ds(n * 128, 128)
            dgu[cols] = dot_tn(whole(x2.at[:, :, cols]), whole(gub)).astype(BF)
        else:
            cols = pl.ds((n - 12) * 128, 128)
            dwd[cols] = dot_tn(whole(inner.at[:, :, cols]), whole(bgg)).astype(BF)

    def away(i):
        return remote(rows_away.at[i], grad_rows.at[p.chip], away_s.at[i], away_r.at[i], p.off(i))

    def from_away(i):
        return remote(rows_away.at[i], grad_rows.at[p.src(i)], away_s.at[i], away_r.at[i], p.off(i))

    moves.start(8, 9)
    space2 = spacing(2)
    for i in tuple(range(1, CHIPS)) + (0,):
        rows = dot_nt(low[...], out_rows((p.chip + i) % CHIPS)).astype(BF)
        wide = dot(rows, space2).astype(BF)
        rows_away[i, pl.ds(0, TOK)] = wide[:, :PAD]
        rows_away[i, pl.ds(TOK, TOK)] = wide[:, PAD:]
        if i > 0:
            away(i).start()
    grad_rows[p.chip] = rows_away[0]
    lanes = pl.ds(pl.multiple_of(p.chip * TOK, TOK), TOK)
    for chip in range(CHIPS):
        value = dot(mx[chip, :, lanes], low[...]).astype(BF)
        for n in range(4):
            wall[4 * head_of(chip) + n] = value[48 * n:48 * n + 48]
    moves.start(16)
    for n in range(12):
        weight_part(n)
    moves.start(10)
    for n in range(12, 16):
        weight_part(n)
    moves.start(11)
    for i in range(1, CHIPS):
        from_away(i).wait_recv()
    moves.start(12)
    for i in range(1, CHIPS):
        away(i).wait_send()
    moves.wait(16)
    moves.wait(*range(14))
    for one in (gather, gather_bg, gather_mix, scatter2, quarters, quarters2):
        one.finish()
    across.sent()
    for i in range(CHIPS):
        for n in range(2):
            kv_copy(i, n).wait_send()


def main(*ins):
    dma = pltpu.SemaphoreType.DMA
    block = ((CHIPS, TOK, 1536), BF)
    heads = ((CHIPS, 2 * TOK, PAD), BF)
    shapes = (block, ((32, 48, 512), BF), heads, heads, heads, ((CHIPS, PAD, 256), F32), ((CHIPS, 1, 256), F32))
    shapes2 = (((TOK, 1536), F32), ((CHIPS, TOK, 512), BF), ((1536, 1024), BF), ((512, 1536), BF), heads)
    outs = shapes + (((TOK, 1536), F32),) + shapes2 + (((2, 2, TOK, 1536), BF), ((32, 48, 1536), BF))
    near = shapes + shapes2 + (
        ((2, TOK, PAD), F32), ((2, CHIPS, PAD), F32),
        ((CHIPS, 48, 512), BF), ((CHIPS, 48, 1024), BF), ((192, 1024), BF), ((CHIPS, PAD, 256), BF), block,
        ((32, 48, 1536), BF), ((2, CHIPS, 2, 48, 1024), BF), ((2, 2, TOK, 1536), BF), ((CHIPS, 192, 1024), BF),
        ((CHIPS, TOK, 1536), F32), block, ((CHIPS, TOK, 1024), BF), ((TOK, 1536), BF), heads, ((TOK, 1536), F32),
        ((TOK, 128), F32))
    return call(
        main_kernel,
        tuple(sds(*shape, dtype=kind) for shape, kind in outs),
        ins,
        [VMEM(shape, kind) for shape, kind in near] + RingScatter.bufs
        + RingGather.sems + Spread.sems + RingGather.sems + Across.sems + Share.sems + RingGather.sems + RingScatter.sems
        + [dma((CHIPS,))] * 6 + Quarters.sems * 2 + [dma, dma, dma((17,))],
        1, far_ins=(10, 11), far_outs=range(15), scalar_ins=(0,), flops=20 * 10**9, nbytes=40 << 20,
    )


def tail_kernel(q_in, keys_in, values_in, rows_in, mix_t_in, stat_in, inner_in, wdown_in, hidden_in, dgu_far, dwd_far,
                xg_in, wqkv_in, grad_in, lengths, dwo_far, tokens,
                result, input_back, got_gu, got_qkv, dout_sum, dwd_sum,
                rope_rows, rope_starts, q, keys, values, grad_rows, mix_t, stat, inner, wdown, hidden, dgu, dwd, xg, wqkv, grad,
                kt, dk, dv, dkv_low, dkv_in, back_out, dqkv, part, out, held, out2, held2,
                gu1, gu2, gu3, gu4, qk1, qk2, qk3, qk4, d_in, d_pair, d_y, wo1, wo2, wo3, wo4, wo5, wo6,
                rs_s, rs_r, rs2_s, rs2_r, a1, a2, a3, a4, a5, a6, c1, c2, c3, c4, c5, c6,
                ds, dr, xs, xr, o1, o2, o3, o4, o5, o6, move_s):
    p = Place()
    moves = Moves(move_s, (inner_in, inner), (wdown_in, wdown), (q_in, q), (keys_in, keys), (values_in, values),
                  (rows_in, grad_rows), (mix_t_in, mix_t), (stat_in, stat), (dgu_far.at[:, :, p.core], dgu),
                  (dwd_far.at[:, p.core], dwd), (hidden_in, hidden), (xg_in, xg), (wqkv_in, wqkv), (grad_in, grad),
                  (dwo_far.at[:, :, p.core], wo1))
    moves.start()
    length = lengths[0].astype(F32)
    greet(all_to_all_devices(p) + [p.sib, p.ynb])
    scatter = RingScatter(p, out, held, rs_s, rs_r)
    scatter2 = RingScatter(p, out2, held2, rs2_s, rs2_r)
    collect = Collect(p, dgu_far, lambda g, chip: dgu[g, chip], got_gu, (gu1, gu2, gu3, gu4), (a1, a2, a3, a4, a5, a6))
    collect2 = Collect(p, dqkv, lambda g, chip: dqkv[g, chip, p.core], got_qkv, (qk1, qk2, qk3, qk4),
                       (c1, c2, c3, c4, c5, c6))
    collect.start()
    fold = remote(dwd_far.at[:, 1 - p.core], d_in, ds.at[0], dr.at[0], p.sib)
    fold.start()
    y_fold = remote(d_pair.at[1 - p.g], d_y, ds.at[1], dr.at[1], p.ynb)
    reduce = Reduce(p, dwo_far, (wo1, wo2, wo3, wo4, wo5, wo6), (o1, o2, o3, o4, o5, o6))
    reduce.start()

    def branch(t):
        part[...] = dot(inner[scatter.dest(t)], wdown[...])
        if t < CHIPS - 1:
            scatter.push(t, lambda k: part[rows_of(k)])

    make_tables(p, rope_rows, rope_starts)
    moves.wait(0, 1)
    branch(0)
    moves.wait(*range(2, 10))

    def turn(n, carry):
        kt[n] = keys[n].astype(F32).T.astype(BF)
        dk[n] = jnp.zeros((256, PAD), F32)
        dv[n] = jnp.zeros((256, PAD), F32)
        return carry

    lax.fori_loop(0, CHIPS, turn, 0)

    def attend(i):
        query = q[i]
        limit = limit_of(p, i, length)
        do = grad_rows[i]
        lse = stat[i]
        delta = jnp.sum(do.astype(F32).T * mix_t[i], axis=0, keepdims=True)

        def chunk(j, acc):
            w = jnp.exp2(scores_of(keys, query, limit, j) - lse)
            dp = dot_nt(values[j], do)
            ds_low = (w * (dp - delta)).astype(BF)
            dk[j] += dot(ds_low, query)
            dv[j] += dot(w.astype(BF), do)
            return acc + dot(kt[j], ds_low)

        acc = lax.fori_loop(0, i + 1, chunk, jnp.zeros((PAD, 256), F32))
        dq = acc.T * SCALE
        cosine, sine = tables(rope_rows, rope_starts, i)
        sine = -sine
        back_out[i, :, pl.ds(0, PAD)] = rope(dq[:TOK], cosine, sine).astype(BF)
        back_out[i, :, pl.ds(PAD, PAD)] = rope(dq[TOK:], cosine, sine).astype(BF)

    def fold_pairs():
        fold.wait_recv()
        for n in range(2):
            d_pair[n] = (dwd[n].astype(F32) + d_in[n].astype(F32)).astype(BF)
        y_fold.start()

    for m in range(3):
        collect.pair_up(m)

    def again(b):
        h = xg[b].astype(F32)
        xg[b] = (h * norm_column(h)).astype(BF)

    moves.wait(11)
    for i in range(CHIPS):
        attend(i)
        again(i)
        if i < 5:
            collect.pair_up(i + 3)
        if 0 < i < CHIPS - 1:
            branch(i)
            collect.send(i - 1)
        if i == 4:
            fold_pairs()
            moves.wait(14)
        if i >= 4:
            reduce.pair_up(p.behind(2 * i - 7))
            reduce.pair_up(p.behind(2 * i - 6))
    collect.send(6)
    collect.send(7)
    for n in range(CHIPS):
        for c in range(2):
            rows = pl.ds(c * TOK, TOK)
            dkv_low[0, n, c] = dk[n, rows].astype(BF)
            dkv_low[1, n, c] = dv[n, rows].astype(BF)
    swap = remote(dkv_low.at[:, :, 1 - p.core], dkv_in, xs, xr, p.sib)
    swap.start()
    branch(CHIPS - 1)
    moves.wait(10, 12, 13)
    for k in range(CHUNKS):
        rows = rows_of(k)
        result[rows] = (valid_of(p, k * ROWS, ROWS, length)
                        * (hidden[rows] + part[rows] + scatter.last(k))).astype(BF)
    swap.wait_recv()

    def keys_back(n, carry):
        own = pl.ds(pl.multiple_of(p.core * TOK, TOK), TOK)
        cosine, sine = tables(rope_rows, rope_starts, n)
        back_out[n, :, pl.ds(2 * PAD, PAD)] = rope(
            (dk[n, own] + dkv_in[0, n].astype(F32)) * SCALE, cosine, -sine).astype(BF)
        back_out[n, :, pl.ds(3 * PAD, PAD)] = (dv[n, own] + dkv_in[1, n].astype(F32)).astype(BF)
        return carry

    lax.fori_loop(0, CHIPS, keys_back, 0)

    def weight_part(n):
        value = dot_tn(whole(xg.at[:, :, pl.ds(n * 384, 384)]), whole(back_out)).astype(BF)
        dqkv[n // 2, pl.ds((n % 2) * 4, 4)] = value.reshape(4, 2, 48, 512)

    for t in range(CHIPS):
        part[...] = dot_nt(back_out[scatter2.dest(t)], whole(wqkv))
        if t < CHIPS - 1:
            scatter2.push(t, lambda k: part[rows_of(k)])
        if t == 0:
            for n in range(4):
                weight_part(n)
            collect2.start()
        if 1 <= t <= 4:
            collect2.pair_up(2 * t - 2)
            collect2.pair_up(2 * t - 1)
        if 2 <= t <= 5:
            collect2.send(2 * t - 4)
            collect2.send(2 * t - 3)
        if t == 5:
            y_fold.wait_recv()
            dwd_sum[...] = (d_pair[p.g].astype(F32) + d_y[...].astype(F32)).astype(BF)
        if t == 6:
            collect.receive()
        if t < CHIPS - 1:
            reduce.push(t)
    dout_sum[...] = reduce.term(CHIPS - 1).astype(BF)
    for k in range(CHUNKS):
        rows = rows_of(k)
        c = part[rows] + scatter2.last(k)
        h = tokens[rows].astype(F32)
        r = norm_column(h)
        input_back[rows] = (grad[rows] + r * c
                            - h * (r * r * r) * jnp.mean(c * h, axis=-1, keepdims=True)).astype(BF)
    collect2.receive()
    collect.finish()
    collect2.finish()
    scatter.finish()
    scatter2.finish()
    reduce.finish()
    for copy in (fold, y_fold, swap):
        copy.wait_send()


def tail(*ins):
    dma = pltpu.SemaphoreType.DMA
    heads = (CHIPS, 2 * TOK, PAD)
    near = [VMEM((2, TOK, PAD), F32), VMEM((2, CHIPS, PAD), F32)] + [VMEM(heads, BF)] * 4 + [
        VMEM((CHIPS, PAD, 256), F32), VMEM((CHIPS, 1, 256), F32), VMEM((CHIPS, TOK, 512), BF), VMEM((512, 1536), BF),
        VMEM((TOK, 1536), F32), VMEM((2, CHIPS, 48, 1024), BF), VMEM((2, TOK, 1536), BF), VMEM((CHIPS, TOK, 1536), BF),
        VMEM((32, 48, 512), BF), VMEM((TOK, 1536), F32)]
    return call(
        tail_kernel,
        (sds(TOK, 1536), sds(TOK, 1536), sds(CHIPS, 48, 1024), sds(CHIPS, 48, 512), sds(48, 1536), sds(TOK, 1536)),
        ins,
        near + [VMEM((CHIPS, PAD, 256), BF), VMEM((CHIPS, 256, PAD), F32), VMEM((CHIPS, 256, PAD), F32),
         VMEM((2, CHIPS, 2, TOK, PAD), BF), VMEM((2, CHIPS, TOK, PAD), BF), VMEM((CHIPS, TOK, 4 * PAD), BF),
         VMEM((2, CHIPS, 2, 48, 512), BF), VMEM((TOK, 1536), F32)]
        + RingScatter.bufs * 2 + Collect.bufs(48, 1024) + Collect.bufs(48, 512)
        + [VMEM((2, TOK, 1536), BF), VMEM((2, TOK, 1536), BF), VMEM((TOK, 1536), BF)]
        + Reduce.bufs(48, 1536)
        + RingScatter.sems * 2 + Collect.sems * 2 + [dma((2,)), dma((2,)), dma, dma] + Reduce.sems + [dma((15,))],
        5, far_ins=tuple(range(14)) + (15,), scalar_ins=(14,), flops=10 * 10**9, nbytes=20 << 20,
    )


def place_kernel(got_gu_in, got_qkv_in, dout_in, dwd_in, block_in, back_in, wq_in, wk_in, wv_in, wg_in, wu_in, gain_one, gain_two,
                 block_out, back_out, d_gain_one, d_q_out, d_k_out, d_v_out, d_out_out, d_gain_two, d_gate_out, d_up_out,
                 d_down_out,
                 got_gu, got_qkv, dout, dwd, wq, wk, wv, wg, wu, d_q, d_k, d_v, d_out, d_gate, d_up, d_down, block, back, move_s):
    moves = Moves(move_s, (wg_in, wg), (wu_in, wu), (got_gu_in, got_gu), (dwd_in, dwd), (dout_in, dout),
                  (got_qkv_in, got_qkv), (wq_in, wq), (wk_in, wk), (wv_in, wv), (block_in, block), (back_in, back),
                  (d_gate, d_gate_out), (d_up, d_up_out), (d_down, d_down_out), (d_out, d_out_out), (d_q, d_q_out),
                  (d_k, d_k_out), (d_v, d_v_out), (block, block_out), (back, back_out))
    moves.start(0, 1, 2, 9, 10, 3, 4, 5, 6, 7, 8)
    space = spacing()
    gain_column = to_column(gain_one[...].astype(F32))
    gain_column2 = to_column(gain_two[...].astype(F32))
    lanes = lambda v: jnp.sum(v, axis=-1, keepdims=True)
    moves.wait(0, 1, 2)
    total = jnp.zeros((48, 256), F32)
    for n, (target, weight) in enumerate(((d_gate, wg), (d_up, wu))):
        for chip in range(CHIPS):
            for g in range(2):
                cols = pl.ds(g * 2048 + chip * 256, 256)
                piece = got_gu[chip, :, pl.ds(n * 512 + g * 256, 256)].astype(F32)
                target[:, cols] = piece * gain_column2
                total = total + piece * weight[:, cols].astype(F32)
        moves.start(11 + n)
    d_gain_two[...] = to_row(lanes(total))
    moves.wait(3, 4)
    d_down[...] = dwd[...].astype(F32)
    moves.start(13)
    d_out[...] = dout[...].astype(F32)
    moves.start(14)
    moves.wait(9, 10)
    moves.start(18, 19)
    moves.wait(5, 6, 7, 8)
    total = jnp.zeros((48, 1), F32)
    for n in range(4):
        cols = pl.ds(n * 384, 384)
        wide = jnp.concatenate([got_qkv[chip_of_head(2 * n + m), :, pl.ds(0, 256)] for m in range(2)], axis=-1)
        value = dot_nt(wide, space)
        total = total + lanes(value * wq[:, cols].astype(F32))
        d_q[:, cols] = value * gain_column
    moves.start(15)
    for n in range(2):
        cols = pl.ds(n * 384, 384)
        for source, target, place in ((wk, d_k, 256), (wv, d_v, 384)):
            wide = jnp.concatenate([got_qkv[chip_of_head(4 * n + m), :, pl.ds(place, 128)] for m in range(4)], axis=-1)
            value = dot_nt(wide, space)
            total = total + lanes(value * source[:, cols].astype(F32))
            target[:, cols] = value * gain_column
    moves.start(16, 17)
    d_gain_one[...] = to_row(total)
    moves.wait(*range(11, 20))


def place_all(*ins):
    f = lambda *shape: sds(*shape, dtype=F32)
    near = (((CHIPS, 48, 1024), BF), ((CHIPS, 48, 512), BF), ((48, 1536), BF), ((TOK, 1536), BF), ((48, 1536), BF),
            ((48, 768), BF), ((48, 768), BF), ((48, 4096), BF), ((48, 4096), BF), ((48, 1536), F32), ((48, 768), F32),
            ((48, 768), F32), ((48, 1536), F32), ((48, 4096), F32), ((48, 4096), F32), ((TOK, 1536), F32), ((TOK, 1536), BF), ((TOK, 1536), BF))
    return call(
        place_kernel,
        (sds(TOK, 1536), sds(TOK, 1536), f(1, 48), f(48, 1536), f(48, 768), f(48, 768), f(48, 1536), f(1, 48), f(48, 4096),
         f(48, 4096), f(TOK, 1536)),
        ins, [VMEM(shape, kind) for shape, kind in near] + [pltpu.SemaphoreType.DMA((20,))], None,
        far_ins=range(11), far_outs=(0, 1, 3, 4, 5, 6, 8, 9, 10), nbytes=10 << 20,
    )


def plane_device(hidden_in, lengths, attn_gain, w_query, w_key, w_value, w_out, mlp_gain, w_gate, w_up,
                 w_down, out_grad):
    gain_one = attn_gain[None]
    gain_two = mlp_gain[None]
    tokens = hidden_in[0]
    tg, wqkv, q, keys, values, mix_t, stat, hidden, grad, inner, dgu, dwd, grad_rows, wdown, dwo = main(
        lengths, tokens, w_query, w_key, w_value, gain_one, out_grad[0],
        w_gate, w_up, gain_two, w_out, w_down)
    block, back, got_gu, got_qkv, dout_sum, dwd_sum = tail(
        q, keys, values, grad_rows, mix_t, stat, inner, wdown.reshape(512, 1536), hidden,
        dgu.reshape(2, CHIPS, 2, 48, 1024), dwd.reshape(2, 2, TOK, 1536), tg, wqkv, grad,
        lengths, dwo.reshape(2, CHIPS, 2, 48, 1536), tokens)
    block, back, d_gain_one, d_q, d_k, d_v, d_out, d_gain_two, d_gate, d_up, d_down = place_all(
        got_gu, got_qkv, dout_sum, dwd_sum, block, back, w_query, w_key, w_value, w_gate, w_up, gain_one, gain_two)
    return (block[None], back[None], d_gain_one[0], d_q, d_k, d_v, d_out, d_gain_two[0], d_gate, d_up, d_down)


def solution(mesh):
    placed = (
        P("grp", "seq", None),
        P("grp"),
        P(("grp", "seq")),
        P(("grp", "seq"), None),
        P(("grp", "seq"), None),
        P(("grp", "seq"), None),
        P(("grp", "seq"), None),
        P(("grp", "seq")),
        P(("grp", "seq"), None),
        P(("grp", "seq"), None),
        P(("grp", "seq"), None),
        P("grp", "seq", None),
    )
    small = mesh.shape["grp"] == 2 and mesh.shape["seq"] == 2 * CHIPS
    return jax.shard_map(
        plane_device if small else per_device,
        mesh=mesh,
        in_specs=placed,
        out_specs=(
            P("grp", "seq", None),
            P("grp", "seq", None),
            P(("grp", "seq")),
            P(("grp", "seq"), None),
            P(("grp", "seq"), None),
            P(("grp", "seq"), None),
            P(("grp", "seq"), None),
            P(("grp", "seq")),
            P(("grp", "seq"), None),
            P(("grp", "seq"), None),
            P(("grp", "seq"), None),
        ),
        check_vma=False,
    )
```
